32 devices in a mesh: dp: 16 (over z, y, core), seq: 2 (over x).
Axes of the slice: x: 2, y: 2, z: 4, core: 2. Of those that a mesh axis runs over, the one named last changes fastest.
Arguments:
- tokens: bfloat16 [2, 16, 1408, 1280], P(None, 'dp', 'seq'), may hold values from -6 to 6
- cotangent: bfloat16 [2, 16, 1408, 1280], P(None, 'dp', 'seq'), may hold values from -6 to 6
- parents: int32 [2, 16, 44], P(None, 'dp'), may hold values from 0 to 43, as said below
- owners: int32 [122], replicated, may hold values from 0 to 15, as said below
- weight_store: float32 [256, 64, 1280], P('dp')
- gain_store: float32 [32, 1280], P('dp'), may hold values from 0.5 to 1.5
- weight_first: float32 [256, 64, 1280], P('dp')
- gain_first: float32 [32, 1280], P('dp'), may hold values from -1280 to 1280
- weight_second: float32 [256, 64, 1280], P('dp')
- gain_second: float32 [32, 1280], P('dp'), may hold values from 22528 to 360448
Outputs:
- mixed: bfloat16 [2, 16, 1408, 1280], P(None, 'dp', 'seq')
- token_grad: bfloat16 [2, 16, 1408, 1280], P(None, 'dp', 'seq')
- weight_new: float32 [256, 64, 1280], P('dp')
- gain_new: float32 [32, 1280], P('dp')
- weight_first_new: float32 [256, 64, 1280], P('dp')
- gain_first_new: float32 [32, 1280], P('dp')
- weight_second_new: float32 [256, 64, 1280], P('dp')
- gain_second_new: float32 [32, 1280], P('dp')
- weight_copies: bfloat16 [6, 1280, 1280], replicated
- gain_copies: bfloat16 [2, 1280], replicated
The draws below stay inside these ranges and needn't reach their ends.
Inputs may be any that keep to these rules, and one draw needn't show every extreme that they name: `parents`: in every tree, segments 0 to 31 form the trunk: segment 0 is its own parent and each other trunk segment has the one before it as parent. The other 12 segments are 4 branches, each with a parent among trunk segments 32 // 2 to 31, and 8 leaves, two with each branch as parent. The last segment is always a branch; which of the others are branches and which are leaves is drawn from the seed. No index of dp owns more than 16 of the first 120 entries, and one owns exactly 16 in every draw; the last two entries are the owners of g1 and g2.
All inputs are finite; a program needn't handle non-finite values.
Results may differ from the reference program's by a relative error of at most 0.015.
Values may be sent and summed in bfloat16 or wider, within the bound.
A program may use at most 640 MiB of HBM per device.

```python
import math
import jax
import jax.numpy as jnp
from jax import lax

D = 1280
HEADS = 16
HEAD = 80
SEG = 32
TRUNK_SEGS = 32
MICRO = 2
STEP = 7
PIECE = 64
NSEG = 44
TREE_TOK = 1408
TREES = 16
TOKENS_ALL = 45056
PIECES = 120
SLOT_DEV = 16
SLOTS = 256
GAIN_SLOTS = 32


def single_tree(tree_key):
    order_key, attach_key = jax.random.split(tree_key)
    trunk = jnp.arange(TRUNK_SEGS, dtype=jnp.int32)
    trunk_parents = jnp.maximum(trunk - 1, 0)
    shuffled = jax.random.permutation(order_key, 11).astype(jnp.int32)
    last_slot = jnp.full((1,), 11, jnp.int32)
    slots = jnp.concatenate([shuffled[:3], last_slot, shuffled[3:]])
    attach = jax.random.randint(attach_key, (4,), TRUNK_SEGS // 2, TRUNK_SEGS).astype(jnp.int32)
    branch_slots = slots[:4]
    leaf_slots = slots[4:]
    leaf_parents = jnp.repeat(branch_slots + TRUNK_SEGS, 2)
    others = jnp.zeros((12,), jnp.int32).at[branch_slots].set(attach).at[leaf_slots].set(leaf_parents)
    return jnp.concatenate([trunk_parents, others])


def draw_parents(key, part):
    key = jax.random.fold_in(key, 11)
    tree_keys = jax.random.split(key, MICRO * TREES)
    return jax.vmap(single_tree)(tree_keys).reshape(MICRO, TREES, TRUNK_SEGS + 12).astype(jnp.int32)


def owner_list(key):
    order_key, device_key, gain_key = jax.random.split(key, 3)
    device_count = SLOTS // SLOT_DEV
    share = SLOT_DEV // 2
    labels = jnp.arange(PIECES, dtype=jnp.int32)
    group = jnp.where(labels < SLOT_DEV, 0, 1 + (labels - SLOT_DEV) // share).astype(jnp.int32)
    devices = jax.random.permutation(device_key, device_count).astype(jnp.int32)
    placed = devices[group]
    shuffled = jax.random.permutation(order_key, PIECES).astype(jnp.int32)
    piece_owner = placed[shuffled]
    gain_owner = jax.random.randint(gain_key, (2,), 0, device_count).astype(jnp.int32)
    return jnp.concatenate([piece_owner, gain_owner]).astype(jnp.int32)


def slot_kinds(owners):
    piece_owner = owners[:PIECES]
    labels = jnp.arange(PIECES, dtype=jnp.int32)
    same = (piece_owner[:, None] == piece_owner[None, :]) & (labels[None, :] < labels[:, None])
    rank = jnp.sum(same.astype(jnp.int32), axis=1).astype(jnp.int32)
    piece_slot = piece_owner * SLOT_DEV + rank
    kinds = labels // (D // PIECE)
    return jnp.zeros((SLOTS,), jnp.int32).at[piece_slot].set(kinds)


def draw_owners(key, part):
    return owner_list(key)


def kind_table(values):
    return jnp.array(values, jnp.float32)


def draw_weight_store(key, part):
    kinds = slot_kinds(owner_list(key))
    key = jax.random.fold_in(key, 21)
    matrix_scale = D ** (-0.5)
    out_scale = max(D * 4 // TREE_TOK, 1) ** (-0.5)
    table = kind_table([matrix_scale, matrix_scale, matrix_scale, out_scale, matrix_scale, matrix_scale])
    noise = jnp.clip(jax.random.normal(key, (SLOTS, PIECE, D), jnp.float32), -6.0, 6.0)
    return noise * table[kinds][:, None, None]


def draw_weight_first(key, part):
    kinds = slot_kinds(owner_list(key))
    key = jax.random.fold_in(key, 22)
    qkv_scale = (0.5 * TOKENS_ALL) ** 0.5
    out_scale = (3.0 * TOKENS_ALL / TREE_TOK) ** 0.5
    mlp_scale = (0.36 * TOKENS_ALL) ** 0.5
    table = kind_table([qkv_scale, qkv_scale, qkv_scale, out_scale, mlp_scale, mlp_scale])
    noise = jnp.clip(jax.random.normal(key, (SLOTS, PIECE, D), jnp.float32), -6.0, 6.0)
    return noise * table[kinds][:, None, None]


def draw_weight_second(key, part):
    kinds = slot_kinds(owner_list(key))
    key = jax.random.fold_in(key, 23)
    qkv_low = 0.25 * TOKENS_ALL
    out_low = 1.5 * TOKENS_ALL / TREE_TOK
    mlp_low = 0.18 * TOKENS_ALL
    table = kind_table([qkv_low, qkv_low, qkv_low, out_low, mlp_low, mlp_low])
    spread = jax.random.uniform(key, (SLOTS, PIECE, D), jnp.float32)
    return table[kinds][:, None, None] * jnp.exp(spread * jnp.log(16.0))


def block_scale(key, dims, cuts, smallest, top_value):
    def one(dim, blocks):
        heights = jax.random.uniform(jax.random.fold_in(jax.random.fold_in(key, 6), dim), (blocks,), jnp.float32, smallest / len(cuts), top_value / len(cuts))
        return jnp.repeat(jnp.exp(heights), dims[dim] // blocks).reshape((-1,) + (1,) * (len(dims) - dim - 1))

    gain = one(*cuts[0])
    for cut in cuts[1:]:
        gain = gain * one(*cut)
    return gain


def gaussian(stream_key, extent, width, bound, cuts=(), held_as=jnp.bfloat16):
    gain = block_scale(stream_key, extent, cuts, -0.22, 0.18) if cuts else 1.0
    entries = jax.random.normal(stream_key, extent, jnp.float32) * width * gain
    return jnp.minimum(jnp.maximum(entries, -bound), bound).astype(held_as)


def setup_inputs(seed: int = 0) -> dict:
    streams_of = jax.random.split(jax.random.key(seed), 11)
    tokens = gaussian(streams_of[0], (MICRO, TREES, TREE_TOK, D), 1.0, 6.0, ((1, 16), (2, 2)))
    cotangent = gaussian(streams_of[1], (MICRO, TREES, TREE_TOK, D), 1.0, 6.0, ((1, 16), (2, 2)))
    parents = draw_parents(jax.random.fold_in(streams_of[10], 71), 0)
    owners = draw_owners(jax.random.fold_in(streams_of[10], 71), 0)
    weight_store = draw_weight_store(jax.random.fold_in(streams_of[10], 71), 0)
    gain_store = jnp.clip(1.0 + 0.1 * jax.random.normal(streams_of[5], (GAIN_SLOTS, D), jnp.float32), 0.5, 1.5)
    weight_first = draw_weight_first(jax.random.fold_in(streams_of[10], 71), 0)
    gain_first = gaussian(streams_of[7], (GAIN_SLOTS, D), ((1.0 * TOKENS_ALL) ** 0.5), 1280.0, ((0, 16),), jnp.float32)
    weight_second = draw_weight_second(jax.random.fold_in(streams_of[10], 71), 0)
    gain_second = jnp.clip(jnp.exp(math.log(360448.0) - 2.7725887 * jax.random.uniform(streams_of[9], (GAIN_SLOTS, D), jnp.float32) ** block_scale(streams_of[9], (GAIN_SLOTS, D), ((0, 16),), -0.2, 0.2)), 22528.0, 360448.0)
    return dict(tokens=tokens, cotangent=cotangent, parents=parents, owners=owners, weight_store=weight_store, gain_store=gain_store, weight_first=weight_first, gain_first=gain_first, weight_second=weight_second, gain_second=gain_second)


@jax.custom_vjp
def low(v):
    return lax.optimization_barrier(v.astype(jnp.bfloat16)).astype(jnp.float32)

@jax.custom_vjp
def low_back(v):
    return v

def low_keep(v):
    return (low(v), None)

def low_pass(kept, grad):
    return (grad,)

def back_keep(v):
    return (v, None)

def back_low(kept, grad):
    return (low(grad),)
low.defvjp(low_keep, low_pass)
low_back.defvjp(back_keep, back_low)
NORM_EPS = 1e-06
BETA_ONE = 0.5
BETA_TWO = 0.5
ADAM_EPS = 1e-08
MATRIX_DECAY = 0.1
RATE_QKV = 0.03
RATE_OUT = 0.4
RATE_GAIN = 0.4
HIGHEST = lax.Precision.HIGHEST
MASKED = -1e+30

def owner_slots(owners, slot_dev):
    count = owners.shape[0] - 2
    piece_owner = owners[:count]
    labels = jnp.arange(count, dtype=jnp.int32)
    same = (piece_owner[:, None] == piece_owner[None, :]) & (labels[None, :] < labels[:, None])
    rank = lax.optimization_barrier(jnp.sum(same.astype(jnp.int32), axis=1)).astype(jnp.int32)
    piece_slot = (piece_owner * slot_dev + rank).astype(jnp.int32)
    gain_slot = (owners[count:] * 2 + jnp.arange(2, dtype=jnp.int32)).astype(jnp.int32)
    return (piece_slot, gain_slot)

def ancestors(parent_ids):
    segment_count = parent_ids.shape[0]
    labels = jnp.arange(segment_count, dtype=jnp.int32)
    table = ((labels[None, :] == labels[:, None]) | (labels[None, :] == parent_ids[:, None])).astype(jnp.float32)
    for repeat in range(segment_count.bit_length()):
        table = jnp.minimum(jnp.dot(table, table, precision=HIGHEST), 1.0)
    return table

def rms_scale(values):
    return lax.rsqrt(lax.optimization_barrier(jnp.mean(values * values, axis=-1, keepdims=True)) + NORM_EPS)

def tree_forward(inputs, parent_ids, w_query, w_key, w_value, w_out, w_up, w_down, gain_one, gain_two):
    length = inputs.shape[0]
    table = ancestors(parent_ids)
    position = jnp.arange(length, dtype=jnp.int32)
    segment = position // SEG
    reach = table[segment][:, segment] > 0.5
    allowed = reach & ((segment[:, None] != segment[None, :]) | (position[None, :] <= position[:, None]))
    normed = low(inputs * rms_scale(inputs) * gain_one)
    queries = low_back(low(jnp.dot(normed, w_query, precision=HIGHEST)))
    keys_all = low_back(low(jnp.dot(normed, w_key, precision=HIGHEST)))
    values_all = low_back(low(jnp.dot(normed, w_value, precision=HIGHEST)))
    query_heads = queries.reshape(length, HEADS, HEAD)
    key_heads = keys_all.reshape(length, HEADS, HEAD)
    value_heads = values_all.reshape(length, HEADS, HEAD)
    raw = low_back(jnp.einsum('qhd,khd->hqk', query_heads, key_heads, precision=HIGHEST))
    scores = jnp.where(allowed[None], raw * HEAD ** (-0.5), MASKED)
    top = lax.optimization_barrier(jnp.max(scores, axis=-1, keepdims=True))
    lse = top + jnp.log(lax.optimization_barrier(jnp.sum(jnp.exp(scores - top), axis=-1, keepdims=True)))
    probs = low(jnp.exp(scores - lse))
    attended = jnp.einsum('hqk,khd->qhd', probs, value_heads, precision=HIGHEST).reshape(length, D)
    attended = low_back(low(attended))
    hidden_one = inputs + low_back(jnp.dot(attended, w_out, precision=HIGHEST))
    normed_two = low(hidden_one * rms_scale(hidden_one) * gain_two)
    up_rows = low_back(jnp.dot(normed_two, w_up, precision=HIGHEST))
    activated = low(jax.nn.silu(up_rows))
    return hidden_one + jnp.dot(activated, w_down, precision=HIGHEST)

def adam_update(master, first, second, grad, rate, decay):
    first_new = BETA_ONE * first + (1.0 - BETA_ONE) * grad
    second_new = BETA_TWO * second + (1.0 - BETA_TWO) * grad * grad
    fix_one = 1.0 - BETA_ONE ** STEP
    fix_two = 1.0 - BETA_TWO ** STEP
    step_size = first_new / fix_one / (jnp.sqrt(second_new / fix_two) + ADAM_EPS)
    return (master - rate * (step_size + decay * master), first_new, second_new)

def reference(tokens, cotangent, parents, owners, weight_store, gain_store, weight_first, gain_first, weight_second, gain_second):
    count = MICRO * TREES
    piece_slot, gain_slot = owner_slots(owners, SLOT_DEV)
    matrices = weight_store[piece_slot].reshape(6, D, D)
    gains = gain_store[gain_slot]
    flat_inputs = tokens.astype(jnp.float32).reshape(count, TREE_TOK, D)
    flat_parents = parents.reshape(count, NSEG)
    flat_cot = cotangent.astype(jnp.float32).reshape(count, TREE_TOK, D)

    def forward(inputs_all, mats, gain_rows):
        mat_low = low(mats)
        gain_low = low(gain_rows)
        checked = jax.checkpoint(tree_forward)

        def visit(carry, item):
            tree_inputs, tree_parents = item
            result = checked(tree_inputs, tree_parents, mat_low[0], mat_low[1], mat_low[2], mat_low[3], mat_low[4], mat_low[5], gain_low[0], gain_low[1])
            return (carry, result)
        unused, outputs = lax.scan(visit, jnp.zeros((), jnp.float32), (inputs_all, flat_parents))
        return outputs
    outputs, pullback = jax.vjp(forward, flat_inputs, matrices, gains)
    input_grad, mat_grad, gain_grad = pullback(flat_cot)
    slot_grad = jnp.zeros((SLOTS, PIECE, D), jnp.float32).at[piece_slot].set(mat_grad.reshape(PIECES, PIECE, D))
    gain_slot_grad = jnp.zeros((GAIN_SLOTS, D), jnp.float32).at[gain_slot].set(gain_grad)
    kinds = jnp.arange(PIECES, dtype=jnp.int32) // (D // PIECE)
    rate_piece = jnp.where(kinds == 3, RATE_OUT, RATE_QKV).astype(jnp.float32)
    slot_rate = jnp.full((SLOTS,), RATE_QKV, jnp.float32).at[piece_slot].set(rate_piece)
    weight_new, weight_first_new, weight_second_new = adam_update(weight_store, weight_first, weight_second, slot_grad, slot_rate[:, None, None], MATRIX_DECAY)
    gain_new, gain_first_new, gain_second_new = adam_update(gain_store, gain_first, gain_second, gain_slot_grad, RATE_GAIN, 0.0)
    weight_copies = weight_new[piece_slot].reshape(6, D, D).astype(jnp.bfloat16)
    gain_copies = gain_new[gain_slot].astype(jnp.bfloat16)
    mixed = outputs.reshape(tokens.shape).astype(jnp.bfloat16)
    token_grad = input_grad.reshape(tokens.shape).astype(jnp.bfloat16)
    return (mixed, token_grad, weight_new, gain_new, weight_first_new, gain_first_new, weight_second_new, gain_second_new, weight_copies, gain_copies)
```

```python
import functools

import jax
import jax.numpy as jnp
from jax import lax
from jax.experimental import pallas as pl
from jax.experimental.pallas import tpu as pltpu
from jax.sharding import Mesh
from jax.sharding import PartitionSpec as P

HEAD = 80
SEG = 32
TRUNK_SEGS = 32
ALWAYS_SEGS = TRUNK_SEGS // 2
STEP = 7
LANES = 128
WINDOW = 256
QUERY_BLOCK = 256

NORM_EPS = 1e-06
BETA_ONE = 0.5
BETA_TWO = 0.5
ADAM_EPS = 1e-08
MATRIX_DECAY = 0.1
RATE_QKV = 0.03
RATE_OUT = 0.4
RATE_GAIN = 0.4
MASKED = -1e30
SCALE = HEAD**-0.5
LOG2E = 1.4426950408889634
ALL = ("chip", "core", "seq")
NT = (((1,), (1,)), ((), ()))
TN = (((0,), (0,)), ((), ()))


def transposed(value):
    chips = lax.axis_size("chip")
    pairs = [(k * 4 + c * 2 + 1 - c, k * 4 + 2 - 2 * c + c) for k in range(chips) for c in range(2)]
    moved = lax.ppermute(value, ALL, pairs)
    return jnp.where(lax.axis_index("core") == lax.axis_index("seq"), value, moved)


def partner(value):
    return lax.ppermute(value, "core", [(0, 1), (1, 0)])


def owner_slots(owners, slot_dev):
    count = owners.shape[0] - 2
    piece_owner = owners[:count]
    labels = jnp.arange(count, dtype=jnp.int32)
    same = (piece_owner[:, None] == piece_owner[None, :]) & (labels[None, :] < labels[:, None])
    rank = jnp.sum(same.astype(jnp.int32), axis=1)
    return (piece_owner, rank)


def tail_limits(parents):
    up = parents[:, TRUNK_SEGS:]
    leaf = up >= TRUNK_SEGS
    above = jnp.where(leaf, up - TRUNK_SEGS, 0)
    labels = jnp.arange(up.shape[1], dtype=jnp.int32)
    hot = above[:, :, None] == labels[None, None, :]
    upper = jnp.sum(jnp.where(hot, up[:, None, :], 0), axis=2)
    attach = jnp.where(leaf, upper, up)
    limit = (attach + 1) * SEG
    branch = jnp.where(leaf, above, -1)
    return (jnp.repeat(limit, SEG, axis=1), jnp.repeat(branch, SEG, axis=1))


def query_blocks(length):
    trunk = TRUNK_SEGS * SEG
    blocks = []
    for first in range(0, trunk, QUERY_BLOCK):
        parts = [(0, first, "all")] if first else []
        blocks.append((first, QUERY_BLOCK, parts + [(first, QUERY_BLOCK, "causal")]))
    always = ALWAYS_SEGS * SEG
    tail = length - trunk
    blocks.append(
        (trunk, tail, [(0, always, "all"), (always, trunk - always, "trunk"), (trunk, tail, "tail")])
    )
    return blocks


def allowed_pairs(kind, key_first, key, query, limit, branch):
    if kind == "causal":
        return key <= query
    if kind == "trunk":
        return key + key_first < limit
    key_seg = key // SEG
    return ((key_seg == query // SEG) & (key <= query)) | (key_seg == branch)


def head_window(head, width):
    start = pl.multiple_of(
        jnp.minimum((head * HEAD) // LANES, width // LANES - WINDOW // LANES) * LANES, LANES
    )
    lane = lax.broadcasted_iota(jnp.int32, (1, WINDOW), 1) + start
    mine = (lane >= head * HEAD) & (lane < (head + 1) * HEAD)
    return (pl.ds(start, WINDOW), mine)


def attend_kernel(limit_ref, branch_ref, q_ref, k_ref, v_ref, out_ref, lse_ref):
    head = pl.program_id(1)
    window, mine = head_window(head, q_ref.shape[2])
    stat_lane = lax.broadcasted_iota(jnp.int32, (1, LANES), 1)
    for first, count, parts in query_blocks(q_ref.shape[1]):
        rows = pl.ds(first, count)
        query = jnp.where(mine, q_ref[0, rows, window], 0)
        scores = []
        for key_first, keys, kind in parts:
            raw = lax.dot_general(
                query, k_ref[0, pl.ds(key_first, keys), window], NT, preferred_element_type=jnp.float32
            ) * (SCALE * LOG2E)
            if kind != "all":
                ok = allowed_pairs(
                    kind,
                    key_first,
                    lax.broadcasted_iota(jnp.int32, (count, keys), 1),
                    lax.broadcasted_iota(jnp.int32, (count, keys), 0),
                    limit_ref[0],
                    branch_ref[0],
                )
                raw = jnp.where(ok, raw, MASKED)
            scores.append(raw)
        top = functools.reduce(jnp.maximum, [jnp.max(s, axis=1, keepdims=True) for s in scores])
        total = 0.0
        gained = 0.0
        for raw, (key_first, keys, kind) in zip(scores, parts):
            weight = jnp.exp2(raw - top)
            total = total + jnp.sum(weight, axis=1, keepdims=True)
            gained = gained + jnp.dot(
                weight.astype(jnp.bfloat16),
                v_ref[0, pl.ds(key_first, keys), window],
                preferred_element_type=jnp.float32,
            )
        gained = (gained / total).astype(jnp.bfloat16)
        out_ref[0, rows, window] = jnp.where(mine, gained, out_ref[0, rows, window])
        lse_ref[0, rows, :] = jnp.where(
            stat_lane == head, top + jnp.log2(total), lse_ref[0, rows, :]
        )


def attend(qkv, limit, branch):
    micro, length, columns = qkv.shape
    width = columns // 3
    heads = width // HEAD
    tail = length - TRUNK_SEGS * SEG

    def part(index):
        return pl.BlockSpec((1, length, width), lambda m, h, index=index: (m, 0, index))

    column = pl.BlockSpec((1, tail, 1), lambda m, h: (m, 0, 0))
    return pl.pallas_call(
        attend_kernel,
        grid=(micro, heads),
        in_specs=[column, column, part(0), part(1), part(2)],
        out_specs=[
            pl.BlockSpec((1, length, width), lambda m, h: (m, 0, 0)),
            pl.BlockSpec((1, length, LANES), lambda m, h: (m, 0, 0)),
        ],
        out_shape=[
            jax.ShapeDtypeStruct((micro, length, width), jnp.bfloat16),
            jax.ShapeDtypeStruct((micro, length, LANES), jnp.float32),
        ],
        compiler_params=pltpu.CompilerParams(vmem_limit_bytes=48 << 20),
        cost_estimate=pl.CostEstimate(
            flops=micro * heads * length * length * WINDOW * 3,
            bytes_accessed=micro * length * width * 8,
            transcendentals=micro * heads * length * length // 2,
        ),
    )(limit[:, :, None], branch[:, :, None], qkv, qkv, qkv)


def attend_back_kernel(
    limit_ref, branch_ref, lse_ref, q_ref, k_ref, v_ref, g_ref, dq_ref, dk_ref, dv_ref, dk_sum, dv_sum
):
    head = pl.program_id(1)
    window, mine = head_window(head, q_ref.shape[2])

    @pl.when(head == 0)
    def clear():
        dk_sum[...] = jnp.zeros_like(dk_sum)
        dv_sum[...] = jnp.zeros_like(dv_sum)

    for first, count, parts in query_blocks(q_ref.shape[1]):
        rows = pl.ds(first, count)
        query = jnp.where(mine, q_ref[0, rows, window], 0)
        grad = jnp.where(mine, g_ref[0, rows, window], 0)
        lse = lse_ref[0, pl.ds(head, 1), rows]
        held = []
        row_total = 0.0
        for key_first, keys, kind in parts:
            where = pl.ds(key_first, keys)
            raw = lax.dot_general(
                k_ref[0, where, window], query, NT, preferred_element_type=jnp.float32
            )
            prob = jnp.exp2(raw * (SCALE * LOG2E) - lse)
            if kind != "all":
                ok = allowed_pairs(
                    kind,
                    key_first,
                    lax.broadcasted_iota(jnp.int32, (keys, count), 0),
                    lax.broadcasted_iota(jnp.int32, (keys, count), 1),
                    limit_ref[0],
                    branch_ref[0],
                )
                prob = jnp.where(ok, prob, 0.0)
            grad_prob = lax.dot_general(
                v_ref[0, where, window], grad, NT, preferred_element_type=jnp.float32
            )
            row_total = row_total + jnp.sum(prob * grad_prob, axis=0, keepdims=True)
            held.append((where, prob, grad_prob))
        grad_query = 0.0
        for where, prob, grad_prob in held:
            grad_raw = (prob * (grad_prob - row_total)).astype(jnp.bfloat16)
            dv_sum[where, window] += jnp.dot(
                prob.astype(jnp.bfloat16), grad, preferred_element_type=jnp.float32
            )
            dk_sum[where, window] += jnp.dot(grad_raw, query, preferred_element_type=jnp.float32)
            grad_query = grad_query + lax.dot_general(
                grad_raw, k_ref[0, where, window], TN, preferred_element_type=jnp.float32
            )
        dq_ref[0, rows, window] = jnp.where(
            mine, (grad_query * SCALE).astype(jnp.bfloat16), dq_ref[0, rows, window]
        )

    @pl.when(head == pl.num_programs(1) - 1)
    def write():
        dk_ref[0] = (dk_sum[...] * SCALE).astype(jnp.bfloat16)
        dv_ref[0] = dv_sum[...].astype(jnp.bfloat16)


def attend_back(qkv, grad, lse, limit, branch):
    micro, length, columns = qkv.shape
    width = columns // 3
    heads = width // HEAD
    tail = length - TRUNK_SEGS * SEG

    def part(index):
        return pl.BlockSpec((1, length, width), lambda m, h, index=index: (m, 0, index))

    row = pl.BlockSpec((1, 1, tail), lambda m, h: (m, 0, 0))
    shape = jax.ShapeDtypeStruct((micro, length, width), jnp.bfloat16)
    return pl.pallas_call(
        attend_back_kernel,
        grid=(micro, heads),
        in_specs=[
            row,
            row,
            pl.BlockSpec((1, heads, length), lambda m, h: (m, 0, 0)),
            part(0),
            part(1),
            part(2),
            part(0),
        ],
        out_specs=[part(0), part(0), part(0)],
        out_shape=[shape, shape, shape],
        scratch_shapes=[pltpu.VMEM((length, width), jnp.float32)] * 2,
        compiler_params=pltpu.CompilerParams(vmem_limit_bytes=56 << 20),
        cost_estimate=pl.CostEstimate(
            flops=micro * heads * length * length * WINDOW * 7,
            bytes_accessed=micro * length * width * 14,
            transcendentals=micro * heads * length * length // 2,
        ),
    )(limit[:, None, :], branch[:, None, :], lse, qkv, qkv, qkv, grad)


def norm_back(grad_normed, normed_unit, scale_rows, gain_row):
    scaled_grad = grad_normed * gain_row
    return scale_rows * (
        scaled_grad - normed_unit * jnp.mean(scaled_grad * normed_unit, axis=-1, keepdims=True)
    )


def adam_update(master, first, second, grad, rate, decay):
    first_new = BETA_ONE * first + (1.0 - BETA_ONE) * grad
    second_new = BETA_TWO * second + (1.0 - BETA_TWO) * grad * grad
    fix_one = 1.0 - BETA_ONE**STEP
    fix_two = 1.0 - BETA_TWO**STEP
    step_size = first_new / fix_one / (jnp.sqrt(second_new / fix_two) + ADAM_EPS)
    return (master - rate * (step_size + decay * master), first_new, second_new)


def product(left, right, spec):
    return jnp.einsum(spec, left, right, preferred_element_type=jnp.float32)


Y_CHIPS = 2
CAPACITY = 8
SPARE = 8
GROUP = 16
MESH_IDS = pl.DeviceIdType.MESH


def place():
    chip = lax.axis_index("chip")
    return (
        chip // Y_CHIPS,
        lax.rem(chip, Y_CHIPS),
        lax.axis_index("core"),
        lax.axis_index("seq"),
        lax.axis_size("chip") // Y_CHIPS,
    )


def at_z(z, y):
    return {"chip": z * Y_CHIPS + y}


def neighbours():
    z, y, core, x, depth = place()
    peers = [at_z(lax.rem(z + d, depth), y) for d in range(1, depth)]
    return peers + [at_z(z, 1 - y), {"seq": 1 - x}, {"core": 1 - core}]


def greet():
    barrier = pltpu.get_barrier_semaphore()
    peers = neighbours()
    for peer in peers:
        pl.semaphore_signal(barrier, inc=1, device_id=peer, device_id_type=MESH_IDS)
    pl.semaphore_wait(barrier, len(peers))


def send(source, target, sems, index, device):
    copy = pltpu.make_async_remote_copy(
        src_ref=source,
        dst_ref=target,
        send_sem=sems[0].at[index],
        recv_sem=sems[1].at[index],
        device_id=device,
        device_id_type=MESH_IDS,
    )
    copy.start()
    return copy


def spread_sems(depth):
    shapes = [(depth,), (depth,), (depth, 2), (depth, 4)]
    return [pltpu.SemaphoreType.DMA(shape) for shape in shapes for _ in range(2)]


class Spread:
    def __init__(self, source, window, second, sems):
        self.z, self.y, self.core, self.x, self.depth = place()
        self.source = source
        self.window = window
        self.second = second
        self.sems = [(sems[2 * i], sems[2 * i + 1]) for i in range(4)]
        self.sent = []

    def where(self, d, swap_second, swap_third, swap_core):
        y, x = self.y, self.x
        if swap_second if self.second == "y" else swap_third:
            y = 1 - y
        if swap_third if self.second == "y" else swap_second:
            x = 1 - x
        core = 1 - self.core if swap_core else self.core
        return self.window(lax.rem(self.z - d + self.depth, self.depth), y, core, x)

    def partner(self, axis):
        return at_z(self.z, 1 - self.y) if axis == "y" else {"seq": 1 - self.x}

    def push(self, stage, index, d, swaps, device):
        here = self.where(d, *swaps)
        source = self.source if d == 0 and not any(swaps) else here
        self.sent.append(send(source, here, self.sems[stage], index, device))

    def arrive(self, stage, index, d, swaps):
        here = self.where(d, *swaps)
        pltpu.make_async_remote_copy(
            src_ref=here,
            dst_ref=here,
            send_sem=self.sems[stage][0].at[index],
            recv_sem=self.sems[stage][1].at[index],
            device_id={"core": 1 - self.core},
            device_id_type=MESH_IDS,
        ).wait_recv()

    @property
    def third(self):
        return "x" if self.second == "y" else "y"

    def to_core(self, d, second, third):
        self.push(3, (d, 2 * second + third), d, (second, third, False), {"core": 1 - self.core})

    def begin(self):
        for d in range(1, self.depth):
            target = at_z(lax.rem(self.z + d, self.depth), self.y)
            self.push(0, (d,), 0, (False, False, False), target)
        self.onward(0)

    def onward(self, d):
        self.push(1, (d,), d, (False, False, False), self.partner(self.second))
        self.push(2, (d, 0), d, (False, False, False), self.partner(self.third))
        self.to_core(d, False, False)

    def from_z(self, d):
        self.arrive(0, (d,), d, (False, False, False))
        self.onward(d)

    def from_second(self, d):
        self.arrive(1, (d,), d, (True, False, False))
        self.push(2, (d, 1), d, (True, False, False), self.partner(self.third))
        self.to_core(d, True, False)

    def from_third(self, d):
        for second in (False, True):
            self.arrive(2, (d, int(second)), d, (second, True, False))
            self.to_core(d, second, True)

    def finish(self):
        for d in range(self.depth):
            for second in (False, True):
                for third in (False, True):
                    self.arrive(3, (d, 2 * second + third), d, (second, third, True))
        for copy in self.sent:
            copy.wait_send()


def run_spreads(flows):
    depth = flows[0].depth
    for d in range(1, depth):
        for flow in flows:
            flow.from_z(d)
        for flow in flows:
            flow.from_second(d - 1)
    for flow in flows:
        flow.from_second(depth - 1)
    for d in range(depth):
        for flow in flows:
            flow.from_third(d)
    for flow in flows:
        flow.finish()


def device_block(z, y, core, x):
    return ((z * Y_CHIPS + y) * 2 + core) * 2 + x


def spare_sum(spare_ref, core_in, y_in, z_in, held, sems):
    z, y, core, x, depth = place()
    rows = core_in.shape[0]
    first = x * 2 * rows
    pairs = [(sems[2 * i], sems[2 * i + 1]) for i in range(3)]

    def total(*parts):
        return functools.reduce(jnp.add, [p.astype(jnp.float32) for p in parts]).astype(jnp.bfloat16)

    theirs = pl.ds(pl.multiple_of(first + (1 - core) * rows, GROUP), rows)
    own = pl.ds(pl.multiple_of(first + core * rows, GROUP), rows)
    copy = send(spare_ref.at[theirs], core_in, pairs[0], (0,), {"core": 1 - core})
    copy.wait()
    held[...] = total(spare_ref[own], core_in[...])
    half = rows // 2
    theirs = pl.ds(pl.multiple_of((1 - y) * half, GROUP), half)
    own = pl.ds(pl.multiple_of(y * half, GROUP), half)
    copy = send(held.at[theirs], y_in, pairs[1], (0,), at_z(z, 1 - y))
    copy.wait()
    y_in[...] = total(held[own], y_in[...])
    copies = []
    for d in range(1, depth):
        to = lax.rem(z + d, depth)
        rows_to = pl.ds(pl.multiple_of(to * GROUP, GROUP), GROUP)
        copies.append(send(y_in.at[rows_to], z_in.at[d], pairs[2], (d,), at_z(to, y)))
    for copy in copies:
        copy.wait()
    own = pl.ds(pl.multiple_of(z * GROUP, GROUP), GROUP)
    return total(y_in[own], *[z_in[d] for d in range(1, depth)])


def gather_kernel(cut, spares, *refs):
    if spares:
        share_ref, spare_ref, out_ref, late, core_in, y_in, z_in, held = refs[:8]
        rest = refs[8:]
    else:
        share_ref, out_ref, late = refs[:3]
        rest = refs[3:]
    local_sem = rest[0]
    depth = place()[4]
    z, y, core, x, _ = place()
    rows = share_ref.shape[0]
    greet()

    def window(first, count):
        return lambda *who: out_ref.at[device_block(*who), pl.ds(first, count)]

    early_flow = Spread(share_ref.at[pl.ds(0, cut)], window(0, cut), "y", rest[1:9])
    late_flow = Spread(late, window(cut, rows - cut), "x", rest[9:17])
    early_copy = pltpu.make_async_copy(early_flow.source, early_flow.where(0, 0, 0, 0), local_sem.at[0])
    early_copy.start()
    early_flow.begin()
    late[...] = share_ref[pl.ds(cut, rows - cut)]
    if spares:
        late[pl.ds(rows - cut - GROUP, GROUP)] = spare_sum(
            spare_ref, core_in, y_in, z_in, held, rest[17:23]
        )
    late_copy = pltpu.make_async_copy(late, late_flow.where(0, 0, 0, 0), local_sem.at[1])
    late_copy.start()
    late_flow.begin()
    run_spreads([early_flow, late_flow])
    early_copy.wait()
    late_copy.wait()


def gather_shares(share, spare):
    rows, width = share.shape
    chips = lax.axis_size("chip")
    depth = chips // Y_CHIPS
    cut = -(-rows // (2 * GROUP)) * GROUP
    vmem = pl.BlockSpec(memory_space=pltpu.VMEM)
    scratch = [pltpu.VMEM((rows - cut, width), jnp.bfloat16)]
    operands = [share]
    if spare is not None:
        operands.append(spare)
        lane = spare.shape[0] // 4
        scratch += [
            pltpu.VMEM((lane, width), jnp.bfloat16),
            pltpu.VMEM((lane // 2, width), jnp.bfloat16),
            pltpu.VMEM((depth, GROUP, width), jnp.bfloat16),
            pltpu.VMEM((lane, width), jnp.bfloat16),
        ]
    scratch += [pltpu.SemaphoreType.DMA((2,))] + spread_sems(depth) + spread_sems(depth)
    if spare is not None:
        scratch += [pltpu.SemaphoreType.DMA((1,))] * 4 + [pltpu.SemaphoreType.DMA((depth,))] * 2
    return pl.pallas_call(
        functools.partial(gather_kernel, cut, spare is not None),
        in_specs=[vmem] * len(operands),
        out_specs=pl.BlockSpec(memory_space=pl.ANY),
        out_shape=jax.ShapeDtypeStruct((4 * chips, rows, width), jnp.bfloat16),
        scratch_shapes=scratch,
        compiler_params=pltpu.CompilerParams(
            collective_id=0, has_side_effects=True, vmem_limit_bytes=32 << 20
        ),
        cost_estimate=pl.CostEstimate(
            flops=0, bytes_accessed=8 * chips * rows * width * 2, transcendentals=0
        ),
    )(*operands)


def store_plan(owners, slot_dev, piece, base):
    piece_owner, rank = owner_slots(owners, slot_dev)
    half = max(base // 2, 1)
    spare = rank >= base
    order = jnp.cumsum(spare.astype(jnp.int32)) - 1
    group = jnp.arange(piece // GROUP, dtype=jnp.int32)[None, :]
    block = (piece_owner * 2 + rank // half)[:, None] + 0 * group
    row = (rank % half)[:, None] * piece + group * GROUP
    if slot_dev > base:
        x, core, y = (order // 4, (order // 2) % 2, order % 2)
        spare_block = device_block(group, y[:, None], core[:, None], x[:, None])
        block = jnp.where(spare[:, None], spare_block, block)
        row = jnp.where(spare[:, None], half * piece + GROUP, row)
    return (piece_owner, rank, spare, order, block, row)


def assemble_kernel(layout, block_ref, row_ref, loose_ref, core_ref, whole_ref, *refs):
    outs, sem = (refs[:-1], refs[-1])
    piece, side, width = layout
    groups = piece // GROUP
    per_matrix = side // piece
    half = width // 2
    split = len(outs) == 2

    for matrix in range(6):
        if split and matrix < 3:
            out, index = (outs[0], 0)
            columns = pl.ds(pl.multiple_of(core_ref[0] * half, LANES), half)
        else:
            out, index = (outs[-1], len(outs) - 1)
            columns = slice(None)

        def place_rows(first, count):
            if split and matrix < 3:
                return out.at[pl.ds(first, count), pl.ds(matrix * half, half)]
            return out.at[matrix - 3 if split else matrix, pl.ds(first, count)]

        def step(i, carry):
            at = (matrix * per_matrix + i) * groups
            first = pl.multiple_of(i * piece, piece)

            @pl.when(loose_ref[matrix * per_matrix + i] == 0)
            def one():
                rows = pl.ds(pl.multiple_of(row_ref[at], GROUP), piece)
                pltpu.make_async_copy(
                    whole_ref.at[block_ref[at], rows, columns], place_rows(first, piece), sem.at[index]
                ).start()

            @pl.when(loose_ref[matrix * per_matrix + i] != 0)
            def several():
                for g in range(groups):
                    rows = pl.ds(pl.multiple_of(row_ref[at + g], GROUP), GROUP)
                    pltpu.make_async_copy(
                        whole_ref.at[block_ref[at + g], rows, columns],
                        place_rows(first + g * GROUP, GROUP),
                        sem.at[index],
                    ).start()

            return carry

        lax.fori_loop(0, per_matrix, step, 0)
    for index, out in enumerate(outs):
        pltpu.make_async_copy(out, out, sem.at[index]).wait()


def assemble(whole, block, row, loose, core, piece, split):
    width = whole.shape[2]
    side = width
    shapes = [(side, 3 * (width // 2)), (3, side, width)] if split else [(6, side, width)]
    outs = pl.pallas_call(
        functools.partial(assemble_kernel, (piece, side, width)),
        grid_spec=pltpu.PrefetchScalarGridSpec(
            num_scalar_prefetch=4,
            grid=(1,),
            in_specs=[pl.BlockSpec(memory_space=pl.ANY)],
            out_specs=[pl.BlockSpec(memory_space=pl.ANY)] * len(shapes),
            scratch_shapes=[pltpu.SemaphoreType.DMA((len(shapes),))],
        ),
        out_shape=[jax.ShapeDtypeStruct(s, jnp.bfloat16) for s in shapes],
        cost_estimate=pl.CostEstimate(
            flops=0, bytes_accessed=6 * side * width * 4, transcendentals=0
        ),
    )(block.reshape(-1), row.reshape(-1), loose, core.reshape(1), whole)
    return outs


def gather_store(store, gains, owners, split):
    slots, piece, width = store.shape
    core = lax.axis_index("core")
    dp_pos = lax.axis_index("chip") * 2 + core
    low = store.astype(jnp.bfloat16)
    gain_low = gains.astype(jnp.bfloat16)
    gain_owner = owners[-2:]

    def shares(base, spare_rows):
        half = max(base // 2, 1)
        part = lax.dynamic_slice_in_dim(low, lax.axis_index("seq") * half, half, axis=0)
        filler = jnp.zeros((GROUP - 2 + spare_rows, width), jnp.bfloat16)
        return jnp.concatenate([part.reshape(half * piece, width), gain_low, filler], axis=0)

    def finish(whole, plan, base):
        spare, block, row = (plan[2], plan[4], plan[5])
        outs = assemble(whole, block, row, spare.astype(jnp.int32), core, piece, split)
        gain_rows = whole[gain_owner * 2, max(base // 2, 1) * piece + jnp.arange(2)]
        return (*outs, gain_rows)

    if slots <= CAPACITY:
        plan = store_plan(owners, slots, piece, slots)
        return finish(gather_shares(shares(slots, 0), None), plan, slots)

    plan = store_plan(owners, slots, piece, CAPACITY)
    piece_owner, rank, spare, order = plan[:4]
    labels = jnp.arange(SPARE, dtype=jnp.int32)
    hot = spare[None, :] & (order[None, :] == labels[:, None]) & (piece_owner == dp_pos)[None, :]
    spare_rank = jnp.sum(jnp.where(hot, rank[None, :], 0), axis=1)
    spare_mine = jnp.any(hot, axis=1)

    def few_spares():
        spare_rows = jnp.where(spare_mine[:, None, None], low[spare_rank], 0)
        whole = gather_shares(shares(CAPACITY, GROUP), spare_rows.reshape(SPARE * piece, width))
        return finish(whole, plan, CAPACITY)

    def many_spares():
        whole = lax.all_gather(shares(slots, 0), ALL, axis=0, tiled=False)
        return finish(whole, store_plan(owners, slots, piece, slots), slots)

    return lax.cond(order[-1] < SPARE, few_spares, many_spares)


def local(
    tokens,
    cotangent,
    parents,
    owners,
    weight_store,
    gain_store,
    weight_first,
    gain_first,
    weight_second,
    gain_second,
):
    core = lax.axis_index("core")
    dp_pos = lax.axis_index("chip") * 2 + core
    slot_dev, piece, width = weight_store.shape
    pieces = owners.shape[0] - 2
    piece_owner, rank = owner_slots(owners, slot_dev)
    gain_owner = owners[pieces:]
    micro, _, rows, _ = tokens.shape
    half = width // 2
    own_rows = core * rows
    own_columns = core * half

    def mine(value, axis, size, index):
        return lax.dynamic_slice_in_dim(value, index * size, size, axis=axis)

    own_tokens = transposed(tokens[:, 0])
    own_cot = transposed(cotangent[:, 0])
    limit, branch = tail_limits(transposed(parents[:, 0]))
    other_tokens = partner(own_tokens)

    def by_core(own, other, axis):
        return jnp.where(
            core == 0,
            jnp.concatenate([own, other], axis=axis),
            jnp.concatenate([other, own], axis=axis),
        )

    all_tokens = by_core(own_tokens, other_tokens, 1)
    qkv_weight, late_weights, gain_low = gather_store(weight_store, gain_store, owners, True)
    gain_one = gain_low[0].astype(jnp.float32)
    gain_two = gain_low[1].astype(jnp.float32)
    out_weight, up_weight, down_weight = late_weights[0], late_weights[1], late_weights[2]

    def unit(values):
        scale = lax.rsqrt(jnp.mean(values * values, axis=-1, keepdims=True) + NORM_EPS)
        return (values * scale, scale)

    normed_one = (unit(all_tokens.astype(jnp.float32))[0] * gain_one).astype(jnp.bfloat16)
    qkv = product(normed_one, qkv_weight, "mtd,de->mte").astype(jnp.bfloat16)
    attended_half, lse = attend(qkv, limit, branch)
    lse_rows = jnp.transpose(lse[:, :, : half // HEAD], (0, 2, 1))
    attended = by_core(
        mine(attended_half, 1, rows, core), partner(mine(attended_half, 1, rows, 1 - core)), 2
    )
    residual = own_tokens.astype(jnp.float32)
    hidden_one = residual + product(attended, out_weight, "mti,io->mto")
    unit_two, scale_two = unit(hidden_one)
    normed_two = (unit_two * gain_two).astype(jnp.bfloat16)
    up_rows = product(normed_two, up_weight, "mti,io->mto")
    sigmoid_up = jax.nn.sigmoid(up_rows)
    activated = (up_rows * sigmoid_up).astype(jnp.bfloat16)
    mixed_rows = (hidden_one + product(activated, down_weight, "mti,io->mto")).astype(jnp.bfloat16)
    mixed = transposed(mixed_rows)

    grad_down = product(activated, own_cot, "mti,mto->io")
    grad_hidden = product(own_cot, down_weight, "mto,io->mti")
    grad_up_rows = (grad_hidden * (sigmoid_up * (1.0 + up_rows * (1.0 - sigmoid_up)))).astype(
        jnp.bfloat16
    )
    grad_up = product(normed_two, grad_up_rows, "mti,mto->io")
    grad_normed_two = product(grad_up_rows, up_weight, "mto,io->mti")
    gain_two_grad = jnp.sum(grad_normed_two * unit_two, axis=(0, 1))
    grad_hidden_one = own_cot.astype(jnp.float32) + norm_back(
        grad_normed_two, unit_two, scale_two, gain_two
    )
    branch_grad = grad_hidden_one.astype(jnp.bfloat16)
    grad_out = product(attended, branch_grad, "mti,mto->io")
    late = jnp.stack([grad_out, grad_up, grad_down]).astype(jnp.bfloat16).reshape(3 * width, width)
    late_share = lax.psum_scatter(late, ALL, scatter_dimension=0, tiled=True)
    late_sum = lax.all_gather(late_share, ALL, axis=0, tiled=True)

    grad_attended = product(branch_grad, out_weight, "mto,io->mti").astype(jnp.bfloat16)
    grad_half = by_core(
        mine(grad_attended, 2, half, core), partner(mine(grad_attended, 2, half, 1 - core)), 1
    )
    grad_query, grad_key, grad_value = attend_back(qkv, grad_half, lse_rows, limit, branch)
    grad_qkv_rows = jnp.concatenate([grad_query, grad_key, grad_value], axis=2)
    grad_qkv = product(normed_one, grad_qkv_rows, "mti,mto->io")
    early = jnp.transpose(grad_qkv.astype(jnp.bfloat16).reshape(width, 3, half), (1, 0, 2))
    early_share = lax.psum_scatter(
        early.reshape(3 * width, half), ("chip", "seq"), scatter_dimension=0, tiled=True
    )
    early_sum = lax.all_gather(early_share, ALL, axis=0, tiled=False)
    early_sum = jnp.transpose(
        early_sum.reshape(lax.axis_size("chip"), 2, lax.axis_size("seq"), -1, half), (0, 2, 3, 1, 4)
    ).reshape(3 * width, width)

    grad_normed_part = product(grad_qkv_rows, qkv_weight, "mte,de->mtd")
    grad_normed_one = mine(grad_normed_part, 1, rows, core) + partner(
        mine(grad_normed_part, 1, rows, 1 - core).astype(jnp.bfloat16)
    ).astype(jnp.float32)
    unit_one, scale_one = unit(residual)
    gain_one_grad = jnp.sum(grad_normed_one * unit_one, axis=(0, 1))
    token_rows = (
        grad_hidden_one + norm_back(grad_normed_one, unit_one, scale_one, gain_one)
    ).astype(jnp.bfloat16)
    token_grad = transposed(token_rows)
    gain_sum = lax.psum(jnp.stack([gain_one_grad, gain_two_grad]), ALL)

    labels = jnp.arange(slot_dev, dtype=jnp.int32)
    match = (piece_owner[None, :] == dp_pos) & (rank[None, :] == labels[:, None])
    held = jnp.any(match, axis=1)
    piece_of = jnp.sum(jnp.where(match, jnp.arange(pieces, dtype=jnp.int32)[None, :], 0), axis=1)
    sums = jnp.concatenate([early_sum, late_sum], axis=0).reshape(pieces, piece, width)
    slot_grad = jnp.where(held[:, None, None], sums[piece_of].astype(jnp.float32), 0.0)
    is_out = held & (piece_of // (width // piece) == 3)
    slot_rate = jnp.where(is_out, RATE_OUT, RATE_QKV).astype(jnp.float32)
    weight_new, weight_first_new, weight_second_new = adam_update(
        weight_store, weight_first, weight_second, slot_grad, slot_rate[:, None, None], MATRIX_DECAY
    )
    gain_slot_grad = jnp.where((gain_owner == dp_pos)[:, None], gain_sum, 0.0)
    gain_new, gain_first_new, gain_second_new = adam_update(
        gain_store, gain_first, gain_second, gain_slot_grad, RATE_GAIN, 0.0
    )
    weight_copies, gain_copies = gather_store(weight_new, gain_new, owners, False)
    return (
        mixed[:, None],
        token_grad[:, None],
        weight_new,
        gain_new,
        weight_first_new,
        gain_first_new,
        weight_second_new,
        gain_second_new,
        weight_copies,
        gain_copies,
    )


def solution(mesh):
    dp_count, seq_count = mesh.devices.shape
    fine = Mesh(mesh.devices.reshape(dp_count // 2, 2, seq_count), ALL)
    dp = ("chip", "core")
    rows = P(None, dp, "seq", None)
    store = P(dp, None, None)
    gains = P(dp, None)
    in_specs = (rows, rows, P(None, dp, None), P(), store, gains, store, gains, store, gains)
    out_specs = (rows, rows, store, gains, store, gains, store, gains, P(), P())
    return jax.shard_map(local, mesh=fine, in_specs=in_specs, out_specs=out_specs, check_vma=False)
```

```python
import functools

import jax
import jax.numpy as jnp
from jax import lax
from jax.experimental import pallas as pl
from jax.experimental.pallas import tpu as pltpu
from jax.sharding import Mesh
from jax.sharding import PartitionSpec as P

HEAD = 80
SEG = 32
TRUNK_SEGS = 32
ALWAYS_SEGS = TRUNK_SEGS // 2
STEP = 7
LANES = 128
WINDOW = 256
QUERY_BLOCK = 256

NORM_EPS = 1e-06
BETA_ONE = 0.5
BETA_TWO = 0.5
ADAM_EPS = 1e-08
MATRIX_DECAY = 0.1
RATE_QKV = 0.03
RATE_OUT = 0.4
RATE_GAIN = 0.4
MASKED = -1e30
SCALE = HEAD**-0.5
LOG2E = 1.4426950408889634
ALL = ("chip", "core", "seq")
NT = (((1,), (1,)), ((), ()))
TN = (((0,), (0,)), ((), ()))


def transposed(value):
    chips = lax.axis_size("chip")
    pairs = [(k * 4 + c * 2 + 1 - c, k * 4 + 2 - 2 * c + c) for k in range(chips) for c in range(2)]
    moved = lax.ppermute(value, ALL, pairs)
    return jnp.where(lax.axis_index("core") == lax.axis_index("seq"), value, moved)


def partner(value):
    return lax.ppermute(value, "core", [(0, 1), (1, 0)])


def owner_slots(owners, slot_dev):
    count = owners.shape[0] - 2
    piece_owner = owners[:count]
    labels = jnp.arange(count, dtype=jnp.int32)
    same = (piece_owner[:, None] == piece_owner[None, :]) & (labels[None, :] < labels[:, None])
    rank = jnp.sum(same.astype(jnp.int32), axis=1)
    return (piece_owner, rank)


def tail_limits(parents):
    up = parents[:, TRUNK_SEGS:]
    leaf = up >= TRUNK_SEGS
    above = jnp.where(leaf, up - TRUNK_SEGS, 0)
    labels = jnp.arange(up.shape[1], dtype=jnp.int32)
    hot = above[:, :, None] == labels[None, None, :]
    upper = jnp.sum(jnp.where(hot, up[:, None, :], 0), axis=2)
    attach = jnp.where(leaf, upper, up)
    limit = (attach + 1) * SEG
    branch = jnp.where(leaf, above, -1)
    return (jnp.repeat(limit, SEG, axis=1), jnp.repeat(branch, SEG, axis=1))


def query_blocks(length):
    trunk = TRUNK_SEGS * SEG
    blocks = []
    for first in range(0, trunk, QUERY_BLOCK):
        parts = [(0, first, "all")] if first else []
        blocks.append((first, QUERY_BLOCK, parts + [(first, QUERY_BLOCK, "causal")]))
    always = ALWAYS_SEGS * SEG
    tail = length - trunk
    blocks.append(
        (trunk, tail, [(0, always, "all"), (always, trunk - always, "trunk"), (trunk, tail, "tail")])
    )
    return blocks


def allowed_pairs(kind, key_first, key, query, limit, branch):
    if kind == "causal":
        return key <= query
    if kind == "trunk":
        return key + key_first < limit
    key_seg = key // SEG
    return ((key_seg == query // SEG) & (key <= query)) | (key_seg == branch)


def head_window(head, width):
    start = pl.multiple_of(
        jnp.minimum((head * HEAD) // LANES, width // LANES - WINDOW // LANES) * LANES, LANES
    )
    lane = lax.broadcasted_iota(jnp.int32, (1, WINDOW), 1) + start
    mine = (lane >= head * HEAD) & (lane < (head + 1) * HEAD)
    return (pl.ds(start, WINDOW), mine)


def attend_kernel(limit_ref, branch_ref, q_ref, k_ref, v_ref, out_ref, lse_ref):
    head = pl.program_id(1)
    window, mine = head_window(head, q_ref.shape[2])
    stat_lane = lax.broadcasted_iota(jnp.int32, (1, LANES), 1)
    for first, count, parts in query_blocks(q_ref.shape[1]):
        rows = pl.ds(first, count)
        query = jnp.where(mine, q_ref[0, rows, window], 0)
        scores = []
        for key_first, keys, kind in parts:
            raw = lax.dot_general(
                query, k_ref[0, pl.ds(key_first, keys), window], NT, preferred_element_type=jnp.float32
            ) * (SCALE * LOG2E)
            if kind != "all":
                ok = allowed_pairs(
                    kind,
                    key_first,
                    lax.broadcasted_iota(jnp.int32, (count, keys), 1),
                    lax.broadcasted_iota(jnp.int32, (count, keys), 0),
                    limit_ref[0],
                    branch_ref[0],
                )
                raw = jnp.where(ok, raw, MASKED)
            scores.append(raw)
        top = functools.reduce(jnp.maximum, [jnp.max(s, axis=1, keepdims=True) for s in scores])
        total = 0.0
        gained = 0.0
        for raw, (key_first, keys, kind) in zip(scores, parts):
            weight = jnp.exp2(raw - top)
            total = total + jnp.sum(weight, axis=1, keepdims=True)
            gained = gained + jnp.dot(
                weight.astype(jnp.bfloat16),
                v_ref[0, pl.ds(key_first, keys), window],
                preferred_element_type=jnp.float32,
            )
        gained = (gained / total).astype(jnp.bfloat16)
        out_ref[0, rows, window] = jnp.where(mine, gained, out_ref[0, rows, window])
        lse_ref[0, rows, :] = jnp.where(
            stat_lane == head, top + jnp.log2(total), lse_ref[0, rows, :]
        )


def attend(qkv, limit, branch):
    micro, length, columns = qkv.shape
    width = columns // 3
    heads = width // HEAD
    tail = length - TRUNK_SEGS * SEG

    def part(index):
        return pl.BlockSpec((1, length, width), lambda m, h, index=index: (m, 0, index))

    column = pl.BlockSpec((1, tail, 1), lambda m, h: (m, 0, 0))
    return pl.pallas_call(
        attend_kernel,
        grid=(micro, heads),
        in_specs=[column, column, part(0), part(1), part(2)],
        out_specs=[
            pl.BlockSpec((1, length, width), lambda m, h: (m, 0, 0)),
            pl.BlockSpec((1, length, LANES), lambda m, h: (m, 0, 0)),
        ],
        out_shape=[
            jax.ShapeDtypeStruct((micro, length, width), jnp.bfloat16),
            jax.ShapeDtypeStruct((micro, length, LANES), jnp.float32),
        ],
        compiler_params=pltpu.CompilerParams(vmem_limit_bytes=48 << 20),
        cost_estimate=pl.CostEstimate(
            flops=micro * heads * length * length * WINDOW * 3,
            bytes_accessed=micro * length * width * 8,
            transcendentals=micro * heads * length * length // 2,
        ),
    )(limit[:, :, None], branch[:, :, None], qkv, qkv, qkv)


def attend_back_kernel(
    limit_ref, branch_ref, lse_ref, q_ref, k_ref, v_ref, g_ref, dq_ref, dk_ref, dv_ref, dk_sum, dv_sum
):
    head = pl.program_id(1)
    window, mine = head_window(head, q_ref.shape[2])

    @pl.when(head == 0)
    def clear():
        dk_sum[...] = jnp.zeros_like(dk_sum)
        dv_sum[...] = jnp.zeros_like(dv_sum)

    for first, count, parts in query_blocks(q_ref.shape[1]):
        rows = pl.ds(first, count)
        query = jnp.where(mine, q_ref[0, rows, window], 0)
        grad = jnp.where(mine, g_ref[0, rows, window], 0)
        lse = lse_ref[0, pl.ds(head, 1), rows]
        held = []
        row_total = 0.0
        for key_first, keys, kind in parts:
            where = pl.ds(key_first, keys)
            raw = lax.dot_general(
                k_ref[0, where, window], query, NT, preferred_element_type=jnp.float32
            )
            prob = jnp.exp2(raw * (SCALE * LOG2E) - lse)
            if kind != "all":
                ok = allowed_pairs(
                    kind,
                    key_first,
                    lax.broadcasted_iota(jnp.int32, (keys, count), 0),
                    lax.broadcasted_iota(jnp.int32, (keys, count), 1),
                    limit_ref[0],
                    branch_ref[0],
                )
                prob = jnp.where(ok, prob, 0.0)
            grad_prob = lax.dot_general(
                v_ref[0, where, window], grad, NT, preferred_element_type=jnp.float32
            )
            row_total = row_total + jnp.sum(prob * grad_prob, axis=0, keepdims=True)
            held.append((where, prob, grad_prob))
        grad_query = 0.0
        for where, prob, grad_prob in held:
            grad_raw = (prob * (grad_prob - row_total)).astype(jnp.bfloat16)
            dv_sum[where, window] += jnp.dot(
                prob.astype(jnp.bfloat16), grad, preferred_element_type=jnp.float32
            )
            dk_sum[where, window] += jnp.dot(grad_raw, query, preferred_element_type=jnp.float32)
            grad_query = grad_query + lax.dot_general(
                grad_raw, k_ref[0, where, window], TN, preferred_element_type=jnp.float32
            )
        dq_ref[0, rows, window] = jnp.where(
            mine, (grad_query * SCALE).astype(jnp.bfloat16), dq_ref[0, rows, window]
        )

    @pl.when(head == pl.num_programs(1) - 1)
    def write():
        dk_ref[0] = (dk_sum[...] * SCALE).astype(jnp.bfloat16)
        dv_ref[0] = dv_sum[...].astype(jnp.bfloat16)


def attend_back(qkv, grad, lse, limit, branch):
    micro, length, columns = qkv.shape
    width = columns // 3
    heads = width // HEAD
    tail = length - TRUNK_SEGS * SEG

    def part(index):
        return pl.BlockSpec((1, length, width), lambda m, h, index=index: (m, 0, index))

    row = pl.BlockSpec((1, 1, tail), lambda m, h: (m, 0, 0))
    shape = jax.ShapeDtypeStruct((micro, length, width), jnp.bfloat16)
    return pl.pallas_call(
        attend_back_kernel,
        grid=(micro, heads),
        in_specs=[
            row,
            row,
            pl.BlockSpec((1, heads, length), lambda m, h: (m, 0, 0)),
            part(0),
            part(1),
            part(2),
            part(0),
        ],
        out_specs=[part(0), part(0), part(0)],
        out_shape=[shape, shape, shape],
        scratch_shapes=[pltpu.VMEM((length, width), jnp.float32)] * 2,
        compiler_params=pltpu.CompilerParams(vmem_limit_bytes=56 << 20),
        cost_estimate=pl.CostEstimate(
            flops=micro * heads * length * length * WINDOW * 7,
            bytes_accessed=micro * length * width * 14,
            transcendentals=micro * heads * length * length // 2,
        ),
    )(limit[:, None, :], branch[:, None, :], lse, qkv, qkv, qkv, grad)


def norm_back(grad_normed, normed_unit, scale_rows, gain_row):
    scaled_grad = grad_normed * gain_row
    return scale_rows * (
        scaled_grad - normed_unit * jnp.mean(scaled_grad * normed_unit, axis=-1, keepdims=True)
    )


def adam_update(master, first, second, grad, rate, decay):
    first_new = BETA_ONE * first + (1.0 - BETA_ONE) * grad
    second_new = BETA_TWO * second + (1.0 - BETA_TWO) * grad * grad
    fix_one = 1.0 - BETA_ONE**STEP
    fix_two = 1.0 - BETA_TWO**STEP
    step_size = first_new / fix_one / (jnp.sqrt(second_new / fix_two) + ADAM_EPS)
    return (master - rate * (step_size + decay * master), first_new, second_new)


def product(left, right, spec):
    return jnp.einsum(spec, left, right, preferred_element_type=jnp.float32)


Y_CHIPS = 2
CAPACITY = 8
SPARE = 8
GROUP = 16
CHUNK = 256
KERNEL_BYTES = 30 << 20
MESH_IDS = pl.DeviceIdType.MESH


def place():
    chip = lax.axis_index("chip")
    return (
        chip // Y_CHIPS,
        lax.rem(chip, Y_CHIPS),
        lax.axis_index("core"),
        lax.axis_index("seq"),
        lax.axis_size("chip") // Y_CHIPS,
    )


def at_z(z, y):
    return {"chip": z * Y_CHIPS + y}


def across(axis):
    z, y, core, x, _ = place()
    return {"y": at_z(z, 1 - y), "x": {"seq": 1 - x}, "core": {"core": 1 - core}}[axis]


def greet():
    z, y, core, x, depth = place()
    barrier = pltpu.get_barrier_semaphore()
    peers = [at_z(lax.rem(z + d, depth), y) for d in range(1, depth)]
    peers += [across("y"), across("x"), across("core")]
    for peer in peers:
        pl.semaphore_signal(barrier, inc=1, device_id=peer, device_id_type=MESH_IDS)
    pl.semaphore_wait(barrier, len(peers))


def sem_pair(*shape):
    return [pltpu.SemaphoreType.DMA(shape), pltpu.SemaphoreType.DMA(shape)]


def remote(source, target, sems, index, device):
    return pltpu.make_async_remote_copy(
        src_ref=source,
        dst_ref=target,
        send_sem=sems[0].at[index],
        recv_sem=sems[1].at[index],
        device_id=device,
        device_id_type=MESH_IDS,
    )


def total(*parts):
    return functools.reduce(jnp.add, [p.astype(jnp.float32) for p in parts]).astype(jnp.bfloat16)


class Flow:
    def __init__(self):
        self.sent = []

    def push(self, source, target, sems, index, device):
        copy = remote(source, target, sems, index, device)
        copy.start()
        self.sent.append(copy)

    def arrive(self, here, sems, index):
        remote(here, here, sems, index, across("core")).wait_recv()

    def drain(self):
        for copy in self.sent:
            copy.wait_send()


def spread_sems(depth):
    return sem_pair(depth) + sem_pair(depth) + sem_pair(depth, 2) + sem_pair(depth, 4)


class Spread(Flow):
    def __init__(self, window, second, sems):
        super().__init__()
        self.window = window
        self.second = second
        self.third = "x" if second == "y" else "y"
        self.sems = [(sems[2 * i], sems[2 * i + 1]) for i in range(4)]

    def where(self, d, second=False, third=False, other_core=False):
        z, y, core, x, depth = place()
        if second if self.second == "y" else third:
            y = 1 - y
        if third if self.second == "y" else second:
            x = 1 - x
        return self.window(lax.rem(z - d + depth, depth), y, 1 - core if other_core else core, x)

    def forward(self, stage, index, block, device):
        self.push(block, block, self.sems[stage], index, device)

    def begin(self):
        z, y, core, x, depth = place()
        for d in range(1, depth):
            self.forward(0, (d,), self.where(0), at_z(lax.rem(z + d, depth), y))
        self.onward(0)

    def onward(self, d):
        block = self.where(d)
        self.forward(1, (d,), block, across(self.second))
        self.forward(2, (d, 0), block, across(self.third))
        self.forward(3, (d, 0), block, across("core"))

    def from_z(self, d):
        self.arrive(self.where(d), self.sems[0], (d,))
        self.onward(d)

    def from_second(self, d):
        block = self.where(d, True)
        self.arrive(block, self.sems[1], (d,))
        self.forward(2, (d, 1), block, across(self.third))
        self.forward(3, (d, 2), block, across("core"))

    def from_third(self, d):
        for second in range(2):
            block = self.where(d, bool(second), True)
            self.arrive(block, self.sems[2], (d, second))
            self.forward(3, (d, 2 * second + 1), block, across("core"))

    def finish(self):
        for d in range(place()[4]):
            for second in range(2):
                for third in range(2):
                    block = self.where(d, bool(second), bool(third), True)
                    self.arrive(block, self.sems[3], (d, 2 * second + third))
        self.drain()


def run_spreads(flows):
    depth = place()[4]
    for d in range(1, depth):
        for flow in flows:
            flow.from_z(d)
        for flow in flows:
            flow.from_second(d - 1)
    for flow in flows:
        flow.from_second(depth - 1)
    for d in range(depth):
        for flow in flows:
            flow.from_third(d)
    for flow in flows:
        flow.finish()


def device_block(z, y, core, x):
    return ((z * Y_CHIPS + y) * 2 + core) * 2 + x


def spare_sum(spare, core_in, y_in, z_in, held, sems):
    z, y, core, x, depth = place()
    rows = core_in.shape[0]
    half = rows // 2
    flow = Flow()

    def part(index, size):
        return pl.ds(pl.multiple_of(index * size, GROUP), size)

    flow.push(spare.at[part(1 - core, rows)], core_in, sems[0:2], (0,), across("core"))
    flow.arrive(core_in, sems[0:2], (0,))
    held[...] = total(spare[part(core, rows)], core_in[...])
    flow.push(held.at[part(1 - y, half)], y_in, sems[2:4], (0,), across("y"))
    flow.arrive(y_in, sems[2:4], (0,))
    y_in[...] = total(held[part(y, half)], y_in[...])
    for d in range(1, depth):
        to = lax.rem(z + d, depth)
        flow.push(y_in.at[part(to, GROUP)], z_in.at[d], sems[4:6], (d,), at_z(to, y))
    for d in range(1, depth):
        flow.arrive(z_in.at[d], sems[4:6], (d,))
    flow.drain()
    return total(y_in[part(z, GROUP)], *[z_in[d] for d in range(1, depth)])


def gather_kernel(
    split,
    block_ref,
    row_ref,
    spare_rank_ref,
    gain_block_ref,
    spare_mine_ref,
    low_ref,
    gain_ref,
    *refs,
):
    outs = refs[: 2 if split else 1]
    gain_out, whole, stage, stage_sem, spare, core_in, y_in, z_in, held = refs[len(outs) : len(outs) + 9]
    sems = refs[len(outs) + 9 :]
    z, y, core, x, depth = place()
    piece, width = low_ref.shape[1:]
    half = CAPACITY // 2
    base = half * piece
    rows = whole.shape[1]
    cut = rows // 2
    me = device_block(z, y, core, x)
    per_piece = piece // GROUP
    for i in range(base // GROUP):
        source = pl.ds(i % per_piece * GROUP, GROUP)
        whole[me, i] = low_ref[x * half + i // per_piece, source]
    whole[me, base // GROUP] = gain_ref[...]
    greet()

    def window(first, count):
        return lambda *who: whole.at[device_block(*who), pl.ds(first, count)]

    early = Spread(window(0, cut), "y", sems[0:8])
    late = Spread(window(cut, rows - cut), "x", sems[8:16])
    early.begin()
    count = SPARE // 2
    for i in range(count):
        loose = low_ref[spare_rank_ref[x * count + i]]
        spare[pl.ds(i * piece, piece)] = jnp.where(spare_mine_ref[x * count + i] > 0, loose, 0)
    whole[me, base // GROUP + 1] = spare_sum(spare, core_in, y_in, z_in, held, sems[16:22])
    late.begin()
    run_spreads([early, late])

    buffers = stage.shape[0]
    per_chunk = CHUNK // GROUP
    narrow = width // 2
    copies = []
    for index in range(6 * width // CHUNK):
        matrix, first = divmod(index * CHUNK, width)
        slot = index % buffers
        if index >= buffers:
            copies[index - buffers].wait()
        thin = split and matrix < 3
        columns = pl.ds(pl.multiple_of(core * narrow, LANES), narrow) if thin else slice(None)
        count = narrow if thin else width

        def step(g, carry, index=index, slot=slot, columns=columns, count=count):
            at = index * per_chunk + g
            stage[slot, pl.ds(pl.multiple_of(g * GROUP, GROUP), GROUP), pl.ds(0, count)] = whole[
                block_ref[at], row_ref[at], :, columns
            ]
            return carry

        lax.fori_loop(0, per_chunk, step, 0)
        if thin:
            target = outs[0].at[pl.ds(first, CHUNK), pl.ds(matrix * narrow, narrow)]
        else:
            target = outs[-1].at[matrix - 3 if split else matrix, pl.ds(first, CHUNK)]
        copies.append(
            pltpu.make_async_copy(stage.at[slot, :, pl.ds(0, count)], target, stage_sem.at[slot])
        )
        copies[-1].start()
    line = lax.broadcasted_iota(jnp.int32, (GROUP, 1), 0)
    gain_rows = [whole[gain_block_ref[j], base // GROUP].astype(jnp.float32) for j in range(2)]
    gain_out[...] = jnp.where(line == 0, gain_rows[0], gain_rows[1])
    for copy in copies[-buffers:]:
        copy.wait()


def gather_pieces(low, gains, plan, split):
    slots, piece, width = low.shape
    block, row, spare_rank, spare_mine, gain_owner = plan
    chips = lax.axis_size("chip")
    depth = chips // Y_CHIPS
    rows = CAPACITY // 2 * piece // GROUP + 2
    shapes = [(width, 3 * (width // 2)), (3, width, width)] if split else [(6, width, width)]
    lane = SPARE * piece // 4
    buffers = 4
    padded = jnp.concatenate([gains, jnp.zeros((GROUP - 2, width), gains.dtype)], axis=0)
    vmem = pl.BlockSpec(memory_space=pltpu.VMEM)
    smem = pl.BlockSpec(memory_space=pltpu.SMEM)
    outs = pl.pallas_call(
        functools.partial(gather_kernel, split),
        in_specs=[smem] * 4 + [vmem] * 3,
        out_specs=[pl.BlockSpec(memory_space=pl.ANY)] * len(shapes) + [vmem],
        out_shape=[jax.ShapeDtypeStruct(s, jnp.bfloat16) for s in shapes]
        + [jax.ShapeDtypeStruct((GROUP, width), jnp.float32)],
        scratch_shapes=[
            pltpu.VMEM((4 * chips, rows, GROUP, width), jnp.bfloat16),
            pltpu.VMEM((buffers, CHUNK, width), jnp.bfloat16),
            pltpu.SemaphoreType.DMA((buffers,)),
            pltpu.VMEM((2 * lane, width), jnp.bfloat16),
            pltpu.VMEM((lane, width), jnp.bfloat16),
            pltpu.VMEM((lane // 2, width), jnp.bfloat16),
            pltpu.VMEM((depth, GROUP, width), jnp.bfloat16),
            pltpu.VMEM((lane, width), jnp.bfloat16),
        ]
        + spread_sems(depth)
        + spread_sems(depth)
        + sem_pair(1)
        + sem_pair(1)
        + sem_pair(depth),
        compiler_params=pltpu.CompilerParams(
            collective_id=0 if split else 1, has_side_effects=True, vmem_limit_bytes=48 << 20
        ),
        cost_estimate=pl.CostEstimate(
            flops=0, bytes_accessed=6 * width * width * 16, transcendentals=0
        ),
    )(
        block.reshape(-1),
        row.reshape(-1),
        spare_rank,
        gain_owner * 2,
        jnp.broadcast_to(spare_mine[:, None, None], (SPARE, 1, width)),
        low,
        padded,
    )
    return (*outs[:-1], outs[-1][:2].astype(jnp.bfloat16))


def gather_slots(low, gains, owners, split):
    slots, piece, width = low.shape
    piece_owner, rank = owner_slots(owners, slots)
    rows = slots * piece
    half = -(-(rows // 2 + 1) // GROUP) * GROUP
    filler = jnp.zeros((2 * half - rows - 2, width), jnp.bfloat16)
    packed = jnp.concatenate([low.reshape(rows, width), gains, filler], axis=0)
    share = lax.dynamic_slice_in_dim(packed, lax.axis_index("seq") * half, half, axis=0)
    groups = lax.all_gather(share, ALL, axis=0, tiled=True).reshape(-1, GROUP, width)
    per_owner = 2 * half // GROUP
    base = piece_owner * per_owner + rank * (piece // GROUP)
    index = base[:, None] + jnp.arange(piece // GROUP, dtype=jnp.int32)[None, :]
    matrices = groups[index.reshape(-1)].reshape(6, width, width)
    gain_rows = groups[owners[-2:] * per_owner + rows // GROUP][jnp.arange(2), jnp.arange(2)]
    if not split:
        return (matrices, gain_rows)
    narrow = width // 2
    thin = lax.dynamic_slice_in_dim(matrices[:3], lax.axis_index("core") * narrow, narrow, axis=2)
    return (jnp.transpose(thin, (1, 0, 2)).reshape(width, 3 * narrow), matrices[3:], gain_rows)


def gather_store(low, gains, owners, split):
    slots, piece, width = low.shape
    chips = lax.axis_size("chip")
    held_bytes = 4 * chips * (CAPACITY // 2 * piece + 2 * GROUP) * width * 2
    fits = slots > CAPACITY and held_bytes < KERNEL_BYTES and piece == GROUP * (chips // Y_CHIPS)
    if not fits:
        return gather_slots(low, gains, owners, split)
    dp_pos = lax.axis_index("chip") * 2 + lax.axis_index("core")
    piece_owner, rank = owner_slots(owners, slots)
    half = CAPACITY // 2
    spare = rank >= CAPACITY
    order = jnp.cumsum(spare.astype(jnp.int32)) - 1
    group = jnp.arange(piece // GROUP, dtype=jnp.int32)[None, :]
    block = jnp.where(
        spare[:, None],
        device_block(group, (order % 2)[:, None], ((order // 2) % 2)[:, None], (order // 4)[:, None]),
        (piece_owner * 2 + rank // half)[:, None],
    )
    groups = piece // GROUP
    row = jnp.where(spare[:, None], half * groups + 1, (rank % half)[:, None] * groups + group)
    labels = jnp.arange(SPARE, dtype=jnp.int32)
    hot = spare[None, :] & (order[None, :] == labels[:, None]) & (piece_owner == dp_pos)[None, :]
    spare_rank = jnp.sum(jnp.where(hot, rank[None, :], 0), axis=1)
    plan = (block, row, spare_rank, jnp.any(hot, axis=1).astype(jnp.int32), owners[-2:])
    return lax.cond(
        order[-1] < SPARE,
        lambda: gather_pieces(low, gains, plan, split),
        lambda: gather_slots(low, gains, owners, split),
    )


class Reduce(Flow):
    def __init__(self, first, shard, one, two, three, sems):
        super().__init__()
        self.first = first
        self.other = "y" if first == "x" else "x"
        self.shard = shard
        self.one, self.two, self.three = (one, two, three)
        self.sems = [sems[0:2], sems[2:4], sems[4:6]]

    def start(self, d, b):
        self.push(self.shard(d, b, 1), self.one.at[d, b], self.sems[0], (d, b), across(self.first))

    def from_first(self, d, b):
        here = self.one.at[d, b]
        self.arrive(here, self.sems[0], (d, b))
        here[...] = total(here[...], self.shard(d, b, 0)[...])
        if b:
            self.push(here, self.two.at[d], self.sems[1], (d,), across(self.other))

    def from_second(self, d):
        z, y, core, x, depth = place()
        here = self.two.at[d]
        self.arrive(here, self.sems[1], (d,))
        here[...] = total(here[...], self.one[d, 0])
        if d:
            self.push(here, self.three.at[d], self.sems[2], (d,), at_z(lax.rem(z + d, depth), y))

    def result(self):
        depth = place()[4]
        for d in range(1, depth):
            self.arrive(self.three.at[d], self.sems[2], (d,))
        value = total(self.two[0], *[self.three[d] for d in range(1, depth)])
        self.drain()
        return value


def reduce_kernel(
    kind_ref,
    matrix_ref,
    row_ref,
    held_ref,
    early_ref,
    late_ref,
    gain_ref,
    slot_ref,
    gain_out,
    sums,
    early_one,
    early_two,
    early_three,
    late_zero,
    late_one,
    late_two,
    late_three,
    gain_sum,
    gain_in,
    *sems,
):
    z, y, core, x, depth = place()
    rows = early_one.shape[2]
    narrow = late_one.shape[4]
    order = [d for d in range(1, depth)] + [0]

    def shard_rows(z_at, y_at, x_at):
        index = (z_at * Y_CHIPS + y_at) * 2 + x_at
        return pl.ds(pl.multiple_of(index * rows, GROUP), rows)

    def relative_rows(d, swap_y, swap_x):
        y_at = 1 - y if swap_y else y
        x_at = 1 - x if swap_x else x
        return shard_rows(lax.rem(z + d, depth), y_at, x_at)

    def half(which):
        return pl.ds(pl.multiple_of(which * narrow, LANES), narrow)

    early = Reduce(
        "x",
        lambda d, b, a: early_ref.at[relative_rows(d, b, a)],
        early_one,
        early_two,
        early_three,
        sems[0:6],
    )
    late = Reduce(
        "y", lambda d, b, a: late_zero.at[d, b, a], late_one, late_two, late_three, sems[6:12]
    )
    pair = Flow()
    gain = Flow()
    pair_sems, gain_sems = (sems[12:14], sems[14:16])
    gain_sum[0] = gain_ref[...]
    greet()
    gain.push(gain_sum.at[0], gain_in.at[0], gain_sems, (0,), across("core"))
    for d in order:
        for b in (1, 0):
            early.start(d, b)
            for a in (1, 0):
                source = late_ref.at[:, relative_rows(d, a, b), half(1 - core)]
                pair.push(source, late_zero.at[d, b, a], pair_sems, (d, b, a), across("core"))
    for d in order:
        for b in (1, 0):
            for a in (1, 0):
                here = late_zero.at[d, b, a]
                pair.arrive(here, pair_sems, (d, b, a))
                here[...] = total(here[...], late_ref[:, relative_rows(d, a, b), half(core)])
                if a:
                    late.start(d, b)

    def gain_step(step, axis):
        gain.arrive(gain_in.at[step], gain_sems, (step,))
        gain_sum[step + 1] = gain_sum[step] + gain_in[step]
        if axis:
            here = gain_sum.at[step + 1]
            gain.push(here, gain_in.at[step + 1], gain_sems, (step + 1,), across(axis))

    gain_step(0, "x")
    for d in order:
        for flow in (early, late):
            for b in (1, 0):
                flow.from_first(d, b)
    gain_step(1, "y")
    for d in order:
        for flow in (early, late):
            flow.from_second(d)
    gain_step(2, None)
    for d in range(1, depth):
        target = at_z(lax.rem(z + d, depth), y)
        gain.push(gain_sum.at[3], gain_in.at[2 + d], gain_sems, (2 + d,), target)
    own = (z * Y_CHIPS + y) * 2 + x
    value = early.result()
    groups = rows // GROUP

    def keep(kind, matrix, block):
        for g in range(groups):
            sums[kind, core, matrix, own * groups + g] = block[g * GROUP : (g + 1) * GROUP]

    for matrix in range(3):
        keep(0, matrix, value[:, matrix * narrow : (matrix + 1) * narrow])

    def window(kind):
        def of(z_at, y_at, core_at, x_at):
            first = ((z_at * Y_CHIPS + y_at) * 2 + x_at) * groups
            return sums.at[kind, core_at, :, pl.ds(first, groups)]

        return of

    early_spread = Spread(window(0), "y", sems[16:24])
    late_spread = Spread(window(1), "x", sems[24:32])
    early_spread.begin()
    value = late.result()
    for matrix in range(3):
        keep(1, matrix, value[matrix])
    late_spread.begin()
    for d in range(1, depth):
        gain.arrive(gain_in.at[2 + d], gain_sems, (2 + d,))
    gain_out[...] = functools.reduce(
        jnp.add, [gain_in[2 + d] for d in range(1, depth)], gain_sum[3]
    )
    run_spreads([early_spread, late_spread])
    gain.drain()
    pair.drain()

    def pick(slot, carry):
        for g in range(slot_ref.shape[1] // GROUP):
            for side in range(2):
                found = sums[kind_ref[slot], side, matrix_ref[slot], row_ref[slot] + g]
                slot_ref[slot, pl.ds(g * GROUP, GROUP), pl.ds(side * narrow, narrow)] = jnp.where(
                    held_ref[slot] > 0, found, 0
                )
        return carry

    lax.fori_loop(0, slot_ref.shape[0], pick, 0)


def reduce_slots(early, late, gains, piece_of, held, piece):
    width = late.shape[1]
    narrow = width // 2
    slots = piece_of.shape[0]
    chips = lax.axis_size("chip")
    depth = chips // Y_CHIPS
    rows = width // (2 * chips)
    per_matrix = width // piece
    wide_block = (rows, 3 * narrow)
    thin_block = (3, rows, narrow)
    padded = jnp.concatenate([gains, jnp.zeros((8 - gains.shape[0], width), jnp.float32)], axis=0)
    vmem = pl.BlockSpec(memory_space=pltpu.VMEM)
    smem = pl.BlockSpec(memory_space=pltpu.SMEM)

    def held_blocks(block):
        return [
            pltpu.VMEM((depth, 2) + block, jnp.bfloat16),
            pltpu.VMEM((depth,) + block, jnp.bfloat16),
            pltpu.VMEM((depth,) + block, jnp.bfloat16),
        ]

    flow_sems = sem_pair(depth, 2) + sem_pair(depth) + sem_pair(depth)
    slot_grad, gain_sum = pl.pallas_call(
        reduce_kernel,
        in_specs=[smem] * 3 + [vmem] * 4,
        out_specs=[vmem, vmem],
        out_shape=[
            jax.ShapeDtypeStruct((slots, piece, width), jnp.bfloat16),
            jax.ShapeDtypeStruct((8, width), jnp.float32),
        ],
        scratch_shapes=[pltpu.VMEM((2, 2, 3, width // GROUP, GROUP, narrow), jnp.bfloat16)]
        + held_blocks(wide_block)
        + [pltpu.VMEM((depth, 2, 2) + thin_block, jnp.bfloat16)]
        + held_blocks(thin_block)
        + [pltpu.VMEM((4, 8, width), jnp.float32), pltpu.VMEM((2 + depth, 8, width), jnp.float32)]
        + flow_sems
        + flow_sems
        + sem_pair(depth, 2, 2)
        + sem_pair(2 + depth)
        + spread_sems(depth)
        + spread_sems(depth),
        compiler_params=pltpu.CompilerParams(
            collective_id=2, has_side_effects=True, vmem_limit_bytes=60 << 20
        ),
        cost_estimate=pl.CostEstimate(
            flops=0, bytes_accessed=6 * width * width * 8, transcendentals=0
        ),
    )(
        piece_of // (3 * per_matrix),
        piece_of // per_matrix % 3,
        piece_of % per_matrix * (piece // GROUP),
        jnp.broadcast_to(held.astype(jnp.int32)[:, None, None], (slots, 1, narrow)),
        early,
        late,
        padded,
    )
    return (slot_grad, gain_sum[:2])


def reduce_all(early, late, gains, piece_of, held, piece):
    width = late.shape[1]
    half = width // 2
    chips = lax.axis_size("chip")
    if width % (2 * chips * GROUP) == 0:
        return reduce_slots(early, late, gains, piece_of, held, piece)
    early = jnp.transpose(early.reshape(width, 3, half), (1, 0, 2)).reshape(3 * width, half)
    early_share = lax.psum_scatter(early, ("chip", "seq"), scatter_dimension=0, tiled=True)
    early_sum = lax.all_gather(early_share, ALL, axis=0, tiled=False)
    early_sum = jnp.transpose(early_sum.reshape(chips, 2, 2, -1, half), (0, 2, 3, 1, 4))
    late_share = lax.psum_scatter(late.reshape(3 * width, width), ALL, scatter_dimension=0, tiled=True)
    late_sum = lax.all_gather(late_share, ALL, axis=0, tiled=True)
    sums = jnp.concatenate([early_sum.reshape(3 * width, width), late_sum], axis=0)
    slot_grad = jnp.where(held[:, None, None], sums.reshape(-1, piece, width)[piece_of], 0)
    return (slot_grad, lax.psum(gains, ALL))


def adam_kernel(rate_ref, master_ref, first_ref, second_ref, grad_ref, *outs):
    new, first_new, second_new = adam_update(
        master_ref[...],
        first_ref[...],
        second_ref[...],
        grad_ref[...].astype(jnp.float32),
        rate_ref[pl.program_id(0)],
        MATRIX_DECAY,
    )
    outs[0][...] = new
    outs[1][...] = first_new
    outs[2][...] = second_new
    outs[3][...] = new.astype(jnp.bfloat16)


def adam_slots(master, first, second, grad, rate):
    slots, piece, width = master.shape
    block = pl.BlockSpec((1, piece, width), lambda i: (i, 0, 0))
    shape = jax.ShapeDtypeStruct(master.shape, jnp.float32)
    return pl.pallas_call(
        adam_kernel,
        grid=(slots,),
        in_specs=[pl.BlockSpec(memory_space=pltpu.SMEM)] + [block] * 4,
        out_specs=[block] * 4,
        out_shape=[shape] * 3 + [jax.ShapeDtypeStruct(master.shape, jnp.bfloat16)],
        cost_estimate=pl.CostEstimate(
            flops=20 * slots * piece * width,
            bytes_accessed=28 * slots * piece * width,
            transcendentals=slots * piece * width,
        ),
    )(rate, master, first, second, grad)


def local(
    tokens,
    cotangent,
    parents,
    owners,
    weight_store,
    gain_store,
    weight_first,
    gain_first,
    weight_second,
    gain_second,
):
    core = lax.axis_index("core")
    dp_pos = lax.axis_index("chip") * 2 + core
    slot_dev, piece, width = weight_store.shape
    pieces = owners.shape[0] - 2
    piece_owner, rank = owner_slots(owners, slot_dev)
    gain_owner = owners[pieces:]
    micro, _, rows, _ = tokens.shape
    half = width // 2
    own_rows = core * rows
    own_columns = core * half

    def mine(value, axis, size, index):
        return lax.dynamic_slice_in_dim(value, index * size, size, axis=axis)

    own_tokens = transposed(tokens[:, 0])
    own_cot = transposed(cotangent[:, 0])
    limit, branch = tail_limits(transposed(parents[:, 0]))
    other_tokens = partner(own_tokens)

    def by_core(own, other, axis):
        return jnp.where(
            core == 0,
            jnp.concatenate([own, other], axis=axis),
            jnp.concatenate([other, own], axis=axis),
        )

    all_tokens = by_core(own_tokens, other_tokens, 1)
    qkv_weight, late_weights, gain_low = gather_store(
        weight_store.astype(jnp.bfloat16), gain_store.astype(jnp.bfloat16), owners, True
    )
    gain_one = gain_low[0].astype(jnp.float32)
    gain_two = gain_low[1].astype(jnp.float32)
    out_weight, up_weight, down_weight = late_weights[0], late_weights[1], late_weights[2]

    def unit(values):
        scale = lax.rsqrt(jnp.mean(values * values, axis=-1, keepdims=True) + NORM_EPS)
        return (values * scale, scale)

    normed_one = (unit(all_tokens.astype(jnp.float32))[0] * gain_one).astype(jnp.bfloat16)
    qkv = product(normed_one, qkv_weight, "mtd,de->mte").astype(jnp.bfloat16)
    attended_half, lse = attend(qkv, limit, branch)
    lse_rows = jnp.transpose(lse[:, :, : half // HEAD], (0, 2, 1))
    attended = by_core(
        mine(attended_half, 1, rows, core), partner(mine(attended_half, 1, rows, 1 - core)), 2
    )
    residual = own_tokens.astype(jnp.float32)
    hidden_one = residual + product(attended, out_weight, "mti,io->mto")
    unit_two, scale_two = unit(hidden_one)
    normed_two = (unit_two * gain_two).astype(jnp.bfloat16)
    up_rows = product(normed_two, up_weight, "mti,io->mto")
    sigmoid_up = jax.nn.sigmoid(up_rows)
    activated = (up_rows * sigmoid_up).astype(jnp.bfloat16)
    mixed_rows = (hidden_one + product(activated, down_weight, "mti,io->mto")).astype(jnp.bfloat16)
    mixed = transposed(mixed_rows)

    grad_down = product(activated, own_cot, "mti,mto->io")
    grad_hidden = product(own_cot, down_weight, "mto,io->mti")
    grad_up_rows = (grad_hidden * (sigmoid_up * (1.0 + up_rows * (1.0 - sigmoid_up)))).astype(
        jnp.bfloat16
    )
    grad_up = product(normed_two, grad_up_rows, "mti,mto->io")
    grad_normed_two = product(grad_up_rows, up_weight, "mto,io->mti")
    gain_two_grad = jnp.sum(grad_normed_two * unit_two, axis=(0, 1))
    grad_hidden_one = own_cot.astype(jnp.float32) + norm_back(
        grad_normed_two, unit_two, scale_two, gain_two
    )
    branch_grad = grad_hidden_one.astype(jnp.bfloat16)
    grad_out = product(attended, branch_grad, "mti,mto->io")
    late = jnp.stack([grad_out, grad_up, grad_down]).astype(jnp.bfloat16)

    grad_attended = product(branch_grad, out_weight, "mto,io->mti").astype(jnp.bfloat16)
    grad_half = by_core(
        mine(grad_attended, 2, half, core), partner(mine(grad_attended, 2, half, 1 - core)), 1
    )
    grad_query, grad_key, grad_value = attend_back(qkv, grad_half, lse_rows, limit, branch)
    grad_qkv_rows = jnp.concatenate([grad_query, grad_key, grad_value], axis=2)
    grad_qkv = product(normed_one, grad_qkv_rows, "mti,mto->io")
    early = grad_qkv.astype(jnp.bfloat16)

    grad_normed_part = product(grad_qkv_rows, qkv_weight, "mte,de->mtd")
    grad_normed_one = mine(grad_normed_part, 1, rows, core) + partner(
        mine(grad_normed_part, 1, rows, 1 - core).astype(jnp.bfloat16)
    ).astype(jnp.float32)
    unit_one, scale_one = unit(residual)
    gain_one_grad = jnp.sum(grad_normed_one * unit_one, axis=(0, 1))
    token_rows = (
        grad_hidden_one + norm_back(grad_normed_one, unit_one, scale_one, gain_one)
    ).astype(jnp.bfloat16)
    token_grad = transposed(token_rows)
    gain_grads = jnp.stack([gain_one_grad, gain_two_grad])

    labels = jnp.arange(slot_dev, dtype=jnp.int32)
    match = (piece_owner[None, :] == dp_pos) & (rank[None, :] == labels[:, None])
    held = jnp.any(match, axis=1)
    piece_of = jnp.sum(jnp.where(match, jnp.arange(pieces, dtype=jnp.int32)[None, :], 0), axis=1)
    slot_grad, gain_sum = reduce_all(early, late, gain_grads, piece_of, held, piece)
    is_out = held & (piece_of // (width // piece) == 3)
    slot_rate = jnp.where(is_out, RATE_OUT, RATE_QKV).astype(jnp.float32)
    weight_new, weight_first_new, weight_second_new, weight_low = adam_slots(
        weight_store, weight_first, weight_second, slot_grad, slot_rate
    )
    gain_slot_grad = jnp.where((gain_owner == dp_pos)[:, None], gain_sum, 0.0)
    gain_new, gain_first_new, gain_second_new = adam_update(
        gain_store, gain_first, gain_second, gain_slot_grad, RATE_GAIN, 0.0
    )
    weight_copies, gain_copies = gather_store(
        weight_low, gain_new.astype(jnp.bfloat16), owners, False
    )
    return (
        mixed[:, None],
        token_grad[:, None],
        weight_new,
        gain_new,
        weight_first_new,
        gain_first_new,
        weight_second_new,
        gain_second_new,
        weight_copies,
        gain_copies,
    )


def solution(mesh):
    dp_count, seq_count = mesh.devices.shape
    fine = Mesh(mesh.devices.reshape(dp_count // 2, 2, seq_count), ALL)
    dp = ("chip", "core")
    rows = P(None, dp, "seq", None)
    store = P(dp, None, None)
    gains = P(dp, None)
    in_specs = (rows, rows, P(None, dp, None), P(), store, gains, store, gains, store, gains)
    out_specs = (rows, rows, store, gains, store, gains, store, gains, P(), P())
    return jax.shard_map(local, mesh=fine, in_specs=in_specs, out_specs=out_specs, check_vma=False)
```

```python
import functools

import jax
import jax.numpy as jnp
from jax import lax
from jax.experimental import pallas as pl
from jax.experimental.pallas import tpu as pltpu
from jax.sharding import Mesh
from jax.sharding import PartitionSpec as P

HEAD = 80
SEG = 32
TRUNK_SEGS = 32
ALWAYS_SEGS = TRUNK_SEGS // 2
STEP = 7
LANES = 128
WINDOW = 256
QUERY_BLOCK = 256

NORM_EPS = 1e-06
BETA_ONE = 0.5
BETA_TWO = 0.5
ADAM_EPS = 1e-08
MATRIX_DECAY = 0.1
RATE_QKV = 0.03
RATE_OUT = 0.4
RATE_GAIN = 0.4
MASKED = -1e30
SCALE = HEAD**-0.5
LOG2E = 1.4426950408889634
ALL = ("chip", "core", "seq")
NT = (((1,), (1,)), ((), ()))
TN = (((0,), (0,)), ((), ()))


def moved(value):
    chips = lax.axis_size("chip")
    pairs = [(k * 4 + c * 2 + 1 - c, k * 4 + 2 - 2 * c + c) for k in range(chips) for c in range(2)]
    return lax.ppermute(value, ALL, pairs)


def settled(value, arrived):
    return jnp.where(lax.axis_index("core") == lax.axis_index("seq"), value, arrived)


def transposed(value):
    return settled(value, moved(value))


def partner(value):
    return lax.ppermute(value, "core", [(0, 1), (1, 0)])


def owner_slots(owners, slot_dev):
    count = owners.shape[0] - 2
    piece_owner = owners[:count]
    labels = jnp.arange(count, dtype=jnp.int32)
    same = (piece_owner[:, None] == piece_owner[None, :]) & (labels[None, :] < labels[:, None])
    rank = jnp.sum(same.astype(jnp.int32), axis=1)
    return (piece_owner, rank)


def tail_limits(parents):
    up = parents[:, TRUNK_SEGS:]
    leaf = up >= TRUNK_SEGS
    above = jnp.where(leaf, up - TRUNK_SEGS, 0)
    labels = jnp.arange(up.shape[1], dtype=jnp.int32)
    hot = above[:, :, None] == labels[None, None, :]
    upper = jnp.sum(jnp.where(hot, up[:, None, :], 0), axis=2)
    attach = jnp.where(leaf, upper, up)
    limit = (attach + 1) * SEG
    branch = jnp.where(leaf, above, -1)
    return (jnp.repeat(limit, SEG, axis=1), jnp.repeat(branch, SEG, axis=1))


def query_blocks(length):
    trunk = TRUNK_SEGS * SEG
    blocks = []
    for first in range(0, trunk, QUERY_BLOCK):
        parts = [(0, first, "all")] if first else []
        blocks.append((first, QUERY_BLOCK, parts + [(first, QUERY_BLOCK, "causal")]))
    always = ALWAYS_SEGS * SEG
    tail = length - trunk
    blocks.append(
        (trunk, tail, [(0, always, "all"), (always, trunk - always, "trunk"), (trunk, tail, "tail")])
    )
    return blocks


def allowed_pairs(kind, key_first, key, query, limit, branch):
    if kind == "causal":
        return key <= query
    if kind == "trunk":
        return key + key_first < limit
    key_seg = key // SEG
    return ((key_seg == query // SEG) & (key <= query)) | (key_seg == branch)


def head_window(head, width):
    start = pl.multiple_of(
        jnp.minimum((head * HEAD) // LANES, width // LANES - WINDOW // LANES) * LANES, LANES
    )
    lane = lax.broadcasted_iota(jnp.int32, (1, WINDOW), 1) + start
    mine = (lane >= head * HEAD) & (lane < (head + 1) * HEAD)
    return (pl.ds(start, WINDOW), mine)


def attend_kernel(limit_ref, branch_ref, q_ref, k_ref, v_ref, out_ref, lse_ref):
    head = pl.program_id(1)
    window, mine = head_window(head, q_ref.shape[2])
    stat_lane = lax.broadcasted_iota(jnp.int32, (1, LANES), 1)
    for first, count, parts in query_blocks(q_ref.shape[1]):
        rows = pl.ds(first, count)
        query = jnp.where(mine, q_ref[0, rows, window], 0)
        scores = []
        for key_first, keys, kind in parts:
            raw = lax.dot_general(
                query, k_ref[0, pl.ds(key_first, keys), window], NT, preferred_element_type=jnp.float32
            ) * (SCALE * LOG2E)
            if kind != "all":
                ok = allowed_pairs(
                    kind,
                    key_first,
                    lax.broadcasted_iota(jnp.int32, (count, keys), 1),
                    lax.broadcasted_iota(jnp.int32, (count, keys), 0),
                    limit_ref[0],
                    branch_ref[0],
                )
                raw = jnp.where(ok, raw, MASKED)
            scores.append(raw)
        top = functools.reduce(jnp.maximum, [jnp.max(s, axis=1, keepdims=True) for s in scores])
        total = 0.0
        gained = 0.0
        for raw, (key_first, keys, kind) in zip(scores, parts):
            weight = jnp.exp2(raw - top)
            total = total + jnp.sum(weight, axis=1, keepdims=True)
            gained = gained + jnp.dot(
                weight.astype(jnp.bfloat16),
                v_ref[0, pl.ds(key_first, keys), window],
                preferred_element_type=jnp.float32,
            )
        gained = (gained / total).astype(jnp.bfloat16)
        out_ref[0, rows, window] = jnp.where(mine, gained, out_ref[0, rows, window])
        lse_ref[0, rows, :] = jnp.where(
            stat_lane == head, top + jnp.log2(total), lse_ref[0, rows, :]
        )


def attend(qkv, limit, branch):
    micro, length, columns = qkv.shape
    width = columns // 3
    heads = width // HEAD
    tail = length - TRUNK_SEGS * SEG

    def part(index):
        return pl.BlockSpec((1, length, width), lambda m, h, index=index: (m, 0, index))

    column = pl.BlockSpec((1, tail, 1), lambda m, h: (m, 0, 0))
    return pl.pallas_call(
        attend_kernel,
        grid=(micro, heads),
        in_specs=[column, column, part(0), part(1), part(2)],
        out_specs=[
            pl.BlockSpec((1, length, width), lambda m, h: (m, 0, 0)),
            pl.BlockSpec((1, length, LANES), lambda m, h: (m, 0, 0)),
        ],
        out_shape=[
            jax.ShapeDtypeStruct((micro, length, width), jnp.bfloat16),
            jax.ShapeDtypeStruct((micro, length, LANES), jnp.float32),
        ],
        compiler_params=pltpu.CompilerParams(vmem_limit_bytes=48 << 20),
        cost_estimate=pl.CostEstimate(
            flops=micro * heads * length * length * WINDOW * 3,
            bytes_accessed=micro * length * width * 8,
            transcendentals=micro * heads * length * length // 2,
        ),
    )(limit[:, :, None], branch[:, :, None], qkv, qkv, qkv)


def attend_back_kernel(
    limit_ref, branch_ref, lse_ref, q_ref, k_ref, v_ref, g_ref, dq_ref, dk_ref, dv_ref, dk_sum, dv_sum
):
    head = pl.program_id(1)
    window, mine = head_window(head, q_ref.shape[2])

    @pl.when(head == 0)
    def clear():
        dk_sum[...] = jnp.zeros_like(dk_sum)
        dv_sum[...] = jnp.zeros_like(dv_sum)

    for first, count, parts in query_blocks(q_ref.shape[1]):
        rows = pl.ds(first, count)
        query = jnp.where(mine, q_ref[0, rows, window], 0)
        grad = jnp.where(mine, g_ref[0, rows, window], 0)
        lse = lse_ref[0, pl.ds(head, 1), rows]
        held = []
        row_total = 0.0
        for key_first, keys, kind in parts:
            where = pl.ds(key_first, keys)
            raw = lax.dot_general(
                k_ref[0, where, window], query, NT, preferred_element_type=jnp.float32
            )
            prob = jnp.exp2(raw * (SCALE * LOG2E) - lse)
            if kind != "all":
                ok = allowed_pairs(
                    kind,
                    key_first,
                    lax.broadcasted_iota(jnp.int32, (keys, count), 0),
                    lax.broadcasted_iota(jnp.int32, (keys, count), 1),
                    limit_ref[0],
                    branch_ref[0],
                )
                prob = jnp.where(ok, prob, 0.0)
            grad_prob = lax.dot_general(
                v_ref[0, where, window], grad, NT, preferred_element_type=jnp.float32
            )
            row_total = row_total + jnp.sum(prob * grad_prob, axis=0, keepdims=True)
            held.append((where, prob, grad_prob))
        grad_query = 0.0
        for where, prob, grad_prob in held:
            grad_raw = (prob * (grad_prob - row_total)).astype(jnp.bfloat16)
            dv_sum[where, window] += jnp.dot(
                prob.astype(jnp.bfloat16), grad, preferred_element_type=jnp.float32
            )
            dk_sum[where, window] += jnp.dot(grad_raw, query, preferred_element_type=jnp.float32)
            grad_query = grad_query + lax.dot_general(
                grad_raw, k_ref[0, where, window], TN, preferred_element_type=jnp.float32
            )
        dq_ref[0, rows, window] = jnp.where(
            mine, (grad_query * SCALE).astype(jnp.bfloat16), dq_ref[0, rows, window]
        )

    @pl.when(head == pl.num_programs(1) - 1)
    def write():
        dk_ref[0] = (dk_sum[...] * SCALE).astype(jnp.bfloat16)
        dv_ref[0] = dv_sum[...].astype(jnp.bfloat16)


def attend_back(qkv, grad, lse, limit, branch):
    micro, length, columns = qkv.shape
    width = columns // 3
    heads = width // HEAD
    tail = length - TRUNK_SEGS * SEG

    def part(index):
        return pl.BlockSpec((1, length, width), lambda m, h, index=index: (m, 0, index))

    row = pl.BlockSpec((1, 1, tail), lambda m, h: (m, 0, 0))
    shape = jax.ShapeDtypeStruct((micro, length, width), jnp.bfloat16)
    return pl.pallas_call(
        attend_back_kernel,
        grid=(micro, heads),
        in_specs=[
            row,
            row,
            pl.BlockSpec((1, heads, length), lambda m, h: (m, 0, 0)),
            part(0),
            part(1),
            part(2),
            part(0),
        ],
        out_specs=[part(0), part(0), part(0)],
        out_shape=[shape, shape, shape],
        scratch_shapes=[pltpu.VMEM((length, width), jnp.float32)] * 2,
        compiler_params=pltpu.CompilerParams(vmem_limit_bytes=56 << 20),
        cost_estimate=pl.CostEstimate(
            flops=micro * heads * length * length * WINDOW * 7,
            bytes_accessed=micro * length * width * 14,
            transcendentals=micro * heads * length * length // 2,
        ),
    )(limit[:, None, :], branch[:, None, :], lse, qkv, qkv, qkv, grad)


def norm_back(grad_normed, normed_unit, scale_rows, gain_row):
    scaled_grad = grad_normed * gain_row
    return scale_rows * (
        scaled_grad - normed_unit * jnp.mean(scaled_grad * normed_unit, axis=-1, keepdims=True)
    )


def adam_update(master, first, second, grad, rate, decay):
    first_new = BETA_ONE * first + (1.0 - BETA_ONE) * grad
    second_new = BETA_TWO * second + (1.0 - BETA_TWO) * grad * grad
    fix_one = 1.0 - BETA_ONE**STEP
    fix_two = 1.0 - BETA_TWO**STEP
    step_size = first_new / fix_one / (jnp.sqrt(second_new / fix_two) + ADAM_EPS)
    return (master - rate * (step_size + decay * master), first_new, second_new)


def product(left, right, spec):
    return jnp.einsum(spec, left, right, preferred_element_type=jnp.float32)


Y_CHIPS = 2
CAPACITY = 8
SPARE = 8
GROUP = 16
CHUNK = 256
MESH_IDS = pl.DeviceIdType.MESH


def place():
    chip = lax.axis_index("chip")
    return (
        chip // Y_CHIPS,
        lax.rem(chip, Y_CHIPS),
        lax.axis_index("core"),
        lax.axis_index("seq"),
        lax.axis_size("chip") // Y_CHIPS,
    )


def at_z(z, y):
    return {"chip": z * Y_CHIPS + y}


def ahead(d):
    z, y, core, x, depth = place()
    return at_z(lax.rem(z + d, depth), y)


def across(axis):
    z, y, core, x, _ = place()
    return {"y": at_z(z, 1 - y), "x": {"seq": 1 - x}, "core": {"core": 1 - core}}[axis]


def greet():
    depth = place()[4]
    barrier = pltpu.get_barrier_semaphore()
    peers = [ahead(d) for d in range(1, depth)] + [across("y"), across("x"), across("core")]
    for peer in peers:
        pl.semaphore_signal(barrier, inc=1, device_id=peer, device_id_type=MESH_IDS)
    pl.semaphore_wait(barrier, len(peers))


def sem_pair(*shape):
    return [pltpu.SemaphoreType.DMA(shape), pltpu.SemaphoreType.DMA(shape)]


def remote(source, target, sems, index, device):
    return pltpu.make_async_remote_copy(
        src_ref=source,
        dst_ref=target,
        send_sem=sems[0].at[index],
        recv_sem=sems[1].at[index],
        device_id=device,
        device_id_type=MESH_IDS,
    )


def total(*parts):
    return functools.reduce(jnp.add, [p.astype(jnp.float32) for p in parts]).astype(jnp.bfloat16)


class Flow:
    def __init__(self):
        self.sent = []

    def push(self, source, target, sems, index, device):
        copy = remote(source, target, sems, index, device)
        copy.start()
        self.sent.append(copy)

    def arrive(self, here, sems, index):
        remote(here, here, sems, index, across("core")).wait_recv()

    def drain(self):
        for copy in self.sent:
            copy.wait_send()


class Total(Flow):
    def __init__(self, axes, sums, inbox, sems):
        super().__init__()
        self.axes, self.sums, self.inbox, self.sems = (axes, sums, inbox, sems)
        self.done = 0

    def begin(self, value):
        self.sums[0] = value
        self.push(self.sums.at[0], self.inbox.at[0], self.sems, (0,), across(self.axes[0]))

    def step(self):
        i = self.done
        self.done += 1
        self.arrive(self.inbox.at[i], self.sems, (i,))
        self.sums[i + 1] = self.sums[i] + self.inbox[i]
        here = self.sums.at[i + 1]
        if i + 1 < len(self.axes):
            self.push(here, self.inbox.at[i + 1], self.sems, (i + 1,), across(self.axes[i + 1]))
            return
        for d in range(1, place()[4]):
            self.push(here, self.inbox.at[i + d], self.sems, (i + d,), ahead(d))

    def result(self):
        last = len(self.axes)
        value = self.sums[last]
        for d in range(1, place()[4]):
            self.arrive(self.inbox.at[last - 1 + d], self.sems, (last - 1 + d,))
            value = value + self.inbox[last - 1 + d]
        self.drain()
        return value


def total_scratch(axes, depth, width):
    return [
        pltpu.VMEM((axes + 1, 8, width), jnp.float32),
        pltpu.VMEM((axes + depth - 1, 8, width), jnp.float32),
    ] + sem_pair(axes + depth - 1)


def spread_sems(depth):
    return sem_pair(depth) + sem_pair(depth) + sem_pair(depth, 2) + sem_pair(depth, 4)


class Spread(Flow):
    def __init__(self, window, second, sems):
        super().__init__()
        self.window = window
        self.second = second
        self.third = "x" if second == "y" else "y"
        self.sems = [(sems[2 * i], sems[2 * i + 1]) for i in range(4)]

    def where(self, d, second=False, third=False, other_core=False):
        z, y, core, x, depth = place()
        if second if self.second == "y" else third:
            y = 1 - y
        if third if self.second == "y" else second:
            x = 1 - x
        return self.window(lax.rem(z - d + depth, depth), y, 1 - core if other_core else core, x)

    def forward(self, stage, index, block, device):
        self.push(block, block, self.sems[stage], index, device)

    def begin(self):
        for d in range(1, place()[4]):
            self.forward(0, (d,), self.where(0), ahead(d))
        self.onward(0)

    def onward(self, d):
        block = self.where(d)
        self.forward(1, (d,), block, across(self.second))
        self.forward(2, (d, 0), block, across(self.third))
        self.forward(3, (d, 0), block, across("core"))

    def from_z(self, d):
        self.arrive(self.where(d), self.sems[0], (d,))
        self.onward(d)

    def from_second(self, d):
        block = self.where(d, True)
        self.arrive(block, self.sems[1], (d,))
        self.forward(2, (d, 1), block, across(self.third))
        self.forward(3, (d, 2), block, across("core"))

    def from_third(self, d):
        for second in range(2):
            block = self.where(d, bool(second), True)
            self.arrive(block, self.sems[2], (d, second))
            self.forward(3, (d, 2 * second + 1), block, across("core"))

    def finish(self):
        for d in range(place()[4]):
            for second in range(2):
                for third in range(2):
                    block = self.where(d, bool(second), bool(third), True)
                    self.arrive(block, self.sems[3], (d, 2 * second + third))
        self.drain()


def device_block(z, y, core, x):
    return ((z * Y_CHIPS + y) * 2 + core) * 2 + x


def chip_block(z, y, x):
    return (z * Y_CHIPS + y) * 2 + x


def gather_kernel(
    split,
    cut,
    block_ref,
    row_ref,
    spare_rank_ref,
    spare_mine_ref,
    low_ref,
    gain_ref,
    *refs,
):
    outs = refs[: 4 if split else 1]
    gain_out, whole, stage, stage_sem, spare, core_in, y_in, z_in, held = refs[len(outs) : len(outs) + 9]
    gain_sum, gain_in = refs[len(outs) + 9 : len(outs) + 11]
    sems = refs[len(outs) + 11 :]
    z, y, core, x, depth = place()
    piece, width = low_ref.shape[1:]
    half = CAPACITY // 2
    base = half * piece // GROUP
    me = device_block(z, y, core, x)
    per_piece = piece // GROUP
    for i in range(base):
        source = pl.ds(i % per_piece * GROUP, GROUP)
        whole[me, i] = low_ref[x * half + i // per_piece, source]
    greet()

    def window(first, count):
        return lambda *who: whole.at[device_block(*who), pl.ds(first, count)]

    flow_sems = 8
    early = Spread(window(0, cut), "y", sems[2 : 2 + flow_sems])
    late = Spread(window(cut, base - cut), "x", sems[10 : 10 + flow_sems])
    loose = Spread(window(base, 1), "x", sems[18 : 18 + flow_sems])
    gains = Total(["core", "y"], gain_sum, gain_in, sems[0:2])
    spare_sems = sems[26:32]
    spare_flow = Flow()
    early.begin()
    late.begin()
    gains.begin(gain_ref[...])
    count = SPARE // 2
    for i in range(count):
        found = low_ref[spare_rank_ref[x * count + i]]
        spare[pl.ds(i * piece, piece)] = jnp.where(spare_mine_ref[x * count + i] > 0, found, 0)
    rows = core_in.shape[0]

    def part(index, size):
        return pl.ds(pl.multiple_of(index * size, GROUP), size)

    spare_flow.push(spare.at[part(1 - core, rows)], core_in, spare_sems[0:2], (0,), across("core"))
    flows = [early, late]

    def from_z(d):
        for flow in flows:
            flow.from_z(d)

    def from_second(d):
        for flow in flows:
            flow.from_second(d)

    from_z(1)
    spare_flow.arrive(core_in, spare_sems[0:2], (0,))
    held[...] = total(spare[part(core, rows)], core_in[...])
    spare_flow.push(held.at[part(1 - y, rows // 2)], y_in, spare_sems[2:4], (0,), across("y"))
    gains.step()
    from_second(0)
    for d in range(2, depth):
        from_z(d)
        if d == 2:
            spare_flow.arrive(y_in, spare_sems[2:4], (0,))
            y_in[...] = total(held[part(y, rows // 2)], y_in[...])
            for e in range(1, depth):
                to = part(lax.rem(z + e, depth), GROUP)
                spare_flow.push(y_in.at[to], z_in.at[e], spare_sems[4:6], (e,), ahead(e))
            gains.step()
        from_second(d - 1)
    for d in range(1, depth):
        spare_flow.arrive(z_in.at[d], spare_sems[4:6], (d,))
    whole[me, base] = total(y_in[part(z, GROUP)], *[z_in[d] for d in range(1, depth)])
    loose.begin()
    from_second(depth - 1)
    gain_out[...] = gains.result()
    for d in range(1, depth):
        loose.from_z(d)
    for flow in flows:
        flow.from_third(0)
    for d in range(depth):
        loose.from_second(d)
    for d in range(1, depth):
        for flow in flows:
            flow.from_third(d)
    for d in range(depth):
        loose.from_third(d)
    for flow in flows + [loose]:
        flow.finish()
    spare_flow.drain()

    buffers = stage.shape[0]
    per_chunk = CHUNK // GROUP
    narrow = width // 2
    copies = []
    for index in range(6 * width // CHUNK):
        matrix, first = divmod(index * CHUNK, width)
        slot = index % buffers
        if index >= buffers:
            copies[index - buffers].wait()
        thin = split and matrix < 3
        columns = pl.ds(pl.multiple_of(core * narrow, LANES), narrow) if thin else slice(None)
        count = narrow if thin else width

        def step(i, carry, index=index, slot=slot, columns=columns, count=count):
            for g in range(per_piece):
                at = index * per_chunk + i * per_piece + g
                target = pl.ds(pl.multiple_of(i * piece + g * GROUP, GROUP), GROUP)
                stage[slot, target, pl.ds(0, count)] = whole[block_ref[at], row_ref[at], :, columns]
            return carry

        lax.fori_loop(0, per_chunk // per_piece, step, 0)
        if thin:
            target = outs[0].at[pl.ds(first, CHUNK), pl.ds(matrix * narrow, narrow)]
        elif split:
            target = outs[matrix - 2].at[pl.ds(first, CHUNK)]
        else:
            target = outs[0].at[matrix, pl.ds(first, CHUNK)]
        copies.append(
            pltpu.make_async_copy(stage.at[slot, :, pl.ds(0, count)], target, stage_sem.at[slot])
        )
        copies[-1].start()
    for copy in copies[-buffers:]:
        copy.wait()


def gather_pieces(low, gains, plan, split):
    slots, piece, width = low.shape
    block, row, spare_rank, spare_mine, gain_mine = plan
    chips = lax.axis_size("chip")
    depth = chips // Y_CHIPS
    base = CAPACITY // 2 * piece // GROUP
    shapes = [(width, 3 * (width // 2))] + [(width, width)] * 3 if split else [(6, width, width)]
    lane = SPARE * piece // 4
    buffers = 4
    picked = jnp.where(gain_mine[:, None], gains[: gain_mine.shape[0]].astype(jnp.float32), 0.0)
    padded = jnp.concatenate([picked, jnp.zeros((6, width), jnp.float32)], axis=0)
    vmem = pl.BlockSpec(memory_space=pltpu.VMEM)
    smem = pl.BlockSpec(memory_space=pltpu.SMEM)
    outs = pl.pallas_call(
        functools.partial(gather_kernel, split, base // 4 if split else base // 2),
        in_specs=[smem] * 3 + [vmem] * 3,
        out_specs=[pl.BlockSpec(memory_space=pl.ANY)] * len(shapes) + [vmem],
        out_shape=[jax.ShapeDtypeStruct(s, jnp.bfloat16) for s in shapes]
        + [jax.ShapeDtypeStruct((8, width), jnp.float32)],
        scratch_shapes=[
            pltpu.VMEM((4 * chips, base + 1, GROUP, width), jnp.bfloat16),
            pltpu.VMEM((buffers, CHUNK, width), jnp.bfloat16),
            pltpu.SemaphoreType.DMA((buffers,)),
            pltpu.VMEM((2 * lane, width), jnp.bfloat16),
            pltpu.VMEM((lane, width), jnp.bfloat16),
            pltpu.VMEM((lane // 2, width), jnp.bfloat16),
            pltpu.VMEM((depth, GROUP, width), jnp.bfloat16),
            pltpu.VMEM((lane, width), jnp.bfloat16),
        ]
        + total_scratch(2, depth, width)
        + spread_sems(depth) * 3
        + sem_pair(1)
        + sem_pair(1)
        + sem_pair(depth),
        compiler_params=pltpu.CompilerParams(
            collective_id=0 if split else 1, has_side_effects=True, vmem_limit_bytes=48 << 20
        ),
        cost_estimate=pl.CostEstimate(
            flops=0, bytes_accessed=6 * width * width * 16, transcendentals=0
        ),
    )(
        block.reshape(-1),
        row.reshape(-1),
        spare_rank,
        jnp.broadcast_to(spare_mine[:, None, None], (SPARE, 1, width)),
        low,
        padded,
    )
    return (*outs[:-1], outs[-1][:2].astype(jnp.bfloat16))


def halves(matrices, split):
    if not split:
        return (matrices,)
    width = matrices.shape[1]
    narrow = width // 2
    thin = lax.dynamic_slice_in_dim(matrices[:3], lax.axis_index("core") * narrow, narrow, axis=2)
    side = jnp.concatenate([thin[0], thin[1], thin[2]], axis=1)
    return (side, matrices[3], matrices[4], matrices[5])


def gather_slots(low, gains, owners, split):
    slots, piece, width = low.shape
    piece_owner, rank = owner_slots(owners, slots)
    rows = slots * piece
    half = -(-(rows // 2 + 1) // GROUP) * GROUP
    filler = jnp.zeros((2 * half - rows - 2, width), jnp.bfloat16)
    packed = jnp.concatenate([low.reshape(rows, width), gains, filler], axis=0)
    share = lax.dynamic_slice_in_dim(packed, lax.axis_index("seq") * half, half, axis=0)
    groups = lax.all_gather(share, ALL, axis=0, tiled=True).reshape(-1, GROUP, width)
    per_owner = 2 * half // GROUP
    base = piece_owner * per_owner + rank * (piece // GROUP)
    index = base[:, None] + jnp.arange(piece // GROUP, dtype=jnp.int32)[None, :]
    matrices = groups[index.reshape(-1)].reshape(6, width, width)
    gain_rows = groups[owners[-2:] * per_owner + rows // GROUP][jnp.arange(2), jnp.arange(2)]
    return (*halves(matrices, split), gain_rows)


def kernels_fit(slots, piece, width):
    chips = lax.axis_size("chip")
    return slots == 2 * CAPACITY and piece == GROUP * (chips // Y_CHIPS) and width % CHUNK == 0


def spare_pieces(owners, slots):
    piece_owner, rank = owner_slots(owners, slots)
    spare = rank >= CAPACITY
    return (piece_owner, rank, spare, jnp.cumsum(spare.astype(jnp.int32)) - 1)


def more_rounds(order):
    return (order[-1] + SPARE) // SPARE - 1


def gather_store(low, gains, owners, split):
    slots, piece, width = low.shape
    if not kernels_fit(slots, piece, width):
        return gather_slots(low, gains, owners, split)
    dp_pos = lax.axis_index("chip") * 2 + lax.axis_index("core")
    piece_owner, rank, spare, order = spare_pieces(owners, slots)
    half = CAPACITY // 2
    groups = piece // GROUP
    group = jnp.arange(groups, dtype=jnp.int32)[None, :]
    block = jnp.where(
        spare[:, None],
        device_block(group, (order % 2)[:, None], ((order // 2) % 2)[:, None], (order // 4 % 2)[:, None]),
        (piece_owner * 2 + rank // half)[:, None],
    )
    row = jnp.where(spare[:, None], half * groups, (rank % half)[:, None] * groups + group)

    def mine(first):
        labels = first + jnp.arange(SPARE, dtype=jnp.int32)
        hot = spare[None, :] & (order[None, :] == labels[:, None])
        own = hot & (piece_owner == dp_pos)[None, :]
        at = jnp.sum(jnp.where(own, rank[None, :], 0), axis=1)
        return (hot, at, jnp.any(own, axis=1))

    _, spare_rank, spare_mine = mine(0)
    plan = (block, row, spare_rank, spare_mine.astype(jnp.int32), owners[-2:] == dp_pos)
    *matrices, gain_rows = gather_pieces(low, gains, plan, split)

    def more(state):
        index, *held = state
        hot, at, own = mine(index * SPARE)
        found = lax.psum(jnp.where(own[:, None, None], low[at], 0), ("chip", "core"))
        which = jnp.argmax(hot, axis=0)
        whole = found[which].reshape(6, width, width)
        taken = jnp.any(hot, axis=0).astype(jnp.bfloat16)
        mask = jnp.broadcast_to(taken[:, None, None], (taken.shape[0], piece, width))
        masks = halves(mask.reshape(6, width, width), split)
        new = [jnp.where(m > 0, n, h) for m, n, h in zip(masks, halves(whole, split), held)]
        return (index + 1, *new)

    rounds = more_rounds(order)
    state = lax.while_loop(lambda s: s[0] <= rounds, more, (jnp.int32(1), *matrices))
    return (*state[1:], gain_rows)


class Reduce(Flow):
    def __init__(self, first, shard, one, two, three, sems):
        super().__init__()
        self.first = first
        self.other = "y" if first == "x" else "x"
        self.shard = shard
        self.one, self.two, self.three = (one, two, three)
        self.sems = [sems[0:2], sems[2:4], sems[4:6]]

    def start(self, d, b):
        self.push(self.shard(d, b, 1), self.one.at[d, b], self.sems[0], (d, b), across(self.first))

    def from_first(self, d, b):
        here = self.one.at[d, b]
        self.arrive(here, self.sems[0], (d, b))
        here[...] = total(here[...], self.shard(d, b, 0)[...])
        if b:
            self.push(here, self.two.at[d], self.sems[1], (d,), across(self.other))

    def from_second(self, d):
        here = self.two.at[d]
        self.arrive(here, self.sems[1], (d,))
        here[...] = total(here[...], self.one[d, 0])
        if d:
            self.push(here, self.three.at[d], self.sems[2], (d,), ahead(d))

    def result(self):
        depth = place()[4]
        for d in range(1, depth):
            self.arrive(self.three.at[d], self.sems[2], (d,))
        value = total(self.two[0], *[self.three[d] for d in range(1, depth)])
        self.drain()
        return value


def reduce_kernel(
    source_ref,
    spare_z_ref,
    spare_y_ref,
    spare_x_ref,
    spare_sub_ref,
    spare_mine_ref,
    early_ref,
    late_ref,
    gain_ref,
    slot_ref,
    gain_out,
    pieces,
    blocks,
    early_one,
    early_two,
    early_three,
    late_one,
    late_two,
    late_three,
    final,
    pair_in,
    full,
    full_in,
    spares,
    gain_sum,
    gain_in,
    load_sem,
    *sems,
):
    z, y, core, x, depth = place()
    narrow = pieces.shape[2]
    groups = late_ref.shape[1]
    per_block = blocks.shape[1]
    cut = per_block // 2
    owned = CAPACITY // 2 * slot_ref.shape[1]
    order = [d for d in range(1, depth)] + [0]
    loads = []
    for matrix in range(3):
        columns = pl.ds(matrix * narrow, narrow)
        loads.append((early_ref.at[:, :, columns], matrix))
        loads.append((late_ref.at[matrix], matrix + 3))
    loads = [
        pltpu.make_async_copy(source, pieces.at[pl.ds(m * groups, groups)], load_sem.at[m])
        for source, m in loads
    ]
    for load in loads:
        load.start()
    pieces[6 * groups] = jnp.zeros((GROUP, narrow), jnp.bfloat16)
    greet()
    gains = Total(["core", "x", "y"], gain_sum, gain_in, sems[0:2])
    gains.begin(gain_ref[...])
    for load in loads:
        load.wait()

    def block_at(d, swap_y, swap_x):
        return chip_block(
            lax.rem(z + d, depth), 1 - y if swap_y else y, 1 - x if swap_x else x
        )

    early = Reduce(
        "x",
        lambda d, b, a: blocks.at[block_at(d, b, a), pl.ds(0, cut)],
        early_one,
        early_two,
        early_three,
        sems[2:8],
    )
    late = Reduce(
        "y",
        lambda d, b, a: blocks.at[block_at(d, a, b), pl.ds(cut, per_block - cut)],
        late_one,
        late_two,
        late_three,
        sems[8:14],
    )

    def fill(d, swap_y, swap_x):
        block = block_at(d, swap_y, swap_x)

        def step(i, carry):
            for g in range(2):
                blocks[block, 2 * i + g] = pieces[source_ref[block * per_block + 2 * i + g]]
            return carry

        lax.fori_loop(0, per_block // 2, step, 0)

    for d in order:
        fill(d, 1, 1)
        early.start(d, 1)
        late.start(d, 1)
        fill(d, 0, 1)
        early.start(d, 0)
        fill(d, 1, 0)
        late.start(d, 0)
        fill(d, 0, 0)
    gains.step()
    for d in order:
        for b in (1, 0):
            for flow in (early, late):
                flow.from_first(d, b)
    gains.step()
    for d in order:
        for flow in (early, late):
            flow.from_second(d)
    gains.step()
    final[pl.ds(0, cut)] = early.result()
    final[pl.ds(cut, per_block - cut)] = late.result()

    ends = Flow()
    own_spare = spares.at[z, y, x, core]
    ends.push(final.at[pl.ds((1 - core) * owned, owned)], pair_in, sems[14:16], (0,), across("core"))
    spares[z, y, x, core] = final[pl.ds(2 * owned, 2)]
    for d in range(1, depth):
        ends.push(own_spare, own_spare, sems[16:18], (d,), ahead(d))
    gain_out[...] = gains.result()
    ends.arrive(pair_in, sems[14:16], (0,))
    for g in range(owned):
        mine = final[core * owned + g]
        theirs = pair_in[g]
        first = core == 0
        full[g, :, pl.ds(pl.multiple_of(core * narrow, LANES), narrow)] = mine
        full[g, :, pl.ds(pl.multiple_of((1 - core) * narrow, LANES), narrow)] = theirs
    ends.push(full, full_in, sems[14:16], (1,), across("x"))
    for d in range(1, depth):
        from_z = spares.at[lax.rem(z - d + depth, depth), y, x, core]
        ends.arrive(from_z, sems[16:18], (d,))
    here = spares.at[:, y, x, core]
    ends.push(here, here, sems[14:16], (2,), across("y"))
    ends.arrive(spares.at[:, 1 - y, x, core], sems[14:16], (2,))
    here = spares.at[:, :, x, core]
    ends.push(here, here, sems[14:16], (3,), across("x"))
    ends.arrive(spares.at[:, :, 1 - x, core], sems[14:16], (3,))
    here = spares.at[:, :, :, core]
    ends.push(here, here, sems[14:16], (4,), across("core"))
    ends.arrive(spares.at[:, :, :, 1 - core], sems[14:16], (4,))
    ends.arrive(full_in, sems[14:16], (1,))
    per_piece = slot_ref.shape[1]
    half = CAPACITY // 2
    for i in range(half):
        for g in range(per_piece):
            slot_ref[x * half + i, g] = full[i * per_piece + g]
            slot_ref[(1 - x) * half + i, g] = full_in[i * per_piece + g]

    def pick(slot, carry):
        for g in range(per_piece):
            at = slot * per_piece + g
            for side in range(2):
                found = spares[
                    spare_z_ref[at], spare_y_ref[at], spare_x_ref[at], side, spare_sub_ref[at]
                ]
                slot_ref[CAPACITY + slot, g, :, pl.ds(side * narrow, narrow)] = jnp.where(
                    spare_mine_ref[slot] > 0, found, 0
                )
        return carry

    lax.fori_loop(0, slot_ref.shape[0] - CAPACITY, pick, 0)
    ends.drain()


def reduce_slots(early, late, gains, owners, slots, piece):
    width = late.shape[1]
    narrow = width // 2
    chips = lax.axis_size("chip")
    depth = chips // Y_CHIPS
    groups = width // GROUP
    per_piece = piece // GROUP
    dp_pos = lax.axis_index("chip") * 2 + lax.axis_index("core")
    piece_owner, rank, spare, order = spare_pieces(owners, slots)
    half = CAPACITY // 2
    labels = jnp.arange(piece_owner.shape[0], dtype=jnp.int32)
    empty = 6 * groups

    def groups_of(match):
        first = jnp.sum(jnp.where(match, labels, 0), axis=-1)[..., None] * per_piece
        groups_at = first + jnp.arange(per_piece, dtype=jnp.int32)
        return jnp.where(jnp.any(match, axis=-1)[..., None], groups_at, empty)

    block = jnp.arange(2 * chips, dtype=jnp.int32)[:, None]
    entry = jnp.arange(CAPACITY, dtype=jnp.int32)[None, :]
    owner_at = block // 2 * 2 + entry // half
    rank_at = block % 2 * half + entry % half
    base_groups = groups_of(
        (piece_owner == owner_at[..., None]) & (rank == rank_at[..., None])
    ).reshape(2 * chips, -1)
    spare_hot = spare & (order == jnp.arange(SPARE, dtype=jnp.int32)[:, None])
    spare_groups = groups_of(spare_hot).reshape(2 * chips, -1)
    source = jnp.concatenate([base_groups, spare_groups], axis=1)
    per_block = source.shape[1]
    mine = (piece_owner == dp_pos) & spare & (order < SPARE)
    slot_hot = mine & (rank == CAPACITY + jnp.arange(slots - CAPACITY, dtype=jnp.int32)[:, None])
    spare_at = jnp.sum(jnp.where(slot_hot, order, 0), axis=1)
    at = (spare_at[:, None] * per_piece + jnp.arange(per_piece, dtype=jnp.int32)).reshape(-1)
    subs = SPARE * per_piece // (2 * chips)
    chip_at = at // subs

    vmem = pl.BlockSpec(memory_space=pltpu.VMEM)
    smem = pl.BlockSpec(memory_space=pltpu.SMEM)
    hbm = pl.BlockSpec(memory_space=pl.ANY)
    cut = per_block // 2
    owned = half * per_piece
    padded = jnp.concatenate([gains, jnp.zeros((8 - gains.shape[0], width), jnp.float32)], axis=0)

    def group_block(*shape):
        return pltpu.VMEM(shape + (GROUP, narrow), jnp.bfloat16)

    def flow_blocks(count):
        return [group_block(depth, 2, count), group_block(depth, count), group_block(depth, count)]

    flow_sems = sem_pair(depth, 2) + sem_pair(depth) + sem_pair(depth)
    slot_grad, gain_sum = pl.pallas_call(
        reduce_kernel,
        in_specs=[smem] * 5 + [vmem, hbm, hbm, vmem],
        out_specs=[vmem, vmem],
        out_shape=[
            jax.ShapeDtypeStruct((slots, per_piece, GROUP, width), jnp.bfloat16),
            jax.ShapeDtypeStruct((8, width), jnp.float32),
        ],
        scratch_shapes=[group_block(6 * groups + 1), group_block(2 * chips, per_block)]
        + flow_blocks(cut)
        + flow_blocks(per_block - cut)
        + [
            group_block(per_block),
            group_block(owned),
            pltpu.VMEM((owned, GROUP, width), jnp.bfloat16),
            pltpu.VMEM((owned, GROUP, width), jnp.bfloat16),
            group_block(depth, Y_CHIPS, 2, 2, subs),
        ]
        + total_scratch(3, depth, width)[:2]
        + [pltpu.SemaphoreType.DMA((6,))]
        + total_scratch(3, depth, width)[2:]
        + flow_sems
        + flow_sems
        + sem_pair(5)
        + sem_pair(depth),
        compiler_params=pltpu.CompilerParams(
            collective_id=2, has_side_effects=True, vmem_limit_bytes=56 << 20
        ),
        cost_estimate=pl.CostEstimate(
            flops=0, bytes_accessed=6 * width * width * 8, transcendentals=0
        ),
    )(
        source.reshape(-1),
        chip_at // 2 // Y_CHIPS,
        chip_at // 2 % Y_CHIPS,
        chip_at % 2,
        at % subs,
        jnp.broadcast_to(jnp.any(slot_hot, axis=1).astype(jnp.int32)[:, None, None], (slots - CAPACITY, 1, narrow)),
        early.reshape(groups, GROUP, 3 * narrow),
        late.reshape(3, groups, GROUP, narrow),
        padded,
    )
    return (slot_grad.reshape(slots, piece, width), gain_sum[:2])


def reduce_all(early, late, gains, owners, slots, piece):
    width = late.shape[1]
    narrow = width // 2
    core = lax.axis_index("core")
    dp_pos = lax.axis_index("chip") * 2 + core
    pieces = owners.shape[0] - 2
    if kernels_fit(slots, piece, width):
        slot_grad, gain_sum = reduce_slots(early, late, gains, owners, slots, piece)
        piece_owner, rank, spare, order = spare_pieces(owners, slots)
        labels = jnp.arange(slots, dtype=jnp.int32)

        def more(state):
            index, held = state
            hot = spare & (order == index * SPARE + jnp.arange(SPARE, dtype=jnp.int32)[:, None])
            which = jnp.argmax(hot, axis=1)
            per_matrix = width // piece
            matrix, row = (which // per_matrix, which % per_matrix * piece)
            zero = jnp.int32(0)
            terms = []
            for i in range(SPARE):
                kind = matrix[i] % 3
                one = lax.dynamic_slice(early, (row[i], kind * narrow), (piece, narrow))
                two = lax.dynamic_slice(late, (kind, row[i], zero), (1, piece, narrow))[0]
                terms.append(jnp.where(matrix[i] < 3, one, two))
            terms = jnp.stack(terms)
            terms = jnp.where(jnp.any(hot, axis=1)[:, None, None], terms.astype(jnp.float32), 0.0)
            sums = lax.psum(terms, ("chip", "seq"))
            both = lax.all_gather(sums, "core", axis=2, tiled=True)
            mine = hot & (piece_owner == dp_pos)
            rank_of = jnp.sum(jnp.where(mine, rank, 0), axis=1, dtype=jnp.int32)
            take = jnp.any(mine, axis=1) & (rank_of == labels[:, None])
            new = both[jnp.argmax(take, axis=1)].astype(jnp.bfloat16)
            return (index + 1, jnp.where(jnp.any(take, axis=1)[:, None, None], new, held))

        rounds = more_rounds(order)
        state = lax.while_loop(lambda s: s[0] <= rounds, more, (jnp.int32(1), slot_grad))
        return (state[1], gain_sum)
    chips = lax.axis_size("chip")
    local = jnp.concatenate([jnp.transpose(early.reshape(width, 3, narrow), (1, 0, 2)), late], axis=0)
    share = lax.psum_scatter(
        local.reshape(6 * width, narrow), ("chip", "seq"), scatter_dimension=0, tiled=True
    )
    sums = lax.all_gather(share, ALL, axis=0, tiled=False).reshape(chips, 2, 2, -1, narrow)
    sums = jnp.transpose(sums, (0, 2, 3, 1, 4)).reshape(pieces, piece, width)
    piece_owner, rank = owner_slots(owners, slots)
    labels = jnp.arange(slots, dtype=jnp.int32)
    match = (piece_owner == dp_pos) & (rank == labels[:, None])
    slot_grad = jnp.where(jnp.any(match, axis=1)[:, None, None], sums[jnp.argmax(match, axis=1)], 0)
    return (slot_grad, lax.psum(gains, ALL))


def adam_kernel(rate_ref, master_ref, first_ref, second_ref, grad_ref, *outs):
    count = master_ref.shape[0]
    for i in range(count):
        new, first_new, second_new = adam_update(
            master_ref[i],
            first_ref[i],
            second_ref[i],
            grad_ref[i].astype(jnp.float32),
            rate_ref[pl.program_id(0) * count + i],
            MATRIX_DECAY,
        )
        outs[0][i] = new
        outs[1][i] = first_new
        outs[2][i] = second_new
        outs[3][i] = new.astype(jnp.bfloat16)


def adam_slots(master, first, second, grad, rate):
    slots, piece, width = master.shape
    count = min(slots, 2)
    block = pl.BlockSpec((count, piece, width), lambda i: (i, 0, 0))
    shape = jax.ShapeDtypeStruct(master.shape, jnp.float32)
    return pl.pallas_call(
        adam_kernel,
        grid=(slots // count,),
        in_specs=[pl.BlockSpec(memory_space=pltpu.SMEM)] + [block] * 4,
        out_specs=[block] * 4,
        out_shape=[shape] * 3 + [jax.ShapeDtypeStruct(master.shape, jnp.bfloat16)],
        compiler_params=pltpu.CompilerParams(vmem_limit_bytes=32 << 20),
        cost_estimate=pl.CostEstimate(
            flops=20 * slots * piece * width,
            bytes_accessed=28 * slots * piece * width,
            transcendentals=slots * piece * width,
        ),
    )(rate, master, first, second, grad)


def local(
    tokens,
    cotangent,
    parents,
    owners,
    weight_store,
    gain_store,
    weight_first,
    gain_first,
    weight_second,
    gain_second,
):
    core = lax.axis_index("core")
    dp_pos = lax.axis_index("chip") * 2 + core
    slot_dev, piece, width = weight_store.shape
    pieces = owners.shape[0] - 2
    piece_owner, rank = owner_slots(owners, slot_dev)
    gain_owner = owners[pieces:]
    micro, _, rows, _ = tokens.shape
    half = width // 2
    own_rows = core * rows
    own_columns = core * half

    def mine(value, axis, size, index):
        return lax.dynamic_slice_in_dim(value, index * size, size, axis=axis)

    limit, branch = tail_limits(transposed(parents[:, 0]))
    arrived = moved(tokens[:, 0])
    qkv_weight, out_weight, up_weight, down_weight, gain_low = gather_store(
        weight_store.astype(jnp.bfloat16), gain_store.astype(jnp.bfloat16), owners, True
    )
    gain_low, arrived, cot = lax.optimization_barrier((gain_low, arrived, cotangent[:, 0]))
    own_tokens = settled(tokens[:, 0], arrived)
    own_cot = transposed(cot)
    other_tokens = partner(own_tokens)

    def by_core(own, other, axis):
        return jnp.where(
            core == 0,
            jnp.concatenate([own, other], axis=axis),
            jnp.concatenate([other, own], axis=axis),
        )

    all_tokens = by_core(own_tokens, other_tokens, 1)
    gain_one = gain_low[0].astype(jnp.float32)
    gain_two = gain_low[1].astype(jnp.float32)

    def unit(values):
        scale = lax.rsqrt(jnp.mean(values * values, axis=-1, keepdims=True) + NORM_EPS)
        return (values * scale, scale)

    normed_one = (unit(all_tokens.astype(jnp.float32))[0] * gain_one).astype(jnp.bfloat16)
    qkv = product(normed_one, qkv_weight, "mtd,de->mte").astype(jnp.bfloat16)
    attended_half, lse = attend(qkv, limit, branch)
    lse_rows = jnp.transpose(lse[:, :, : half // HEAD], (0, 2, 1))
    attended = by_core(
        mine(attended_half, 1, rows, core), partner(mine(attended_half, 1, rows, 1 - core)), 2
    )
    residual = own_tokens.astype(jnp.float32)
    hidden_one = residual + product(attended, out_weight, "mti,io->mto")
    unit_two, scale_two = unit(hidden_one)
    normed_two = (unit_two * gain_two).astype(jnp.bfloat16)
    up_rows = product(normed_two, up_weight, "mti,io->mto")
    sigmoid_up = jax.nn.sigmoid(up_rows)
    activated = (up_rows * sigmoid_up).astype(jnp.bfloat16)
    mixed_rows = (hidden_one + product(activated, down_weight, "mti,io->mto")).astype(jnp.bfloat16)
    mixed = transposed(mixed_rows)

    grad_down = product(activated, own_cot, "mti,mto->io")
    grad_hidden = product(own_cot, down_weight, "mto,io->mti")
    grad_up_rows = (grad_hidden * (sigmoid_up * (1.0 + up_rows * (1.0 - sigmoid_up)))).astype(
        jnp.bfloat16
    )
    grad_up = product(normed_two, grad_up_rows, "mti,mto->io")
    grad_normed_two = product(grad_up_rows, up_weight, "mto,io->mti")
    gain_two_grad = jnp.sum(grad_normed_two * unit_two, axis=(0, 1))
    grad_hidden_one = own_cot.astype(jnp.float32) + norm_back(
        grad_normed_two, unit_two, scale_two, gain_two
    )
    branch_grad = grad_hidden_one.astype(jnp.bfloat16)
    grad_out = product(attended, branch_grad, "mti,mto->io")
    late = jnp.stack([grad_out, grad_up, grad_down]).astype(jnp.bfloat16)
    late_back = partner(mine(late, 2, half, 1 - core))

    branch_grad, late = lax.optimization_barrier((branch_grad, late))
    grad_attended = product(branch_grad, out_weight, "mto,io->mti").astype(jnp.bfloat16)
    grad_half = by_core(
        mine(grad_attended, 2, half, core), partner(mine(grad_attended, 2, half, 1 - core)), 1
    )
    grad_query, grad_key, grad_value = attend_back(qkv, grad_half, lse_rows, limit, branch)
    grad_qkv_rows = jnp.concatenate([grad_query, grad_key, grad_value], axis=2)
    grad_qkv = product(normed_one, grad_qkv_rows, "mti,mto->io")
    early = grad_qkv.astype(jnp.bfloat16)

    grad_normed_part = product(grad_qkv_rows, qkv_weight, "mte,de->mtd")
    grad_normed_one = mine(grad_normed_part, 1, rows, core) + partner(
        mine(grad_normed_part, 1, rows, 1 - core).astype(jnp.bfloat16)
    ).astype(jnp.float32)
    unit_one, scale_one = unit(residual)
    gain_one_grad = jnp.sum(grad_normed_one * unit_one, axis=(0, 1))
    token_rows = (
        grad_hidden_one + norm_back(grad_normed_one, unit_one, scale_one, gain_one)
    ).astype(jnp.bfloat16)
    token_grad = transposed(token_rows)
    gain_grads = jnp.stack([gain_one_grad, gain_two_grad])
    late = (mine(late, 2, half, core).astype(jnp.float32) + late_back.astype(jnp.float32)).astype(
        jnp.bfloat16
    )

    labels = jnp.arange(slot_dev, dtype=jnp.int32)
    match = (piece_owner[None, :] == dp_pos) & (rank[None, :] == labels[:, None])
    held = jnp.any(match, axis=1)
    piece_of = jnp.sum(jnp.where(match, jnp.arange(pieces, dtype=jnp.int32)[None, :], 0), axis=1)
    slot_grad, gain_sum = reduce_all(early, late, gain_grads, owners, slot_dev, piece)
    is_out = held & (piece_of // (width // piece) == 3)
    slot_rate = jnp.where(is_out, RATE_OUT, RATE_QKV).astype(jnp.float32)
    weight_new, weight_first_new, weight_second_new, weight_low = adam_slots(
        weight_store, weight_first, weight_second, slot_grad, slot_rate
    )
    gain_slot_grad = jnp.where((gain_owner == dp_pos)[:, None], gain_sum, 0.0)
    gain_new, gain_first_new, gain_second_new = adam_update(
        gain_store, gain_first, gain_second, gain_slot_grad, RATE_GAIN, 0.0
    )
    weight_copies, gain_copies = gather_store(
        weight_low, gain_new.astype(jnp.bfloat16), owners, False
    )
    return (
        mixed[:, None],
        token_grad[:, None],
        weight_new,
        gain_new,
        weight_first_new,
        gain_first_new,
        weight_second_new,
        gain_second_new,
        weight_copies,
        gain_copies,
    )


def solution(mesh):
    dp_count, seq_count = mesh.devices.shape
    fine = Mesh(mesh.devices.reshape(dp_count // 2, 2, seq_count), ALL)
    dp = ("chip", "core")
    rows = P(None, dp, "seq", None)
    store = P(dp, None, None)
    gains = P(dp, None)
    in_specs = (rows, rows, P(None, dp, None), P(), store, gains, store, gains, store, gains)
    out_specs = (rows, rows, store, gains, store, gains, store, gains, P(), P())
    return jax.shard_map(local, mesh=fine, in_specs=in_specs, out_specs=out_specs, check_vma=False)
```

```python
import functools

import jax
import jax.numpy as jnp
from jax import lax
from jax.experimental import pallas as pl
from jax.experimental.pallas import tpu as pltpu
from jax.sharding import Mesh
from jax.sharding import PartitionSpec as P

HEAD = 80
SEG = 32
TRUNK_SEGS = 32
ALWAYS_SEGS = TRUNK_SEGS // 2
STEP = 7
LANES = 128
WINDOW = 256
QUERY_BLOCK = 256

NORM_EPS = 1e-06
BETA_ONE = 0.5
BETA_TWO = 0.5
ADAM_EPS = 1e-08
MATRIX_DECAY = 0.1
RATE_QKV = 0.03
RATE_OUT = 0.4
RATE_GAIN = 0.4
MASKED = -1e30
SCALE = HEAD**-0.5
LOG2E = 1.4426950408889634
ALL = ("chip", "core", "seq")
NT = (((1,), (1,)), ((), ()))
TN = (((0,), (0,)), ((), ()))


def moved(value):
    chips = lax.axis_size("chip")
    pairs = [(k * 4 + c * 2 + 1 - c, k * 4 + 2 - 2 * c + c) for k in range(chips) for c in range(2)]
    return lax.ppermute(value, ALL, pairs)


def settled(value, arrived):
    return jnp.where(lax.axis_index("core") == lax.axis_index("seq"), value, arrived)


def transposed(value):
    return settled(value, moved(value))


def partner(value):
    return lax.ppermute(value, "core", [(0, 1), (1, 0)])


def owner_slots(owners, slot_dev):
    count = owners.shape[0] - 2
    piece_owner = owners[:count]
    labels = jnp.arange(count, dtype=jnp.int32)
    same = (piece_owner[:, None] == piece_owner[None, :]) & (labels[None, :] < labels[:, None])
    rank = jnp.sum(same.astype(jnp.int32), axis=1)
    return (piece_owner, rank)


def tail_limits(parents):
    up = parents[:, TRUNK_SEGS:]
    leaf = up >= TRUNK_SEGS
    above = jnp.where(leaf, up - TRUNK_SEGS, 0)
    labels = jnp.arange(up.shape[1], dtype=jnp.int32)
    hot = above[:, :, None] == labels[None, None, :]
    upper = jnp.sum(jnp.where(hot, up[:, None, :], 0), axis=2)
    attach = jnp.where(leaf, upper, up)
    limit = (attach + 1) * SEG
    branch = jnp.where(leaf, above, -1)
    return (jnp.repeat(limit, SEG, axis=1), jnp.repeat(branch, SEG, axis=1))


def query_blocks(length):
    trunk = TRUNK_SEGS * SEG
    blocks = []
    for first in range(0, trunk, QUERY_BLOCK):
        parts = [(0, first, "all")] if first else []
        blocks.append((first, QUERY_BLOCK, parts + [(first, QUERY_BLOCK, "causal")]))
    always = ALWAYS_SEGS * SEG
    tail = length - trunk
    blocks.append(
        (trunk, tail, [(0, always, "all"), (always, trunk - always, "trunk"), (trunk, tail, "tail")])
    )
    return blocks


def allowed_pairs(kind, key_first, key, query, limit, branch):
    if kind == "causal":
        return key <= query
    if kind == "trunk":
        return key + key_first < limit
    key_seg = key // SEG
    return ((key_seg == query // SEG) & (key <= query)) | (key_seg == branch)


def head_window(head, width):
    start = pl.multiple_of(
        jnp.minimum((head * HEAD) // LANES, width // LANES - WINDOW // LANES) * LANES, LANES
    )
    lane = lax.broadcasted_iota(jnp.int32, (1, WINDOW), 1) + start
    mine = (lane >= head * HEAD) & (lane < (head + 1) * HEAD)
    return (pl.ds(start, WINDOW), mine)


def attend_kernel(limit_ref, branch_ref, q_ref, k_ref, v_ref, out_ref, lse_ref):
    head = pl.program_id(1)
    window, mine = head_window(head, q_ref.shape[2])
    stat_lane = lax.broadcasted_iota(jnp.int32, (1, LANES), 1)
    for first, count, parts in query_blocks(q_ref.shape[1]):
        rows = pl.ds(first, count)
        query = jnp.where(mine, q_ref[0, rows, window], 0)
        scores = []
        for key_first, keys, kind in parts:
            raw = lax.dot_general(
                query, k_ref[0, pl.ds(key_first, keys), window], NT, preferred_element_type=jnp.float32
            ) * (SCALE * LOG2E)
            if kind != "all":
                ok = allowed_pairs(
                    kind,
                    key_first,
                    lax.broadcasted_iota(jnp.int32, (count, keys), 1),
                    lax.broadcasted_iota(jnp.int32, (count, keys), 0),
                    limit_ref[0],
                    branch_ref[0],
                )
                raw = jnp.where(ok, raw, MASKED)
            scores.append(raw)
        top = functools.reduce(jnp.maximum, [jnp.max(s, axis=1, keepdims=True) for s in scores])
        total = 0.0
        gained = 0.0
        for raw, (key_first, keys, kind) in zip(scores, parts):
            weight = jnp.exp2(raw - top)
            total = total + jnp.sum(weight, axis=1, keepdims=True)
            gained = gained + jnp.dot(
                weight.astype(jnp.bfloat16),
                v_ref[0, pl.ds(key_first, keys), window],
                preferred_element_type=jnp.float32,
            )
        gained = (gained / total).astype(jnp.bfloat16)
        out_ref[0, rows, window] = jnp.where(mine, gained, out_ref[0, rows, window])
        lse_ref[0, rows, :] = jnp.where(
            stat_lane == head, top + jnp.log2(total), lse_ref[0, rows, :]
        )


def attend(qkv, limit, branch):
    micro, length, columns = qkv.shape
    width = columns // 3
    heads = width // HEAD
    tail = length - TRUNK_SEGS * SEG

    def part(index):
        return pl.BlockSpec((1, length, width), lambda m, h, index=index: (m, 0, index))

    column = pl.BlockSpec((1, tail, 1), lambda m, h: (m, 0, 0))
    return pl.pallas_call(
        attend_kernel,
        grid=(micro, heads),
        in_specs=[column, column, part(0), part(1), part(2)],
        out_specs=[
            pl.BlockSpec((1, length, width), lambda m, h: (m, 0, 0)),
            pl.BlockSpec((1, length, LANES), lambda m, h: (m, 0, 0)),
        ],
        out_shape=[
            jax.ShapeDtypeStruct((micro, length, width), jnp.bfloat16),
            jax.ShapeDtypeStruct((micro, length, LANES), jnp.float32),
        ],
        compiler_params=pltpu.CompilerParams(vmem_limit_bytes=48 << 20),
        cost_estimate=pl.CostEstimate(
            flops=micro * heads * length * length * WINDOW * 3,
            bytes_accessed=micro * length * width * 8,
            transcendentals=micro * heads * length * length // 2,
        ),
    )(limit[:, :, None], branch[:, :, None], qkv, qkv, qkv)


def attend_back_kernel(
    limit_ref, branch_ref, lse_ref, q_ref, k_ref, v_ref, g_ref, out_ref, dk_sum, dv_sum
):
    head = pl.program_id(1)
    width = q_ref.shape[2]
    window, mine = head_window(head, width)

    @pl.when(head == 0)
    def clear():
        dk_sum[...] = jnp.zeros_like(dk_sum)
        dv_sum[...] = jnp.zeros_like(dv_sum)

    for first, count, parts in query_blocks(q_ref.shape[1]):
        rows = pl.ds(first, count)
        query = jnp.where(mine, q_ref[0, rows, window], 0)
        grad = jnp.where(mine, g_ref[0, rows, window], 0)
        lse = lse_ref[0, pl.ds(head, 1), rows]
        held = []
        row_total = 0.0
        for key_first, keys, kind in parts:
            where = pl.ds(key_first, keys)
            raw = lax.dot_general(
                k_ref[0, where, window], query, NT, preferred_element_type=jnp.float32
            )
            prob = jnp.exp2(raw * (SCALE * LOG2E) - lse)
            if kind != "all":
                ok = allowed_pairs(
                    kind,
                    key_first,
                    lax.broadcasted_iota(jnp.int32, (keys, count), 0),
                    lax.broadcasted_iota(jnp.int32, (keys, count), 1),
                    limit_ref[0],
                    branch_ref[0],
                )
                prob = jnp.where(ok, prob, 0.0)
            grad_prob = lax.dot_general(
                v_ref[0, where, window], grad, NT, preferred_element_type=jnp.float32
            )
            row_total = row_total + jnp.sum(prob * grad_prob, axis=0, keepdims=True)
            held.append((where, prob, grad_prob))
        grad_query = 0.0
        for where, prob, grad_prob in held:
            grad_raw = (prob * (grad_prob - row_total)).astype(jnp.bfloat16)
            dv_sum[where, window] += jnp.dot(
                prob.astype(jnp.bfloat16), grad, preferred_element_type=jnp.float32
            )
            dk_sum[where, window] += jnp.dot(grad_raw, query, preferred_element_type=jnp.float32)
            grad_query = grad_query + lax.dot_general(
                grad_raw, k_ref[0, where, window], TN, preferred_element_type=jnp.float32
            )
        out_ref[0, rows, window] = jnp.where(
            mine, (grad_query * SCALE).astype(jnp.bfloat16), out_ref[0, rows, window]
        )

    @pl.when(head == pl.num_programs(1) - 1)
    def write():
        out_ref[0, :, pl.ds(width, width)] = (dk_sum[...] * SCALE).astype(jnp.bfloat16)
        out_ref[0, :, pl.ds(2 * width, width)] = dv_sum[...].astype(jnp.bfloat16)


def attend_back(qkv, grad, lse, limit, branch):
    micro, length, columns = qkv.shape
    width = columns // 3
    heads = width // HEAD
    tail = length - TRUNK_SEGS * SEG

    def part(index):
        return pl.BlockSpec((1, length, width), lambda m, h, index=index: (m, 0, index))

    row = pl.BlockSpec((1, 1, tail), lambda m, h: (m, 0, 0))
    return pl.pallas_call(
        attend_back_kernel,
        grid=(micro, heads),
        in_specs=[
            row,
            row,
            pl.BlockSpec((1, heads, length), lambda m, h: (m, 0, 0)),
            part(0),
            part(1),
            part(2),
            part(0),
        ],
        out_specs=pl.BlockSpec((1, length, columns), lambda m, h: (m, 0, 0)),
        out_shape=jax.ShapeDtypeStruct((micro, length, columns), jnp.bfloat16),
        scratch_shapes=[pltpu.VMEM((length, width), jnp.float32)] * 2,
        compiler_params=pltpu.CompilerParams(vmem_limit_bytes=56 << 20),
        cost_estimate=pl.CostEstimate(
            flops=micro * heads * length * length * WINDOW * 7,
            bytes_accessed=micro * length * width * 14,
            transcendentals=micro * heads * length * length // 2,
        ),
    )(limit[:, None, :], branch[:, None, :], lse, qkv, qkv, qkv, grad)


def norm_back(grad_normed, normed_unit, scale_rows, gain_row):
    scaled_grad = grad_normed * gain_row
    return scale_rows * (
        scaled_grad - normed_unit * jnp.mean(scaled_grad * normed_unit, axis=-1, keepdims=True)
    )


def adam_update(master, first, second, grad, rate, decay):
    first_new = BETA_ONE * first + (1.0 - BETA_ONE) * grad
    second_new = BETA_TWO * second + (1.0 - BETA_TWO) * grad * grad
    fix_one = 1.0 - BETA_ONE**STEP
    fix_two = 1.0 - BETA_TWO**STEP
    step_size = first_new / fix_one / (jnp.sqrt(second_new / fix_two) + ADAM_EPS)
    return (master - rate * (step_size + decay * master), first_new, second_new)


def product(left, right, spec):
    return jnp.einsum(spec, left, right, preferred_element_type=jnp.float32)


Y_CHIPS = 2
CAPACITY = 8
SPARE = 8
GROUP = 16
CHUNK = 256
MESH_IDS = pl.DeviceIdType.MESH


def place():
    chip = lax.axis_index("chip")
    return (
        chip // Y_CHIPS,
        lax.rem(chip, Y_CHIPS),
        lax.axis_index("core"),
        lax.axis_index("seq"),
        lax.axis_size("chip") // Y_CHIPS,
    )


def at_z(z, y):
    return {"chip": z * Y_CHIPS + y}


def ahead(d):
    z, y, core, x, depth = place()
    return at_z(lax.rem(z + d, depth), y)


def across(axis):
    z, y, core, x, _ = place()
    return {"y": at_z(z, 1 - y), "x": {"seq": 1 - x}, "core": {"core": 1 - core}}[axis]


def greet():
    depth = place()[4]
    barrier = pltpu.get_barrier_semaphore()
    peers = [ahead(d) for d in range(1, depth)] + [across("y"), across("x"), across("core")]
    for peer in peers:
        pl.semaphore_signal(barrier, inc=1, device_id=peer, device_id_type=MESH_IDS)
    pl.semaphore_wait(barrier, len(peers))


def sem_pair(*shape):
    return [pltpu.SemaphoreType.DMA(shape), pltpu.SemaphoreType.DMA(shape)]


def remote(source, target, sems, index, device):
    return pltpu.make_async_remote_copy(
        src_ref=source,
        dst_ref=target,
        send_sem=sems[0].at[index],
        recv_sem=sems[1].at[index],
        device_id=device,
        device_id_type=MESH_IDS,
    )


def total(*parts):
    return functools.reduce(jnp.add, [p.astype(jnp.float32) for p in parts]).astype(jnp.bfloat16)


class Flow:
    def __init__(self):
        self.sent = []

    def push(self, source, target, sems, index, device):
        copy = remote(source, target, sems, index, device)
        copy.start()
        self.sent.append(copy)

    def arrive(self, here, sems, index):
        remote(here, here, sems, index, across("core")).wait_recv()

    def drain(self):
        for copy in self.sent:
            copy.wait_send()


class Total(Flow):
    def __init__(self, axes, sums, inbox, sems):
        super().__init__()
        self.axes, self.sums, self.inbox, self.sems = (axes, sums, inbox, sems)
        self.done = 0

    def begin(self, value):
        self.sums[0] = value
        self.push(self.sums.at[0], self.inbox.at[0], self.sems, (0,), across(self.axes[0]))

    def step(self):
        i = self.done
        self.done += 1
        self.arrive(self.inbox.at[i], self.sems, (i,))
        self.sums[i + 1] = self.sums[i] + self.inbox[i]
        here = self.sums.at[i + 1]
        if i + 1 < len(self.axes):
            self.push(here, self.inbox.at[i + 1], self.sems, (i + 1,), across(self.axes[i + 1]))
            return
        for d in range(1, place()[4]):
            self.push(here, self.inbox.at[i + d], self.sems, (i + d,), ahead(d))

    def result(self):
        last = len(self.axes)
        value = self.sums[last]
        for d in range(1, place()[4]):
            self.arrive(self.inbox.at[last - 1 + d], self.sems, (last - 1 + d,))
            value = value + self.inbox[last - 1 + d]
        self.drain()
        return value


def distances(depth):
    return sorted(range(1, depth), key=lambda d: min(d, depth - d))


def total_scratch(axes, depth, width):
    return [
        pltpu.VMEM((axes + 1, 8, width), jnp.float32),
        pltpu.VMEM((axes + depth - 1, 8, width), jnp.float32),
    ] + sem_pair(axes + depth - 1)


def spread_sems(depth):
    return sem_pair(depth) + sem_pair(depth) + sem_pair(depth, 2) + sem_pair(depth, 4)


class Spread(Flow):
    def __init__(self, window, second, sems):
        super().__init__()
        self.window = window
        self.second = second
        self.third = "x" if second == "y" else "y"
        self.sems = [(sems[2 * i], sems[2 * i + 1]) for i in range(4)]

    def where(self, d, second=False, third=False, other_core=False):
        z, y, core, x, depth = place()
        if second if self.second == "y" else third:
            y = 1 - y
        if third if self.second == "y" else second:
            x = 1 - x
        return self.window(lax.rem(z - d + depth, depth), y, 1 - core if other_core else core, x)

    def forward(self, stage, index, block, device):
        self.push(block, block, self.sems[stage], index, device)

    def begin(self):
        self.waiting = distances(place()[4])
        self.along_z()
        self.onward(0)

    def along_z(self):
        if self.waiting:
            d = self.waiting.pop(0)
            self.forward(0, (d,), self.where(0), ahead(d))

    def onward(self, d):
        block = self.where(d)
        self.forward(1, (d,), block, across(self.second))
        self.forward(2, (d, 0), block, across(self.third))
        self.forward(3, (d, 0), block, across("core"))

    def from_z(self, d):
        self.arrive(self.where(d), self.sems[0], (d,))
        self.along_z()
        self.onward(d)

    def from_second(self, d):
        block = self.where(d, True)
        self.arrive(block, self.sems[1], (d,))
        self.forward(2, (d, 1), block, across(self.third))
        self.forward(3, (d, 2), block, across("core"))

    def from_third(self, d):
        for second in range(2):
            block = self.where(d, bool(second), True)
            self.arrive(block, self.sems[2], (d, second))
            self.forward(3, (d, 2 * second + 1), block, across("core"))

    def finish(self):
        for d in range(place()[4]):
            for second in range(2):
                for third in range(2):
                    block = self.where(d, bool(second), bool(third), True)
                    self.arrive(block, self.sems[3], (d, 2 * second + third))
        self.drain()


def device_block(z, y, core, x):
    return ((z * Y_CHIPS + y) * 2 + core) * 2 + x


def chip_block(z, y, x):
    return (z * Y_CHIPS + y) * 2 + x


def gather_kernel(
    split,
    cut,
    block_ref,
    row_ref,
    spare_rank_ref,
    spare_mine_ref,
    low_ref,
    gain_ref,
    *refs,
):
    outs = refs[: 4 if split else 1]
    gain_out, whole, stage, stage_sem, spare, core_in, y_in, z_in, held = refs[len(outs) : len(outs) + 9]
    gain_sum, gain_in = refs[len(outs) + 9 : len(outs) + 11]
    sems = refs[len(outs) + 11 :]
    z, y, core, x, depth = place()
    piece, width = low_ref.shape[1:]
    half = CAPACITY // 2
    base = half * piece // GROUP
    me = device_block(z, y, core, x)
    per_piece = piece // GROUP
    for i in range(base):
        source = pl.ds(i % per_piece * GROUP, GROUP)
        whole[me, i] = low_ref[x * half + i // per_piece, source]
    greet()

    def window(first, count):
        return lambda *who: whole.at[device_block(*who), pl.ds(first, count)]

    flow_sems = 8
    early = Spread(window(0, cut), "y", sems[2 : 2 + flow_sems])
    late = Spread(window(cut, base - cut), "x", sems[10 : 10 + flow_sems])
    loose = Spread(window(base, 1), "x", sems[18 : 18 + flow_sems])
    gains = Total(["core", "y"], gain_sum, gain_in, sems[0:2])
    spare_sems = sems[26:32]
    spare_flow = Flow()
    early.begin()
    late.begin()
    gains.begin(gain_ref[...])
    count = SPARE // 2
    for i in range(count):
        found = low_ref[spare_rank_ref[x * count + i]]
        spare[pl.ds(i * piece, piece)] = jnp.where(spare_mine_ref[x * count + i] > 0, found, 0)
    rows = core_in.shape[0]

    def part(index, size):
        return pl.ds(pl.multiple_of(index * size, GROUP), size)

    spare_flow.push(spare.at[part(1 - core, rows)], core_in, spare_sems[0:2], (0,), across("core"))
    flows = [early, late]

    def from_z(d):
        for flow in flows:
            flow.from_z(d)

    def from_second(d):
        for flow in flows:
            flow.from_second(d)

    order = distances(depth)
    from_z(order[0])
    spare_flow.arrive(core_in, spare_sems[0:2], (0,))
    held[...] = total(spare[part(core, rows)], core_in[...])
    spare_flow.push(held.at[part(1 - y, rows // 2)], y_in, spare_sems[2:4], (0,), across("y"))
    gains.step()
    from_second(0)
    for i in range(1, depth - 1):
        from_z(order[i])
        if i == 1:
            spare_flow.arrive(y_in, spare_sems[2:4], (0,))
            y_in[...] = total(held[part(y, rows // 2)], y_in[...])
            for e in range(1, depth):
                to = part(lax.rem(z + e, depth), GROUP)
                spare_flow.push(y_in.at[to], z_in.at[e], spare_sems[4:6], (e,), ahead(e))
            gains.step()
        from_second(order[i - 1])
        for flow in flows:
            flow.from_third(([0] + order)[i - 1])
    for d in range(1, depth):
        spare_flow.arrive(z_in.at[d], spare_sems[4:6], (d,))
    whole[me, base] = total(y_in[part(z, GROUP)], *[z_in[d] for d in range(1, depth)])
    loose.begin()
    from_second(order[-1])
    gain_out[...] = gains.result()
    for d in order:
        loose.from_z(d)
    for flow in flows:
        flow.from_third(order[-2])
    for d in range(depth):
        loose.from_second(d)
    for flow in flows:
        flow.from_third(order[-1])
    for d in range(depth):
        loose.from_third(d)
    for flow in flows + [loose]:
        flow.finish()
    spare_flow.drain()

    buffers = stage.shape[0]
    per_chunk = CHUNK // GROUP
    narrow = width // 2
    copies = []
    for index in range(6 * width // CHUNK):
        matrix, first = divmod(index * CHUNK, width)
        slot = index % buffers
        if index >= buffers:
            copies[index - buffers].wait()
        thin = split and matrix < 3
        columns = pl.ds(pl.multiple_of(core * narrow, LANES), narrow) if thin else slice(None)
        count = narrow if thin else width

        def step(i, carry, index=index, slot=slot, columns=columns, count=count):
            for g in range(per_piece):
                at = index * per_chunk + i * per_piece + g
                target = pl.ds(pl.multiple_of(i * piece + g * GROUP, GROUP), GROUP)
                stage[slot, target, pl.ds(0, count)] = whole[block_ref[at], row_ref[at], :, columns]
            return carry

        lax.fori_loop(0, per_chunk // per_piece, step, 0)
        if thin:
            target = outs[0].at[pl.ds(first, CHUNK), pl.ds(matrix * narrow, narrow)]
        elif split:
            target = outs[matrix - 2].at[pl.ds(first, CHUNK)]
        else:
            target = outs[0].at[matrix, pl.ds(first, CHUNK)]
        copies.append(
            pltpu.make_async_copy(stage.at[slot, :, pl.ds(0, count)], target, stage_sem.at[slot])
        )
        copies[-1].start()
    for copy in copies[-buffers:]:
        copy.wait()


def gather_pieces(low, gains, plan, split):
    slots, piece, width = low.shape
    block, row, spare_rank, spare_mine, gain_mine = plan
    chips = lax.axis_size("chip")
    depth = chips // Y_CHIPS
    base = CAPACITY // 2 * piece // GROUP
    shapes = [(width, 3 * (width // 2))] + [(width, width)] * 3 if split else [(6, width, width)]
    lane = SPARE * piece // 4
    buffers = 4
    picked = jnp.where(gain_mine[:, None], gains[: gain_mine.shape[0]].astype(jnp.float32), 0.0)
    padded = jnp.concatenate([picked, jnp.zeros((6, width), jnp.float32)], axis=0)
    vmem = pl.BlockSpec(memory_space=pltpu.VMEM)
    smem = pl.BlockSpec(memory_space=pltpu.SMEM)
    outs = pl.pallas_call(
        functools.partial(gather_kernel, split, base // 4 if split else base // 2),
        in_specs=[smem] * 3 + [vmem] * 3,
        out_specs=[pl.BlockSpec(memory_space=pl.ANY)] * len(shapes) + [vmem],
        out_shape=[jax.ShapeDtypeStruct(s, jnp.bfloat16) for s in shapes]
        + [jax.ShapeDtypeStruct((8, width), jnp.float32)],
        scratch_shapes=[
            pltpu.VMEM((4 * chips, base + 1, GROUP, width), jnp.bfloat16),
            pltpu.VMEM((buffers, CHUNK, width), jnp.bfloat16),
            pltpu.SemaphoreType.DMA((buffers,)),
            pltpu.VMEM((2 * lane, width), jnp.bfloat16),
            pltpu.VMEM((lane, width), jnp.bfloat16),
            pltpu.VMEM((lane // 2, width), jnp.bfloat16),
            pltpu.VMEM((depth, GROUP, width), jnp.bfloat16),
            pltpu.VMEM((lane, width), jnp.bfloat16),
        ]
        + total_scratch(2, depth, width)
        + spread_sems(depth) * 3
        + sem_pair(1)
        + sem_pair(1)
        + sem_pair(depth),
        compiler_params=pltpu.CompilerParams(
            collective_id=0 if split else 1, has_side_effects=True, vmem_limit_bytes=48 << 20
        ),
        cost_estimate=pl.CostEstimate(
            flops=0, bytes_accessed=6 * width * width * 16, transcendentals=0
        ),
    )(
        block.reshape(-1),
        row.reshape(-1),
        spare_rank,
        jnp.broadcast_to(spare_mine[:, None, None], (SPARE, 1, width)),
        low,
        padded,
    )
    return (*outs[:-1], outs[-1][:2].astype(jnp.bfloat16))


def halves(matrices, split):
    if not split:
        return (matrices,)
    width = matrices.shape[1]
    narrow = width // 2
    thin = lax.dynamic_slice_in_dim(matrices[:3], lax.axis_index("core") * narrow, narrow, axis=2)
    side = jnp.concatenate([thin[0], thin[1], thin[2]], axis=1)
    return (side, matrices[3], matrices[4], matrices[5])


def gather_slots(low, gains, owners, split):
    slots, piece, width = low.shape
    piece_owner, rank = owner_slots(owners, slots)
    rows = slots * piece
    half = -(-(rows // 2 + 1) // GROUP) * GROUP
    filler = jnp.zeros((2 * half - rows - 2, width), jnp.bfloat16)
    packed = jnp.concatenate([low.reshape(rows, width), gains, filler], axis=0)
    share = lax.dynamic_slice_in_dim(packed, lax.axis_index("seq") * half, half, axis=0)
    groups = lax.all_gather(share, ALL, axis=0, tiled=True).reshape(-1, GROUP, width)
    per_owner = 2 * half // GROUP
    base = piece_owner * per_owner + rank * (piece // GROUP)
    index = base[:, None] + jnp.arange(piece // GROUP, dtype=jnp.int32)[None, :]
    matrices = groups[index.reshape(-1)].reshape(6, width, width)
    gain_rows = groups[owners[-2:] * per_owner + rows // GROUP][jnp.arange(2), jnp.arange(2)]
    return (*halves(matrices, split), gain_rows)


def kernels_fit(slots, piece, width):
    chips = lax.axis_size("chip")
    return slots == 2 * CAPACITY and piece == GROUP * (chips // Y_CHIPS) and width % CHUNK == 0


def spare_pieces(owners, slots):
    piece_owner, rank = owner_slots(owners, slots)
    spare = rank >= CAPACITY
    return (piece_owner, rank, spare, jnp.cumsum(spare.astype(jnp.int32)) - 1)


def more_rounds(order):
    return (order[-1] + SPARE) // SPARE - 1


def gather_store(low, gains, owners, split):
    slots, piece, width = low.shape
    if not kernels_fit(slots, piece, width):
        return gather_slots(low, gains, owners, split)
    dp_pos = lax.axis_index("chip") * 2 + lax.axis_index("core")
    piece_owner, rank, spare, order = spare_pieces(owners, slots)
    half = CAPACITY // 2
    groups = piece // GROUP
    group = jnp.arange(groups, dtype=jnp.int32)[None, :]
    block = jnp.where(
        spare[:, None],
        device_block(group, (order % 2)[:, None], ((order // 2) % 2)[:, None], (order // 4 % 2)[:, None]),
        (piece_owner * 2 + rank // half)[:, None],
    )
    row = jnp.where(spare[:, None], half * groups, (rank % half)[:, None] * groups + group)

    def mine(first):
        labels = first + jnp.arange(SPARE, dtype=jnp.int32)
        hot = spare[None, :] & (order[None, :] == labels[:, None])
        own = hot & (piece_owner == dp_pos)[None, :]
        at = jnp.sum(jnp.where(own, rank[None, :], 0), axis=1)
        return (hot, at, jnp.any(own, axis=1))

    _, spare_rank, spare_mine = mine(0)
    plan = (block, row, spare_rank, spare_mine.astype(jnp.int32), owners[-2:] == dp_pos)
    *matrices, gain_rows = gather_pieces(low, gains, plan, split)

    def more(state):
        index, *held = state
        hot, at, own = mine(index * SPARE)
        found = lax.psum(jnp.where(own[:, None, None], low[at], 0), ("chip", "core"))
        which = jnp.argmax(hot, axis=0)
        whole = found[which].reshape(6, width, width)
        taken = jnp.any(hot, axis=0).astype(jnp.bfloat16)
        mask = jnp.broadcast_to(taken[:, None, None], (taken.shape[0], piece, width))
        masks = halves(mask.reshape(6, width, width), split)
        new = [jnp.where(m > 0, n, h) for m, n, h in zip(masks, halves(whole, split), held)]
        return (index + 1, *new)

    rounds = more_rounds(order)
    state = lax.while_loop(lambda s: s[0] <= rounds, more, (jnp.int32(1), *matrices))
    return (*state[1:], gain_rows)


class Reduce(Flow):
    def __init__(self, first, shard, one, two, three, sems):
        super().__init__()
        self.first = first
        self.other = "y" if first == "x" else "x"
        self.shard = shard
        self.one, self.two, self.three = (one, two, three)
        self.sems = [sems[0:2], sems[2:4], sems[4:6]]

    def start(self, d, b):
        self.push(self.shard(d, b, 1), self.one.at[d, b], self.sems[0], (d, b), across(self.first))

    def from_first(self, d, b):
        here = self.one.at[d, b]
        self.arrive(here, self.sems[0], (d, b))
        here[...] = total(here[...], self.shard(d, b, 0)[...])
        if b:
            self.push(here, self.two.at[d], self.sems[1], (d,), across(self.other))

    def from_second(self, d):
        here = self.two.at[d]
        self.arrive(here, self.sems[1], (d,))
        here[...] = total(here[...], self.one[d, 0])
        if d:
            self.push(here, self.three.at[d], self.sems[2], (d,), ahead(d))

    def result(self):
        depth = place()[4]
        for d in range(1, depth):
            self.arrive(self.three.at[d], self.sems[2], (d,))
        value = total(self.two[0], *[self.three[d] for d in range(1, depth)])
        self.drain()
        return value


def reduce_kernel(
    source_ref,
    spare_ref,
    spare_mine_ref,
    early_ref,
    late_ref,
    gain_ref,
    slot_ref,
    gain_out,
    pieces,
    blocks,
    early_one,
    early_two,
    early_three,
    late_one,
    late_two,
    late_three,
    final,
    pair_in,
    full,
    full_in,
    spares,
    gain_sum,
    gain_in,
    load_sem,
    *sems,
):
    z, y, core, x, depth = place()
    narrow = pieces.shape[2]
    groups = late_ref.shape[1]
    per_block = blocks.shape[1]
    cut = per_block // 2
    owned = CAPACITY // 2 * slot_ref.shape[1]
    order = distances(depth)[::-1] + [0]
    loads = []
    for matrix in range(3):
        columns = pl.ds(matrix * narrow, narrow)
        loads.append((early_ref.at[:, :, columns], matrix))
        loads.append((late_ref.at[matrix], matrix + 3))
    loads = [
        pltpu.make_async_copy(source, pieces.at[pl.ds(m * groups, groups)], load_sem.at[m])
        for source, m in loads
    ]
    for load in loads:
        load.start()
    pieces[6 * groups] = jnp.zeros((GROUP, narrow), jnp.bfloat16)
    greet()
    gains = Total(["core", "x", "y"], gain_sum, gain_in, sems[0:2])
    gains.begin(gain_ref[...])
    for load in loads:
        load.wait()

    def block_at(d, swap_y, swap_x):
        return chip_block(
            lax.rem(z + d, depth), 1 - y if swap_y else y, 1 - x if swap_x else x
        )

    early = Reduce(
        "x",
        lambda d, b, a: blocks.at[block_at(d, b, a), pl.ds(0, cut)],
        early_one,
        early_two,
        early_three,
        sems[2:8],
    )
    late = Reduce(
        "y",
        lambda d, b, a: blocks.at[block_at(d, a, b), pl.ds(cut, per_block - cut)],
        late_one,
        late_two,
        late_three,
        sems[8:14],
    )

    def fill(d, swap_y, swap_x):
        block = block_at(d, swap_y, swap_x)

        def step(i, carry):
            for g in range(2):
                blocks[block, 2 * i + g] = pieces[source_ref[block * per_block + 2 * i + g]]
            return carry

        lax.fori_loop(0, per_block // 2, step, 0)

    def start(d, b):
        for flow in (early, late):
            flow.start(d, b)

    fill(order[0], 1, 1)
    start(order[0], 1)
    fill(order[0], 0, 1)
    fill(order[0], 1, 0)
    start(order[0], 0)
    fill(order[0], 0, 0)
    for i, d in enumerate(order):
        later = order[i + 1] if i + 1 < len(order) else None
        if later is not None:
            fill(later, 1, 1)
        for flow in (early, late):
            flow.from_first(d, 1)
        if later is not None:
            start(later, 1)
            fill(later, 0, 1)
            fill(later, 1, 0)
        for flow in (early, late):
            flow.from_first(d, 0)
        if later is not None:
            start(later, 0)
            fill(later, 0, 0)
        if i:
            for flow in (early, late):
                flow.from_second(order[i - 1])
        if i < 3:
            gains.step()
    for flow in (early, late):
        flow.from_second(order[-1])
    final[pl.ds(0, cut)] = early.result()
    final[pl.ds(cut, per_block - cut)] = late.result()

    ends = Flow()
    own_spare = spares.at[z, y, x, core]
    ends.push(final.at[pl.ds((1 - core) * owned, owned)], pair_in, sems[14:16], (0,), across("core"))
    spares[z, y, x, core] = final[pl.ds(2 * owned, 2)]
    for d in range(1, depth):
        ends.push(own_spare, own_spare, sems[16:18], (d,), ahead(d))
    gain_out[...] = gains.result()
    ends.arrive(pair_in, sems[14:16], (0,))
    for g in range(owned):
        mine = final[core * owned + g]
        theirs = pair_in[g]
        first = core == 0
        full[g, :, pl.ds(pl.multiple_of(core * narrow, LANES), narrow)] = mine
        full[g, :, pl.ds(pl.multiple_of((1 - core) * narrow, LANES), narrow)] = theirs
    ends.push(full, full_in, sems[14:16], (1,), across("x"))
    for d in range(1, depth):
        from_z = spares.at[lax.rem(z - d + depth, depth), y, x, core]
        ends.arrive(from_z, sems[16:18], (d,))
    here = spares.at[:, y, x, core]
    ends.push(here, here, sems[14:16], (2,), across("y"))
    ends.arrive(spares.at[:, 1 - y, x, core], sems[14:16], (2,))
    here = spares.at[:, :, x, core]
    ends.push(here, here, sems[14:16], (3,), across("x"))
    ends.arrive(spares.at[:, :, 1 - x, core], sems[14:16], (3,))
    here = spares.at[:, :, :, core]
    ends.push(here, here, sems[14:16], (4,), across("core"))
    ends.arrive(spares.at[:, :, :, 1 - core], sems[14:16], (4,))
    ends.arrive(full_in, sems[14:16], (1,))
    per_piece = slot_ref.shape[1]
    half = CAPACITY // 2
    for i in range(half):
        for g in range(per_piece):
            slot_ref[x * half + i, g] = full[i * per_piece + g]
            slot_ref[(1 - x) * half + i, g] = full_in[i * per_piece + g]

    def pick(slot, carry):
        for g in range(per_piece):
            at = spare_ref[slot] * per_piece + g
            sub = spares.shape[4]
            chip = lax.div(at, 2 * sub)
            where = (lax.div(chip, Y_CHIPS), lax.rem(chip, Y_CHIPS), lax.rem(lax.div(at, sub), 2))
            for side in range(2):
                found = spares[(*where, side, lax.rem(at, sub))]
                slot_ref[CAPACITY + slot, g, :, pl.ds(side * narrow, narrow)] = jnp.where(
                    spare_mine_ref[slot] > 0, found, 0
                )
        return carry

    lax.fori_loop(0, slot_ref.shape[0] - CAPACITY, pick, 0)
    ends.drain()


def reduce_slots(early, late, gains, owners, slots, piece):
    width = late.shape[1]
    narrow = width // 2
    chips = lax.axis_size("chip")
    depth = chips // Y_CHIPS
    groups = width // GROUP
    per_piece = piece // GROUP
    dp_pos = lax.axis_index("chip") * 2 + lax.axis_index("core")
    piece_owner, rank, spare, order = spare_pieces(owners, slots)
    half = CAPACITY // 2
    labels = jnp.arange(piece_owner.shape[0], dtype=jnp.int32)
    empty = 6 * groups

    def groups_of(match):
        first = jnp.sum(jnp.where(match, labels, 0), axis=-1)[..., None] * per_piece
        groups_at = first + jnp.arange(per_piece, dtype=jnp.int32)
        return jnp.where(jnp.any(match, axis=-1)[..., None], groups_at, empty)

    block = jnp.arange(2 * chips, dtype=jnp.int32)[:, None]
    entry = jnp.arange(CAPACITY, dtype=jnp.int32)[None, :]
    owner_at = block // 2 * 2 + entry // half
    rank_at = block % 2 * half + entry % half
    base_groups = groups_of(
        (piece_owner == owner_at[..., None]) & (rank == rank_at[..., None])
    ).reshape(2 * chips, -1)
    spare_hot = spare & (order == jnp.arange(SPARE, dtype=jnp.int32)[:, None])
    spare_groups = groups_of(spare_hot).reshape(2 * chips, -1)
    source = jnp.concatenate([base_groups, spare_groups], axis=1)
    per_block = source.shape[1]
    mine = (piece_owner == dp_pos) & spare & (order < SPARE)
    slot_hot = mine & (rank == CAPACITY + jnp.arange(slots - CAPACITY, dtype=jnp.int32)[:, None])
    spare_at = jnp.sum(jnp.where(slot_hot, order, 0), axis=1)
    subs = SPARE * per_piece // (2 * chips)

    vmem = pl.BlockSpec(memory_space=pltpu.VMEM)
    smem = pl.BlockSpec(memory_space=pltpu.SMEM)
    hbm = pl.BlockSpec(memory_space=pl.ANY)
    cut = per_block // 2
    owned = half * per_piece
    padded = jnp.concatenate([gains, jnp.zeros((8 - gains.shape[0], width), jnp.float32)], axis=0)

    def group_block(*shape):
        return pltpu.VMEM(shape + (GROUP, narrow), jnp.bfloat16)

    def flow_blocks(count):
        return [group_block(depth, 2, count), group_block(depth, count), group_block(depth, count)]

    flow_sems = sem_pair(depth, 2) + sem_pair(depth) + sem_pair(depth)
    slot_grad, gain_sum = pl.pallas_call(
        reduce_kernel,
        in_specs=[smem] * 2 + [vmem, hbm, hbm, vmem],
        out_specs=[vmem, vmem],
        out_shape=[
            jax.ShapeDtypeStruct((slots, per_piece, GROUP, width), jnp.bfloat16),
            jax.ShapeDtypeStruct((8, width), jnp.float32),
        ],
        scratch_shapes=[group_block(6 * groups + 1), group_block(2 * chips, per_block)]
        + flow_blocks(cut)
        + flow_blocks(per_block - cut)
        + [
            group_block(per_block),
            group_block(owned),
            pltpu.VMEM((owned, GROUP, width), jnp.bfloat16),
            pltpu.VMEM((owned, GROUP, width), jnp.bfloat16),
            group_block(depth, Y_CHIPS, 2, 2, subs),
        ]
        + total_scratch(3, depth, width)[:2]
        + [pltpu.SemaphoreType.DMA((6,))]
        + total_scratch(3, depth, width)[2:]
        + flow_sems
        + flow_sems
        + sem_pair(5)
        + sem_pair(depth),
        compiler_params=pltpu.CompilerParams(
            collective_id=2, has_side_effects=True, vmem_limit_bytes=56 << 20
        ),
        cost_estimate=pl.CostEstimate(
            flops=0, bytes_accessed=6 * width * width * 8, transcendentals=0
        ),
    )(
        source.reshape(-1),
        spare_at,
        jnp.broadcast_to(jnp.any(slot_hot, axis=1).astype(jnp.int32)[:, None, None], (slots - CAPACITY, 1, narrow)),
        early.reshape(groups, GROUP, 3 * narrow),
        late.reshape(3, groups, GROUP, narrow),
        padded,
    )
    return (slot_grad.reshape(slots, piece, width), gain_sum[:2])


def reduce_all(early, late, gains, owners, slots, piece):
    width = late.shape[1]
    narrow = width // 2
    core = lax.axis_index("core")
    dp_pos = lax.axis_index("chip") * 2 + core
    pieces = owners.shape[0] - 2
    if kernels_fit(slots, piece, width):
        slot_grad, gain_sum = reduce_slots(early, late, gains, owners, slots, piece)
        piece_owner, rank, spare, order = spare_pieces(owners, slots)
        labels = jnp.arange(slots, dtype=jnp.int32)

        def more(state):
            index, held = state
            hot = spare & (order == index * SPARE + jnp.arange(SPARE, dtype=jnp.int32)[:, None])
            which = jnp.argmax(hot, axis=1)
            per_matrix = width // piece
            matrix, row = (which // per_matrix, which % per_matrix * piece)
            zero = jnp.int32(0)
            terms = []
            for i in range(SPARE):
                kind = matrix[i] % 3
                one = lax.dynamic_slice(early, (row[i], kind * narrow), (piece, narrow))
                two = lax.dynamic_slice(late, (kind, row[i], zero), (1, piece, narrow))[0]
                terms.append(jnp.where(matrix[i] < 3, one, two))
            terms = jnp.stack(terms)
            terms = jnp.where(jnp.any(hot, axis=1)[:, None, None], terms.astype(jnp.float32), 0.0)
            sums = lax.psum(terms, ("chip", "seq"))
            both = lax.all_gather(sums, "core", axis=2, tiled=True)
            mine = hot & (piece_owner == dp_pos)
            rank_of = jnp.sum(jnp.where(mine, rank, 0), axis=1, dtype=jnp.int32)
            take = jnp.any(mine, axis=1) & (rank_of == labels[:, None])
            new = both[jnp.argmax(take, axis=1)].astype(jnp.bfloat16)
            return (index + 1, jnp.where(jnp.any(take, axis=1)[:, None, None], new, held))

        rounds = more_rounds(order)
        state = lax.while_loop(lambda s: s[0] <= rounds, more, (jnp.int32(1), slot_grad))
        return (state[1], gain_sum)
    chips = lax.axis_size("chip")
    local = jnp.concatenate([jnp.transpose(early.reshape(width, 3, narrow), (1, 0, 2)), late], axis=0)
    share = lax.psum_scatter(
        local.reshape(6 * width, narrow), ("chip", "seq"), scatter_dimension=0, tiled=True
    )
    sums = lax.all_gather(share, ALL, axis=0, tiled=False).reshape(chips, 2, 2, -1, narrow)
    sums = jnp.transpose(sums, (0, 2, 3, 1, 4)).reshape(pieces, piece, width)
    piece_owner, rank = owner_slots(owners, slots)
    labels = jnp.arange(slots, dtype=jnp.int32)
    match = (piece_owner == dp_pos) & (rank == labels[:, None])
    slot_grad = jnp.where(jnp.any(match, axis=1)[:, None, None], sums[jnp.argmax(match, axis=1)], 0)
    return (slot_grad, lax.psum(gains, ALL))


def adam_kernel(rate_ref, master_ref, first_ref, second_ref, grad_ref, *outs):
    count = master_ref.shape[0]
    for i in range(count):
        new, first_new, second_new = adam_update(
            master_ref[i],
            first_ref[i],
            second_ref[i],
            grad_ref[i].astype(jnp.float32),
            rate_ref[pl.program_id(0) * count + i],
            MATRIX_DECAY,
        )
        outs[0][i] = new
        outs[1][i] = first_new
        outs[2][i] = second_new
        outs[3][i] = new.astype(jnp.bfloat16)


def adam_slots(master, first, second, grad, rate):
    slots, piece, width = master.shape
    count = min(slots, 2)
    block = pl.BlockSpec((count, piece, width), lambda i: (i, 0, 0))
    shape = jax.ShapeDtypeStruct(master.shape, jnp.float32)
    return pl.pallas_call(
        adam_kernel,
        grid=(slots // count,),
        in_specs=[pl.BlockSpec(memory_space=pltpu.SMEM)] + [block] * 4,
        out_specs=[block] * 4,
        out_shape=[shape] * 3 + [jax.ShapeDtypeStruct(master.shape, jnp.bfloat16)],
        compiler_params=pltpu.CompilerParams(vmem_limit_bytes=32 << 20),
        cost_estimate=pl.CostEstimate(
            flops=20 * slots * piece * width,
            bytes_accessed=28 * slots * piece * width,
            transcendentals=slots * piece * width,
        ),
    )(rate, master, first, second, grad)


def local(
    tokens,
    cotangent,
    parents,
    owners,
    weight_store,
    gain_store,
    weight_first,
    gain_first,
    weight_second,
    gain_second,
):
    core = lax.axis_index("core")
    dp_pos = lax.axis_index("chip") * 2 + core
    slot_dev, piece, width = weight_store.shape
    pieces = owners.shape[0] - 2
    piece_owner, rank = owner_slots(owners, slot_dev)
    gain_owner = owners[pieces:]
    micro, _, rows, _ = tokens.shape
    half = width // 2
    own_rows = core * rows
    own_columns = core * half

    def mine(value, axis, size, index):
        return lax.dynamic_slice_in_dim(value, index * size, size, axis=axis)

    limit, branch = tail_limits(transposed(parents[:, 0]))
    arrived = moved(tokens[:, 0])
    qkv_weight, out_weight, up_weight, down_weight, gain_low = gather_store(
        weight_store.astype(jnp.bfloat16), gain_store.astype(jnp.bfloat16), owners, True
    )
    gain_low, arrived, cot = lax.optimization_barrier((gain_low, arrived, cotangent[:, 0]))
    own_tokens = settled(tokens[:, 0], arrived)
    own_cot = transposed(cot)
    other_tokens = partner(own_tokens)

    def by_core(own, other, axis):
        return jnp.where(
            core == 0,
            jnp.concatenate([own, other], axis=axis),
            jnp.concatenate([other, own], axis=axis),
        )

    all_tokens = by_core(own_tokens, other_tokens, 1)
    gain_one = gain_low[0].astype(jnp.float32)
    gain_two = gain_low[1].astype(jnp.float32)

    def unit(values):
        scale = lax.rsqrt(jnp.mean(values * values, axis=-1, keepdims=True) + NORM_EPS)
        return (values * scale, scale)

    normed_one = (unit(all_tokens.astype(jnp.float32))[0] * gain_one).astype(jnp.bfloat16)
    qkv = product(normed_one, qkv_weight, "mtd,de->mte").astype(jnp.bfloat16)
    attended_half, lse = attend(qkv, limit, branch)
    lse_rows = jnp.transpose(lse[:, :, : half // HEAD], (0, 2, 1))
    attended = by_core(
        mine(attended_half, 1, rows, core), partner(mine(attended_half, 1, rows, 1 - core)), 2
    )
    residual = own_tokens.astype(jnp.float32)
    hidden_one = residual + product(attended, out_weight, "mti,io->mto")
    unit_two, scale_two = unit(hidden_one)
    normed_two = (unit_two * gain_two).astype(jnp.bfloat16)
    up_rows = product(normed_two, up_weight, "mti,io->mto")
    sigmoid_up = jax.nn.sigmoid(up_rows)
    activated = (up_rows * sigmoid_up).astype(jnp.bfloat16)
    mixed_rows = (hidden_one + product(activated, down_weight, "mti,io->mto")).astype(jnp.bfloat16)
    mixed = transposed(mixed_rows)

    grad_down = product(activated, own_cot, "mti,mto->io")
    grad_hidden = product(own_cot, down_weight, "mto,io->mti")
    grad_up_rows = (grad_hidden * (sigmoid_up * (1.0 + up_rows * (1.0 - sigmoid_up)))).astype(
        jnp.bfloat16
    )
    grad_up = product(normed_two, grad_up_rows, "mti,mto->io")
    grad_normed_two = product(grad_up_rows, up_weight, "mto,io->mti")
    gain_two_grad = jnp.sum(grad_normed_two * unit_two, axis=(0, 1))
    grad_hidden_one = own_cot.astype(jnp.float32) + norm_back(
        grad_normed_two, unit_two, scale_two, gain_two
    )
    branch_grad = grad_hidden_one.astype(jnp.bfloat16)
    grad_out = product(attended, branch_grad, "mti,mto->io")
    late = jnp.stack([grad_out, grad_up, grad_down]).astype(jnp.bfloat16)
    late_back = partner(mine(late, 2, half, 1 - core))

    branch_grad, late = lax.optimization_barrier((branch_grad, late))
    grad_attended = product(branch_grad, out_weight, "mto,io->mti").astype(jnp.bfloat16)
    grad_half = by_core(
        mine(grad_attended, 2, half, core), partner(mine(grad_attended, 2, half, 1 - core)), 1
    )
    grad_qkv_rows = attend_back(qkv, grad_half, lse_rows, limit, branch)
    grad_qkv = product(normed_one, grad_qkv_rows, "mti,mto->io")
    early = grad_qkv.astype(jnp.bfloat16)

    grad_normed_part = product(grad_qkv_rows, qkv_weight, "mte,de->mtd")
    grad_normed_one = mine(grad_normed_part, 1, rows, core) + partner(
        mine(grad_normed_part, 1, rows, 1 - core).astype(jnp.bfloat16)
    ).astype(jnp.float32)
    unit_one, scale_one = unit(residual)
    gain_one_grad = jnp.sum(grad_normed_one * unit_one, axis=(0, 1))
    token_rows = (
        grad_hidden_one + norm_back(grad_normed_one, unit_one, scale_one, gain_one)
    ).astype(jnp.bfloat16)
    token_grad = transposed(token_rows)
    gain_grads = jnp.stack([gain_one_grad, gain_two_grad])
    late = (mine(late, 2, half, core).astype(jnp.float32) + late_back.astype(jnp.float32)).astype(
        jnp.bfloat16
    )

    labels = jnp.arange(slot_dev, dtype=jnp.int32)
    match = (piece_owner[None, :] == dp_pos) & (rank[None, :] == labels[:, None])
    held = jnp.any(match, axis=1)
    piece_of = jnp.sum(jnp.where(match, jnp.arange(pieces, dtype=jnp.int32)[None, :], 0), axis=1)
    slot_grad, gain_sum = reduce_all(early, late, gain_grads, owners, slot_dev, piece)
    is_out = held & (piece_of // (width // piece) == 3)
    slot_rate = jnp.where(is_out, RATE_OUT, RATE_QKV).astype(jnp.float32)
    weight_new, weight_first_new, weight_second_new, weight_low = adam_slots(
        weight_store, weight_first, weight_second, slot_grad, slot_rate
    )
    gain_slot_grad = jnp.where((gain_owner == dp_pos)[:, None], gain_sum, 0.0)
    gain_new, gain_first_new, gain_second_new = adam_update(
        gain_store, gain_first, gain_second, gain_slot_grad, RATE_GAIN, 0.0
    )
    weight_copies, gain_copies = gather_store(
        weight_low, gain_new.astype(jnp.bfloat16), owners, False
    )
    return (
        mixed[:, None],
        token_grad[:, None],
        weight_new,
        gain_new,
        weight_first_new,
        gain_first_new,
        weight_second_new,
        gain_second_new,
        weight_copies,
        gain_copies,
    )


def solution(mesh):
    dp_count, seq_count = mesh.devices.shape
    fine = Mesh(mesh.devices.reshape(dp_count // 2, 2, seq_count), ALL)
    dp = ("chip", "core")
    rows = P(None, dp, "seq", None)
    store = P(dp, None, None)
    gains = P(dp, None)
    in_specs = (rows, rows, P(None, dp, None), P(), store, gains, store, gains, store, gains)
    out_specs = (rows, rows, store, gains, store, gains, store, gains, P(), P())
    return jax.shard_map(local, mesh=fine, in_specs=in_specs, out_specs=out_specs, check_vma=False)
```

```python
import functools

import jax
import jax.numpy as jnp
from jax import lax
from jax.experimental import pallas as pl
from jax.experimental.pallas import tpu as pltpu
from jax.sharding import Mesh
from jax.sharding import PartitionSpec as P

HEAD = 80
SEG = 32
TRUNK_SEGS = 32
ALWAYS_SEGS = TRUNK_SEGS // 2
STEP = 7
LANES = 128
WINDOW = 256
QUERY_BLOCK = 256

NORM_EPS = 1e-06
BETA_ONE = 0.5
BETA_TWO = 0.5
ADAM_EPS = 1e-08
MATRIX_DECAY = 0.1
RATE_QKV = 0.03
RATE_OUT = 0.4
RATE_GAIN = 0.4
MASKED = -1e30
SCALE = HEAD**-0.5
LOG2E = 1.4426950408889634
ALL = ("chip", "core", "seq")
NT = (((1,), (1,)), ((), ()))
TN = (((0,), (0,)), ((), ()))


def moved(value):
    chips = lax.axis_size("chip")
    pairs = [(k * 4 + c * 2 + 1 - c, k * 4 + 2 - 2 * c + c) for k in range(chips) for c in range(2)]
    return lax.ppermute(value, ALL, pairs)


def settled(value, arrived):
    return jnp.where(lax.axis_index("core") == lax.axis_index("seq"), value, arrived)


def transposed(value):
    return settled(value, moved(value))


def partner(value):
    return lax.ppermute(value, "core", [(0, 1), (1, 0)])


def owner_slots(owners, slot_dev):
    count = owners.shape[0] - 2
    piece_owner = owners[:count]
    labels = jnp.arange(count, dtype=jnp.int32)
    same = (piece_owner[:, None] == piece_owner[None, :]) & (labels[None, :] < labels[:, None])
    rank = jnp.sum(same.astype(jnp.int32), axis=1)
    return (piece_owner, rank)


def tail_limits(parents):
    up = parents[:, TRUNK_SEGS:]
    leaf = up >= TRUNK_SEGS
    above = jnp.where(leaf, up - TRUNK_SEGS, 0)
    labels = jnp.arange(up.shape[1], dtype=jnp.int32)
    hot = above[:, :, None] == labels[None, None, :]
    upper = jnp.sum(jnp.where(hot, up[:, None, :], 0), axis=2)
    attach = jnp.where(leaf, upper, up)
    limit = (attach + 1) * SEG
    branch = jnp.where(leaf, above, -1)
    return (jnp.repeat(limit, SEG, axis=1), jnp.repeat(branch, SEG, axis=1))


def query_blocks(length):
    trunk = TRUNK_SEGS * SEG
    blocks = []
    for first in range(0, trunk, QUERY_BLOCK):
        parts = [(0, first, "all")] if first else []
        blocks.append((first, QUERY_BLOCK, parts + [(first, QUERY_BLOCK, "causal")]))
    always = ALWAYS_SEGS * SEG
    tail = length - trunk
    blocks.append(
        (trunk, tail, [(0, always, "all"), (always, trunk - always, "trunk"), (trunk, tail, "tail")])
    )
    return blocks


def allowed_pairs(kind, key_first, key, query, limit, branch):
    if kind == "causal":
        return key <= query
    if kind == "trunk":
        return key + key_first < limit
    key_seg = key // SEG
    return ((key_seg == query // SEG) & (key <= query)) | (key_seg == branch)


def head_window(head, width):
    start = pl.multiple_of(
        jnp.minimum((head * HEAD) // LANES, width // LANES - WINDOW // LANES) * LANES, LANES
    )
    lane = lax.broadcasted_iota(jnp.int32, (1, WINDOW), 1) + start
    mine = (lane >= head * HEAD) & (lane < (head + 1) * HEAD)
    return (pl.ds(start, WINDOW), mine)


def scaled_query(rows, mine):
    return jnp.where(mine, rows.astype(jnp.float32) * (SCALE * LOG2E), 0.0).astype(jnp.bfloat16)


def attend_kernel(limit_ref, branch_ref, q_ref, k_ref, v_ref, out_ref, lse_ref):
    head = pl.program_id(1)
    window, mine = head_window(head, q_ref.shape[2])
    stat_lane = lax.broadcasted_iota(jnp.int32, (1, LANES), 1)
    values = jnp.where(mine, v_ref[0, :, window], 1)
    for first, count, parts in query_blocks(q_ref.shape[1]):
        rows = pl.ds(first, count)
        query = scaled_query(q_ref[0, rows, window], mine)
        scores = []
        for key_first, keys, kind in parts:
            raw = lax.dot_general(
                query, k_ref[0, pl.ds(key_first, keys), window], NT, preferred_element_type=jnp.float32
            )
            if kind != "all":
                ok = allowed_pairs(
                    kind,
                    key_first,
                    lax.broadcasted_iota(jnp.int32, (count, keys), 1),
                    lax.broadcasted_iota(jnp.int32, (count, keys), 0),
                    limit_ref[0],
                    branch_ref[0],
                )
                raw = jnp.where(ok, raw, MASKED)
            scores.append(raw)
        top = functools.reduce(jnp.maximum, [jnp.max(s, axis=1, keepdims=True) for s in scores])
        gained = 0.0
        for raw, (key_first, keys, kind) in zip(scores, parts):
            gained = gained + jnp.dot(
                jnp.exp2(raw - top).astype(jnp.bfloat16),
                values[key_first : key_first + keys],
                preferred_element_type=jnp.float32,
            )
        weight_sum = jnp.max(jnp.where(mine, 0.0, gained), axis=1, keepdims=True)
        gained = (gained * (1.0 / weight_sum)).astype(jnp.bfloat16)
        out_ref[0, rows, window] = jnp.where(mine, gained, out_ref[0, rows, window])
        lse_ref[0, rows, :] = jnp.where(
            stat_lane == head, top + jnp.log2(weight_sum), lse_ref[0, rows, :]
        )


def attend(qkv, limit, branch):
    micro, length, columns = qkv.shape
    width = columns // 3
    heads = width // HEAD
    tail = length - TRUNK_SEGS * SEG

    def part(index):
        return pl.BlockSpec((1, length, width), lambda m, h, index=index: (m, 0, index))

    column = pl.BlockSpec((1, tail, 1), lambda m, h: (m, 0, 0))
    return pl.pallas_call(
        attend_kernel,
        grid=(micro, heads),
        in_specs=[column, column, part(0), part(1), part(2)],
        out_specs=[
            pl.BlockSpec((1, length, width), lambda m, h: (m, 0, 0)),
            pl.BlockSpec((1, length, LANES), lambda m, h: (m, 0, 0)),
        ],
        out_shape=[
            jax.ShapeDtypeStruct((micro, length, width), jnp.bfloat16),
            jax.ShapeDtypeStruct((micro, length, LANES), jnp.float32),
        ],
        compiler_params=pltpu.CompilerParams(vmem_limit_bytes=48 << 20),
        cost_estimate=pl.CostEstimate(
            flops=micro * heads * length * length * WINDOW * 3,
            bytes_accessed=micro * length * width * 8,
            transcendentals=micro * heads * length * length // 2,
        ),
    )(limit[:, :, None], branch[:, :, None], qkv, qkv, qkv)


def attend_back_kernel(
    limit_ref, branch_ref, lse_ref, q_ref, k_ref, v_ref, g_ref, a_ref, out_ref, dk_sum, dv_sum
):
    head = pl.program_id(1)
    width = q_ref.shape[2]
    window, mine = head_window(head, width)

    @pl.when(head == 0)
    def clear():
        dk_sum[...] = jnp.zeros_like(dk_sum)
        dv_sum[...] = jnp.zeros_like(dv_sum)

    ones = jnp.ones((8, WINDOW), jnp.float32)
    for first, count, parts in query_blocks(q_ref.shape[1]):
        rows = pl.ds(first, count)
        query = jnp.where(mine, q_ref[0, rows, window], 0)
        scaled = scaled_query(q_ref[0, rows, window], mine)
        grad = jnp.where(mine, g_ref[0, rows, window], 0)
        lse = lse_ref[0, pl.ds(head, 1), rows]
        gains = grad.astype(jnp.float32) * a_ref[0, rows, window].astype(jnp.float32)
        row_total = lax.dot_general(
            ones, gains, NT, precision=lax.Precision.HIGHEST, preferred_element_type=jnp.float32
        )[0:1]
        grad_query = 0.0
        for key_first, keys, kind in parts:
            where = pl.ds(key_first, keys)
            raw = lax.dot_general(
                k_ref[0, where, window], scaled, NT, preferred_element_type=jnp.float32
            )
            prob = jnp.exp2(raw - lse)
            if kind != "all":
                ok = allowed_pairs(
                    kind,
                    key_first,
                    lax.broadcasted_iota(jnp.int32, (keys, count), 0),
                    lax.broadcasted_iota(jnp.int32, (keys, count), 1),
                    limit_ref[0],
                    branch_ref[0],
                )
                prob = jnp.where(ok, prob, 0.0)
            grad_prob = lax.dot_general(
                v_ref[0, where, window], grad, NT, preferred_element_type=jnp.float32
            )
            grad_raw = (prob * (grad_prob - row_total)).astype(jnp.bfloat16)
            dv_sum[where, window] += jnp.dot(
                prob.astype(jnp.bfloat16), grad, preferred_element_type=jnp.float32
            )
            dk_sum[where, window] += jnp.dot(grad_raw, query, preferred_element_type=jnp.float32)
            grad_query = grad_query + lax.dot_general(
                grad_raw, k_ref[0, where, window], TN, preferred_element_type=jnp.float32
            )
        out_ref[0, rows, window] = jnp.where(
            mine, (grad_query * SCALE).astype(jnp.bfloat16), out_ref[0, rows, window]
        )

    @pl.when(head == pl.num_programs(1) - 1)
    def write():
        out_ref[0, :, pl.ds(width, width)] = (dk_sum[...] * SCALE).astype(jnp.bfloat16)
        out_ref[0, :, pl.ds(2 * width, width)] = dv_sum[...].astype(jnp.bfloat16)


def attend_back(qkv, grad, attended, lse, limit, branch):
    micro, length, columns = qkv.shape
    width = columns // 3
    heads = width // HEAD
    tail = length - TRUNK_SEGS * SEG

    def part(index):
        return pl.BlockSpec((1, length, width), lambda m, h, index=index: (m, 0, index))

    row = pl.BlockSpec((1, 1, tail), lambda m, h: (m, 0, 0))
    return pl.pallas_call(
        attend_back_kernel,
        grid=(micro, heads),
        in_specs=[
            row,
            row,
            pl.BlockSpec((1, heads, length), lambda m, h: (m, 0, 0)),
            part(0),
            part(1),
            part(2),
            part(0),
            part(0),
        ],
        out_specs=pl.BlockSpec((1, length, columns), lambda m, h: (m, 0, 0)),
        out_shape=jax.ShapeDtypeStruct((micro, length, columns), jnp.bfloat16),
        scratch_shapes=[pltpu.VMEM((length, width), jnp.float32)] * 2,
        compiler_params=pltpu.CompilerParams(vmem_limit_bytes=56 << 20),
        cost_estimate=pl.CostEstimate(
            flops=micro * heads * length * length * WINDOW * 7,
            bytes_accessed=micro * length * width * 14,
            transcendentals=micro * heads * length * length // 2,
        ),
    )(limit[:, None, :], branch[:, None, :], lse, qkv, qkv, qkv, grad, attended)


def norm_back(grad_normed, normed_unit, scale_rows, gain_row):
    scaled_grad = grad_normed * gain_row
    return scale_rows * (
        scaled_grad - normed_unit * jnp.mean(scaled_grad * normed_unit, axis=-1, keepdims=True)
    )


def adam_update(master, first, second, grad, rate, decay):
    first_new = BETA_ONE * first + (1.0 - BETA_ONE) * grad
    second_new = BETA_TWO * second + (1.0 - BETA_TWO) * grad * grad
    fix_one = 1.0 - BETA_ONE**STEP
    fix_two = 1.0 - BETA_TWO**STEP
    step_size = first_new / fix_one / (jnp.sqrt(second_new / fix_two) + ADAM_EPS)
    return (master - rate * (step_size + decay * master), first_new, second_new)


def product(left, right, spec):
    return jnp.einsum(spec, left, right, preferred_element_type=jnp.float32)


Y_CHIPS = 2
CAPACITY = 8
SPARE = 8
GROUP = 16
CHUNK = 256
MESH_IDS = pl.DeviceIdType.MESH


def place():
    chip = lax.axis_index("chip")
    return (
        chip // Y_CHIPS,
        lax.rem(chip, Y_CHIPS),
        lax.axis_index("core"),
        lax.axis_index("seq"),
        lax.axis_size("chip") // Y_CHIPS,
    )


def at_z(z, y):
    return {"chip": z * Y_CHIPS + y}


def ahead(d):
    z, y, core, x, depth = place()
    return at_z(lax.rem(z + d, depth), y)


def across(axis):
    z, y, core, x, _ = place()
    return {"y": at_z(z, 1 - y), "x": {"seq": 1 - x}, "core": {"core": 1 - core}}[axis]


def greet():
    depth = place()[4]
    barrier = pltpu.get_barrier_semaphore()
    peers = [ahead(d) for d in range(1, depth)] + [across("y"), across("x"), across("core")]
    for peer in peers:
        pl.semaphore_signal(barrier, inc=1, device_id=peer, device_id_type=MESH_IDS)
    pl.semaphore_wait(barrier, len(peers))


def sem_pair(*shape):
    return [pltpu.SemaphoreType.DMA(shape), pltpu.SemaphoreType.DMA(shape)]


def remote(source, target, sems, index, device):
    return pltpu.make_async_remote_copy(
        src_ref=source,
        dst_ref=target,
        send_sem=sems[0].at[index],
        recv_sem=sems[1].at[index],
        device_id=device,
        device_id_type=MESH_IDS,
    )


def total(*parts):
    return functools.reduce(jnp.add, [p.astype(jnp.float32) for p in parts]).astype(jnp.bfloat16)


class Flow:
    def __init__(self):
        self.sent = []

    def push(self, source, target, sems, index, device):
        copy = remote(source, target, sems, index, device)
        copy.start()
        self.sent.append(copy)

    def arrive(self, here, sems, index):
        remote(here, here, sems, index, across("core")).wait_recv()

    def drain(self):
        for copy in self.sent:
            copy.wait_send()


class Total(Flow):
    def __init__(self, axes, sums, inbox, sems):
        super().__init__()
        self.axes, self.sums, self.inbox, self.sems = (axes, sums, inbox, sems)
        self.done = 0

    def begin(self, value):
        self.sums[0] = value
        self.push(self.sums.at[0], self.inbox.at[0], self.sems, (0,), across(self.axes[0]))

    def step(self):
        i = self.done
        self.done += 1
        self.arrive(self.inbox.at[i], self.sems, (i,))
        self.sums[i + 1] = self.sums[i] + self.inbox[i]
        here = self.sums.at[i + 1]
        if i + 1 < len(self.axes):
            self.push(here, self.inbox.at[i + 1], self.sems, (i + 1,), across(self.axes[i + 1]))
            return
        for d in range(1, place()[4]):
            self.push(here, self.inbox.at[i + d], self.sems, (i + d,), ahead(d))

    def result(self):
        last = len(self.axes)
        value = self.sums[last]
        for d in range(1, place()[4]):
            self.arrive(self.inbox.at[last - 1 + d], self.sems, (last - 1 + d,))
            value = value + self.inbox[last - 1 + d]
        self.drain()
        return value


def distances(depth):
    return sorted(range(1, depth), key=lambda d: min(d, depth - d))


def total_scratch(axes, depth, width):
    return [
        pltpu.VMEM((axes + 1, 8, width), jnp.float32),
        pltpu.VMEM((axes + depth - 1, 8, width), jnp.float32),
    ] + sem_pair(axes + depth - 1)


def spread_sems(depth):
    return sem_pair(depth) + sem_pair(depth) + sem_pair(depth, 2) + sem_pair(depth, 4)


class Spread(Flow):
    def __init__(self, window, second, sems):
        super().__init__()
        self.window = window
        self.second = second
        self.third = "x" if second == "y" else "y"
        self.sems = [(sems[2 * i], sems[2 * i + 1]) for i in range(4)]

    def where(self, d, second=False, third=False, other_core=False):
        z, y, core, x, depth = place()
        if second if self.second == "y" else third:
            y = 1 - y
        if third if self.second == "y" else second:
            x = 1 - x
        return self.window(lax.rem(z - d + depth, depth), y, 1 - core if other_core else core, x)

    def forward(self, stage, index, block, device):
        self.push(block, block, self.sems[stage], index, device)

    def begin(self):
        self.waiting = distances(place()[4])
        self.along_z()
        self.onward(0)

    def along_z(self):
        if self.waiting:
            d = self.waiting.pop(0)
            self.forward(0, (d,), self.where(0), ahead(d))

    def onward(self, d):
        block = self.where(d)
        self.forward(1, (d,), block, across(self.second))
        self.forward(2, (d, 0), block, across(self.third))
        self.forward(3, (d, 0), block, across("core"))

    def from_z(self, d):
        self.arrive(self.where(d), self.sems[0], (d,))
        self.along_z()
        self.onward(d)

    def from_second(self, d):
        block = self.where(d, True)
        self.arrive(block, self.sems[1], (d,))
        self.forward(2, (d, 1), block, across(self.third))
        self.forward(3, (d, 2), block, across("core"))

    def from_third(self, d):
        for second in range(2):
            block = self.where(d, bool(second), True)
            self.arrive(block, self.sems[2], (d, second))
            self.forward(3, (d, 2 * second + 1), block, across("core"))

    def finish(self):
        for d in range(place()[4]):
            for second in range(2):
                for third in range(2):
                    block = self.where(d, bool(second), bool(third), True)
                    self.arrive(block, self.sems[3], (d, 2 * second + third))
        self.drain()


def device_block(z, y, core, x):
    return ((z * Y_CHIPS + y) * 2 + core) * 2 + x


def chip_block(z, y, x):
    return (z * Y_CHIPS + y) * 2 + x


def gather_kernel(
    split,
    cut,
    block_ref,
    row_ref,
    spare_rank_ref,
    spare_mine_ref,
    low_ref,
    gain_ref,
    *refs,
):
    outs = refs[: 4 if split else 1]
    gain_out, whole, stage, stage_sem, spare, core_in, y_in, z_in, held = refs[len(outs) : len(outs) + 9]
    gain_sum, gain_in = refs[len(outs) + 9 : len(outs) + 11]
    sems = refs[len(outs) + 11 :]
    z, y, core, x, depth = place()
    piece, width = low_ref.shape[1:]
    half = CAPACITY // 2
    base = half * piece // GROUP
    me = device_block(z, y, core, x)
    per_piece = piece // GROUP
    for i in range(base):
        source = pl.ds(i % per_piece * GROUP, GROUP)
        whole[me, i] = low_ref[x * half + i // per_piece, source]
    greet()

    def window(first, count):
        return lambda *who: whole.at[device_block(*who), pl.ds(first, count)]

    flow_sems = 8
    early = Spread(window(0, cut), "y", sems[2 : 2 + flow_sems])
    late = Spread(window(cut, base - cut), "x", sems[10 : 10 + flow_sems])
    loose = Spread(window(base, 1), "x", sems[18 : 18 + flow_sems])
    gains = Total(["core", "y"], gain_sum, gain_in, sems[0:2])
    spare_sems = sems[26:32]
    spare_flow = Flow()
    early.begin()
    late.begin()
    gains.begin(gain_ref[...])
    count = SPARE // 2
    for i in range(count):
        found = low_ref[spare_rank_ref[x * count + i]]
        spare[pl.ds(i * piece, piece)] = jnp.where(spare_mine_ref[x * count + i] > 0, found, 0)
    rows = core_in.shape[0]

    def part(index, size):
        return pl.ds(pl.multiple_of(index * size, GROUP), size)

    spare_flow.push(spare.at[part(1 - core, rows)], core_in, spare_sems[0:2], (0,), across("core"))
    flows = [early, late]

    def from_z(d):
        for flow in flows:
            flow.from_z(d)

    def from_second(d):
        for flow in flows:
            flow.from_second(d)

    order = distances(depth)
    from_z(order[0])
    spare_flow.arrive(core_in, spare_sems[0:2], (0,))
    held[...] = total(spare[part(core, rows)], core_in[...])
    spare_flow.push(held.at[part(1 - y, rows // 2)], y_in, spare_sems[2:4], (0,), across("y"))
    gains.step()
    from_second(0)
    for i in range(1, depth - 1):
        from_z(order[i])
        if i == 1:
            spare_flow.arrive(y_in, spare_sems[2:4], (0,))
            y_in[...] = total(held[part(y, rows // 2)], y_in[...])
            for e in range(1, depth):
                to = part(lax.rem(z + e, depth), GROUP)
                spare_flow.push(y_in.at[to], z_in.at[e], spare_sems[4:6], (e,), ahead(e))
            gains.step()
        from_second(order[i - 1])
        for flow in flows:
            flow.from_third(([0] + order)[i - 1])
    for d in range(1, depth):
        spare_flow.arrive(z_in.at[d], spare_sems[4:6], (d,))
    whole[me, base] = total(y_in[part(z, GROUP)], *[z_in[d] for d in range(1, depth)])
    loose.begin()
    from_second(order[-1])
    gain_out[...] = gains.result()
    for d in order:
        loose.from_z(d)
    for flow in flows:
        flow.from_third(order[-2])
    for d in range(depth):
        loose.from_second(d)
    for flow in flows:
        flow.from_third(order[-1])
    for d in range(depth):
        loose.from_third(d)
    for flow in flows + [loose]:
        flow.finish()
    spare_flow.drain()

    buffers = stage.shape[0]
    per_chunk = CHUNK // GROUP
    narrow = width // 2
    copies = []
    for index in range(6 * width // CHUNK):
        matrix, first = divmod(index * CHUNK, width)
        slot = index % buffers
        if index >= buffers:
            copies[index - buffers].wait()
        thin = split and matrix < 3
        columns = pl.ds(pl.multiple_of(core * narrow, LANES), narrow) if thin else slice(None)
        count = narrow if thin else width

        def step(i, carry, index=index, slot=slot, columns=columns, count=count):
            for g in range(per_piece):
                at = index * per_chunk + i * per_piece + g
                target = pl.ds(pl.multiple_of(i * piece + g * GROUP, GROUP), GROUP)
                stage[slot, target, pl.ds(0, count)] = whole[block_ref[at], row_ref[at], :, columns]
            return carry

        lax.fori_loop(0, per_chunk // per_piece, step, 0)
        if thin:
            target = outs[0].at[pl.ds(first, CHUNK), pl.ds(matrix * narrow, narrow)]
        elif split:
            target = outs[matrix - 2].at[pl.ds(first, CHUNK)]
        else:
            target = outs[0].at[matrix, pl.ds(first, CHUNK)]
        copies.append(
            pltpu.make_async_copy(stage.at[slot, :, pl.ds(0, count)], target, stage_sem.at[slot])
        )
        copies[-1].start()
    for copy in copies[-buffers:]:
        copy.wait()


def gather_pieces(low, gains, plan, split):
    slots, piece, width = low.shape
    block, row, spare_rank, spare_mine, gain_mine = plan
    chips = lax.axis_size("chip")
    depth = chips // Y_CHIPS
    base = CAPACITY // 2 * piece // GROUP
    shapes = [(width, 3 * (width // 2))] + [(width, width)] * 3 if split else [(6, width, width)]
    lane = SPARE * piece // 4
    buffers = 4
    picked = jnp.where(gain_mine[:, None], gains[: gain_mine.shape[0]].astype(jnp.float32), 0.0)
    padded = jnp.concatenate([picked, jnp.zeros((6, width), jnp.float32)], axis=0)
    vmem = pl.BlockSpec(memory_space=pltpu.VMEM)
    smem = pl.BlockSpec(memory_space=pltpu.SMEM)
    outs = pl.pallas_call(
        functools.partial(gather_kernel, split, base // 4 if split else base // 2),
        in_specs=[smem] * 3 + [vmem] * 3,
        out_specs=[pl.BlockSpec(memory_space=pl.ANY)] * len(shapes) + [vmem],
        out_shape=[jax.ShapeDtypeStruct(s, jnp.bfloat16) for s in shapes]
        + [jax.ShapeDtypeStruct((8, width), jnp.float32)],
        scratch_shapes=[
            pltpu.VMEM((4 * chips, base + 1, GROUP, width), jnp.bfloat16),
            pltpu.VMEM((buffers, CHUNK, width), jnp.bfloat16),
            pltpu.SemaphoreType.DMA((buffers,)),
            pltpu.VMEM((2 * lane, width), jnp.bfloat16),
            pltpu.VMEM((lane, width), jnp.bfloat16),
            pltpu.VMEM((lane // 2, width), jnp.bfloat16),
            pltpu.VMEM((depth, GROUP, width), jnp.bfloat16),
            pltpu.VMEM((lane, width), jnp.bfloat16),
        ]
        + total_scratch(2, depth, width)
        + spread_sems(depth) * 3
        + sem_pair(1)
        + sem_pair(1)
        + sem_pair(depth),
        compiler_params=pltpu.CompilerParams(
            collective_id=0 if split else 1, has_side_effects=True, vmem_limit_bytes=48 << 20
        ),
        cost_estimate=pl.CostEstimate(
            flops=0, bytes_accessed=6 * width * width * 16, transcendentals=0
        ),
    )(
        block.reshape(-1),
        row.reshape(-1),
        spare_rank,
        jnp.broadcast_to(spare_mine[:, None, None], (SPARE, 1, width)),
        low,
        padded,
    )
    return (*outs[:-1], outs[-1][:2].astype(jnp.bfloat16))


def halves(matrices, split):
    if not split:
        return (matrices,)
    width = matrices.shape[1]
    narrow = width // 2
    thin = lax.dynamic_slice_in_dim(matrices[:3], lax.axis_index("core") * narrow, narrow, axis=2)
    side = jnp.concatenate([thin[0], thin[1], thin[2]], axis=1)
    return (side, matrices[3], matrices[4], matrices[5])


def gather_slots(low, gains, owners, split):
    slots, piece, width = low.shape
    piece_owner, rank = owner_slots(owners, slots)
    rows = slots * piece
    half = -(-(rows // 2 + 1) // GROUP) * GROUP
    filler = jnp.zeros((2 * half - rows - 2, width), jnp.bfloat16)
    packed = jnp.concatenate([low.reshape(rows, width), gains, filler], axis=0)
    share = lax.dynamic_slice_in_dim(packed, lax.axis_index("seq") * half, half, axis=0)
    groups = lax.all_gather(share, ALL, axis=0, tiled=True).reshape(-1, GROUP, width)
    per_owner = 2 * half // GROUP
    base = piece_owner * per_owner + rank * (piece // GROUP)
    index = base[:, None] + jnp.arange(piece // GROUP, dtype=jnp.int32)[None, :]
    matrices = groups[index.reshape(-1)].reshape(6, width, width)
    gain_rows = groups[owners[-2:] * per_owner + rows // GROUP][jnp.arange(2), jnp.arange(2)]
    return (*halves(matrices, split), gain_rows)


def kernels_fit(slots, piece, width):
    chips = lax.axis_size("chip")
    return slots == 2 * CAPACITY and piece == GROUP * (chips // Y_CHIPS) and width % CHUNK == 0


def spare_pieces(owners, slots):
    piece_owner, rank = owner_slots(owners, slots)
    spare = rank >= CAPACITY
    return (piece_owner, rank, spare, jnp.cumsum(spare.astype(jnp.int32)) - 1)


def gather_store(low, gains, owners, split, few):
    if not few:
        return gather_slots(low, gains, owners, split)
    slots, piece, width = low.shape
    dp_pos = lax.axis_index("chip") * 2 + lax.axis_index("core")
    piece_owner, rank, spare, order = spare_pieces(owners, slots)
    half = CAPACITY // 2
    groups = piece // GROUP
    group = jnp.arange(groups, dtype=jnp.int32)[None, :]
    block = jnp.where(
        spare[:, None],
        device_block(group, (order % 2)[:, None], ((order // 2) % 2)[:, None], (order // 4)[:, None]),
        (piece_owner * 2 + rank // half)[:, None],
    )
    row = jnp.where(spare[:, None], half * groups, (rank % half)[:, None] * groups + group)
    labels = jnp.arange(SPARE, dtype=jnp.int32)
    own = (spare & (piece_owner == dp_pos))[None, :] & (order[None, :] == labels[:, None])
    spare_rank = jnp.sum(jnp.where(own, rank[None, :], 0), axis=1)
    spare_mine = jnp.any(own, axis=1).astype(jnp.int32)
    plan = (block, row, spare_rank, spare_mine, owners[-2:] == dp_pos)
    return gather_pieces(low, gains, plan, split)


class Reduce(Flow):
    def __init__(self, first, shard, one, two, three, sems):
        super().__init__()
        self.first = first
        self.other = "y" if first == "x" else "x"
        self.shard = shard
        self.one, self.two, self.three = (one, two, three)
        self.sems = [sems[0:2], sems[2:4], sems[4:6]]

    def start(self, d, b):
        self.push(self.shard(d, b, 1), self.one.at[d, b], self.sems[0], (d, b), across(self.first))

    def from_first(self, d, b):
        here = self.one.at[d, b]
        self.arrive(here, self.sems[0], (d, b))
        here[...] = total(here[...], self.shard(d, b, 0)[...])
        if b:
            self.push(here, self.two.at[d], self.sems[1], (d,), across(self.other))

    def from_second(self, d):
        here = self.two.at[d]
        self.arrive(here, self.sems[1], (d,))
        here[...] = total(here[...], self.one[d, 0])
        if d:
            self.push(here, self.three.at[d], self.sems[2], (d,), ahead(d))

    def result(self):
        depth = place()[4]
        for d in range(1, depth):
            self.arrive(self.three.at[d], self.sems[2], (d,))
        value = total(self.two[0], *[self.three[d] for d in range(1, depth)])
        self.drain()
        return value


def reduce_kernel(
    source_ref,
    spare_ref,
    spare_mine_ref,
    early_ref,
    late_ref,
    gain_ref,
    slot_ref,
    gain_out,
    pieces,
    blocks,
    early_one,
    early_two,
    early_three,
    late_one,
    late_two,
    late_three,
    final,
    pair_in,
    full,
    full_in,
    spares,
    gain_sum,
    gain_in,
    load_sem,
    *sems,
):
    z, y, core, x, depth = place()
    narrow = pieces.shape[2]
    groups = late_ref.shape[1]
    per_block = blocks.shape[1]
    cut = early_one.shape[2]
    owned = CAPACITY // 2 * slot_ref.shape[1]
    order = distances(depth)[::-1] + [0]
    loads = []
    for matrix in range(3):
        columns = pl.ds(matrix * narrow, narrow)
        loads.append((early_ref.at[:, :, columns], matrix))
        loads.append((late_ref.at[matrix], matrix + 3))
    loads = [
        pltpu.make_async_copy(source, pieces.at[pl.ds(m * groups, groups)], load_sem.at[m])
        for source, m in loads
    ]
    for load in loads:
        load.start()
    pieces[6 * groups] = jnp.zeros((GROUP, narrow), jnp.bfloat16)
    greet()
    gains = Total(["core", "x", "y"], gain_sum, gain_in, sems[0:2])
    gains.begin(gain_ref[...])
    for load in loads:
        load.wait()

    def block_at(d, swap_y, swap_x):
        return chip_block(
            lax.rem(z + d, depth), 1 - y if swap_y else y, 1 - x if swap_x else x
        )

    early = Reduce(
        "x",
        lambda d, b, a: blocks.at[block_at(d, b, a), pl.ds(0, cut)],
        early_one,
        early_two,
        early_three,
        sems[2:8],
    )
    late = Reduce(
        "y",
        lambda d, b, a: blocks.at[block_at(d, a, b), pl.ds(cut, per_block - cut)],
        late_one,
        late_two,
        late_three,
        sems[8:14],
    )

    def fill(d, swap_y, swap_x):
        block = block_at(d, swap_y, swap_x)

        def step(i, carry):
            for g in range(2):
                blocks[block, 2 * i + g] = pieces[source_ref[block * per_block + 2 * i + g]]
            return carry

        lax.fori_loop(0, per_block // 2, step, 0)

    def start(d, b):
        for flow in (early, late):
            flow.start(d, b)

    fill(order[0], 1, 1)
    start(order[0], 1)
    fill(order[0], 0, 1)
    fill(order[0], 1, 0)
    start(order[0], 0)
    fill(order[0], 0, 0)
    for i, d in enumerate(order):
        later = order[i + 1] if i + 1 < len(order) else None
        if later is not None:
            fill(later, 1, 1)
        for flow in (early, late):
            flow.from_first(d, 1)
        if later is not None:
            start(later, 1)
            fill(later, 0, 1)
            fill(later, 1, 0)
        for flow in (early, late):
            flow.from_first(d, 0)
        if later is not None:
            start(later, 0)
            fill(later, 0, 0)
        if i:
            for flow in (early, late):
                flow.from_second(order[i - 1])
        if i < 3:
            gains.step()
    for flow in (early, late):
        flow.from_second(order[-1])
    final[pl.ds(0, cut)] = early.result()
    final[pl.ds(cut, per_block - cut)] = late.result()

    ends = Flow()
    own_spare = spares.at[z, y, x, core]
    ends.push(final.at[pl.ds((1 - core) * owned, owned)], pair_in, sems[14:16], (0,), across("core"))
    spares[z, y, x, core] = final[pl.ds(2 * owned, 2)]
    for d in range(1, depth):
        ends.push(own_spare, own_spare, sems[16:18], (d,), ahead(d))
    gain_out[...] = gains.result()
    ends.arrive(pair_in, sems[14:16], (0,))
    for g in range(owned):
        mine = final[core * owned + g]
        theirs = pair_in[g]
        first = core == 0
        full[g, :, pl.ds(pl.multiple_of(core * narrow, LANES), narrow)] = mine
        full[g, :, pl.ds(pl.multiple_of((1 - core) * narrow, LANES), narrow)] = theirs
    ends.push(full, full_in, sems[14:16], (1,), across("x"))
    for d in range(1, depth):
        from_z = spares.at[lax.rem(z - d + depth, depth), y, x, core]
        ends.arrive(from_z, sems[16:18], (d,))
    here = spares.at[:, y, x, core]
    ends.push(here, here, sems[14:16], (2,), across("y"))
    ends.arrive(spares.at[:, 1 - y, x, core], sems[14:16], (2,))
    here = spares.at[:, :, x, core]
    ends.push(here, here, sems[14:16], (3,), across("x"))
    ends.arrive(spares.at[:, :, 1 - x, core], sems[14:16], (3,))
    here = spares.at[:, :, :, core]
    ends.push(here, here, sems[14:16], (4,), across("core"))
    ends.arrive(spares.at[:, :, :, 1 - core], sems[14:16], (4,))
    ends.arrive(full_in, sems[14:16], (1,))
    per_piece = slot_ref.shape[1]
    half = CAPACITY // 2
    for i in range(half):
        for g in range(per_piece):
            slot_ref[x * half + i, g] = full[i * per_piece + g]
            slot_ref[(1 - x) * half + i, g] = full_in[i * per_piece + g]

    def pick(slot, carry):
        for g in range(per_piece):
            at = spare_ref[slot] * per_piece + g
            sub = spares.shape[4]
            chip = lax.div(at, 2 * sub)
            where = (lax.div(chip, Y_CHIPS), lax.rem(chip, Y_CHIPS), lax.rem(lax.div(at, sub), 2))
            for side in range(2):
                found = spares[(*where, side, lax.rem(at, sub))]
                slot_ref[CAPACITY + slot, g, :, pl.ds(side * narrow, narrow)] = jnp.where(
                    spare_mine_ref[slot] > 0, found, 0
                )
        return carry

    lax.fori_loop(0, slot_ref.shape[0] - CAPACITY, pick, 0)
    ends.drain()


def reduce_slots(early, late, gains, owners, slots, piece):
    width = late.shape[1]
    narrow = width // 2
    chips = lax.axis_size("chip")
    depth = chips // Y_CHIPS
    groups = width // GROUP
    per_piece = piece // GROUP
    dp_pos = lax.axis_index("chip") * 2 + lax.axis_index("core")
    piece_owner, rank, spare, order = spare_pieces(owners, slots)
    half = CAPACITY // 2
    labels = jnp.arange(piece_owner.shape[0], dtype=jnp.int32)
    empty = 6 * groups

    def groups_of(match):
        first = jnp.sum(jnp.where(match, labels, 0), axis=-1)[..., None] * per_piece
        groups_at = first + jnp.arange(per_piece, dtype=jnp.int32)
        return jnp.where(jnp.any(match, axis=-1)[..., None], groups_at, empty)

    block = jnp.arange(2 * chips, dtype=jnp.int32)[:, None]
    entry = jnp.arange(CAPACITY, dtype=jnp.int32)[None, :]
    owner_at = block // 2 * 2 + entry // half
    rank_at = block % 2 * half + entry % half
    base_groups = groups_of(
        (piece_owner == owner_at[..., None]) & (rank == rank_at[..., None])
    ).reshape(2 * chips, -1)
    spare_hot = spare & (order == jnp.arange(SPARE, dtype=jnp.int32)[:, None])
    spare_groups = groups_of(spare_hot).reshape(2 * chips, -1)
    source = jnp.concatenate([base_groups, spare_groups], axis=1)
    per_block = source.shape[1]
    mine = (piece_owner == dp_pos) & spare & (order < SPARE)
    slot_hot = mine & (rank == CAPACITY + jnp.arange(slots - CAPACITY, dtype=jnp.int32)[:, None])
    spare_at = jnp.sum(jnp.where(slot_hot, order, 0), axis=1)
    subs = SPARE * per_piece // (2 * chips)

    vmem = pl.BlockSpec(memory_space=pltpu.VMEM)
    smem = pl.BlockSpec(memory_space=pltpu.SMEM)
    hbm = pl.BlockSpec(memory_space=pl.ANY)
    cut = per_block // 4 + 1
    owned = half * per_piece
    padded = jnp.concatenate([gains, jnp.zeros((8 - gains.shape[0], width), jnp.float32)], axis=0)

    def group_block(*shape):
        return pltpu.VMEM(shape + (GROUP, narrow), jnp.bfloat16)

    def flow_blocks(count):
        return [group_block(depth, 2, count), group_block(depth, count), group_block(depth, count)]

    flow_sems = sem_pair(depth, 2) + sem_pair(depth) + sem_pair(depth)
    slot_grad, gain_sum = pl.pallas_call(
        reduce_kernel,
        in_specs=[smem] * 2 + [vmem, hbm, hbm, vmem],
        out_specs=[vmem, vmem],
        out_shape=[
            jax.ShapeDtypeStruct((slots, per_piece, GROUP, width), jnp.bfloat16),
            jax.ShapeDtypeStruct((8, width), jnp.float32),
        ],
        scratch_shapes=[group_block(6 * groups + 1), group_block(2 * chips, per_block)]
        + flow_blocks(cut)
        + flow_blocks(per_block - cut)
        + [
            group_block(per_block),
            group_block(owned),
            pltpu.VMEM((owned, GROUP, width), jnp.bfloat16),
            pltpu.VMEM((owned, GROUP, width), jnp.bfloat16),
            group_block(depth, Y_CHIPS, 2, 2, subs),
        ]
        + total_scratch(3, depth, width)[:2]
        + [pltpu.SemaphoreType.DMA((6,))]
        + total_scratch(3, depth, width)[2:]
        + flow_sems
        + flow_sems
        + sem_pair(5)
        + sem_pair(depth),
        compiler_params=pltpu.CompilerParams(
            collective_id=2, has_side_effects=True, vmem_limit_bytes=56 << 20
        ),
        cost_estimate=pl.CostEstimate(
            flops=0, bytes_accessed=6 * width * width * 8, transcendentals=0
        ),
    )(
        source.reshape(-1),
        spare_at,
        jnp.broadcast_to(jnp.any(slot_hot, axis=1).astype(jnp.int32)[:, None, None], (slots - CAPACITY, 1, narrow)),
        early.reshape(groups, GROUP, 3 * narrow),
        late.reshape(3, groups, GROUP, narrow),
        padded,
    )
    return (slot_grad.reshape(slots, piece, width), gain_sum[:2])


def reduce_all(early, late, gains, owners, slots, piece, few):
    if few:
        return reduce_slots(early, late, gains, owners, slots, piece)
    width = late.shape[1]
    narrow = width // 2
    dp_pos = lax.axis_index("chip") * 2 + lax.axis_index("core")
    pieces = owners.shape[0] - 2
    chips = lax.axis_size("chip")
    local = jnp.concatenate([jnp.transpose(early.reshape(width, 3, narrow), (1, 0, 2)), late], axis=0)
    share = lax.psum_scatter(
        local.reshape(6 * width, narrow), ("chip", "seq"), scatter_dimension=0, tiled=True
    )
    sums = lax.all_gather(share, ALL, axis=0, tiled=False).reshape(chips, 2, 2, -1, narrow)
    sums = jnp.transpose(sums, (0, 2, 3, 1, 4)).reshape(pieces, piece, width)
    piece_owner, rank = owner_slots(owners, slots)
    labels = jnp.arange(slots, dtype=jnp.int32)
    match = (piece_owner == dp_pos) & (rank == labels[:, None])
    slot_grad = jnp.where(jnp.any(match, axis=1)[:, None, None], sums[jnp.argmax(match, axis=1)], 0)
    return (slot_grad, lax.psum(gains, ALL))


def adam_kernel(rate_ref, master_ref, first_ref, second_ref, grad_ref, *outs):
    count = master_ref.shape[0]
    for i in range(count):
        new, first_new, second_new = adam_update(
            master_ref[i],
            first_ref[i],
            second_ref[i],
            grad_ref[i].astype(jnp.float32),
            rate_ref[pl.program_id(0) * count + i],
            MATRIX_DECAY,
        )
        outs[0][i] = new
        outs[1][i] = first_new
        outs[2][i] = second_new
        outs[3][i] = new.astype(jnp.bfloat16)


def adam_slots(master, first, second, grad, rate):
    slots, piece, width = master.shape
    count = min(slots, 2)
    block = pl.BlockSpec((count, piece, width), lambda i: (i, 0, 0))
    shape = jax.ShapeDtypeStruct(master.shape, jnp.float32)
    return pl.pallas_call(
        adam_kernel,
        grid=(slots // count,),
        in_specs=[pl.BlockSpec(memory_space=pltpu.SMEM)] + [block] * 4,
        out_specs=[block] * 4,
        out_shape=[shape] * 3 + [jax.ShapeDtypeStruct(master.shape, jnp.bfloat16)],
        compiler_params=pltpu.CompilerParams(vmem_limit_bytes=60 << 20),
        cost_estimate=pl.CostEstimate(
            flops=20 * slots * piece * width,
            bytes_accessed=28 * slots * piece * width,
            transcendentals=slots * piece * width,
        ),
    )(rate, master, first, second, grad)


def local(*arrays):
    owners, weight_store = arrays[3:5]
    if not kernels_fit(*weight_store.shape):
        return step(False, *arrays)
    order = spare_pieces(owners, weight_store.shape[0])[3]
    few = order[-1] < SPARE
    return lax.cond(few, functools.partial(step, True), functools.partial(step, False), *arrays)


def step(
    few,
    tokens,
    cotangent,
    parents,
    owners,
    weight_store,
    gain_store,
    weight_first,
    gain_first,
    weight_second,
    gain_second,
):
    core = lax.axis_index("core")
    dp_pos = lax.axis_index("chip") * 2 + core
    slot_dev, piece, width = weight_store.shape
    pieces = owners.shape[0] - 2
    piece_owner, rank = owner_slots(owners, slot_dev)
    gain_owner = owners[pieces:]
    micro, _, rows, _ = tokens.shape
    half = width // 2
    own_rows = core * rows
    own_columns = core * half

    def mine(value, axis, size, index):
        return lax.dynamic_slice_in_dim(value, index * size, size, axis=axis)

    limit, branch = tail_limits(transposed(parents[:, 0]))
    arrived = moved(tokens[:, 0])
    qkv_weight, out_weight, up_weight, down_weight, gain_low = gather_store(
        weight_store.astype(jnp.bfloat16), gain_store.astype(jnp.bfloat16), owners, True, few
    )
    gain_low, arrived, cot = lax.optimization_barrier((gain_low, arrived, cotangent[:, 0]))
    own_tokens = settled(tokens[:, 0], arrived)
    own_cot = transposed(cot)
    other_tokens = partner(own_tokens)

    def by_core(own, other, axis):
        return jnp.where(
            core == 0,
            jnp.concatenate([own, other], axis=axis),
            jnp.concatenate([other, own], axis=axis),
        )

    all_tokens = by_core(own_tokens, other_tokens, 1)
    gain_one = gain_low[0].astype(jnp.float32)
    gain_two = gain_low[1].astype(jnp.float32)

    def unit(values):
        scale = lax.rsqrt(jnp.mean(values * values, axis=-1, keepdims=True) + NORM_EPS)
        return (values * scale, scale)

    normed_one = (unit(all_tokens.astype(jnp.float32))[0] * gain_one).astype(jnp.bfloat16)
    normed_one = lax.optimization_barrier(normed_one)
    qkv = product(normed_one, qkv_weight, "mtd,de->mte").astype(jnp.bfloat16)
    attended_half, lse = attend(qkv, limit, branch)
    lse_rows = jnp.transpose(lse[:, :, : half // HEAD], (0, 2, 1))
    attended = by_core(
        mine(attended_half, 1, rows, core), partner(mine(attended_half, 1, rows, 1 - core)), 2
    )
    residual = own_tokens.astype(jnp.float32)
    hidden_one = residual + product(attended, out_weight, "mti,io->mto")
    unit_two, scale_two = unit(hidden_one)
    normed_two = (unit_two * gain_two).astype(jnp.bfloat16)
    up_rows = product(normed_two, up_weight, "mti,io->mto")
    sigmoid_up = jax.nn.sigmoid(up_rows)
    activated = (up_rows * sigmoid_up).astype(jnp.bfloat16)
    mixed_rows = (hidden_one + product(activated, down_weight, "mti,io->mto")).astype(jnp.bfloat16)
    mixed = transposed(mixed_rows)

    grad_down = product(activated, own_cot, "mti,mto->io")
    grad_hidden = product(own_cot, down_weight, "mto,io->mti")
    grad_up_rows = (grad_hidden * (sigmoid_up * (1.0 + up_rows * (1.0 - sigmoid_up)))).astype(
        jnp.bfloat16
    )
    grad_up = product(normed_two, grad_up_rows, "mti,mto->io")
    grad_normed_two = product(grad_up_rows, up_weight, "mto,io->mti")
    gain_two_grad = jnp.sum(grad_normed_two * unit_two, axis=(0, 1))
    grad_hidden_one = own_cot.astype(jnp.float32) + norm_back(
        grad_normed_two, unit_two, scale_two, gain_two
    )
    branch_grad = grad_hidden_one.astype(jnp.bfloat16)
    grad_out = product(attended, branch_grad, "mti,mto->io")
    late = jnp.stack([grad_out, grad_up, grad_down]).astype(jnp.bfloat16)
    late_back = partner(mine(late, 2, half, 1 - core))

    branch_grad, late = lax.optimization_barrier((branch_grad, late))
    grad_attended = product(branch_grad, out_weight, "mto,io->mti").astype(jnp.bfloat16)
    grad_half = by_core(
        mine(grad_attended, 2, half, core), partner(mine(grad_attended, 2, half, 1 - core)), 1
    )
    grad_qkv_rows = attend_back(qkv, grad_half, attended_half, lse_rows, limit, branch)
    grad_qkv = product(normed_one, grad_qkv_rows, "mti,mto->io")
    early = grad_qkv.astype(jnp.bfloat16)

    grad_normed_part = product(grad_qkv_rows, qkv_weight, "mte,de->mtd")
    grad_normed_one = mine(grad_normed_part, 1, rows, core) + partner(
        mine(grad_normed_part, 1, rows, 1 - core).astype(jnp.bfloat16)
    ).astype(jnp.float32)
    unit_one, scale_one = unit(residual)
    gain_one_grad = jnp.sum(grad_normed_one * unit_one, axis=(0, 1))
    token_rows = (
        grad_hidden_one + norm_back(grad_normed_one, unit_one, scale_one, gain_one)
    ).astype(jnp.bfloat16)
    token_grad = transposed(token_rows)
    gain_grads = jnp.stack([gain_one_grad, gain_two_grad])
    late = (mine(late, 2, half, core).astype(jnp.float32) + late_back.astype(jnp.float32)).astype(
        jnp.bfloat16
    )

    labels = jnp.arange(slot_dev, dtype=jnp.int32)
    match = (piece_owner[None, :] == dp_pos) & (rank[None, :] == labels[:, None])
    held = jnp.any(match, axis=1)
    piece_of = jnp.sum(jnp.where(match, jnp.arange(pieces, dtype=jnp.int32)[None, :], 0), axis=1)
    slot_grad, gain_sum = reduce_all(early, late, gain_grads, owners, slot_dev, piece, few)
    is_out = held & (piece_of // (width // piece) == 3)
    slot_rate = jnp.where(is_out, RATE_OUT, RATE_QKV).astype(jnp.float32)
    weight_new, weight_first_new, weight_second_new, weight_low = adam_slots(
        weight_store, weight_first, weight_second, slot_grad, slot_rate
    )
    gain_slot_grad = jnp.where((gain_owner == dp_pos)[:, None], gain_sum, 0.0)
    gain_new, gain_first_new, gain_second_new = adam_update(
        gain_store, gain_first, gain_second, gain_slot_grad, RATE_GAIN, 0.0
    )
    weight_copies, gain_copies = gather_store(
        weight_low, gain_new.astype(jnp.bfloat16), owners, False, few
    )
    return (
        mixed[:, None],
        token_grad[:, None],
        weight_new,
        gain_new,
        weight_first_new,
        gain_first_new,
        weight_second_new,
        gain_second_new,
        weight_copies,
        gain_copies,
    )


def solution(mesh):
    dp_count, seq_count = mesh.devices.shape
    fine = Mesh(mesh.devices.reshape(dp_count // 2, 2, seq_count), ALL)
    dp = ("chip", "core")
    rows = P(None, dp, "seq", None)
    store = P(dp, None, None)
    gains = P(dp, None)
    in_specs = (rows, rows, P(None, dp, None), P(), store, gains, store, gains, store, gains)
    out_specs = (rows, rows, store, gains, store, gains, store, gains, P(), P())
    return jax.shard_map(local, mesh=fine, in_specs=in_specs, out_specs=out_specs, check_vma=False)
```

```python
import functools

import jax
import jax.numpy as jnp
from jax import lax
from jax.experimental import pallas as pl
from jax.experimental.pallas import tpu as pltpu
from jax.sharding import Mesh
from jax.sharding import PartitionSpec as P

HEAD = 80
SEG = 32
TRUNK_SEGS = 32
ALWAYS_SEGS = TRUNK_SEGS // 2
STEP = 7
LANES = 128
WINDOW = 256
QUERY_BLOCK = 256

NORM_EPS = 1e-06
BETA_ONE = 0.5
BETA_TWO = 0.5
ADAM_EPS = 1e-08
MATRIX_DECAY = 0.1
RATE_QKV = 0.03
RATE_OUT = 0.4
RATE_GAIN = 0.4
MASKED = -1e30
SCALE = HEAD**-0.5
LOG2E = 1.4426950408889634
ALL = ("chip", "core", "seq")
NT = (((1,), (1,)), ((), ()))
TN = (((0,), (0,)), ((), ()))


def moved(value):
    chips = lax.axis_size("chip")
    pairs = [(k * 4 + c * 2 + 1 - c, k * 4 + 2 - 2 * c + c) for k in range(chips) for c in range(2)]
    return lax.ppermute(value, ALL, pairs)


def settled(value, arrived):
    return jnp.where(lax.axis_index("core") == lax.axis_index("seq"), value, arrived)


def transposed(value):
    return settled(value, moved(value))


def partner(value):
    return lax.ppermute(value, "core", [(0, 1), (1, 0)])


def owner_slots(owners, slot_dev):
    count = owners.shape[0] - 2
    piece_owner = owners[:count]
    labels = jnp.arange(count, dtype=jnp.int32)
    same = (piece_owner[:, None] == piece_owner[None, :]) & (labels[None, :] < labels[:, None])
    rank = jnp.sum(same.astype(jnp.int32), axis=1)
    return (piece_owner, rank)


def tail_limits(parents):
    up = parents[:, TRUNK_SEGS:]
    leaf = up >= TRUNK_SEGS
    above = jnp.where(leaf, up - TRUNK_SEGS, 0)
    labels = jnp.arange(up.shape[1], dtype=jnp.int32)
    hot = above[:, :, None] == labels[None, None, :]
    upper = jnp.sum(jnp.where(hot, up[:, None, :], 0), axis=2)
    attach = jnp.where(leaf, upper, up)
    limit = (attach + 1) * SEG
    branch = jnp.where(leaf, above, -1)
    return (jnp.repeat(limit, SEG, axis=1), jnp.repeat(branch, SEG, axis=1))


def query_blocks(length):
    trunk = TRUNK_SEGS * SEG
    blocks = []
    for first in range(0, trunk, QUERY_BLOCK):
        parts = [(0, first, "all")] if first else []
        blocks.append((first, QUERY_BLOCK, parts + [(first, QUERY_BLOCK, "causal")]))
    always = ALWAYS_SEGS * SEG
    tail = length - trunk
    blocks.append(
        (trunk, tail, [(0, always, "all"), (always, trunk - always, "trunk"), (trunk, tail, "tail")])
    )
    return blocks


def allowed_pairs(kind, key_first, key, query, limit, branch):
    if kind == "causal":
        return key <= query
    if kind == "trunk":
        return key + key_first < limit
    key_seg = key // SEG
    return ((key_seg == query // SEG) & (key <= query)) | (key_seg == branch)


def head_window(head, width):
    start = pl.multiple_of(
        jnp.minimum((head * HEAD) // LANES, width // LANES - WINDOW // LANES) * LANES, LANES
    )
    lane = lax.broadcasted_iota(jnp.int32, (1, WINDOW), 1) + start
    mine = (lane >= head * HEAD) & (lane < (head + 1) * HEAD)
    return (pl.ds(start, WINDOW), mine)


def scaled_query(rows, mine):
    return jnp.where(mine, rows.astype(jnp.float32) * (SCALE * LOG2E), 0.0).astype(jnp.bfloat16)


def attend_kernel(limit_ref, branch_ref, q_ref, k_ref, v_ref, out_ref, lse_ref):
    head = pl.program_id(1)
    window, mine = head_window(head, q_ref.shape[2])
    stat_lane = lax.broadcasted_iota(jnp.int32, (1, LANES), 1)
    values = jnp.where(mine, v_ref[0, :, window], 1)
    keys_side = k_ref[0, :, window].T
    for first, count, parts in query_blocks(q_ref.shape[1]):
        rows = pl.ds(first, count)
        query = scaled_query(q_ref[0, rows, window], mine)
        scores = []
        for key_first, keys, kind in parts:
            raw = jnp.dot(
                query, keys_side[:, key_first : key_first + keys], preferred_element_type=jnp.float32
            )
            if kind != "all":
                ok = allowed_pairs(
                    kind,
                    key_first,
                    lax.broadcasted_iota(jnp.int32, (count, keys), 1),
                    lax.broadcasted_iota(jnp.int32, (count, keys), 0),
                    limit_ref[0],
                    branch_ref[0],
                )
                raw = jnp.where(ok, raw, MASKED)
            scores.append(raw)
        top = functools.reduce(jnp.maximum, [jnp.max(s, axis=1, keepdims=True) for s in scores])
        gained = 0.0
        for raw, (key_first, keys, kind) in zip(scores, parts):
            gained = gained + jnp.dot(
                jnp.exp2(raw - top).astype(jnp.bfloat16),
                values[key_first : key_first + keys],
                preferred_element_type=jnp.float32,
            )
        weight_sum = jnp.max(jnp.where(mine, 0.0, gained), axis=1, keepdims=True)
        gained = (gained * (1.0 / weight_sum)).astype(jnp.bfloat16)
        out_ref[0, rows, window] = jnp.where(mine, gained, out_ref[0, rows, window])
        lse_ref[0, rows, :] = jnp.where(
            stat_lane == head, top + jnp.log2(weight_sum), lse_ref[0, rows, :]
        )


def attend(qkv, limit, branch):
    micro, length, columns = qkv.shape
    width = columns // 3
    heads = width // HEAD
    tail = length - TRUNK_SEGS * SEG

    def part(index):
        return pl.BlockSpec((1, length, width), lambda m, h, index=index: (m, 0, index))

    column = pl.BlockSpec((1, tail, 1), lambda m, h: (m, 0, 0))
    return pl.pallas_call(
        attend_kernel,
        grid=(micro, heads),
        in_specs=[column, column, part(0), part(1), part(2)],
        out_specs=[
            pl.BlockSpec((1, length, width), lambda m, h: (m, 0, 0)),
            pl.BlockSpec((1, length, LANES), lambda m, h: (m, 0, 0)),
        ],
        out_shape=[
            jax.ShapeDtypeStruct((micro, length, width), jnp.bfloat16),
            jax.ShapeDtypeStruct((micro, length, LANES), jnp.float32),
        ],
        compiler_params=pltpu.CompilerParams(vmem_limit_bytes=48 << 20),
        cost_estimate=pl.CostEstimate(
            flops=micro * heads * length * length * WINDOW * 3,
            bytes_accessed=micro * length * width * 8,
            transcendentals=micro * heads * length * length // 2,
        ),
    )(limit[:, :, None], branch[:, :, None], qkv, qkv, qkv)


def attend_back_kernel(
    limit_ref, branch_ref, lse_ref, q_ref, k_ref, v_ref, g_ref, a_ref, out_ref, dk_sum, dv_sum
):
    head = pl.program_id(1)
    width = q_ref.shape[2]
    window, mine = head_window(head, width)

    @pl.when(head == 0)
    def clear():
        dk_sum[...] = jnp.zeros_like(dk_sum)
        dv_sum[...] = jnp.zeros_like(dv_sum)

    lane = lax.broadcasted_iota(jnp.int32, (1, WINDOW), 1)
    after = (head + 1) * HEAD - window.start
    spots = [lane == lax.rem(after + i, WINDOW) for i in range(3)]
    stat_lane = lax.broadcasted_iota(jnp.int32, (1, LANES), 1)
    keys_all = jnp.where(spots[0] | spots[1] | spots[2], 1, k_ref[0, :, window])
    values_all = jnp.where(spots[0] | spots[1], 1, v_ref[0, :, window])

    def less(rows, column, count):
        rest = column
        for spot in spots[:count]:
            piece = rest.astype(jnp.bfloat16).astype(jnp.float32)
            rows = jnp.where(spot, -piece, rows)
            rest = rest - piece
        return rows.astype(jnp.bfloat16)

    for first, count, parts in query_blocks(q_ref.shape[1]):
        rows = pl.ds(first, count)
        raw_query = q_ref[0, rows, window]
        query = jnp.where(mine, raw_query, 0)
        grad = jnp.where(mine, g_ref[0, rows, window], 0)
        wide_grad = grad.astype(jnp.float32)
        lse = jnp.sum(jnp.where(stat_lane == head, lse_ref[0, rows, :], 0.0), axis=1, keepdims=True)
        row_total = jnp.sum(
            wide_grad * a_ref[0, rows, window].astype(jnp.float32), axis=1, keepdims=True
        )
        query_less = less(scaled_query(raw_query, mine).astype(jnp.float32), lse, 3)
        grad_less = less(wide_grad, row_total, 2)
        grad_query = 0.0
        for key_first, keys, kind in parts:
            where = pl.ds(key_first, keys)
            part = slice(key_first, key_first + keys)
            prob = jnp.exp2(
                lax.dot_general(keys_all[part], query_less, NT, preferred_element_type=jnp.float32)
            )
            if kind != "all":
                ok = allowed_pairs(
                    kind,
                    key_first,
                    lax.broadcasted_iota(jnp.int32, (keys, count), 0),
                    lax.broadcasted_iota(jnp.int32, (keys, count), 1),
                    limit_ref[0],
                    branch_ref[0],
                )
                prob = jnp.where(ok, prob, 0.0)
            grad_prob = lax.dot_general(
                values_all[part], grad_less, NT, preferred_element_type=jnp.float32
            )
            grad_raw = (prob * grad_prob).astype(jnp.bfloat16)
            dv_sum[where, window] += jnp.dot(
                prob.astype(jnp.bfloat16), grad, preferred_element_type=jnp.float32
            )
            dk_sum[where, window] += jnp.dot(grad_raw, query, preferred_element_type=jnp.float32)
            grad_query = grad_query + lax.dot_general(
                grad_raw, keys_all[part], TN, preferred_element_type=jnp.float32
            )
        out_ref[0, rows, window] = jnp.where(
            mine, (grad_query * SCALE).astype(jnp.bfloat16), out_ref[0, rows, window]
        )

    @pl.when(head == pl.num_programs(1) - 1)
    def write():
        out_ref[0, :, pl.ds(width, width)] = (dk_sum[...] * SCALE).astype(jnp.bfloat16)
        out_ref[0, :, pl.ds(2 * width, width)] = dv_sum[...].astype(jnp.bfloat16)


def attend_back(qkv, grad, attended, lse, limit, branch):
    micro, length, columns = qkv.shape
    width = columns // 3
    heads = width // HEAD
    tail = length - TRUNK_SEGS * SEG

    def part(index):
        return pl.BlockSpec((1, length, width), lambda m, h, index=index: (m, 0, index))

    row = pl.BlockSpec((1, 1, tail), lambda m, h: (m, 0, 0))
    return pl.pallas_call(
        attend_back_kernel,
        grid=(micro, heads),
        in_specs=[
            row,
            row,
            pl.BlockSpec((1, length, LANES), lambda m, h: (m, 0, 0)),
            part(0),
            part(1),
            part(2),
            part(0),
            part(0),
        ],
        out_specs=pl.BlockSpec((1, length, columns), lambda m, h: (m, 0, 0)),
        out_shape=jax.ShapeDtypeStruct((micro, length, columns), jnp.bfloat16),
        scratch_shapes=[pltpu.VMEM((length, width), jnp.float32)] * 2,
        compiler_params=pltpu.CompilerParams(vmem_limit_bytes=56 << 20),
        cost_estimate=pl.CostEstimate(
            flops=micro * heads * length * length * WINDOW * 7,
            bytes_accessed=micro * length * width * 14,
            transcendentals=micro * heads * length * length // 2,
        ),
    )(limit[:, None, :], branch[:, None, :], lse, qkv, qkv, qkv, grad, attended)


def norm_back(grad_normed, normed_unit, scale_rows, gain_row):
    scaled_grad = grad_normed * gain_row
    return scale_rows * (
        scaled_grad - normed_unit * jnp.mean(scaled_grad * normed_unit, axis=-1, keepdims=True)
    )


def adam_update(master, first, second, grad, rate, decay):
    first_new = BETA_ONE * first + (1.0 - BETA_ONE) * grad
    second_new = BETA_TWO * second + (1.0 - BETA_TWO) * grad * grad
    fix_one = 1.0 - BETA_ONE**STEP
    fix_two = 1.0 - BETA_TWO**STEP
    step_size = first_new / fix_one / (jnp.sqrt(second_new / fix_two) + ADAM_EPS)
    return (master - rate * (step_size + decay * master), first_new, second_new)


def product(left, right, spec):
    return jnp.einsum(spec, left, right, preferred_element_type=jnp.float32)


Y_CHIPS = 2
CAPACITY = 8
SPARE = 8
GROUP = 16
CHUNK = 256
MESH_IDS = pl.DeviceIdType.MESH


def place():
    chip = lax.axis_index("chip")
    return (
        chip // Y_CHIPS,
        lax.rem(chip, Y_CHIPS),
        lax.axis_index("core"),
        lax.axis_index("seq"),
        lax.axis_size("chip") // Y_CHIPS,
    )


def at_z(z, y):
    return {"chip": z * Y_CHIPS + y}


def ahead(d):
    z, y, core, x, depth = place()
    return at_z(lax.rem(z + d, depth), y)


def across(axis):
    z, y, core, x, _ = place()
    return {"y": at_z(z, 1 - y), "x": {"seq": 1 - x}, "core": {"core": 1 - core}}[axis]


def greet():
    depth = place()[4]
    barrier = pltpu.get_barrier_semaphore()
    peers = [ahead(d) for d in range(1, depth)] + [across("y"), across("x"), across("core")]
    for peer in peers:
        pl.semaphore_signal(barrier, inc=1, device_id=peer, device_id_type=MESH_IDS)
    pl.semaphore_wait(barrier, len(peers))


def sem_pair(*shape):
    return [pltpu.SemaphoreType.DMA(shape), pltpu.SemaphoreType.DMA(shape)]


def remote(source, target, sems, index, device):
    return pltpu.make_async_remote_copy(
        src_ref=source,
        dst_ref=target,
        send_sem=sems[0].at[index],
        recv_sem=sems[1].at[index],
        device_id=device,
        device_id_type=MESH_IDS,
    )


def total(*parts):
    return functools.reduce(jnp.add, [p.astype(jnp.float32) for p in parts]).astype(jnp.bfloat16)


class Flow:
    def __init__(self):
        self.sent = []

    def push(self, source, target, sems, index, device):
        copy = remote(source, target, sems, index, device)
        copy.start()
        self.sent.append(copy)

    def arrive(self, here, sems, index):
        remote(here, here, sems, index, across("core")).wait_recv()

    def drain(self):
        for copy in self.sent:
            copy.wait_send()


class Total(Flow):
    def __init__(self, axes, sums, inbox, sems):
        super().__init__()
        self.axes, self.sums, self.inbox, self.sems = (axes, sums, inbox, sems)
        self.done = 0

    def begin(self, value):
        self.sums[0] = value
        self.push(self.sums.at[0], self.inbox.at[0], self.sems, (0,), across(self.axes[0]))

    def step(self):
        i = self.done
        self.done += 1
        self.arrive(self.inbox.at[i], self.sems, (i,))
        self.sums[i + 1] = self.sums[i] + self.inbox[i]
        here = self.sums.at[i + 1]
        if i + 1 < len(self.axes):
            self.push(here, self.inbox.at[i + 1], self.sems, (i + 1,), across(self.axes[i + 1]))
            return
        for d in range(1, place()[4]):
            self.push(here, self.inbox.at[i + d], self.sems, (i + d,), ahead(d))

    def result(self):
        last = len(self.axes)
        value = self.sums[last]
        for d in range(1, place()[4]):
            self.arrive(self.inbox.at[last - 1 + d], self.sems, (last - 1 + d,))
            value = value + self.inbox[last - 1 + d]
        self.drain()
        return value


def distances(depth):
    return sorted(range(1, depth), key=lambda d: min(d, depth - d))


def total_scratch(axes, depth, width):
    return [
        pltpu.VMEM((axes + 1, 8, width), jnp.float32),
        pltpu.VMEM((axes + depth - 1, 8, width), jnp.float32),
    ] + sem_pair(axes + depth - 1)


def spread_sems(depth):
    return sem_pair(depth) + sem_pair(depth) + sem_pair(depth, 2) + sem_pair(depth, 4)


class Spread(Flow):
    def __init__(self, window, second, sems):
        super().__init__()
        self.window = window
        self.second = second
        self.third = "x" if second == "y" else "y"
        self.sems = [(sems[2 * i], sems[2 * i + 1]) for i in range(4)]

    def where(self, d, second=False, third=False, other_core=False):
        z, y, core, x, depth = place()
        if second if self.second == "y" else third:
            y = 1 - y
        if third if self.second == "y" else second:
            x = 1 - x
        return self.window(lax.rem(z - d + depth, depth), y, 1 - core if other_core else core, x)

    def forward(self, stage, index, block, device):
        self.push(block, block, self.sems[stage], index, device)

    def begin(self):
        self.waiting = distances(place()[4])
        self.along_z()
        self.onward(0)

    def along_z(self):
        if self.waiting:
            d = self.waiting.pop(0)
            self.forward(0, (d,), self.where(0), ahead(d))

    def onward(self, d):
        block = self.where(d)
        self.forward(1, (d,), block, across(self.second))
        self.forward(2, (d, 0), block, across(self.third))
        self.forward(3, (d, 0), block, across("core"))

    def from_z(self, d):
        self.arrive(self.where(d), self.sems[0], (d,))
        self.along_z()
        self.onward(d)

    def from_second(self, d):
        block = self.where(d, True)
        self.arrive(block, self.sems[1], (d,))
        self.forward(2, (d, 1), block, across(self.third))
        self.forward(3, (d, 2), block, across("core"))

    def from_third(self, d):
        for second in range(2):
            block = self.where(d, bool(second), True)
            self.arrive(block, self.sems[2], (d, second))
            self.forward(3, (d, 2 * second + 1), block, across("core"))

    def finish(self):
        for d in range(place()[4]):
            for second in range(2):
                for third in range(2):
                    block = self.where(d, bool(second), bool(third), True)
                    self.arrive(block, self.sems[3], (d, 2 * second + third))
        self.drain()


def device_block(z, y, core, x):
    return ((z * Y_CHIPS + y) * 2 + core) * 2 + x


def chip_block(z, y, x):
    return (z * Y_CHIPS + y) * 2 + x


def gather_kernel(
    split,
    cut,
    block_ref,
    row_ref,
    spare_rank_ref,
    spare_mine_ref,
    low_ref,
    gain_ref,
    *refs,
):
    outs = refs[: 4 if split else 1]
    gain_out, whole, stage, stage_sem, spare, core_in, y_in, z_in, held = refs[len(outs) : len(outs) + 9]
    gain_sum, gain_in = refs[len(outs) + 9 : len(outs) + 11]
    sems = refs[len(outs) + 11 :]
    z, y, core, x, depth = place()
    piece, width = low_ref.shape[1:]
    half = CAPACITY // 2
    base = half * piece // GROUP
    me = device_block(z, y, core, x)
    per_piece = piece // GROUP
    for i in range(base):
        source = pl.ds(i % per_piece * GROUP, GROUP)
        whole[me, i] = low_ref[x * half + i // per_piece, source]
    greet()

    def window(first, count):
        return lambda *who: whole.at[device_block(*who), pl.ds(first, count)]

    flow_sems = 8
    early = Spread(window(0, cut), "y", sems[2 : 2 + flow_sems])
    late = Spread(window(cut, base - cut), "x", sems[10 : 10 + flow_sems])
    loose = Spread(window(base, 1), "x", sems[18 : 18 + flow_sems])
    gains = Total(["core", "y"], gain_sum, gain_in, sems[0:2])
    spare_sems = sems[26:32]
    spare_flow = Flow()
    early.begin()
    late.begin()
    gains.begin(gain_ref[...])
    count = SPARE // 2
    for i in range(count):
        found = low_ref[spare_rank_ref[x * count + i]]
        spare[pl.ds(i * piece, piece)] = jnp.where(spare_mine_ref[x * count + i] > 0, found, 0)
    rows = core_in.shape[0]

    def part(index, size):
        return pl.ds(pl.multiple_of(index * size, GROUP), size)

    spare_flow.push(spare.at[part(1 - core, rows)], core_in, spare_sems[0:2], (0,), across("core"))
    flows = [early, late]

    def from_z(d):
        for flow in flows:
            flow.from_z(d)

    def from_second(d):
        for flow in flows:
            flow.from_second(d)

    order = distances(depth)
    from_z(order[0])
    spare_flow.arrive(core_in, spare_sems[0:2], (0,))
    held[...] = total(spare[part(core, rows)], core_in[...])
    spare_flow.push(held.at[part(1 - y, rows // 2)], y_in, spare_sems[2:4], (0,), across("y"))
    gains.step()
    from_second(0)
    for i in range(1, depth - 1):
        from_z(order[i])
        if i == 1:
            spare_flow.arrive(y_in, spare_sems[2:4], (0,))
            y_in[...] = total(held[part(y, rows // 2)], y_in[...])
            for e in range(1, depth):
                to = part(lax.rem(z + e, depth), GROUP)
                spare_flow.push(y_in.at[to], z_in.at[e], spare_sems[4:6], (e,), ahead(e))
            gains.step()
        from_second(order[i - 1])
        for flow in flows:
            flow.from_third(([0] + order)[i - 1])
    for d in range(1, depth):
        spare_flow.arrive(z_in.at[d], spare_sems[4:6], (d,))
    whole[me, base] = total(y_in[part(z, GROUP)], *[z_in[d] for d in range(1, depth)])
    loose.begin()
    from_second(order[-1])
    gain_out[...] = gains.result()
    for d in order:
        loose.from_z(d)
    for flow in flows:
        flow.from_third(order[-2])
    for d in range(depth):
        loose.from_second(d)
    for flow in flows:
        flow.from_third(order[-1])
    for d in range(depth):
        loose.from_third(d)
    for flow in flows + [loose]:
        flow.finish()
    spare_flow.drain()

    buffers = stage.shape[0]
    per_chunk = CHUNK // GROUP
    narrow = width // 2
    copies = []
    for index in range(6 * width // CHUNK):
        matrix, first = divmod(index * CHUNK, width)
        slot = index % buffers
        if index >= buffers:
            copies[index - buffers].wait()
        thin = split and matrix < 3
        columns = pl.ds(pl.multiple_of(core * narrow, LANES), narrow) if thin else slice(None)
        count = narrow if thin else width

        def step(i, carry, index=index, slot=slot, columns=columns, count=count):
            for g in range(per_piece):
                at = index * per_chunk + i * per_piece + g
                target = pl.ds(pl.multiple_of(i * piece + g * GROUP, GROUP), GROUP)
                stage[slot, target, pl.ds(0, count)] = whole[block_ref[at], row_ref[at], :, columns]
            return carry

        lax.fori_loop(0, per_chunk // per_piece, step, 0)
        if thin:
            target = outs[0].at[pl.ds(first, CHUNK), pl.ds(matrix * narrow, narrow)]
        elif split:
            target = outs[matrix - 2].at[pl.ds(first, CHUNK)]
        else:
            target = outs[0].at[matrix, pl.ds(first, CHUNK)]
        copies.append(
            pltpu.make_async_copy(stage.at[slot, :, pl.ds(0, count)], target, stage_sem.at[slot])
        )
        copies[-1].start()
    for copy in copies[-buffers:]:
        copy.wait()


def gather_pieces(low, gains, plan, split):
    slots, piece, width = low.shape
    block, row, spare_rank, spare_mine, gain_mine = plan
    chips = lax.axis_size("chip")
    depth = chips // Y_CHIPS
    base = CAPACITY // 2 * piece // GROUP
    shapes = [(width, 3 * (width // 2))] + [(width, width)] * 3 if split else [(6, width, width)]
    lane = SPARE * piece // 4
    buffers = 4
    picked = jnp.where(gain_mine[:, None], gains[: gain_mine.shape[0]].astype(jnp.float32), 0.0)
    padded = jnp.concatenate([picked, jnp.zeros((6, width), jnp.float32)], axis=0)
    vmem = pl.BlockSpec(memory_space=pltpu.VMEM)
    smem = pl.BlockSpec(memory_space=pltpu.SMEM)
    outs = pl.pallas_call(
        functools.partial(gather_kernel, split, base // 4 if split else base // 2),
        in_specs=[smem] * 3 + [vmem] * 3,
        out_specs=[pl.BlockSpec(memory_space=pl.ANY)] * len(shapes) + [vmem],
        out_shape=[jax.ShapeDtypeStruct(s, jnp.bfloat16) for s in shapes]
        + [jax.ShapeDtypeStruct((8, width), jnp.float32)],
        scratch_shapes=[
            pltpu.VMEM((4 * chips, base + 1, GROUP, width), jnp.bfloat16),
            pltpu.VMEM((buffers, CHUNK, width), jnp.bfloat16),
            pltpu.SemaphoreType.DMA((buffers,)),
            pltpu.VMEM((2 * lane, width), jnp.bfloat16),
            pltpu.VMEM((lane, width), jnp.bfloat16),
            pltpu.VMEM((lane // 2, width), jnp.bfloat16),
            pltpu.VMEM((depth, GROUP, width), jnp.bfloat16),
            pltpu.VMEM((lane, width), jnp.bfloat16),
        ]
        + total_scratch(2, depth, width)
        + spread_sems(depth) * 3
        + sem_pair(1)
        + sem_pair(1)
        + sem_pair(depth),
        compiler_params=pltpu.CompilerParams(
            collective_id=0 if split else 1, has_side_effects=True, vmem_limit_bytes=48 << 20
        ),
        cost_estimate=pl.CostEstimate(
            flops=0, bytes_accessed=6 * width * width * 16, transcendentals=0
        ),
    )(
        block.reshape(-1),
        row.reshape(-1),
        spare_rank,
        jnp.broadcast_to(spare_mine[:, None, None], (SPARE, 1, width)),
        low,
        padded,
    )
    return (*outs[:-1], outs[-1][:2].astype(jnp.bfloat16))


def halves(matrices, split):
    if not split:
        return (matrices,)
    width = matrices.shape[1]
    narrow = width // 2
    thin = lax.dynamic_slice_in_dim(matrices[:3], lax.axis_index("core") * narrow, narrow, axis=2)
    side = jnp.concatenate([thin[0], thin[1], thin[2]], axis=1)
    return (side, matrices[3], matrices[4], matrices[5])


def gather_slots(low, gains, owners, split):
    slots, piece, width = low.shape
    piece_owner, rank = owner_slots(owners, slots)
    rows = slots * piece
    half = -(-(rows // 2 + 1) // GROUP) * GROUP
    filler = jnp.zeros((2 * half - rows - 2, width), jnp.bfloat16)
    packed = jnp.concatenate([low.reshape(rows, width), gains, filler], axis=0)
    share = lax.dynamic_slice_in_dim(packed, lax.axis_index("seq") * half, half, axis=0)
    groups = lax.all_gather(share, ALL, axis=0, tiled=True).reshape(-1, GROUP, width)
    per_owner = 2 * half // GROUP
    base = piece_owner * per_owner + rank * (piece // GROUP)
    index = base[:, None] + jnp.arange(piece // GROUP, dtype=jnp.int32)[None, :]
    matrices = groups[index.reshape(-1)].reshape(6, width, width)
    gain_rows = groups[owners[-2:] * per_owner + rows // GROUP][jnp.arange(2), jnp.arange(2)]
    return (*halves(matrices, split), gain_rows)


def kernels_fit(slots, piece, width):
    chips = lax.axis_size("chip")
    return slots == 2 * CAPACITY and piece == GROUP * (chips // Y_CHIPS) and width % CHUNK == 0


def spare_pieces(owners, slots):
    piece_owner, rank = owner_slots(owners, slots)
    spare = rank >= CAPACITY
    return (piece_owner, rank, spare, jnp.cumsum(spare.astype(jnp.int32)) - 1)


def gather_store(low, gains, owners, split, few):
    if not few:
        return gather_slots(low, gains, owners, split)
    slots, piece, width = low.shape
    dp_pos = lax.axis_index("chip") * 2 + lax.axis_index("core")
    piece_owner, rank, spare, order = spare_pieces(owners, slots)
    half = CAPACITY // 2
    groups = piece // GROUP
    group = jnp.arange(groups, dtype=jnp.int32)[None, :]
    block = jnp.where(
        spare[:, None],
        device_block(group, (order % 2)[:, None], ((order // 2) % 2)[:, None], (order // 4)[:, None]),
        (piece_owner * 2 + rank // half)[:, None],
    )
    row = jnp.where(spare[:, None], half * groups, (rank % half)[:, None] * groups + group)
    labels = jnp.arange(SPARE, dtype=jnp.int32)
    own = (spare & (piece_owner == dp_pos))[None, :] & (order[None, :] == labels[:, None])
    spare_rank = jnp.sum(jnp.where(own, rank[None, :], 0), axis=1)
    spare_mine = jnp.any(own, axis=1).astype(jnp.int32)
    plan = (block, row, spare_rank, spare_mine, owners[-2:] == dp_pos)
    return gather_pieces(low, gains, plan, split)


class Reduce(Flow):
    def __init__(self, first, shard, one, two, three, sems):
        super().__init__()
        self.first = first
        self.other = "y" if first == "x" else "x"
        self.shard = shard
        self.one, self.two, self.three = (one, two, three)
        self.sems = [sems[0:2], sems[2:4], sems[4:6]]

    def start(self, d, b):
        self.push(self.shard(d, b, 1), self.one.at[d, b], self.sems[0], (d, b), across(self.first))

    def from_first(self, d, b):
        here = self.one.at[d, b]
        self.arrive(here, self.sems[0], (d, b))
        here[...] = total(here[...], self.shard(d, b, 0)[...])
        if b:
            self.push(here, self.two.at[d], self.sems[1], (d,), across(self.other))

    def from_second(self, d):
        here = self.two.at[d]
        self.arrive(here, self.sems[1], (d,))
        here[...] = total(here[...], self.one[d, 0])
        if d:
            self.push(here, self.three.at[d], self.sems[2], (d,), ahead(d))

    def result(self):
        depth = place()[4]
        for d in range(1, depth):
            self.arrive(self.three.at[d], self.sems[2], (d,))
        value = total(self.two[0], *[self.three[d] for d in range(1, depth)])
        self.drain()
        return value


def reduce_kernel(
    source_ref,
    spare_ref,
    spare_mine_ref,
    early_ref,
    late_ref,
    gain_ref,
    slot_ref,
    gain_out,
    pieces,
    blocks,
    early_one,
    early_two,
    early_three,
    late_one,
    late_two,
    late_three,
    final,
    pair_in,
    full,
    full_in,
    spares,
    gain_sum,
    gain_in,
    load_sem,
    *sems,
):
    z, y, core, x, depth = place()
    narrow = pieces.shape[2]
    groups = late_ref.shape[1]
    per_block = blocks.shape[1]
    cut = early_one.shape[2]
    owned = CAPACITY // 2 * slot_ref.shape[1]
    order = distances(depth)[::-1] + [0]
    loads = []
    for matrix in range(3):
        columns = pl.ds(matrix * narrow, narrow)
        loads.append((early_ref.at[:, :, columns], matrix))
        loads.append((late_ref.at[matrix], matrix + 3))
    loads = [
        pltpu.make_async_copy(source, pieces.at[pl.ds(m * groups, groups)], load_sem.at[m])
        for source, m in loads
    ]
    for load in loads:
        load.start()
    pieces[6 * groups] = jnp.zeros((GROUP, narrow), jnp.bfloat16)
    greet()
    gains = Total(["core", "x", "y"], gain_sum, gain_in, sems[0:2])
    gains.begin(gain_ref[...])
    for load in loads:
        load.wait()

    def block_at(d, swap_y, swap_x):
        return chip_block(
            lax.rem(z + d, depth), 1 - y if swap_y else y, 1 - x if swap_x else x
        )

    early = Reduce(
        "x",
        lambda d, b, a: blocks.at[block_at(d, b, a), pl.ds(0, cut)],
        early_one,
        early_two,
        early_three,
        sems[2:8],
    )
    late = Reduce(
        "y",
        lambda d, b, a: blocks.at[block_at(d, a, b), pl.ds(cut, per_block - cut)],
        late_one,
        late_two,
        late_three,
        sems[8:14],
    )

    def fill(d, swap_y, swap_x):
        block = block_at(d, swap_y, swap_x)

        def step(i, carry):
            for g in range(2):
                blocks[block, 2 * i + g] = pieces[source_ref[block * per_block + 2 * i + g]]
            return carry

        lax.fori_loop(0, per_block // 2, step, 0)

    def start(d, b):
        for flow in (early, late):
            flow.start(d, b)

    fill(order[0], 1, 1)
    start(order[0], 1)
    fill(order[0], 0, 1)
    fill(order[0], 1, 0)
    start(order[0], 0)
    fill(order[0], 0, 0)
    for i, d in enumerate(order):
        later = order[i + 1] if i + 1 < len(order) else None
        if later is not None:
            fill(later, 1, 1)
        for flow in (early, late):
            flow.from_first(d, 1)
        if later is not None:
            start(later, 1)
            fill(later, 0, 1)
            fill(later, 1, 0)
        for flow in (early, late):
            flow.from_first(d, 0)
        if later is not None:
            start(later, 0)
            fill(later, 0, 0)
        if i:
            for flow in (early, late):
                flow.from_second(order[i - 1])
        if i < 3:
            gains.step()
    for flow in (early, late):
        flow.from_second(order[-1])
    final[pl.ds(0, cut)] = early.result()
    final[pl.ds(cut, per_block - cut)] = late.result()

    ends = Flow()
    own_spare = spares.at[z, y, x, core]
    ends.push(final.at[pl.ds((1 - core) * owned, owned)], pair_in, sems[14:16], (0,), across("core"))
    spares[z, y, x, core] = final[pl.ds(2 * owned, 2)]
    for d in range(1, depth):
        ends.push(own_spare, own_spare, sems[16:18], (d,), ahead(d))
    gain_out[...] = gains.result()
    ends.arrive(pair_in, sems[14:16], (0,))
    for g in range(owned):
        mine = final[core * owned + g]
        theirs = pair_in[g]
        first = core == 0
        full[g, :, pl.ds(pl.multiple_of(core * narrow, LANES), narrow)] = mine
        full[g, :, pl.ds(pl.multiple_of((1 - core) * narrow, LANES), narrow)] = theirs
    ends.push(full, full_in, sems[14:16], (1,), across("x"))
    for d in range(1, depth):
        from_z = spares.at[lax.rem(z - d + depth, depth), y, x, core]
        ends.arrive(from_z, sems[16:18], (d,))
    here = spares.at[:, y, x, core]
    ends.push(here, here, sems[14:16], (2,), across("y"))
    ends.arrive(spares.at[:, 1 - y, x, core], sems[14:16], (2,))
    here = spares.at[:, :, x, core]
    ends.push(here, here, sems[14:16], (3,), across("x"))
    ends.arrive(spares.at[:, :, 1 - x, core], sems[14:16], (3,))
    here = spares.at[:, :, :, core]
    ends.push(here, here, sems[14:16], (4,), across("core"))
    ends.arrive(spares.at[:, :, :, 1 - core], sems[14:16], (4,))
    ends.arrive(full_in, sems[14:16], (1,))
    per_piece = slot_ref.shape[1]
    half = CAPACITY // 2
    for i in range(half):
        for g in range(per_piece):
            slot_ref[x * half + i, g] = full[i * per_piece + g]
            slot_ref[(1 - x) * half + i, g] = full_in[i * per_piece + g]

    def pick(slot, carry):
        for g in range(per_piece):
            at = spare_ref[slot] * per_piece + g
            sub = spares.shape[4]
            chip = lax.div(at, 2 * sub)
            where = (lax.div(chip, Y_CHIPS), lax.rem(chip, Y_CHIPS), lax.rem(lax.div(at, sub), 2))
            for side in range(2):
                found = spares[(*where, side, lax.rem(at, sub))]
                slot_ref[CAPACITY + slot, g, :, pl.ds(side * narrow, narrow)] = jnp.where(
                    spare_mine_ref[slot] > 0, found, 0
                )
        return carry

    lax.fori_loop(0, slot_ref.shape[0] - CAPACITY, pick, 0)
    ends.drain()


def reduce_slots(early, late, gains, owners, slots, piece):
    width = late.shape[1]
    narrow = width // 2
    chips = lax.axis_size("chip")
    depth = chips // Y_CHIPS
    groups = width // GROUP
    per_piece = piece // GROUP
    dp_pos = lax.axis_index("chip") * 2 + lax.axis_index("core")
    piece_owner, rank, spare, order = spare_pieces(owners, slots)
    half = CAPACITY // 2
    labels = jnp.arange(piece_owner.shape[0], dtype=jnp.int32)
    empty = 6 * groups

    def groups_of(match):
        first = jnp.sum(jnp.where(match, labels, 0), axis=-1)[..., None] * per_piece
        groups_at = first + jnp.arange(per_piece, dtype=jnp.int32)
        return jnp.where(jnp.any(match, axis=-1)[..., None], groups_at, empty)

    block = jnp.arange(2 * chips, dtype=jnp.int32)[:, None]
    entry = jnp.arange(CAPACITY, dtype=jnp.int32)[None, :]
    owner_at = block // 2 * 2 + entry // half
    rank_at = block % 2 * half + entry % half
    base_groups = groups_of(
        (piece_owner == owner_at[..., None]) & (rank == rank_at[..., None])
    ).reshape(2 * chips, -1)
    spare_hot = spare & (order == jnp.arange(SPARE, dtype=jnp.int32)[:, None])
    spare_groups = groups_of(spare_hot).reshape(2 * chips, -1)
    source = jnp.concatenate([base_groups, spare_groups], axis=1)
    per_block = source.shape[1]
    mine = (piece_owner == dp_pos) & spare & (order < SPARE)
    slot_hot = mine & (rank == CAPACITY + jnp.arange(slots - CAPACITY, dtype=jnp.int32)[:, None])
    spare_at = jnp.sum(jnp.where(slot_hot, order, 0), axis=1)
    subs = SPARE * per_piece // (2 * chips)

    vmem = pl.BlockSpec(memory_space=pltpu.VMEM)
    smem = pl.BlockSpec(memory_space=pltpu.SMEM)
    hbm = pl.BlockSpec(memory_space=pl.ANY)
    cut = per_block // 4 + 1
    owned = half * per_piece
    padded = jnp.concatenate([gains, jnp.zeros((8 - gains.shape[0], width), jnp.float32)], axis=0)

    def group_block(*shape):
        return pltpu.VMEM(shape + (GROUP, narrow), jnp.bfloat16)

    def flow_blocks(count):
        return [group_block(depth, 2, count), group_block(depth, count), group_block(depth, count)]

    flow_sems = sem_pair(depth, 2) + sem_pair(depth) + sem_pair(depth)
    slot_grad, gain_sum = pl.pallas_call(
        reduce_kernel,
        in_specs=[smem] * 2 + [vmem, hbm, hbm, vmem],
        out_specs=[vmem, vmem],
        out_shape=[
            jax.ShapeDtypeStruct((slots, per_piece, GROUP, width), jnp.bfloat16),
            jax.ShapeDtypeStruct((8, width), jnp.float32),
        ],
        scratch_shapes=[group_block(6 * groups + 1), group_block(2 * chips, per_block)]
        + flow_blocks(cut)
        + flow_blocks(per_block - cut)
        + [
            group_block(per_block),
            group_block(owned),
            pltpu.VMEM((owned, GROUP, width), jnp.bfloat16),
            pltpu.VMEM((owned, GROUP, width), jnp.bfloat16),
            group_block(depth, Y_CHIPS, 2, 2, subs),
        ]
        + total_scratch(3, depth, width)[:2]
        + [pltpu.SemaphoreType.DMA((6,))]
        + total_scratch(3, depth, width)[2:]
        + flow_sems
        + flow_sems
        + sem_pair(5)
        + sem_pair(depth),
        compiler_params=pltpu.CompilerParams(
            collective_id=2, has_side_effects=True, vmem_limit_bytes=56 << 20
        ),
        cost_estimate=pl.CostEstimate(
            flops=0, bytes_accessed=6 * width * width * 8, transcendentals=0
        ),
    )(
        source.reshape(-1),
        spare_at,
        jnp.broadcast_to(jnp.any(slot_hot, axis=1).astype(jnp.int32)[:, None, None], (slots - CAPACITY, 1, narrow)),
        early.reshape(groups, GROUP, 3 * narrow),
        late.reshape(3, groups, GROUP, narrow),
        padded,
    )
    return (slot_grad.reshape(slots, piece, width), gain_sum[:2])


def reduce_all(early, late, gains, owners, slots, piece, few):
    if few:
        return reduce_slots(early, late, gains, owners, slots, piece)
    width = late.shape[1]
    narrow = width // 2
    dp_pos = lax.axis_index("chip") * 2 + lax.axis_index("core")
    pieces = owners.shape[0] - 2
    chips = lax.axis_size("chip")
    local = jnp.concatenate([jnp.transpose(early.reshape(width, 3, narrow), (1, 0, 2)), late], axis=0)
    share = lax.psum_scatter(
        local.reshape(6 * width, narrow), ("chip", "seq"), scatter_dimension=0, tiled=True
    )
    sums = lax.all_gather(share, ALL, axis=0, tiled=False).reshape(chips, 2, 2, -1, narrow)
    sums = jnp.transpose(sums, (0, 2, 3, 1, 4)).reshape(pieces, piece, width)
    piece_owner, rank = owner_slots(owners, slots)
    labels = jnp.arange(slots, dtype=jnp.int32)
    match = (piece_owner == dp_pos) & (rank == labels[:, None])
    slot_grad = jnp.where(jnp.any(match, axis=1)[:, None, None], sums[jnp.argmax(match, axis=1)], 0)
    return (slot_grad, lax.psum(gains, ALL))


def adam_kernel(rate_ref, master_ref, first_ref, second_ref, grad_ref, *outs):
    count = master_ref.shape[0]
    for i in range(count):
        new, first_new, second_new = adam_update(
            master_ref[i],
            first_ref[i],
            second_ref[i],
            grad_ref[i].astype(jnp.float32),
            rate_ref[pl.program_id(0) * count + i],
            MATRIX_DECAY,
        )
        outs[0][i] = new
        outs[1][i] = first_new
        outs[2][i] = second_new
        outs[3][i] = new.astype(jnp.bfloat16)


def adam_slots(master, first, second, grad, rate):
    slots, piece, width = master.shape
    count = min(slots, 2)
    block = pl.BlockSpec((count, piece, width), lambda i: (i, 0, 0))
    shape = jax.ShapeDtypeStruct(master.shape, jnp.float32)
    return pl.pallas_call(
        adam_kernel,
        grid=(slots // count,),
        in_specs=[pl.BlockSpec(memory_space=pltpu.SMEM)] + [block] * 4,
        out_specs=[block] * 4,
        out_shape=[shape] * 3 + [jax.ShapeDtypeStruct(master.shape, jnp.bfloat16)],
        compiler_params=pltpu.CompilerParams(vmem_limit_bytes=60 << 20),
        cost_estimate=pl.CostEstimate(
            flops=20 * slots * piece * width,
            bytes_accessed=28 * slots * piece * width,
            transcendentals=slots * piece * width,
        ),
    )(rate, master, first, second, grad)


def local(*arrays):
    owners, weight_store = arrays[3:5]
    if not kernels_fit(*weight_store.shape):
        return step(False, *arrays)
    order = spare_pieces(owners, weight_store.shape[0])[3]
    few = order[-1] < SPARE
    return lax.cond(few, functools.partial(step, True), functools.partial(step, False), *arrays)


def step(
    few,
    tokens,
    cotangent,
    parents,
    owners,
    weight_store,
    gain_store,
    weight_first,
    gain_first,
    weight_second,
    gain_second,
):
    core = lax.axis_index("core")
    dp_pos = lax.axis_index("chip") * 2 + core
    slot_dev, piece, width = weight_store.shape
    pieces = owners.shape[0] - 2
    piece_owner, rank = owner_slots(owners, slot_dev)
    gain_owner = owners[pieces:]
    micro, _, rows, _ = tokens.shape
    half = width // 2
    own_rows = core * rows
    own_columns = core * half

    def mine(value, axis, size, index):
        return lax.dynamic_slice_in_dim(value, index * size, size, axis=axis)

    limit, branch = tail_limits(transposed(parents[:, 0]))
    arrived = moved(tokens[:, 0])
    qkv_weight, out_weight, up_weight, down_weight, gain_low = gather_store(
        weight_store.astype(jnp.bfloat16), gain_store.astype(jnp.bfloat16), owners, True, few
    )
    gain_low, arrived, cot = lax.optimization_barrier((gain_low, arrived, cotangent[:, 0]))
    own_tokens = settled(tokens[:, 0], arrived)
    own_cot = transposed(cot)
    other_tokens = partner(own_tokens)

    def by_core(own, other, axis):
        return jnp.where(
            core == 0,
            jnp.concatenate([own, other], axis=axis),
            jnp.concatenate([other, own], axis=axis),
        )

    all_tokens = by_core(own_tokens, other_tokens, 1)
    gain_one = gain_low[0].astype(jnp.float32)
    gain_two = gain_low[1].astype(jnp.float32)

    def unit(values):
        scale = lax.rsqrt(jnp.mean(values * values, axis=-1, keepdims=True) + NORM_EPS)
        return (values * scale, scale)

    normed_one = (unit(all_tokens.astype(jnp.float32))[0] * gain_one).astype(jnp.bfloat16)
    normed_one = lax.optimization_barrier(normed_one)
    qkv = product(normed_one, qkv_weight, "mtd,de->mte").astype(jnp.bfloat16)
    attended_half, lse = attend(qkv, limit, branch)
    attended = by_core(
        mine(attended_half, 1, rows, core), partner(mine(attended_half, 1, rows, 1 - core)), 2
    )
    residual = own_tokens.astype(jnp.float32)
    hidden_one = residual + product(attended, out_weight, "mti,io->mto")
    unit_two, scale_two = unit(hidden_one)
    normed_two = (unit_two * gain_two).astype(jnp.bfloat16)
    up_rows = product(normed_two, up_weight, "mti,io->mto")
    sigmoid_up = jax.nn.sigmoid(up_rows)
    activated = (up_rows * sigmoid_up).astype(jnp.bfloat16)
    mixed_rows = (hidden_one + product(activated, down_weight, "mti,io->mto")).astype(jnp.bfloat16)
    mixed = transposed(mixed_rows)

    grad_down = product(activated, own_cot, "mti,mto->io")
    grad_hidden = product(own_cot, down_weight, "mto,io->mti")
    grad_up_rows = (grad_hidden * (sigmoid_up * (1.0 + up_rows * (1.0 - sigmoid_up)))).astype(
        jnp.bfloat16
    )
    grad_up = product(normed_two, grad_up_rows, "mti,mto->io")
    grad_normed_two = product(grad_up_rows, up_weight, "mto,io->mti")
    gain_two_grad = jnp.sum(grad_normed_two * unit_two, axis=(0, 1))
    grad_hidden_one = own_cot.astype(jnp.float32) + norm_back(
        grad_normed_two, unit_two, scale_two, gain_two
    )
    branch_grad = grad_hidden_one.astype(jnp.bfloat16)
    grad_out = product(attended, branch_grad, "mti,mto->io")
    late = jnp.stack([grad_out, grad_up, grad_down]).astype(jnp.bfloat16)
    late_back = partner(mine(late, 2, half, 1 - core))

    branch_grad, late = lax.optimization_barrier((branch_grad, late))
    grad_attended = product(branch_grad, out_weight, "mto,io->mti").astype(jnp.bfloat16)
    grad_half = by_core(
        mine(grad_attended, 2, half, core), partner(mine(grad_attended, 2, half, 1 - core)), 1
    )
    grad_qkv_rows = attend_back(qkv, grad_half, attended_half, lse, limit, branch)
    grad_qkv = product(normed_one, grad_qkv_rows, "mti,mto->io")
    early = grad_qkv.astype(jnp.bfloat16)

    grad_normed_part = product(grad_qkv_rows, qkv_weight, "mte,de->mtd").astype(jnp.bfloat16)
    grad_normed_one = mine(grad_normed_part, 1, rows, core).astype(jnp.float32) + partner(
        mine(grad_normed_part, 1, rows, 1 - core)
    ).astype(jnp.float32)
    unit_one, scale_one = unit(residual)
    gain_one_grad = jnp.sum(grad_normed_one * unit_one, axis=(0, 1))
    token_rows = (
        grad_hidden_one + norm_back(grad_normed_one, unit_one, scale_one, gain_one)
    ).astype(jnp.bfloat16)
    token_grad = transposed(token_rows)
    gain_grads = jnp.stack([gain_one_grad, gain_two_grad])
    late = (mine(late, 2, half, core).astype(jnp.float32) + late_back.astype(jnp.float32)).astype(
        jnp.bfloat16
    )

    labels = jnp.arange(slot_dev, dtype=jnp.int32)
    match = (piece_owner[None, :] == dp_pos) & (rank[None, :] == labels[:, None])
    held = jnp.any(match, axis=1)
    piece_of = jnp.sum(jnp.where(match, jnp.arange(pieces, dtype=jnp.int32)[None, :], 0), axis=1)
    slot_grad, gain_sum = reduce_all(early, late, gain_grads, owners, slot_dev, piece, few)
    is_out = held & (piece_of // (width // piece) == 3)
    slot_rate = jnp.where(is_out, RATE_OUT, RATE_QKV).astype(jnp.float32)
    weight_new, weight_first_new, weight_second_new, weight_low = adam_slots(
        weight_store, weight_first, weight_second, slot_grad, slot_rate
    )
    gain_slot_grad = jnp.where((gain_owner == dp_pos)[:, None], gain_sum, 0.0)
    gain_new, gain_first_new, gain_second_new = adam_update(
        gain_store, gain_first, gain_second, gain_slot_grad, RATE_GAIN, 0.0
    )
    weight_copies, gain_copies = gather_store(
        weight_low, gain_new.astype(jnp.bfloat16), owners, False, few
    )
    return (
        mixed[:, None],
        token_grad[:, None],
        weight_new,
        gain_new,
        weight_first_new,
        gain_first_new,
        weight_second_new,
        gain_second_new,
        weight_copies,
        gain_copies,
    )


def solution(mesh):
    dp_count, seq_count = mesh.devices.shape
    fine = Mesh(mesh.devices.reshape(dp_count // 2, 2, seq_count), ALL)
    dp = ("chip", "core")
    rows = P(None, dp, "seq", None)
    store = P(dp, None, None)
    gains = P(dp, None)
    in_specs = (rows, rows, P(None, dp, None), P(), store, gains, store, gains, store, gains)
    out_specs = (rows, rows, store, gains, store, gains, store, gains, P(), P())
    return jax.shard_map(local, mesh=fine, in_specs=in_specs, out_specs=out_specs, check_vma=False)
```

```python
import functools

import jax
import jax.numpy as jnp
from jax import lax
from jax.experimental import pallas as pl
from jax.experimental.pallas import tpu as pltpu
from jax.sharding import Mesh
from jax.sharding import PartitionSpec as P

HEAD = 80
SEG = 32
TRUNK_SEGS = 32
ALWAYS_SEGS = TRUNK_SEGS // 2
STEP = 7
LANES = 128
WINDOW = 256
QUERY_BLOCK = 256
KEY_BLOCK = 512

NORM_EPS = 1e-06
BETA_ONE = 0.5
BETA_TWO = 0.5
ADAM_EPS = 1e-08
MATRIX_DECAY = 0.1
RATE_QKV = 0.03
RATE_OUT = 0.4
RATE_GAIN = 0.4
MASKED = -1e30
SCALE = HEAD**-0.5
LOG2E = 1.4426950408889634
ALL = ("chip", "core", "seq")
NT = (((1,), (1,)), ((), ()))
TN = (((0,), (0,)), ((), ()))


def moved(value):
    chips = lax.axis_size("chip")
    pairs = [(k * 4 + c * 2 + 1 - c, k * 4 + 2 - 2 * c + c) for k in range(chips) for c in range(2)]
    return lax.ppermute(value, ALL, pairs)


def settled(value, arrived):
    return jnp.where(lax.axis_index("core") == lax.axis_index("seq"), value, arrived)


def transposed(value):
    return settled(value, moved(value))


def partner(value):
    return lax.ppermute(value, "core", [(0, 1), (1, 0)])


def owner_slots(owners, slot_dev):
    count = owners.shape[0] - 2
    piece_owner = owners[:count]
    labels = jnp.arange(count, dtype=jnp.int32)
    same = (piece_owner[:, None] == piece_owner[None, :]) & (labels[None, :] < labels[:, None])
    rank = jnp.sum(same.astype(jnp.int32), axis=1)
    return (piece_owner, rank)


def tail_limits(parents):
    up = parents[:, TRUNK_SEGS:]
    leaf = up >= TRUNK_SEGS
    above = jnp.where(leaf, up - TRUNK_SEGS, 0)
    labels = jnp.arange(up.shape[1], dtype=jnp.int32)
    hot = above[:, :, None] == labels[None, None, :]
    upper = jnp.sum(jnp.where(hot, up[:, None, :], 0), axis=2)
    attach = jnp.where(leaf, upper, up)
    limit = (attach + 1) * SEG
    branch = jnp.where(leaf, above, -1)
    return (jnp.repeat(limit, SEG, axis=1), jnp.repeat(branch, SEG, axis=1))


def query_blocks(length):
    trunk = TRUNK_SEGS * SEG
    blocks = []
    for first in range(0, trunk, QUERY_BLOCK):
        parts = [(0, first, "all")] if first else []
        blocks.append((first, QUERY_BLOCK, parts + [(first, QUERY_BLOCK, "causal")]))
    always = ALWAYS_SEGS * SEG
    tail = length - trunk
    blocks.append(
        (trunk, tail, [(0, always, "all"), (always, trunk - always, "trunk"), (trunk, tail, "tail")])
    )
    return blocks


def allowed_pairs(kind, key_first, key, query, limit, branch):
    if kind == "causal":
        return key <= query
    if kind == "trunk":
        return key + key_first < limit
    key_seg = key // SEG
    return ((key_seg == query // SEG) & (key <= query)) | (key_seg == branch)


def head_window(head, width):
    start = pl.multiple_of(
        jnp.minimum((head * HEAD) // LANES, width // LANES - WINDOW // LANES) * LANES, LANES
    )
    lane = lax.broadcasted_iota(jnp.int32, (1, WINDOW), 1) + start
    mine = (lane >= head * HEAD) & (lane < (head + 1) * HEAD)
    return (pl.ds(start, WINDOW), mine)


def scaled_query(rows, mine):
    return jnp.where(mine, rows.astype(jnp.float32) * (SCALE * LOG2E), 0.0).astype(jnp.bfloat16)


def attend_kernel(limit_ref, branch_ref, q_ref, k_ref, v_ref, out_ref, lse_ref):
    head = pl.program_id(1)
    window, mine = head_window(head, q_ref.shape[2])
    stat_lane = lax.broadcasted_iota(jnp.int32, (1, LANES), 1)
    values = jnp.where(mine, v_ref[0, :, window], 1)
    keys_side = k_ref[0, :, window].T

    def score(first, count, parts):
        query = scaled_query(q_ref[0, pl.ds(first, count), window], mine)
        scores = []
        for key_first, keys, kind in parts:
            raw = jnp.dot(
                query, keys_side[:, key_first : key_first + keys], preferred_element_type=jnp.float32
            )
            if kind != "all":
                ok = allowed_pairs(
                    kind,
                    key_first,
                    lax.broadcasted_iota(jnp.int32, (count, keys), 1),
                    lax.broadcasted_iota(jnp.int32, (count, keys), 0),
                    limit_ref[0],
                    branch_ref[0],
                )
                raw = jnp.where(ok, raw, MASKED)
            scores.append(raw)
        return scores

    def weigh(scores, first, count, parts):
        rows = pl.ds(first, count)
        top = functools.reduce(jnp.maximum, [jnp.max(s, axis=1, keepdims=True) for s in scores])
        gained = 0.0
        for raw, (key_first, keys, kind) in zip(scores, parts):
            gained = gained + jnp.dot(
                jnp.exp2(raw - top).astype(jnp.bfloat16),
                values[key_first : key_first + keys],
                preferred_element_type=jnp.float32,
            )
        weight_sum = jnp.max(jnp.where(mine, 0.0, gained), axis=1, keepdims=True)
        gained = (gained * (1.0 / weight_sum)).astype(jnp.bfloat16)
        out_ref[0, rows, window] = jnp.where(mine, gained, out_ref[0, rows, window])
        lse_ref[0, rows, :] = jnp.where(
            stat_lane == head, top + jnp.log2(weight_sum), lse_ref[0, rows, :]
        )

    blocks = query_blocks(q_ref.shape[1])
    scores = score(*blocks[0])
    for block, following in zip(blocks, blocks[1:] + [None]):
        later = score(*following) if following else None
        weigh(scores, *block)
        scores = later


def attend(qkv, limit, branch):
    micro, length, columns = qkv.shape
    width = columns // 3
    heads = width // HEAD
    tail = length - TRUNK_SEGS * SEG

    def part(index):
        return pl.BlockSpec((1, length, width), lambda m, h, index=index: (m, 0, index))

    column = pl.BlockSpec((1, tail, 1), lambda m, h: (m, 0, 0))
    return pl.pallas_call(
        attend_kernel,
        grid=(micro, heads),
        in_specs=[column, column, part(0), part(1), part(2)],
        out_specs=[
            pl.BlockSpec((1, length, width), lambda m, h: (m, 0, 0)),
            pl.BlockSpec((1, length, LANES), lambda m, h: (m, 0, 0)),
        ],
        out_shape=[
            jax.ShapeDtypeStruct((micro, length, width), jnp.bfloat16),
            jax.ShapeDtypeStruct((micro, length, LANES), jnp.float32),
        ],
        compiler_params=pltpu.CompilerParams(vmem_limit_bytes=48 << 20),
        cost_estimate=pl.CostEstimate(
            flops=micro * heads * length * length * WINDOW * 3,
            bytes_accessed=micro * length * width * 8,
            transcendentals=micro * heads * length * length // 2,
        ),
    )(limit[:, :, None], branch[:, :, None], qkv, qkv, qkv)


def attend_back_kernel(
    limit_ref, branch_ref, lse_ref, q_ref, k_ref, v_ref, g_ref, a_ref, out_ref, dk_sum, dv_sum
):
    head = pl.program_id(1)
    width = q_ref.shape[2]
    window, mine = head_window(head, width)

    @pl.when(head == 0)
    def clear():
        dk_sum[...] = jnp.zeros_like(dk_sum)
        dv_sum[...] = jnp.zeros_like(dv_sum)

    lane = lax.broadcasted_iota(jnp.int32, (1, WINDOW), 1)
    after = (head + 1) * HEAD - window.start
    spots = [lane == lax.rem(after + i, WINDOW) for i in range(3)]
    stat_lane = lax.broadcasted_iota(jnp.int32, (1, LANES), 1)
    keys_all = jnp.where(spots[0] | spots[1] | spots[2], 1, k_ref[0, :, window])
    values_all = jnp.where(spots[0] | spots[1], 1, v_ref[0, :, window])

    def less(rows, column, count):
        rest = column
        for spot in spots[:count]:
            piece = rest.astype(jnp.bfloat16).astype(jnp.float32)
            rows = jnp.where(spot, -piece, rows)
            rest = rest - piece
        return rows.astype(jnp.bfloat16)

    def factors(first, count):
        rows = pl.ds(first, count)
        raw_query = q_ref[0, rows, window]
        query = jnp.where(mine, raw_query, 0)
        grad = jnp.where(mine, g_ref[0, rows, window], 0)
        wide_grad = grad.astype(jnp.float32)
        lse = jnp.sum(jnp.where(stat_lane == head, lse_ref[0, rows, :], 0.0), axis=1, keepdims=True)
        row_total = jnp.sum(
            wide_grad * a_ref[0, rows, window].astype(jnp.float32), axis=1, keepdims=True
        )
        query_less = less(scaled_query(raw_query, mine).astype(jnp.float32), lse, 3)
        return (query, grad, query_less, less(wide_grad, row_total, 2))

    def scores(part, block):
        query, grad, query_less, grad_less = block
        return (
            lax.dot_general(keys_all[part], query_less, NT, preferred_element_type=jnp.float32),
            lax.dot_general(values_all[part], grad_less, NT, preferred_element_type=jnp.float32),
        )

    def spread(found, part, kind, block):
        query, grad, query_less, grad_less = block
        raw, grad_prob = found
        prob = jnp.exp2(raw)
        if kind != "all":
            ok = allowed_pairs(
                kind,
                part.start,
                lax.broadcasted_iota(jnp.int32, raw.shape, 0),
                lax.broadcasted_iota(jnp.int32, raw.shape, 1),
                limit_ref[0],
                branch_ref[0],
            )
            prob = jnp.where(ok, prob, 0.0)
        grad_raw = (prob * grad_prob).astype(jnp.bfloat16)
        dv_sum[part, window] += jnp.dot(
            prob.astype(jnp.bfloat16), grad, preferred_element_type=jnp.float32
        )
        dk_sum[part, window] += jnp.dot(grad_raw, query, preferred_element_type=jnp.float32)
        return lax.dot_general(grad_raw, keys_all[part], TN, preferred_element_type=jnp.float32)

    units = []
    for first, count, parts in query_blocks(q_ref.shape[1]):
        for key_first, keys, kind in parts:
            for cut in range(key_first, key_first + keys, KEY_BLOCK):
                part = slice(cut, min(cut + KEY_BLOCK, key_first + keys))
                units.append((first, count, part, kind))
    block = factors(*units[0][:2])
    found = scores(units[0][2], block)
    grad_query = 0.0
    for unit, following in zip(units, units[1:] + [None]):
        first, count, part, kind = unit
        same = following and following[0] == first
        if following:
            later_block = block if same else factors(*following[:2])
            later = scores(following[2], later_block)
        grad_query = grad_query + spread(found, part, kind, block)
        if not same:
            rows = pl.ds(first, count)
            out_ref[0, rows, window] = jnp.where(
                mine, (grad_query * SCALE).astype(jnp.bfloat16), out_ref[0, rows, window]
            )
            grad_query = 0.0
        if following:
            block, found = (later_block, later)

    @pl.when(head == pl.num_programs(1) - 1)
    def write():
        out_ref[0, :, pl.ds(width, width)] = (dk_sum[...] * SCALE).astype(jnp.bfloat16)
        out_ref[0, :, pl.ds(2 * width, width)] = dv_sum[...].astype(jnp.bfloat16)


def attend_back(qkv, grad, attended, lse, limit, branch):
    micro, length, columns = qkv.shape
    width = columns // 3
    heads = width // HEAD
    tail = length - TRUNK_SEGS * SEG

    def part(index):
        return pl.BlockSpec((1, length, width), lambda m, h, index=index: (m, 0, index))

    row = pl.BlockSpec((1, 1, tail), lambda m, h: (m, 0, 0))
    return pl.pallas_call(
        attend_back_kernel,
        grid=(micro, heads),
        in_specs=[
            row,
            row,
            pl.BlockSpec((1, length, LANES), lambda m, h: (m, 0, 0)),
            part(0),
            part(1),
            part(2),
            part(0),
            part(0),
        ],
        out_specs=pl.BlockSpec((1, length, columns), lambda m, h: (m, 0, 0)),
        out_shape=jax.ShapeDtypeStruct((micro, length, columns), jnp.bfloat16),
        scratch_shapes=[pltpu.VMEM((length, width), jnp.float32)] * 2,
        compiler_params=pltpu.CompilerParams(vmem_limit_bytes=56 << 20),
        cost_estimate=pl.CostEstimate(
            flops=micro * heads * length * length * WINDOW * 7,
            bytes_accessed=micro * length * width * 14,
            transcendentals=micro * heads * length * length // 2,
        ),
    )(limit[:, None, :], branch[:, None, :], lse, qkv, qkv, qkv, grad, attended)


def norm_back(grad_normed, normed_unit, scale_rows, gain_row):
    scaled_grad = grad_normed * gain_row
    return scale_rows * (
        scaled_grad - normed_unit * jnp.mean(scaled_grad * normed_unit, axis=-1, keepdims=True)
    )


def norm_kernel(core_ref, own_ref, other_ref, gain_ref, out_ref):
    def write(source):
        rows = source[0].astype(jnp.float32)
        scale = lax.rsqrt(jnp.mean(rows * rows, axis=-1, keepdims=True) + NORM_EPS)
        out_ref[0] = (rows * scale * gain_ref[...]).astype(jnp.bfloat16)

    @pl.when(pl.program_id(1) == 0)
    def own():
        write(own_ref)

    @pl.when(pl.program_id(1) == 1)
    def other():
        write(other_ref)


def norm_all(own, other, gain, core):
    micro, rows, width = own.shape
    cuts = 2
    block = (1, rows // cuts, width)

    def source(which):
        return lambda m, s, i, core_ref: (m, jnp.where(s == which, i, (cuts - 1) * (1 - which)), 0)

    def target(m, s, i, core_ref):
        return (m, jnp.where(s == 0, core_ref[0], 1 - core_ref[0]) * cuts + i, 0)

    return pl.pallas_call(
        norm_kernel,
        grid_spec=pltpu.PrefetchScalarGridSpec(
            num_scalar_prefetch=1,
            grid=(micro, 2, cuts),
            in_specs=[
                pl.BlockSpec(block, source(0)),
                pl.BlockSpec(block, source(1)),
                pl.BlockSpec((1, width), lambda m, s, i, core_ref: (0, 0)),
            ],
            out_specs=pl.BlockSpec(block, target),
        ),
        out_shape=jax.ShapeDtypeStruct((micro, 2 * rows, width), jnp.bfloat16),
        compiler_params=pltpu.CompilerParams(vmem_limit_bytes=48 << 20),
        cost_estimate=pl.CostEstimate(
            flops=8 * micro * rows * width, bytes_accessed=8 * micro * rows * width, transcendentals=0
        ),
    )(core.reshape(1), own, other, gain[None])


def token_grad_kernel(core_ref, part_ref, back_ref, token_ref, hidden_ref, gain_ref, out_ref, sum_ref):
    rows = token_ref[0].astype(jnp.float32)
    scale = lax.rsqrt(jnp.mean(rows * rows, axis=-1, keepdims=True) + NORM_EPS)
    unit = rows * scale
    grad = part_ref[0].astype(jnp.float32) + back_ref[0].astype(jnp.float32)
    back = norm_back(grad, unit, scale, gain_ref[...])
    out_ref[0] = (hidden_ref[0] + back).astype(jnp.bfloat16)

    @pl.when((pl.program_id(0) == 0) & (pl.program_id(1) == 0))
    def clear():
        sum_ref[...] = jnp.zeros_like(sum_ref)

    sum_ref[0:1] += jnp.sum(grad * unit, axis=0, keepdims=True)


def token_grads(part, back, tokens, hidden, gain, core):
    micro, rows, width = tokens.shape
    cuts = 2
    block = (1, rows // cuts, width)
    here = pl.BlockSpec(block, lambda m, i, core_ref: (m, i, 0))
    token_rows, sums = pl.pallas_call(
        token_grad_kernel,
        grid_spec=pltpu.PrefetchScalarGridSpec(
            num_scalar_prefetch=1,
            grid=(micro, cuts),
            in_specs=[
                pl.BlockSpec(block, lambda m, i, core_ref: (m, core_ref[0] * cuts + i, 0)),
                here,
                here,
                here,
                pl.BlockSpec((1, width), lambda m, i, core_ref: (0, 0)),
            ],
            out_specs=[here, pl.BlockSpec((8, width), lambda m, i, core_ref: (0, 0))],
        ),
        out_shape=[
            jax.ShapeDtypeStruct(tokens.shape, jnp.bfloat16),
            jax.ShapeDtypeStruct((8, width), jnp.float32),
        ],
        compiler_params=pltpu.CompilerParams(vmem_limit_bytes=48 << 20),
        cost_estimate=pl.CostEstimate(
            flops=20 * micro * rows * width, bytes_accessed=12 * micro * rows * width, transcendentals=0
        ),
    )(core.reshape(1), part, back, tokens, hidden, gain[None])
    return (token_rows, sums[0])


def adam_update(master, first, second, grad, rate, decay):
    first_new = BETA_ONE * first + (1.0 - BETA_ONE) * grad
    second_new = BETA_TWO * second + (1.0 - BETA_TWO) * grad * grad
    fix_one = 1.0 - BETA_ONE**STEP
    fix_two = 1.0 - BETA_TWO**STEP
    step_size = first_new / fix_one / (jnp.sqrt(second_new / fix_two) + ADAM_EPS)
    return (master - rate * (step_size + decay * master), first_new, second_new)


def product(left, right, spec):
    return jnp.einsum(spec, left, right, preferred_element_type=jnp.float32)


Y_CHIPS = 2
CAPACITY = 8
SPARE = 8
GROUP = 16
CHUNK = 256
MESH_IDS = pl.DeviceIdType.MESH


def place():
    chip = lax.axis_index("chip")
    return (
        chip // Y_CHIPS,
        lax.rem(chip, Y_CHIPS),
        lax.axis_index("core"),
        lax.axis_index("seq"),
        lax.axis_size("chip") // Y_CHIPS,
    )


def at_z(z, y):
    return {"chip": z * Y_CHIPS + y}


def ahead(d):
    z, y, core, x, depth = place()
    return at_z(lax.rem(z + d, depth), y)


def across(axis):
    z, y, core, x, _ = place()
    return {"y": at_z(z, 1 - y), "x": {"seq": 1 - x}, "core": {"core": 1 - core}}[axis]


def greet():
    depth = place()[4]
    barrier = pltpu.get_barrier_semaphore()
    peers = [ahead(d) for d in range(1, depth)] + [across("y"), across("x"), across("core")]
    for peer in peers:
        pl.semaphore_signal(barrier, inc=1, device_id=peer, device_id_type=MESH_IDS)
    pl.semaphore_wait(barrier, len(peers))


def sem_pair(*shape):
    return [pltpu.SemaphoreType.DMA(shape), pltpu.SemaphoreType.DMA(shape)]


def remote(source, target, sems, index, device):
    return pltpu.make_async_remote_copy(
        src_ref=source,
        dst_ref=target,
        send_sem=sems[0].at[index],
        recv_sem=sems[1].at[index],
        device_id=device,
        device_id_type=MESH_IDS,
    )


def total(*parts):
    return functools.reduce(jnp.add, [p.astype(jnp.float32) for p in parts]).astype(jnp.bfloat16)


class Flow:
    def __init__(self):
        self.sent = []

    def push(self, source, target, sems, index, device):
        copy = remote(source, target, sems, index, device)
        copy.start()
        self.sent.append(copy)

    def arrive(self, here, sems, index):
        remote(here, here, sems, index, across("core")).wait_recv()

    def drain(self):
        for copy in self.sent:
            copy.wait_send()


class Total(Flow):
    def __init__(self, axes, sums, inbox, sems):
        super().__init__()
        self.axes, self.sums, self.inbox, self.sems = (axes, sums, inbox, sems)
        self.done = 0

    def begin(self, value):
        self.sums[0] = value
        self.push(self.sums.at[0], self.inbox.at[0], self.sems, (0,), across(self.axes[0]))

    def step(self):
        i = self.done
        self.done += 1
        self.arrive(self.inbox.at[i], self.sems, (i,))
        self.sums[i + 1] = self.sums[i] + self.inbox[i]
        here = self.sums.at[i + 1]
        if i + 1 < len(self.axes):
            self.push(here, self.inbox.at[i + 1], self.sems, (i + 1,), across(self.axes[i + 1]))
            return
        for d in range(1, place()[4]):
            self.push(here, self.inbox.at[i + d], self.sems, (i + d,), ahead(d))

    def result(self):
        last = len(self.axes)
        value = self.sums[last]
        for d in range(1, place()[4]):
            self.arrive(self.inbox.at[last - 1 + d], self.sems, (last - 1 + d,))
            value = value + self.inbox[last - 1 + d]
        self.drain()
        return value


def distances(depth):
    return sorted(range(1, depth), key=lambda d: min(d, depth - d))


def total_scratch(axes, depth, width):
    return [
        pltpu.VMEM((axes + 1, 8, width), jnp.float32),
        pltpu.VMEM((axes + depth - 1, 8, width), jnp.float32),
    ] + sem_pair(axes + depth - 1)


def spread_sems(depth):
    return sem_pair(depth) + sem_pair(depth) + sem_pair(depth, 2) + sem_pair(depth, 4)


class Spread(Flow):
    def __init__(self, window, second, sems):
        super().__init__()
        self.window = window
        self.second = second
        self.third = "x" if second == "y" else "y"
        self.sems = [(sems[2 * i], sems[2 * i + 1]) for i in range(4)]

    def where(self, d, second=False, third=False, other_core=False):
        z, y, core, x, depth = place()
        if second if self.second == "y" else third:
            y = 1 - y
        if third if self.second == "y" else second:
            x = 1 - x
        return self.window(lax.rem(z - d + depth, depth), y, 1 - core if other_core else core, x)

    def forward(self, stage, index, block, device):
        self.push(block, block, self.sems[stage], index, device)

    def begin(self):
        self.waiting = distances(place()[4])
        self.along_z()
        self.onward(0)

    def along_z(self):
        if self.waiting:
            d = self.waiting.pop(0)
            self.forward(0, (d,), self.where(0), ahead(d))

    def onward(self, d):
        block = self.where(d)
        self.forward(1, (d,), block, across(self.second))
        self.forward(2, (d, 0), block, across(self.third))
        self.forward(3, (d, 0), block, across("core"))

    def from_z(self, d):
        self.arrive(self.where(d), self.sems[0], (d,))
        self.along_z()
        self.onward(d)

    def from_second(self, d):
        block = self.where(d, True)
        self.arrive(block, self.sems[1], (d,))
        self.forward(2, (d, 1), block, across(self.third))
        self.forward(3, (d, 2), block, across("core"))

    def from_third(self, d):
        for second in range(2):
            block = self.where(d, bool(second), True)
            self.arrive(block, self.sems[2], (d, second))
            self.forward(3, (d, 2 * second + 1), block, across("core"))

    def finish(self):
        for d in range(place()[4]):
            for second in range(2):
                for third in range(2):
                    block = self.where(d, bool(second), bool(third), True)
                    self.arrive(block, self.sems[3], (d, 2 * second + third))
        self.drain()


def device_block(z, y, core, x):
    return ((z * Y_CHIPS + y) * 2 + core) * 2 + x


def chip_block(z, y, x):
    return (z * Y_CHIPS + y) * 2 + x


def gather_kernel(
    split,
    cut,
    block_ref,
    row_ref,
    spare_rank_ref,
    spare_mine_ref,
    low_ref,
    gain_ref,
    *refs,
):
    outs = refs[: 4 if split else 1]
    gain_out, whole, stage, stage_sem, spare, core_in, y_in, z_in, held = refs[len(outs) : len(outs) + 9]
    gain_sum, gain_in = refs[len(outs) + 9 : len(outs) + 11]
    sems = refs[len(outs) + 11 :]
    z, y, core, x, depth = place()
    piece, width = low_ref.shape[1:]
    half = CAPACITY // 2
    base = half * piece // GROUP
    me = device_block(z, y, core, x)
    per_piece = piece // GROUP
    for i in range(base):
        source = pl.ds(i % per_piece * GROUP, GROUP)
        whole[me, i] = low_ref[x * half + i // per_piece, source]
    greet()

    def window(first, count):
        return lambda *who: whole.at[device_block(*who), pl.ds(first, count)]

    flow_sems = 8
    early = Spread(window(0, cut), "y", sems[2 : 2 + flow_sems])
    late = Spread(window(cut, base - cut), "x", sems[10 : 10 + flow_sems])
    loose = Spread(window(base, 1), "x", sems[18 : 18 + flow_sems])
    gains = Total(["core", "y"], gain_sum, gain_in, sems[0:2])
    spare_sems = sems[26:32]
    spare_flow = Flow()
    early.begin()
    late.begin()
    gains.begin(gain_ref[...])
    count = SPARE // 2
    for i in range(count):
        found = low_ref[spare_rank_ref[x * count + i]]
        spare[pl.ds(i * piece, piece)] = jnp.where(spare_mine_ref[x * count + i] > 0, found, 0)
    rows = core_in.shape[0]

    def part(index, size):
        return pl.ds(pl.multiple_of(index * size, GROUP), size)

    spare_flow.push(spare.at[part(1 - core, rows)], core_in, spare_sems[0:2], (0,), across("core"))
    flows = [early, late]

    def from_z(d):
        for flow in flows:
            flow.from_z(d)

    def from_second(d):
        for flow in flows:
            flow.from_second(d)

    order = distances(depth)
    from_z(order[0])
    spare_flow.arrive(core_in, spare_sems[0:2], (0,))
    held[...] = total(spare[part(core, rows)], core_in[...])
    spare_flow.push(held.at[part(1 - y, rows // 2)], y_in, spare_sems[2:4], (0,), across("y"))
    gains.step()
    from_second(0)
    for i in range(1, depth - 1):
        from_z(order[i])
        if i == 1:
            spare_flow.arrive(y_in, spare_sems[2:4], (0,))
            y_in[...] = total(held[part(y, rows // 2)], y_in[...])
            for e in range(1, depth):
                to = part(lax.rem(z + e, depth), GROUP)
                spare_flow.push(y_in.at[to], z_in.at[e], spare_sems[4:6], (e,), ahead(e))
            gains.step()
        from_second(order[i - 1])
        for flow in flows:
            flow.from_third(([0] + order)[i - 1])
    for d in range(1, depth):
        spare_flow.arrive(z_in.at[d], spare_sems[4:6], (d,))
    whole[me, base] = total(y_in[part(z, GROUP)], *[z_in[d] for d in range(1, depth)])
    loose.begin()
    from_second(order[-1])
    gain_out[...] = gains.result()
    for d in order:
        loose.from_z(d)
    for flow in flows:
        flow.from_third(order[-2])
    for d in range(depth):
        loose.from_second(d)
    for flow in flows:
        flow.from_third(order[-1])
    for d in range(depth):
        loose.from_third(d)
    for flow in flows + [loose]:
        flow.finish()
    spare_flow.drain()

    buffers = stage.shape[0]
    per_chunk = CHUNK // GROUP
    narrow = width // 2
    copies = []
    for index in range(6 * width // CHUNK):
        matrix, first = divmod(index * CHUNK, width)
        slot = index % buffers
        if index >= buffers:
            copies[index - buffers].wait()
        thin = split and matrix < 3
        columns = pl.ds(pl.multiple_of(core * narrow, LANES), narrow) if thin else slice(None)
        count = narrow if thin else width

        def step(i, carry, index=index, slot=slot, columns=columns, count=count):
            for g in range(per_piece):
                at = index * per_chunk + i * per_piece + g
                target = pl.ds(pl.multiple_of(i * piece + g * GROUP, GROUP), GROUP)
                stage[slot, target, pl.ds(0, count)] = whole[block_ref[at], row_ref[at], :, columns]
            return carry

        lax.fori_loop(0, per_chunk // per_piece, step, 0)
        if thin:
            target = outs[0].at[pl.ds(first, CHUNK), pl.ds(matrix * narrow, narrow)]
        elif split:
            target = outs[matrix - 2].at[pl.ds(first, CHUNK)]
        else:
            target = outs[0].at[matrix, pl.ds(first, CHUNK)]
        copies.append(
            pltpu.make_async_copy(stage.at[slot, :, pl.ds(0, count)], target, stage_sem.at[slot])
        )
        copies[-1].start()
    for copy in copies[-buffers:]:
        copy.wait()


def gather_pieces(low, gains, plan, split):
    slots, piece, width = low.shape
    block, row, spare_rank, spare_mine, gain_mine = plan
    chips = lax.axis_size("chip")
    depth = chips // Y_CHIPS
    base = CAPACITY // 2 * piece // GROUP
    shapes = [(width, 3 * (width // 2))] + [(width, width)] * 3 if split else [(6, width, width)]
    lane = SPARE * piece // 4
    buffers = 4
    picked = jnp.where(gain_mine[:, None], gains[: gain_mine.shape[0]].astype(jnp.float32), 0.0)
    padded = jnp.concatenate([picked, jnp.zeros((6, width), jnp.float32)], axis=0)
    vmem = pl.BlockSpec(memory_space=pltpu.VMEM)
    smem = pl.BlockSpec(memory_space=pltpu.SMEM)
    outs = pl.pallas_call(
        functools.partial(gather_kernel, split, base // 4 if split else base // 2),
        in_specs=[smem] * 3 + [vmem] * 3,
        out_specs=[pl.BlockSpec(memory_space=pl.ANY)] * len(shapes) + [vmem],
        out_shape=[jax.ShapeDtypeStruct(s, jnp.bfloat16) for s in shapes]
        + [jax.ShapeDtypeStruct((8, width), jnp.float32)],
        scratch_shapes=[
            pltpu.VMEM((4 * chips, base + 1, GROUP, width), jnp.bfloat16),
            pltpu.VMEM((buffers, CHUNK, width), jnp.bfloat16),
            pltpu.SemaphoreType.DMA((buffers,)),
            pltpu.VMEM((2 * lane, width), jnp.bfloat16),
            pltpu.VMEM((lane, width), jnp.bfloat16),
            pltpu.VMEM((lane // 2, width), jnp.bfloat16),
            pltpu.VMEM((depth, GROUP, width), jnp.bfloat16),
            pltpu.VMEM((lane, width), jnp.bfloat16),
        ]
        + total_scratch(2, depth, width)
        + spread_sems(depth) * 3
        + sem_pair(1)
        + sem_pair(1)
        + sem_pair(depth),
        compiler_params=pltpu.CompilerParams(
            collective_id=0 if split else 1, has_side_effects=True, vmem_limit_bytes=48 << 20
        ),
        cost_estimate=pl.CostEstimate(
            flops=0, bytes_accessed=6 * width * width * 16, transcendentals=0
        ),
    )(
        block.reshape(-1),
        row.reshape(-1),
        spare_rank,
        jnp.broadcast_to(spare_mine[:, None, None], (SPARE, 1, width)),
        low,
        padded,
    )
    return (*outs[:-1], outs[-1][:2].astype(jnp.bfloat16))


def halves(matrices, split):
    if not split:
        return (matrices,)
    width = matrices.shape[1]
    narrow = width // 2
    thin = lax.dynamic_slice_in_dim(matrices[:3], lax.axis_index("core") * narrow, narrow, axis=2)
    side = jnp.concatenate([thin[0], thin[1], thin[2]], axis=1)
    return (side, matrices[3], matrices[4], matrices[5])


def gather_slots(low, gains, owners, split):
    slots, piece, width = low.shape
    piece_owner, rank = owner_slots(owners, slots)
    rows = slots * piece
    half = -(-(rows // 2 + 1) // GROUP) * GROUP
    filler = jnp.zeros((2 * half - rows - 2, width), jnp.bfloat16)
    packed = jnp.concatenate([low.reshape(rows, width), gains, filler], axis=0)
    share = lax.dynamic_slice_in_dim(packed, lax.axis_index("seq") * half, half, axis=0)
    groups = lax.all_gather(share, ALL, axis=0, tiled=True).reshape(-1, GROUP, width)
    per_owner = 2 * half // GROUP
    base = piece_owner * per_owner + rank * (piece // GROUP)
    index = base[:, None] + jnp.arange(piece // GROUP, dtype=jnp.int32)[None, :]
    matrices = groups[index.reshape(-1)].reshape(6, width, width)
    gain_rows = groups[owners[-2:] * per_owner + rows // GROUP][jnp.arange(2), jnp.arange(2)]
    return (*halves(matrices, split), gain_rows)


def kernels_fit(slots, piece, width):
    chips = lax.axis_size("chip")
    return slots == 2 * CAPACITY and piece == GROUP * (chips // Y_CHIPS) and width % CHUNK == 0


def spare_pieces(owners, slots):
    piece_owner, rank = owner_slots(owners, slots)
    spare = rank >= CAPACITY
    return (piece_owner, rank, spare, jnp.cumsum(spare.astype(jnp.int32)) - 1)


def gather_store(low, gains, owners, split, few):
    if not few:
        return gather_slots(low, gains, owners, split)
    slots, piece, width = low.shape
    dp_pos = lax.axis_index("chip") * 2 + lax.axis_index("core")
    piece_owner, rank, spare, order = spare_pieces(owners, slots)
    half = CAPACITY // 2
    groups = piece // GROUP
    group = jnp.arange(groups, dtype=jnp.int32)[None, :]
    block = jnp.where(
        spare[:, None],
        device_block(group, (order % 2)[:, None], ((order // 2) % 2)[:, None], (order // 4)[:, None]),
        (piece_owner * 2 + rank // half)[:, None],
    )
    row = jnp.where(spare[:, None], half * groups, (rank % half)[:, None] * groups + group)
    labels = jnp.arange(SPARE, dtype=jnp.int32)
    own = (spare & (piece_owner == dp_pos))[None, :] & (order[None, :] == labels[:, None])
    spare_rank = jnp.sum(jnp.where(own, rank[None, :], 0), axis=1)
    spare_mine = jnp.any(own, axis=1).astype(jnp.int32)
    plan = (block, row, spare_rank, spare_mine, owners[-2:] == dp_pos)
    return gather_pieces(low, gains, plan, split)


class Reduce(Flow):
    def __init__(self, first, shard, one, two, three, sems):
        super().__init__()
        self.first = first
        self.other = "y" if first == "x" else "x"
        self.shard = shard
        self.one, self.two, self.three = (one, two, three)
        self.sems = [sems[0:2], sems[2:4], sems[4:6]]

    def start(self, d, b):
        self.push(self.shard(d, b, 1), self.one.at[d, b], self.sems[0], (d, b), across(self.first))

    def from_first(self, d, b):
        here = self.one.at[d, b]
        self.arrive(here, self.sems[0], (d, b))
        here[...] = total(here[...], self.shard(d, b, 0)[...])
        if b:
            self.push(here, self.two.at[d], self.sems[1], (d,), across(self.other))

    def from_second(self, d):
        here = self.two.at[d]
        self.arrive(here, self.sems[1], (d,))
        here[...] = total(here[...], self.one[d, 0])
        if d:
            self.push(here, self.three.at[d], self.sems[2], (d,), ahead(d))

    def result(self):
        depth = place()[4]
        for d in range(1, depth):
            self.arrive(self.three.at[d], self.sems[2], (d,))
        value = total(self.two[0], *[self.three[d] for d in range(1, depth)])
        self.drain()
        return value


def reduce_kernel(
    source_ref,
    spare_ref,
    spare_mine_ref,
    early_ref,
    late_ref,
    gain_ref,
    slot_ref,
    gain_out,
    pieces,
    blocks,
    early_one,
    early_two,
    early_three,
    late_one,
    late_two,
    late_three,
    final,
    pair_in,
    full,
    full_in,
    spares,
    gain_sum,
    gain_in,
    load_sem,
    *sems,
):
    z, y, core, x, depth = place()
    narrow = pieces.shape[2]
    groups = late_ref.shape[1]
    per_block = blocks.shape[1]
    cut = early_one.shape[2]
    owned = CAPACITY // 2 * slot_ref.shape[1]
    order = distances(depth)[::-1] + [0]
    loads = []
    for matrix in range(3):
        columns = pl.ds(matrix * narrow, narrow)
        loads.append((early_ref.at[:, :, columns], matrix))
        loads.append((late_ref.at[matrix], matrix + 3))
    loads = [
        pltpu.make_async_copy(source, pieces.at[pl.ds(m * groups, groups)], load_sem.at[m])
        for source, m in loads
    ]
    for load in loads:
        load.start()
    pieces[6 * groups] = jnp.zeros((GROUP, narrow), jnp.bfloat16)
    greet()
    gains = Total(["core", "x", "y"], gain_sum, gain_in, sems[0:2])
    gains.begin(gain_ref[...])
    for load in loads:
        load.wait()

    def block_at(d, swap_y, swap_x):
        return chip_block(
            lax.rem(z + d, depth), 1 - y if swap_y else y, 1 - x if swap_x else x
        )

    early = Reduce(
        "x",
        lambda d, b, a: blocks.at[block_at(d, b, a), pl.ds(0, cut)],
        early_one,
        early_two,
        early_three,
        sems[2:8],
    )
    late = Reduce(
        "y",
        lambda d, b, a: blocks.at[block_at(d, a, b), pl.ds(cut, per_block - cut)],
        late_one,
        late_two,
        late_three,
        sems[8:14],
    )

    def fill(d, swap_y, swap_x):
        block = block_at(d, swap_y, swap_x)

        def step(i, carry):
            for g in range(2):
                blocks[block, 2 * i + g] = pieces[source_ref[block * per_block + 2 * i + g]]
            return carry

        lax.fori_loop(0, per_block // 2, step, 0)

    def start(d, b):
        for flow in (early, late):
            flow.start(d, b)

    fill(order[0], 1, 1)
    start(order[0], 1)
    fill(order[0], 0, 1)
    fill(order[0], 1, 0)
    start(order[0], 0)
    fill(order[0], 0, 0)
    for i, d in enumerate(order):
        later = order[i + 1] if i + 1 < len(order) else None
        if later is not None:
            fill(later, 1, 1)
        for flow in (early, late):
            flow.from_first(d, 1)
        if later is not None:
            start(later, 1)
            fill(later, 0, 1)
            fill(later, 1, 0)
        for flow in (early, late):
            flow.from_first(d, 0)
        if later is not None:
            start(later, 0)
            fill(later, 0, 0)
        if i:
            for flow in (early, late):
                flow.from_second(order[i - 1])
        if i < 3:
            gains.step()
    for flow in (early, late):
        flow.from_second(order[-1])
    final[pl.ds(0, cut)] = early.result()
    final[pl.ds(cut, per_block - cut)] = late.result()

    ends = Flow()
    own_spare = spares.at[z, y, x, core]
    ends.push(final.at[pl.ds((1 - core) * owned, owned)], pair_in, sems[14:16], (0,), across("core"))
    spares[z, y, x, core] = final[pl.ds(2 * owned, 2)]
    for d in range(1, depth):
        ends.push(own_spare, own_spare, sems[16:18], (d,), ahead(d))
    gain_out[...] = gains.result()
    ends.arrive(pair_in, sems[14:16], (0,))
    for g in range(owned):
        mine = final[core * owned + g]
        theirs = pair_in[g]
        first = core == 0
        full[g, :, pl.ds(pl.multiple_of(core * narrow, LANES), narrow)] = mine
        full[g, :, pl.ds(pl.multiple_of((1 - core) * narrow, LANES), narrow)] = theirs
    ends.push(full, full_in, sems[14:16], (1,), across("x"))
    for d in range(1, depth):
        from_z = spares.at[lax.rem(z - d + depth, depth), y, x, core]
        ends.arrive(from_z, sems[16:18], (d,))
    here = spares.at[:, y, x, core]
    ends.push(here, here, sems[14:16], (2,), across("y"))
    ends.arrive(spares.at[:, 1 - y, x, core], sems[14:16], (2,))
    here = spares.at[:, :, x, core]
    ends.push(here, here, sems[14:16], (3,), across("x"))
    ends.arrive(spares.at[:, :, 1 - x, core], sems[14:16], (3,))
    here = spares.at[:, :, :, core]
    ends.push(here, here, sems[14:16], (4,), across("core"))
    ends.arrive(spares.at[:, :, :, 1 - core], sems[14:16], (4,))
    ends.arrive(full_in, sems[14:16], (1,))
    per_piece = slot_ref.shape[1]
    half = CAPACITY // 2
    for i in range(half):
        for g in range(per_piece):
            slot_ref[x * half + i, g] = full[i * per_piece + g]
            slot_ref[(1 - x) * half + i, g] = full_in[i * per_piece + g]

    def pick(slot, carry):
        for g in range(per_piece):
            at = spare_ref[slot] * per_piece + g
            sub = spares.shape[4]
            chip = lax.div(at, 2 * sub)
            where = (lax.div(chip, Y_CHIPS), lax.rem(chip, Y_CHIPS), lax.rem(lax.div(at, sub), 2))
            for side in range(2):
                found = spares[(*where, side, lax.rem(at, sub))]
                slot_ref[CAPACITY + slot, g, :, pl.ds(side * narrow, narrow)] = jnp.where(
                    spare_mine_ref[slot] > 0, found, 0
                )
        return carry

    lax.fori_loop(0, slot_ref.shape[0] - CAPACITY, pick, 0)
    ends.drain()


def reduce_slots(early, late, gains, owners, slots, piece):
    width = late.shape[1]
    narrow = width // 2
    chips = lax.axis_size("chip")
    depth = chips // Y_CHIPS
    groups = width // GROUP
    per_piece = piece // GROUP
    dp_pos = lax.axis_index("chip") * 2 + lax.axis_index("core")
    piece_owner, rank, spare, order = spare_pieces(owners, slots)
    half = CAPACITY // 2
    labels = jnp.arange(piece_owner.shape[0], dtype=jnp.int32)
    empty = 6 * groups

    def groups_of(match):
        first = jnp.sum(jnp.where(match, labels, 0), axis=-1)[..., None] * per_piece
        groups_at = first + jnp.arange(per_piece, dtype=jnp.int32)
        return jnp.where(jnp.any(match, axis=-1)[..., None], groups_at, empty)

    block = jnp.arange(2 * chips, dtype=jnp.int32)[:, None]
    entry = jnp.arange(CAPACITY, dtype=jnp.int32)[None, :]
    owner_at = block // 2 * 2 + entry // half
    rank_at = block % 2 * half + entry % half
    base_groups = groups_of(
        (piece_owner == owner_at[..., None]) & (rank == rank_at[..., None])
    ).reshape(2 * chips, -1)
    spare_hot = spare & (order == jnp.arange(SPARE, dtype=jnp.int32)[:, None])
    spare_groups = groups_of(spare_hot).reshape(2 * chips, -1)
    source = jnp.concatenate([base_groups, spare_groups], axis=1)
    per_block = source.shape[1]
    mine = (piece_owner == dp_pos) & spare & (order < SPARE)
    slot_hot = mine & (rank == CAPACITY + jnp.arange(slots - CAPACITY, dtype=jnp.int32)[:, None])
    spare_at = jnp.sum(jnp.where(slot_hot, order, 0), axis=1)
    subs = SPARE * per_piece // (2 * chips)

    vmem = pl.BlockSpec(memory_space=pltpu.VMEM)
    smem = pl.BlockSpec(memory_space=pltpu.SMEM)
    hbm = pl.BlockSpec(memory_space=pl.ANY)
    cut = per_block // 4 + 1
    owned = half * per_piece
    padded = jnp.concatenate([gains, jnp.zeros((8 - gains.shape[0], width), jnp.float32)], axis=0)

    def group_block(*shape):
        return pltpu.VMEM(shape + (GROUP, narrow), jnp.bfloat16)

    def flow_blocks(count):
        return [group_block(depth, 2, count), group_block(depth, count), group_block(depth, count)]

    flow_sems = sem_pair(depth, 2) + sem_pair(depth) + sem_pair(depth)
    slot_grad, gain_sum = pl.pallas_call(
        reduce_kernel,
        in_specs=[smem] * 2 + [vmem, hbm, hbm, vmem],
        out_specs=[vmem, vmem],
        out_shape=[
            jax.ShapeDtypeStruct((slots, per_piece, GROUP, width), jnp.bfloat16),
            jax.ShapeDtypeStruct((8, width), jnp.float32),
        ],
        scratch_shapes=[group_block(6 * groups + 1), group_block(2 * chips, per_block)]
        + flow_blocks(cut)
        + flow_blocks(per_block - cut)
        + [
            group_block(per_block),
            group_block(owned),
            pltpu.VMEM((owned, GROUP, width), jnp.bfloat16),
            pltpu.VMEM((owned, GROUP, width), jnp.bfloat16),
            group_block(depth, Y_CHIPS, 2, 2, subs),
        ]
        + total_scratch(3, depth, width)[:2]
        + [pltpu.SemaphoreType.DMA((6,))]
        + total_scratch(3, depth, width)[2:]
        + flow_sems
        + flow_sems
        + sem_pair(5)
        + sem_pair(depth),
        compiler_params=pltpu.CompilerParams(
            collective_id=2, has_side_effects=True, vmem_limit_bytes=56 << 20
        ),
        cost_estimate=pl.CostEstimate(
            flops=0, bytes_accessed=6 * width * width * 8, transcendentals=0
        ),
    )(
        source.reshape(-1),
        spare_at,
        jnp.broadcast_to(jnp.any(slot_hot, axis=1).astype(jnp.int32)[:, None, None], (slots - CAPACITY, 1, narrow)),
        early.reshape(groups, GROUP, 3 * narrow),
        late.reshape(3, groups, GROUP, narrow),
        padded,
    )
    return (slot_grad.reshape(slots, piece, width), gain_sum[:2])


def reduce_all(early, late, gains, owners, slots, piece, few):
    if few:
        return reduce_slots(early, late, gains, owners, slots, piece)
    width = late.shape[1]
    narrow = width // 2
    dp_pos = lax.axis_index("chip") * 2 + lax.axis_index("core")
    pieces = owners.shape[0] - 2
    chips = lax.axis_size("chip")
    local = jnp.concatenate([jnp.transpose(early.reshape(width, 3, narrow), (1, 0, 2)), late], axis=0)
    share = lax.psum_scatter(
        local.reshape(6 * width, narrow), ("chip", "seq"), scatter_dimension=0, tiled=True
    )
    sums = lax.all_gather(share, ALL, axis=0, tiled=False).reshape(chips, 2, 2, -1, narrow)
    sums = jnp.transpose(sums, (0, 2, 3, 1, 4)).reshape(pieces, piece, width)
    piece_owner, rank = owner_slots(owners, slots)
    labels = jnp.arange(slots, dtype=jnp.int32)
    match = (piece_owner == dp_pos) & (rank == labels[:, None])
    slot_grad = jnp.where(jnp.any(match, axis=1)[:, None, None], sums[jnp.argmax(match, axis=1)], 0)
    return (slot_grad, lax.psum(gains, ALL))


def adam_kernel(rate_ref, master_ref, first_ref, second_ref, grad_ref, *outs):
    count = master_ref.shape[0]
    for i in range(count):
        new, first_new, second_new = adam_update(
            master_ref[i],
            first_ref[i],
            second_ref[i],
            grad_ref[i].astype(jnp.float32),
            rate_ref[pl.program_id(0) * count + i],
            MATRIX_DECAY,
        )
        outs[0][i] = new
        outs[1][i] = first_new
        outs[2][i] = second_new
        outs[3][i] = new.astype(jnp.bfloat16)


def adam_slots(master, first, second, grad, rate):
    slots, piece, width = master.shape
    count = min(slots, 2)
    block = pl.BlockSpec((count, piece, width), lambda i: (i, 0, 0))
    shape = jax.ShapeDtypeStruct(master.shape, jnp.float32)
    return pl.pallas_call(
        adam_kernel,
        grid=(slots // count,),
        in_specs=[pl.BlockSpec(memory_space=pltpu.SMEM)] + [block] * 4,
        out_specs=[block] * 4,
        out_shape=[shape] * 3 + [jax.ShapeDtypeStruct(master.shape, jnp.bfloat16)],
        compiler_params=pltpu.CompilerParams(vmem_limit_bytes=60 << 20),
        cost_estimate=pl.CostEstimate(
            flops=20 * slots * piece * width,
            bytes_accessed=28 * slots * piece * width,
            transcendentals=slots * piece * width,
        ),
    )(rate, master, first, second, grad)


def local(*arrays):
    owners, weight_store = arrays[3:5]
    if not kernels_fit(*weight_store.shape):
        return step(False, *arrays)
    order = spare_pieces(owners, weight_store.shape[0])[3]
    few = order[-1] < SPARE
    return lax.cond(few, functools.partial(step, True), functools.partial(step, False), *arrays)


def step(
    few,
    tokens,
    cotangent,
    parents,
    owners,
    weight_store,
    gain_store,
    weight_first,
    gain_first,
    weight_second,
    gain_second,
):
    core = lax.axis_index("core")
    dp_pos = lax.axis_index("chip") * 2 + core
    slot_dev, piece, width = weight_store.shape
    pieces = owners.shape[0] - 2
    piece_owner, rank = owner_slots(owners, slot_dev)
    gain_owner = owners[pieces:]
    micro, _, rows, _ = tokens.shape
    half = width // 2
    own_rows = core * rows
    own_columns = core * half

    def mine(value, axis, size, index):
        return lax.dynamic_slice_in_dim(value, index * size, size, axis=axis)

    limit, branch = tail_limits(transposed(parents[:, 0]))
    arrived = moved(tokens[:, 0])
    qkv_weight, out_weight, up_weight, down_weight, gain_low = gather_store(
        weight_store.astype(jnp.bfloat16), gain_store.astype(jnp.bfloat16), owners, True, few
    )
    gain_low, arrived, cot = lax.optimization_barrier((gain_low, arrived, cotangent[:, 0]))
    own_tokens = settled(tokens[:, 0], arrived)
    own_cot = transposed(cot)
    other_tokens = partner(own_tokens)

    def by_core(own, other, axis):
        return jnp.where(
            core == 0,
            jnp.concatenate([own, other], axis=axis),
            jnp.concatenate([other, own], axis=axis),
        )

    gain_one = gain_low[0].astype(jnp.float32)
    gain_two = gain_low[1].astype(jnp.float32)

    def unit(values):
        scale = lax.rsqrt(jnp.mean(values * values, axis=-1, keepdims=True) + NORM_EPS)
        return (values * scale, scale)

    normed_one = norm_all(own_tokens, other_tokens, gain_one, core)
    qkv = product(normed_one, qkv_weight, "mtd,de->mte").astype(jnp.bfloat16)
    attended_half, lse = attend(qkv, limit, branch)
    attended = by_core(
        mine(attended_half, 1, rows, core), partner(mine(attended_half, 1, rows, 1 - core)), 2
    )
    residual = own_tokens.astype(jnp.float32)
    hidden_one = residual + product(attended, out_weight, "mti,io->mto")
    unit_two, scale_two = unit(hidden_one)
    normed_two = (unit_two * gain_two).astype(jnp.bfloat16)
    up_rows = product(normed_two, up_weight, "mti,io->mto")
    sigmoid_up = jax.nn.sigmoid(up_rows)
    activated = (up_rows * sigmoid_up).astype(jnp.bfloat16)
    mixed_rows = (hidden_one + product(activated, down_weight, "mti,io->mto")).astype(jnp.bfloat16)
    mixed = transposed(mixed_rows)

    grad_down = product(activated, own_cot, "mti,mto->io")
    grad_hidden = product(own_cot, down_weight, "mto,io->mti")
    grad_up_rows = (grad_hidden * (sigmoid_up * (1.0 + up_rows * (1.0 - sigmoid_up)))).astype(
        jnp.bfloat16
    )
    grad_up = product(normed_two, grad_up_rows, "mti,mto->io")
    grad_normed_two = product(grad_up_rows, up_weight, "mto,io->mti")
    gain_two_grad = jnp.sum(grad_normed_two * unit_two, axis=(0, 1))
    grad_hidden_one = own_cot.astype(jnp.float32) + norm_back(
        grad_normed_two, unit_two, scale_two, gain_two
    )
    branch_grad = grad_hidden_one.astype(jnp.bfloat16)
    grad_out = product(attended, branch_grad, "mti,mto->io")
    late = jnp.stack([grad_out, grad_up, grad_down]).astype(jnp.bfloat16)
    late_back = partner(mine(late, 2, half, 1 - core))

    branch_grad, late = lax.optimization_barrier((branch_grad, late))
    grad_attended = product(branch_grad, out_weight, "mto,io->mti").astype(jnp.bfloat16)
    grad_half = by_core(
        mine(grad_attended, 2, half, core), partner(mine(grad_attended, 2, half, 1 - core)), 1
    )
    grad_qkv_rows = attend_back(qkv, grad_half, attended_half, lse, limit, branch)
    grad_qkv = product(normed_one, grad_qkv_rows, "mti,mto->io")
    early = grad_qkv.astype(jnp.bfloat16)

    grad_normed_part = product(grad_qkv_rows, qkv_weight, "mte,de->mtd").astype(jnp.bfloat16)
    grad_back = partner(mine(grad_normed_part, 1, rows, 1 - core))
    token_rows, gain_one_grad = token_grads(
        grad_normed_part, grad_back, own_tokens, grad_hidden_one, gain_one, core
    )
    token_grad = transposed(token_rows)
    gain_grads = jnp.stack([gain_one_grad, gain_two_grad])
    late = (mine(late, 2, half, core).astype(jnp.float32) + late_back.astype(jnp.float32)).astype(
        jnp.bfloat16
    )

    labels = jnp.arange(slot_dev, dtype=jnp.int32)
    match = (piece_owner[None, :] == dp_pos) & (rank[None, :] == labels[:, None])
    held = jnp.any(match, axis=1)
    piece_of = jnp.sum(jnp.where(match, jnp.arange(pieces, dtype=jnp.int32)[None, :], 0), axis=1)
    slot_grad, gain_sum = reduce_all(early, late, gain_grads, owners, slot_dev, piece, few)
    is_out = held & (piece_of // (width // piece) == 3)
    slot_rate = jnp.where(is_out, RATE_OUT, RATE_QKV).astype(jnp.float32)
    weight_new, weight_first_new, weight_second_new, weight_low = adam_slots(
        weight_store, weight_first, weight_second, slot_grad, slot_rate
    )
    gain_slot_grad = jnp.where((gain_owner == dp_pos)[:, None], gain_sum, 0.0)
    gain_new, gain_first_new, gain_second_new = adam_update(
        gain_store, gain_first, gain_second, gain_slot_grad, RATE_GAIN, 0.0
    )
    weight_copies, gain_copies = gather_store(
        weight_low, gain_new.astype(jnp.bfloat16), owners, False, few
    )
    return (
        mixed[:, None],
        token_grad[:, None],
        weight_new,
        gain_new,
        weight_first_new,
        gain_first_new,
        weight_second_new,
        gain_second_new,
        weight_copies,
        gain_copies,
    )


def solution(mesh):
    dp_count, seq_count = mesh.devices.shape
    fine = Mesh(mesh.devices.reshape(dp_count // 2, 2, seq_count), ALL)
    dp = ("chip", "core")
    rows = P(None, dp, "seq", None)
    store = P(dp, None, None)
    gains = P(dp, None)
    in_specs = (rows, rows, P(None, dp, None), P(), store, gains, store, gains, store, gains)
    out_specs = (rows, rows, store, gains, store, gains, store, gains, P(), P())
    return jax.shard_map(local, mesh=fine, in_specs=in_specs, out_specs=out_specs, check_vma=False)
```

```python
import functools

import jax
import jax.numpy as jnp
from jax import lax
from jax.experimental import pallas as pl
from jax.experimental.pallas import tpu as pltpu
from jax.sharding import Mesh
from jax.sharding import PartitionSpec as P

HEAD = 80
SEG = 32
TRUNK_SEGS = 32
ALWAYS_SEGS = TRUNK_SEGS // 2
STEP = 7
LANES = 128
WINDOW = 256
QUERY_BLOCK = 256
KEY_BLOCK = 512

NORM_EPS = 1e-06
BETA_ONE = 0.5
BETA_TWO = 0.5
ADAM_EPS = 1e-08
MATRIX_DECAY = 0.1
RATE_QKV = 0.03
RATE_OUT = 0.4
RATE_GAIN = 0.4
MASKED = -1e30
SCALE = HEAD**-0.5
LOG2E = 1.4426950408889634
ALL = ("chip", "core", "seq")
NT = (((1,), (1,)), ((), ()))
TN = (((0,), (0,)), ((), ()))


def moved(value):
    chips = lax.axis_size("chip")
    pairs = [(k * 4 + c * 2 + 1 - c, k * 4 + 2 - 2 * c + c) for k in range(chips) for c in range(2)]
    return lax.ppermute(value, ALL, pairs)


def settled(value, arrived):
    return jnp.where(lax.axis_index("core") == lax.axis_index("seq"), value, arrived)


def transposed(value):
    return settled(value, moved(value))


def partner(value):
    return lax.ppermute(value, "core", [(0, 1), (1, 0)])


def owner_slots(owners, slot_dev):
    count = owners.shape[0] - 2
    piece_owner = owners[:count]
    labels = jnp.arange(count, dtype=jnp.int32)
    same = (piece_owner[:, None] == piece_owner[None, :]) & (labels[None, :] < labels[:, None])
    rank = jnp.sum(same.astype(jnp.int32), axis=1)
    return (piece_owner, rank)


def tail_limits(parents):
    up = parents[:, TRUNK_SEGS:]
    leaf = up >= TRUNK_SEGS
    above = jnp.where(leaf, up - TRUNK_SEGS, 0)
    labels = jnp.arange(up.shape[1], dtype=jnp.int32)
    hot = above[:, :, None] == labels[None, None, :]
    upper = jnp.sum(jnp.where(hot, up[:, None, :], 0), axis=2)
    attach = jnp.where(leaf, upper, up)
    limit = (attach + 1) * SEG
    branch = jnp.where(leaf, above, -1)
    return (jnp.repeat(limit, SEG, axis=1), jnp.repeat(branch, SEG, axis=1))


def query_blocks(length):
    trunk = TRUNK_SEGS * SEG
    blocks = []
    for first in range(0, trunk, QUERY_BLOCK):
        parts = [(0, first, "all")] if first else []
        blocks.append((first, QUERY_BLOCK, parts + [(first, QUERY_BLOCK, "causal")]))
    always = ALWAYS_SEGS * SEG
    tail = length - trunk
    blocks.append(
        (trunk, tail, [(0, always, "all"), (always, trunk - always, "trunk"), (trunk, tail, "tail")])
    )
    return blocks


def allowed_pairs(kind, key_first, key, query, limit, branch):
    if kind == "causal":
        return key <= query
    if kind == "trunk":
        return key + key_first < limit
    key_seg = key // SEG
    return ((key_seg == query // SEG) & (key <= query)) | (key_seg == branch)


def head_window(head, width):
    start = pl.multiple_of(
        jnp.minimum((head * HEAD) // LANES, width // LANES - WINDOW // LANES) * LANES, LANES
    )
    lane = lax.broadcasted_iota(jnp.int32, (1, WINDOW), 1) + start
    mine = (lane >= head * HEAD) & (lane < (head + 1) * HEAD)
    return (pl.ds(start, WINDOW), mine)


def scaled_query(rows, mine):
    return jnp.where(mine, rows.astype(jnp.float32) * (SCALE * LOG2E), 0.0).astype(jnp.bfloat16)


def attend_kernel(limit_ref, branch_ref, q_ref, k_ref, v_ref, out_ref, lse_ref):
    head = pl.program_id(1)
    window, mine = head_window(head, q_ref.shape[2])
    stat_lane = lax.broadcasted_iota(jnp.int32, (1, LANES), 1)
    values = jnp.where(mine, v_ref[0, :, window], 1)
    keys_side = k_ref[0, :, window].T

    def score(first, count, parts):
        query = scaled_query(q_ref[0, pl.ds(first, count), window], mine)
        scores = []
        for key_first, keys, kind in parts:
            raw = jnp.dot(
                query, keys_side[:, key_first : key_first + keys], preferred_element_type=jnp.float32
            )
            if kind != "all":
                ok = allowed_pairs(
                    kind,
                    key_first,
                    lax.broadcasted_iota(jnp.int32, (count, keys), 1),
                    lax.broadcasted_iota(jnp.int32, (count, keys), 0),
                    limit_ref[0],
                    branch_ref[0],
                )
                raw = jnp.where(ok, raw, MASKED)
            scores.append(raw)
        return scores

    def weigh(scores):
        top = functools.reduce(jnp.maximum, [jnp.max(s, axis=1, keepdims=True) for s in scores])
        return (top, [jnp.exp2(raw - top).astype(jnp.bfloat16) for raw in scores])

    def collect(weighed, first, count, parts):
        top, weights = weighed
        rows = pl.ds(first, count)
        gained = 0.0
        for weight, (key_first, keys, kind) in zip(weights, parts):
            gained = gained + jnp.dot(
                weight, values[key_first : key_first + keys], preferred_element_type=jnp.float32
            )
        weight_sum = jnp.max(jnp.where(mine, 0.0, gained), axis=1, keepdims=True)
        gained = (gained * (1.0 / weight_sum)).astype(jnp.bfloat16)
        out_ref[0, rows, window] = jnp.where(mine, gained, out_ref[0, rows, window])
        lse_ref[0, rows, :] = jnp.where(
            stat_lane == head, top + jnp.log2(weight_sum), lse_ref[0, rows, :]
        )

    blocks = query_blocks(q_ref.shape[1])
    scores = score(*blocks[0])
    weighed = None
    for i in range(len(blocks)):
        later = score(*blocks[i + 1]) if i + 1 < len(blocks) else None
        before = weighed
        weighed = weigh(scores)
        if i:
            collect(before, *blocks[i - 1])
        scores = later
    collect(weighed, *blocks[-1])


def attend(qkv, limit, branch):
    micro, length, columns = qkv.shape
    width = columns // 3
    heads = width // HEAD
    tail = length - TRUNK_SEGS * SEG

    def part(index):
        return pl.BlockSpec((1, length, width), lambda m, h, index=index: (m, 0, index))

    column = pl.BlockSpec((1, tail, 1), lambda m, h: (m, 0, 0))
    return pl.pallas_call(
        attend_kernel,
        grid=(micro, heads),
        in_specs=[column, column, part(0), part(1), part(2)],
        out_specs=[
            pl.BlockSpec((1, length, width), lambda m, h: (m, 0, 0)),
            pl.BlockSpec((1, length, LANES), lambda m, h: (m, 0, 0)),
        ],
        out_shape=[
            jax.ShapeDtypeStruct((micro, length, width), jnp.bfloat16),
            jax.ShapeDtypeStruct((micro, length, LANES), jnp.float32),
        ],
        compiler_params=pltpu.CompilerParams(vmem_limit_bytes=48 << 20),
        cost_estimate=pl.CostEstimate(
            flops=micro * heads * length * length * WINDOW * 3,
            bytes_accessed=micro * length * width * 8,
            transcendentals=micro * heads * length * length // 2,
        ),
    )(limit[:, :, None], branch[:, :, None], qkv, qkv, qkv)


def attend_back_kernel(
    limit_ref, branch_ref, lse_ref, q_ref, k_ref, v_ref, g_ref, a_ref, out_ref, dk_sum, dv_sum
):
    head = pl.program_id(1)
    width = q_ref.shape[2]
    window, mine = head_window(head, width)

    @pl.when(head == 0)
    def clear():
        dk_sum[...] = jnp.zeros_like(dk_sum)
        dv_sum[...] = jnp.zeros_like(dv_sum)

    lane = lax.broadcasted_iota(jnp.int32, (1, WINDOW), 1)
    after = (head + 1) * HEAD - window.start
    spots = [lane == lax.rem(after + i, WINDOW) for i in range(3)]
    stat_lane = lax.broadcasted_iota(jnp.int32, (1, LANES), 1)
    keys_all = jnp.where(spots[0] | spots[1] | spots[2], 1, k_ref[0, :, window])
    values_all = jnp.where(spots[0] | spots[1], 1, v_ref[0, :, window])

    def less(rows, column, count):
        rest = column
        for spot in spots[:count]:
            piece = rest.astype(jnp.bfloat16).astype(jnp.float32)
            rows = jnp.where(spot, -piece, rows)
            rest = rest - piece
        return rows.astype(jnp.bfloat16)

    def factors(first, count):
        rows = pl.ds(first, count)
        raw_query = q_ref[0, rows, window]
        query = jnp.where(mine, raw_query, 0)
        grad = jnp.where(mine, g_ref[0, rows, window], 0)
        wide_grad = grad.astype(jnp.float32)
        lse = jnp.sum(jnp.where(stat_lane == head, lse_ref[0, rows, :], 0.0), axis=1, keepdims=True)
        row_total = jnp.sum(
            wide_grad * a_ref[0, rows, window].astype(jnp.float32), axis=1, keepdims=True
        )
        query_less = less(scaled_query(raw_query, mine).astype(jnp.float32), lse, 3)
        return (query, grad, query_less, less(wide_grad, row_total, 2))

    def scores(part, block):
        query, grad, query_less, grad_less = block
        return (
            lax.dot_general(keys_all[part], query_less, NT, preferred_element_type=jnp.float32),
            lax.dot_general(values_all[part], grad_less, NT, preferred_element_type=jnp.float32),
        )

    def weigh(found, part, kind):
        raw, grad_prob = found
        prob = jnp.exp2(raw)
        if kind != "all":
            ok = allowed_pairs(
                kind,
                part.start,
                lax.broadcasted_iota(jnp.int32, raw.shape, 0),
                lax.broadcasted_iota(jnp.int32, raw.shape, 1),
                limit_ref[0],
                branch_ref[0],
            )
            prob = jnp.where(ok, prob, 0.0)
        return (prob.astype(jnp.bfloat16), (prob * grad_prob).astype(jnp.bfloat16))

    def collect(weighed, part, block):
        prob, grad_raw = weighed
        query, grad = block[:2]
        dv_sum[part, window] += jnp.dot(prob, grad, preferred_element_type=jnp.float32)
        dk_sum[part, window] += jnp.dot(grad_raw, query, preferred_element_type=jnp.float32)
        return lax.dot_general(grad_raw, keys_all[part], TN, preferred_element_type=jnp.float32)

    units = []
    for first, count, parts in query_blocks(q_ref.shape[1]):
        for key_first, keys, kind in parts:
            for cut in range(key_first, key_first + keys, KEY_BLOCK):
                part = slice(cut, min(cut + KEY_BLOCK, key_first + keys))
                units.append((first, count, part, kind))
    def finish(i, weighed, block, grad_query):
        first, count, part, kind = units[i]
        grad_query = grad_query + collect(weighed, part, block)
        if i + 1 < len(units) and units[i + 1][0] == first:
            return grad_query
        rows = pl.ds(first, count)
        out_ref[0, rows, window] = jnp.where(
            mine, (grad_query * SCALE).astype(jnp.bfloat16), out_ref[0, rows, window]
        )
        return 0.0

    held = {units[0][0]: factors(*units[0][:2])}
    found = scores(units[0][2], held[units[0][0]])
    weighed = None
    grad_query = 0.0
    for i, (first, count, part, kind) in enumerate(units):
        later = None
        if i + 1 < len(units):
            following = units[i + 1]
            if following[0] not in held:
                held[following[0]] = factors(*following[:2])
            later = scores(following[2], held[following[0]])
        before = weighed
        weighed = weigh(found, part, kind)
        if i:
            grad_query = finish(i - 1, before, held[units[i - 1][0]], grad_query)
        found = later
    finish(len(units) - 1, weighed, held[units[-1][0]], grad_query)

    @pl.when(head == pl.num_programs(1) - 1)
    def write():
        out_ref[0, :, pl.ds(width, width)] = (dk_sum[...] * SCALE).astype(jnp.bfloat16)
        out_ref[0, :, pl.ds(2 * width, width)] = dv_sum[...].astype(jnp.bfloat16)


def attend_back(qkv, grad, attended, lse, limit, branch):
    micro, length, columns = qkv.shape
    width = columns // 3
    heads = width // HEAD
    tail = length - TRUNK_SEGS * SEG

    def part(index):
        return pl.BlockSpec((1, length, width), lambda m, h, index=index: (m, 0, index))

    row = pl.BlockSpec((1, 1, tail), lambda m, h: (m, 0, 0))
    return pl.pallas_call(
        attend_back_kernel,
        grid=(micro, heads),
        in_specs=[
            row,
            row,
            pl.BlockSpec((1, length, LANES), lambda m, h: (m, 0, 0)),
            part(0),
            part(1),
            part(2),
            part(0),
            part(0),
        ],
        out_specs=pl.BlockSpec((1, length, columns), lambda m, h: (m, 0, 0)),
        out_shape=jax.ShapeDtypeStruct((micro, length, columns), jnp.bfloat16),
        scratch_shapes=[pltpu.VMEM((length, width), jnp.float32)] * 2,
        compiler_params=pltpu.CompilerParams(vmem_limit_bytes=56 << 20),
        cost_estimate=pl.CostEstimate(
            flops=micro * heads * length * length * WINDOW * 7,
            bytes_accessed=micro * length * width * 14,
            transcendentals=micro * heads * length * length // 2,
        ),
    )(limit[:, None, :], branch[:, None, :], lse, qkv, qkv, qkv, grad, attended)


def norm_back(grad_normed, normed_unit, scale_rows, gain_row):
    scaled_grad = grad_normed * gain_row
    return scale_rows * (
        scaled_grad - normed_unit * jnp.mean(scaled_grad * normed_unit, axis=-1, keepdims=True)
    )


def norm_kernel(core_ref, own_ref, other_ref, gain_ref, out_ref):
    def write(source):
        rows = source[0].astype(jnp.float32)
        scale = lax.rsqrt(jnp.mean(rows * rows, axis=-1, keepdims=True) + NORM_EPS)
        out_ref[0] = (rows * scale * gain_ref[...]).astype(jnp.bfloat16)

    @pl.when(pl.program_id(1) == 0)
    def own():
        write(own_ref)

    @pl.when(pl.program_id(1) == 1)
    def other():
        write(other_ref)


def norm_all(own, other, gain, core):
    micro, rows, width = own.shape
    cuts = 2
    block = (1, rows // cuts, width)

    def source(which):
        return lambda m, s, i, core_ref: (m, jnp.where(s == which, i, (cuts - 1) * (1 - which)), 0)

    def target(m, s, i, core_ref):
        return (m, jnp.where(s == 0, core_ref[0], 1 - core_ref[0]) * cuts + i, 0)

    return pl.pallas_call(
        norm_kernel,
        grid_spec=pltpu.PrefetchScalarGridSpec(
            num_scalar_prefetch=1,
            grid=(micro, 2, cuts),
            in_specs=[
                pl.BlockSpec(block, source(0)),
                pl.BlockSpec(block, source(1)),
                pl.BlockSpec((1, width), lambda m, s, i, core_ref: (0, 0)),
            ],
            out_specs=pl.BlockSpec(block, target),
        ),
        out_shape=jax.ShapeDtypeStruct((micro, 2 * rows, width), jnp.bfloat16),
        compiler_params=pltpu.CompilerParams(vmem_limit_bytes=48 << 20),
        cost_estimate=pl.CostEstimate(
            flops=8 * micro * rows * width, bytes_accessed=8 * micro * rows * width, transcendentals=0
        ),
    )(core.reshape(1), own, other, gain[None])


def token_grad_kernel(core_ref, part_ref, back_ref, token_ref, hidden_ref, gain_ref, out_ref, sum_ref):
    rows = token_ref[0].astype(jnp.float32)
    scale = lax.rsqrt(jnp.mean(rows * rows, axis=-1, keepdims=True) + NORM_EPS)
    unit = rows * scale
    grad = part_ref[0].astype(jnp.float32) + back_ref[0].astype(jnp.float32)
    back = norm_back(grad, unit, scale, gain_ref[...])
    out_ref[0] = (hidden_ref[0] + back).astype(jnp.bfloat16)

    @pl.when((pl.program_id(0) == 0) & (pl.program_id(1) == 0))
    def clear():
        sum_ref[...] = jnp.zeros_like(sum_ref)

    sum_ref[0:1] += jnp.sum(grad * unit, axis=0, keepdims=True)


def token_grads(part, back, tokens, hidden, gain, core):
    micro, rows, width = tokens.shape
    cuts = 2
    block = (1, rows // cuts, width)
    here = pl.BlockSpec(block, lambda m, i, core_ref: (m, i, 0))
    token_rows, sums = pl.pallas_call(
        token_grad_kernel,
        grid_spec=pltpu.PrefetchScalarGridSpec(
            num_scalar_prefetch=1,
            grid=(micro, cuts),
            in_specs=[
                pl.BlockSpec(block, lambda m, i, core_ref: (m, core_ref[0] * cuts + i, 0)),
                here,
                here,
                here,
                pl.BlockSpec((1, width), lambda m, i, core_ref: (0, 0)),
            ],
            out_specs=[here, pl.BlockSpec((8, width), lambda m, i, core_ref: (0, 0))],
        ),
        out_shape=[
            jax.ShapeDtypeStruct(tokens.shape, jnp.bfloat16),
            jax.ShapeDtypeStruct((8, width), jnp.float32),
        ],
        compiler_params=pltpu.CompilerParams(vmem_limit_bytes=48 << 20),
        cost_estimate=pl.CostEstimate(
            flops=20 * micro * rows * width, bytes_accessed=12 * micro * rows * width, transcendentals=0
        ),
    )(core.reshape(1), part, back, tokens, hidden, gain[None])
    return (token_rows, sums[0])


def adam_update(master, first, second, grad, rate, decay):
    first_new = BETA_ONE * first + (1.0 - BETA_ONE) * grad
    second_new = BETA_TWO * second + (1.0 - BETA_TWO) * grad * grad
    fix_one = 1.0 - BETA_ONE**STEP
    fix_two = 1.0 - BETA_TWO**STEP
    step_size = first_new / fix_one / (jnp.sqrt(second_new / fix_two) + ADAM_EPS)
    return (master - rate * (step_size + decay * master), first_new, second_new)


def product(left, right, spec):
    return jnp.einsum(spec, left, right, preferred_element_type=jnp.float32)


Y_CHIPS = 2
CAPACITY = 8
SPARE = 8
GROUP = 16
CHUNK = 256
MESH_IDS = pl.DeviceIdType.MESH


def place():
    chip = lax.axis_index("chip")
    return (
        chip // Y_CHIPS,
        lax.rem(chip, Y_CHIPS),
        lax.axis_index("core"),
        lax.axis_index("seq"),
        lax.axis_size("chip") // Y_CHIPS,
    )


def at_z(z, y):
    return {"chip": z * Y_CHIPS + y}


def ahead(d):
    z, y, core, x, depth = place()
    return at_z(lax.rem(z + d, depth), y)


def across(axis):
    z, y, core, x, _ = place()
    return {"y": at_z(z, 1 - y), "x": {"seq": 1 - x}, "core": {"core": 1 - core}}[axis]


def greet():
    depth = place()[4]
    barrier = pltpu.get_barrier_semaphore()
    peers = [ahead(d) for d in range(1, depth)] + [across("y"), across("x"), across("core")]
    for peer in peers:
        pl.semaphore_signal(barrier, inc=1, device_id=peer, device_id_type=MESH_IDS)
    pl.semaphore_wait(barrier, len(peers))


def sem_pair(*shape):
    return [pltpu.SemaphoreType.DMA(shape), pltpu.SemaphoreType.DMA(shape)]


def remote(source, target, sems, index, device):
    return pltpu.make_async_remote_copy(
        src_ref=source,
        dst_ref=target,
        send_sem=sems[0].at[index],
        recv_sem=sems[1].at[index],
        device_id=device,
        device_id_type=MESH_IDS,
    )


def total(*parts):
    return functools.reduce(jnp.add, [p.astype(jnp.float32) for p in parts]).astype(jnp.bfloat16)


class Flow:
    def __init__(self):
        self.sent = []

    def push(self, source, target, sems, index, device):
        copy = remote(source, target, sems, index, device)
        copy.start()
        self.sent.append(copy)

    def arrive(self, here, sems, index):
        remote(here, here, sems, index, across("core")).wait_recv()

    def drain(self):
        for copy in self.sent:
            copy.wait_send()


class Total(Flow):
    def __init__(self, axes, sums, inbox, sems):
        super().__init__()
        self.axes, self.sums, self.inbox, self.sems = (axes, sums, inbox, sems)
        self.done = 0

    def begin(self, value):
        self.sums[0] = value
        self.push(self.sums.at[0], self.inbox.at[0], self.sems, (0,), across(self.axes[0]))

    def step(self):
        i = self.done
        self.done += 1
        self.arrive(self.inbox.at[i], self.sems, (i,))
        self.sums[i + 1] = self.sums[i] + self.inbox[i]
        here = self.sums.at[i + 1]
        if i + 1 < len(self.axes):
            self.push(here, self.inbox.at[i + 1], self.sems, (i + 1,), across(self.axes[i + 1]))
            return
        for d in range(1, place()[4]):
            self.push(here, self.inbox.at[i + d], self.sems, (i + d,), ahead(d))

    def result(self):
        last = len(self.axes)
        value = self.sums[last]
        for d in range(1, place()[4]):
            self.arrive(self.inbox.at[last - 1 + d], self.sems, (last - 1 + d,))
            value = value + self.inbox[last - 1 + d]
        self.drain()
        return value


def distances(depth):
    return sorted(range(1, depth), key=lambda d: min(d, depth - d))


def total_scratch(axes, depth, width):
    return [
        pltpu.VMEM((axes + 1, 8, width), jnp.float32),
        pltpu.VMEM((axes + depth - 1, 8, width), jnp.float32),
    ] + sem_pair(axes + depth - 1)


def spread_sems(depth):
    return sem_pair(depth) + sem_pair(depth) + sem_pair(depth, 2) + sem_pair(depth, 4)


class Spread(Flow):
    def __init__(self, window, second, sems):
        super().__init__()
        self.window = window
        self.second = second
        self.third = "x" if second == "y" else "y"
        self.sems = [(sems[2 * i], sems[2 * i + 1]) for i in range(4)]

    def where(self, d, second=False, third=False, other_core=False):
        z, y, core, x, depth = place()
        if second if self.second == "y" else third:
            y = 1 - y
        if third if self.second == "y" else second:
            x = 1 - x
        return self.window(lax.rem(z - d + depth, depth), y, 1 - core if other_core else core, x)

    def forward(self, stage, index, block, device):
        self.push(block, block, self.sems[stage], index, device)

    def begin(self):
        self.waiting = distances(place()[4])
        self.along_z()
        self.onward(0)

    def along_z(self):
        if self.waiting:
            d = self.waiting.pop(0)
            self.forward(0, (d,), self.where(0), ahead(d))

    def onward(self, d):
        block = self.where(d)
        self.forward(1, (d,), block, across(self.second))
        self.forward(2, (d, 0), block, across(self.third))
        self.forward(3, (d, 0), block, across("core"))

    def from_z(self, d):
        self.arrive(self.where(d), self.sems[0], (d,))
        self.along_z()
        self.onward(d)

    def from_second(self, d):
        block = self.where(d, True)
        self.arrive(block, self.sems[1], (d,))
        self.forward(2, (d, 1), block, across(self.third))
        self.forward(3, (d, 2), block, across("core"))

    def from_third(self, d):
        for second in range(2):
            block = self.where(d, bool(second), True)
            self.arrive(block, self.sems[2], (d, second))
            self.forward(3, (d, 2 * second + 1), block, across("core"))

    def finish(self):
        for d in range(place()[4]):
            for second in range(2):
                for third in range(2):
                    block = self.where(d, bool(second), bool(third), True)
                    self.arrive(block, self.sems[3], (d, 2 * second + third))
        self.drain()


def device_block(z, y, core, x):
    return ((z * Y_CHIPS + y) * 2 + core) * 2 + x


def chip_block(z, y, x):
    return (z * Y_CHIPS + y) * 2 + x


def gather_kernel(
    split,
    cut,
    block_ref,
    row_ref,
    spare_rank_ref,
    spare_mine_ref,
    low_ref,
    gain_ref,
    *refs,
):
    outs = refs[: 4 if split else 1]
    gain_out, whole, stage, stage_sem, spare, core_in, y_in, z_in, held = refs[len(outs) : len(outs) + 9]
    gain_sum, gain_in = refs[len(outs) + 9 : len(outs) + 11]
    sems = refs[len(outs) + 11 :]
    z, y, core, x, depth = place()
    piece, width = low_ref.shape[1:]
    half = CAPACITY // 2
    base = half * piece // GROUP
    me = device_block(z, y, core, x)
    per_piece = piece // GROUP
    for i in range(base):
        source = pl.ds(i % per_piece * GROUP, GROUP)
        whole[me, i] = low_ref[x * half + i // per_piece, source].astype(jnp.bfloat16)
    greet()

    def window(first, count):
        return lambda *who: whole.at[device_block(*who), pl.ds(first, count)]

    flow_sems = 8
    early = Spread(window(0, cut), "y", sems[2 : 2 + flow_sems])
    late = Spread(window(cut, base - cut), "x", sems[10 : 10 + flow_sems])
    loose = Spread(window(base, 1), "x", sems[18 : 18 + flow_sems])
    gains = Total(["core", "y"], gain_sum, gain_in, sems[0:2])
    spare_sems = sems[26:32]
    spare_flow = Flow()
    early.begin()
    late.begin()
    gains.begin(gain_ref[...])
    count = SPARE // 2
    for i in range(count):
        found = low_ref[spare_rank_ref[x * count + i]].astype(jnp.bfloat16)
        spare[pl.ds(i * piece, piece)] = jnp.where(spare_mine_ref[x * count + i] > 0, found, 0)
    rows = core_in.shape[0]

    def part(index, size):
        return pl.ds(pl.multiple_of(index * size, GROUP), size)

    spare_flow.push(spare.at[part(1 - core, rows)], core_in, spare_sems[0:2], (0,), across("core"))
    flows = [early, late]

    def from_z(d):
        for flow in flows:
            flow.from_z(d)

    def from_second(d):
        for flow in flows:
            flow.from_second(d)

    order = distances(depth)
    from_z(order[0])
    spare_flow.arrive(core_in, spare_sems[0:2], (0,))
    held[...] = total(spare[part(core, rows)], core_in[...])
    spare_flow.push(held.at[part(1 - y, rows // 2)], y_in, spare_sems[2:4], (0,), across("y"))
    gains.step()
    from_second(0)
    for i in range(1, depth - 1):
        from_z(order[i])
        if i == 1:
            spare_flow.arrive(y_in, spare_sems[2:4], (0,))
            y_in[...] = total(held[part(y, rows // 2)], y_in[...])
            for e in range(1, depth):
                to = part(lax.rem(z + e, depth), GROUP)
                spare_flow.push(y_in.at[to], z_in.at[e], spare_sems[4:6], (e,), ahead(e))
            gains.step()
        from_second(order[i - 1])
        for flow in flows:
            flow.from_third(([0] + order)[i - 1])
    for d in range(1, depth):
        spare_flow.arrive(z_in.at[d], spare_sems[4:6], (d,))
    whole[me, base] = total(y_in[part(z, GROUP)], *[z_in[d] for d in range(1, depth)])
    loose.begin()
    from_second(order[-1])
    gain_out[...] = gains.result()
    for d in order:
        loose.from_z(d)
    for flow in flows:
        flow.from_third(order[-2])
    for d in range(depth):
        loose.from_second(d)
    for flow in flows:
        flow.from_third(order[-1])
    for d in range(depth):
        loose.from_third(d)
    for flow in flows + [loose]:
        flow.finish()
    spare_flow.drain()

    buffers = stage.shape[0]
    per_chunk = CHUNK // GROUP
    narrow = width // 2
    copies = []
    for index in range(6 * width // CHUNK):
        matrix, first = divmod(index * CHUNK, width)
        slot = index % buffers
        if index >= buffers:
            copies[index - buffers].wait()
        thin = split and matrix < 3
        columns = pl.ds(pl.multiple_of(core * narrow, LANES), narrow) if thin else slice(None)
        count = narrow if thin else width

        def step(i, carry, index=index, slot=slot, columns=columns, count=count):
            for g in range(per_piece):
                at = index * per_chunk + i * per_piece + g
                target = pl.ds(pl.multiple_of(i * piece + g * GROUP, GROUP), GROUP)
                stage[slot, target, pl.ds(0, count)] = whole[block_ref[at], row_ref[at], :, columns]
            return carry

        lax.fori_loop(0, per_chunk // per_piece, step, 0)
        if thin:
            target = outs[0].at[pl.ds(first, CHUNK), pl.ds(matrix * narrow, narrow)]
        elif split:
            target = outs[matrix - 2].at[pl.ds(first, CHUNK)]
        else:
            target = outs[0].at[matrix, pl.ds(first, CHUNK)]
        copies.append(
            pltpu.make_async_copy(stage.at[slot, :, pl.ds(0, count)], target, stage_sem.at[slot])
        )
        copies[-1].start()
    for copy in copies[-buffers:]:
        copy.wait()


def gather_pieces(low, gains, plan, split):
    slots, piece, width = low.shape
    block, row, spare_rank, spare_mine, gain_mine = plan
    chips = lax.axis_size("chip")
    depth = chips // Y_CHIPS
    base = CAPACITY // 2 * piece // GROUP
    shapes = [(width, 3 * (width // 2))] + [(width, width)] * 3 if split else [(6, width, width)]
    lane = SPARE * piece // 4
    buffers = 4
    picked = jnp.where(gain_mine[:, None], gains[: gain_mine.shape[0]].astype(jnp.float32), 0.0)
    padded = jnp.concatenate([picked, jnp.zeros((6, width), jnp.float32)], axis=0)
    vmem = pl.BlockSpec(memory_space=pltpu.VMEM)
    smem = pl.BlockSpec(memory_space=pltpu.SMEM)
    outs = pl.pallas_call(
        functools.partial(gather_kernel, split, base // 4 if split else base // 2),
        in_specs=[smem] * 3 + [vmem] * 3,
        out_specs=[pl.BlockSpec(memory_space=pl.ANY)] * len(shapes) + [vmem],
        out_shape=[jax.ShapeDtypeStruct(s, jnp.bfloat16) for s in shapes]
        + [jax.ShapeDtypeStruct((8, width), jnp.float32)],
        scratch_shapes=[
            pltpu.VMEM((4 * chips, base + 1, GROUP, width), jnp.bfloat16),
            pltpu.VMEM((buffers, CHUNK, width), jnp.bfloat16),
            pltpu.SemaphoreType.DMA((buffers,)),
            pltpu.VMEM((2 * lane, width), jnp.bfloat16),
            pltpu.VMEM((lane, width), jnp.bfloat16),
            pltpu.VMEM((lane // 2, width), jnp.bfloat16),
            pltpu.VMEM((depth, GROUP, width), jnp.bfloat16),
            pltpu.VMEM((lane, width), jnp.bfloat16),
        ]
        + total_scratch(2, depth, width)
        + spread_sems(depth) * 3
        + sem_pair(1)
        + sem_pair(1)
        + sem_pair(depth),
        compiler_params=pltpu.CompilerParams(
            collective_id=0 if split else 1, has_side_effects=True, vmem_limit_bytes=48 << 20
        ),
        cost_estimate=pl.CostEstimate(
            flops=0, bytes_accessed=6 * width * width * 16, transcendentals=0
        ),
    )(
        block.reshape(-1),
        row.reshape(-1),
        spare_rank,
        jnp.broadcast_to(spare_mine[:, None, None], (SPARE, 1, width)),
        low,
        padded,
    )
    return (*outs[:-1], outs[-1][:2].astype(jnp.bfloat16))


def halves(matrices, split):
    if not split:
        return (matrices,)
    width = matrices.shape[1]
    narrow = width // 2
    thin = lax.dynamic_slice_in_dim(matrices[:3], lax.axis_index("core") * narrow, narrow, axis=2)
    side = jnp.concatenate([thin[0], thin[1], thin[2]], axis=1)
    return (side, matrices[3], matrices[4], matrices[5])


def gather_slots(low, gains, owners, split):
    slots, piece, width = low.shape
    low = low.astype(jnp.bfloat16)
    piece_owner, rank = owner_slots(owners, slots)
    rows = slots * piece
    half = -(-(rows // 2 + 1) // GROUP) * GROUP
    filler = jnp.zeros((2 * half - rows - 2, width), jnp.bfloat16)
    packed = jnp.concatenate([low.reshape(rows, width), gains, filler], axis=0)
    share = lax.dynamic_slice_in_dim(packed, lax.axis_index("seq") * half, half, axis=0)
    groups = lax.all_gather(share, ALL, axis=0, tiled=True).reshape(-1, GROUP, width)
    per_owner = 2 * half // GROUP
    base = piece_owner * per_owner + rank * (piece // GROUP)
    index = base[:, None] + jnp.arange(piece // GROUP, dtype=jnp.int32)[None, :]
    matrices = groups[index.reshape(-1)].reshape(6, width, width)
    gain_rows = groups[owners[-2:] * per_owner + rows // GROUP][jnp.arange(2), jnp.arange(2)]
    return (*halves(matrices, split), gain_rows)


def kernels_fit(slots, piece, width):
    chips = lax.axis_size("chip")
    return slots == 2 * CAPACITY and piece == GROUP * (chips // Y_CHIPS) and width % CHUNK == 0


def spare_pieces(owners, slots):
    piece_owner, rank = owner_slots(owners, slots)
    spare = rank >= CAPACITY
    return (piece_owner, rank, spare, jnp.cumsum(spare.astype(jnp.int32)) - 1)


def gather_store(low, gains, owners, split, few):
    if not few:
        return gather_slots(low, gains, owners, split)
    slots, piece, width = low.shape
    dp_pos = lax.axis_index("chip") * 2 + lax.axis_index("core")
    piece_owner, rank, spare, order = spare_pieces(owners, slots)
    half = CAPACITY // 2
    groups = piece // GROUP
    group = jnp.arange(groups, dtype=jnp.int32)[None, :]
    block = jnp.where(
        spare[:, None],
        device_block(group, (order % 2)[:, None], ((order // 2) % 2)[:, None], (order // 4)[:, None]),
        (piece_owner * 2 + rank // half)[:, None],
    )
    row = jnp.where(spare[:, None], half * groups, (rank % half)[:, None] * groups + group)
    labels = jnp.arange(SPARE, dtype=jnp.int32)
    own = (spare & (piece_owner == dp_pos))[None, :] & (order[None, :] == labels[:, None])
    spare_rank = jnp.sum(jnp.where(own, rank[None, :], 0), axis=1)
    spare_mine = jnp.any(own, axis=1).astype(jnp.int32)
    plan = (block, row, spare_rank, spare_mine, owners[-2:] == dp_pos)
    return gather_pieces(low, gains, plan, split)


class Reduce(Flow):
    def __init__(self, first, shard, one, two, three, sems):
        super().__init__()
        self.first = first
        self.other = "y" if first == "x" else "x"
        self.shard = shard
        self.one, self.two, self.three = (one, two, three)
        self.sems = [sems[0:2], sems[2:4], sems[4:6]]

    def start(self, d, b):
        self.push(self.shard(d, b, 1), self.one.at[d, b], self.sems[0], (d, b), across(self.first))

    def from_first(self, d, b):
        here = self.one.at[d, b]
        self.arrive(here, self.sems[0], (d, b))
        here[...] = total(here[...], self.shard(d, b, 0)[...])
        if b:
            self.push(here, self.two.at[d], self.sems[1], (d,), across(self.other))

    def from_second(self, d):
        here = self.two.at[d]
        self.arrive(here, self.sems[1], (d,))
        here[...] = total(here[...], self.one[d, 0])
        if d:
            self.push(here, self.three.at[d], self.sems[2], (d,), ahead(d))

    def result(self):
        depth = place()[4]
        for d in range(1, depth):
            self.arrive(self.three.at[d], self.sems[2], (d,))
        value = total(self.two[0], *[self.three[d] for d in range(1, depth)])
        self.drain()
        return value


def reduce_kernel(
    source_ref,
    spare_ref,
    spare_mine_ref,
    early_ref,
    late_ref,
    gain_ref,
    slot_ref,
    gain_out,
    pieces,
    blocks,
    early_one,
    early_two,
    early_three,
    late_one,
    late_two,
    late_three,
    final,
    pair_in,
    own_in,
    other_in,
    spares,
    gain_sum,
    gain_in,
    load_sem,
    *sems,
):
    z, y, core, x, depth = place()
    narrow = pieces.shape[2]
    groups = late_ref.shape[1]
    per_block = blocks.shape[1]
    cut = early_one.shape[2]
    owned = CAPACITY // 2 * slot_ref.shape[1]
    order = distances(depth)[::-1] + [0]
    loads = []
    for matrix in range(3):
        columns = pl.ds(matrix * narrow, narrow)
        loads.append((early_ref.at[:, :, columns], matrix))
        loads.append((late_ref.at[matrix], matrix + 3))
    loads = [
        pltpu.make_async_copy(source, pieces.at[pl.ds(m * groups, groups)], load_sem.at[m])
        for source, m in loads
    ]
    for load in loads:
        load.start()
    pieces[6 * groups] = jnp.zeros((GROUP, narrow), jnp.bfloat16)
    greet()
    gains = Total(["core", "x", "y"], gain_sum, gain_in, sems[0:2])
    gains.begin(gain_ref[...])
    for load in loads:
        load.wait()

    def block_at(d, swap_y, swap_x):
        return chip_block(
            lax.rem(z + d, depth), 1 - y if swap_y else y, 1 - x if swap_x else x
        )

    early = Reduce(
        "x",
        lambda d, b, a: blocks.at[block_at(d, b, a), pl.ds(0, cut)],
        early_one,
        early_two,
        early_three,
        sems[2:8],
    )
    late = Reduce(
        "y",
        lambda d, b, a: blocks.at[block_at(d, a, b), pl.ds(cut, per_block - cut)],
        late_one,
        late_two,
        late_three,
        sems[8:14],
    )

    def fill(d, swap_y, swap_x):
        block = block_at(d, swap_y, swap_x)

        def step(i, carry):
            for g in range(2):
                blocks[block, 2 * i + g] = pieces[source_ref[block * per_block + 2 * i + g]]
            return carry

        lax.fori_loop(0, per_block // 2, step, 0)

    def start(d, b):
        for flow in (early, late):
            flow.start(d, b)

    fill(order[0], 1, 1)
    start(order[0], 1)
    fill(order[0], 0, 1)
    fill(order[0], 1, 0)
    start(order[0], 0)
    fill(order[0], 0, 0)
    for i, d in enumerate(order):
        later = order[i + 1] if i + 1 < len(order) else None
        if later is not None:
            fill(later, 1, 1)
        for flow in (early, late):
            flow.from_first(d, 1)
        if later is not None:
            start(later, 1)
            fill(later, 0, 1)
            fill(later, 1, 0)
        for flow in (early, late):
            flow.from_first(d, 0)
        if later is not None:
            start(later, 0)
            fill(later, 0, 0)
        if i:
            for flow in (early, late):
                flow.from_second(order[i - 1])
        if i < 3:
            gains.step()
    for flow in (early, late):
        flow.from_second(order[-1])
    final[pl.ds(0, cut)] = early.result()
    final[pl.ds(cut, per_block - cut)] = late.result()

    ends = Flow()
    own_spare = spares.at[z, y, x, core]
    ends.push(final.at[pl.ds((1 - core) * owned, owned)], pair_in, sems[14:16], (0,), across("core"))
    ends.push(final.at[pl.ds(core * owned, owned)], own_in, sems[14:16], (1,), across("x"))
    spares[z, y, x, core] = final[pl.ds(2 * owned, 2)]
    for d in range(1, depth):
        ends.push(own_spare, own_spare, sems[16:18], (d,), ahead(d))
    gain_out[...] = gains.result()
    ends.arrive(pair_in, sems[14:16], (0,))
    ends.push(pair_in, other_in, sems[14:16], (5,), across("x"))
    for d in range(1, depth):
        from_z = spares.at[lax.rem(z - d + depth, depth), y, x, core]
        ends.arrive(from_z, sems[16:18], (d,))
    here = spares.at[:, y, x, core]
    ends.push(here, here, sems[14:16], (2,), across("y"))
    ends.arrive(spares.at[:, 1 - y, x, core], sems[14:16], (2,))
    here = spares.at[:, :, x, core]
    ends.push(here, here, sems[14:16], (3,), across("x"))
    ends.arrive(spares.at[:, :, 1 - x, core], sems[14:16], (3,))
    here = spares.at[:, :, :, core]
    ends.push(here, here, sems[14:16], (4,), across("core"))
    ends.arrive(spares.at[:, :, :, 1 - core], sems[14:16], (4,))
    ends.arrive(own_in, sems[14:16], (1,))
    ends.arrive(other_in, sems[14:16], (5,))
    per_piece = slot_ref.shape[1]
    half = CAPACITY // 2
    own_columns = pl.ds(pl.multiple_of(core * narrow, LANES), narrow)
    other_columns = pl.ds(pl.multiple_of((1 - core) * narrow, LANES), narrow)
    for i in range(half):
        for g in range(per_piece):
            at = i * per_piece + g
            slot_ref[x * half + i, g, :, own_columns] = final[core * owned + at]
            slot_ref[x * half + i, g, :, other_columns] = pair_in[at]
            slot_ref[(1 - x) * half + i, g, :, own_columns] = own_in[at]
            slot_ref[(1 - x) * half + i, g, :, other_columns] = other_in[at]

    def pick(slot, carry):
        for g in range(per_piece):
            at = spare_ref[slot] * per_piece + g
            sub = spares.shape[4]
            chip = lax.div(at, 2 * sub)
            where = (lax.div(chip, Y_CHIPS), lax.rem(chip, Y_CHIPS), lax.rem(lax.div(at, sub), 2))
            for side in range(2):
                found = spares[(*where, side, lax.rem(at, sub))]
                slot_ref[CAPACITY + slot, g, :, pl.ds(side * narrow, narrow)] = jnp.where(
                    spare_mine_ref[slot] > 0, found, 0
                )
        return carry

    lax.fori_loop(0, slot_ref.shape[0] - CAPACITY, pick, 0)
    ends.drain()


def reduce_slots(early, late, gains, owners, slots, piece):
    width = late.shape[1]
    narrow = width // 2
    chips = lax.axis_size("chip")
    depth = chips // Y_CHIPS
    groups = width // GROUP
    per_piece = piece // GROUP
    dp_pos = lax.axis_index("chip") * 2 + lax.axis_index("core")
    piece_owner, rank, spare, order = spare_pieces(owners, slots)
    half = CAPACITY // 2
    labels = jnp.arange(piece_owner.shape[0], dtype=jnp.int32)
    empty = 6 * groups

    def groups_of(match):
        first = jnp.sum(jnp.where(match, labels, 0), axis=-1)[..., None] * per_piece
        groups_at = first + jnp.arange(per_piece, dtype=jnp.int32)
        return jnp.where(jnp.any(match, axis=-1)[..., None], groups_at, empty)

    block = jnp.arange(2 * chips, dtype=jnp.int32)[:, None]
    entry = jnp.arange(CAPACITY, dtype=jnp.int32)[None, :]
    owner_at = block // 2 * 2 + entry // half
    rank_at = block % 2 * half + entry % half
    base_groups = groups_of(
        (piece_owner == owner_at[..., None]) & (rank == rank_at[..., None])
    ).reshape(2 * chips, -1)
    spare_hot = spare & (order == jnp.arange(SPARE, dtype=jnp.int32)[:, None])
    spare_groups = groups_of(spare_hot).reshape(2 * chips, -1)
    source = jnp.concatenate([base_groups, spare_groups], axis=1)
    per_block = source.shape[1]
    mine = (piece_owner == dp_pos) & spare & (order < SPARE)
    slot_hot = mine & (rank == CAPACITY + jnp.arange(slots - CAPACITY, dtype=jnp.int32)[:, None])
    spare_at = jnp.sum(jnp.where(slot_hot, order, 0), axis=1)
    subs = SPARE * per_piece // (2 * chips)

    vmem = pl.BlockSpec(memory_space=pltpu.VMEM)
    smem = pl.BlockSpec(memory_space=pltpu.SMEM)
    hbm = pl.BlockSpec(memory_space=pl.ANY)
    cut = per_block // 4 + 1
    owned = half * per_piece
    padded = jnp.concatenate([gains, jnp.zeros((8 - gains.shape[0], width), jnp.float32)], axis=0)

    def group_block(*shape):
        return pltpu.VMEM(shape + (GROUP, narrow), jnp.bfloat16)

    def flow_blocks(count):
        return [group_block(depth, 2, count), group_block(depth, count), group_block(depth, count)]

    flow_sems = sem_pair(depth, 2) + sem_pair(depth) + sem_pair(depth)
    slot_grad, gain_sum = pl.pallas_call(
        reduce_kernel,
        in_specs=[smem] * 2 + [vmem, hbm, hbm, vmem],
        out_specs=[vmem, vmem],
        out_shape=[
            jax.ShapeDtypeStruct((slots, per_piece, GROUP, width), jnp.bfloat16),
            jax.ShapeDtypeStruct((8, width), jnp.float32),
        ],
        scratch_shapes=[group_block(6 * groups + 1), group_block(2 * chips, per_block)]
        + flow_blocks(cut)
        + flow_blocks(per_block - cut)
        + [
            group_block(per_block),
            group_block(owned),
            group_block(owned),
            group_block(owned),
            group_block(depth, Y_CHIPS, 2, 2, subs),
        ]
        + total_scratch(3, depth, width)[:2]
        + [pltpu.SemaphoreType.DMA((6,))]
        + total_scratch(3, depth, width)[2:]
        + flow_sems
        + flow_sems
        + sem_pair(6)
        + sem_pair(depth),
        compiler_params=pltpu.CompilerParams(
            collective_id=2, has_side_effects=True, vmem_limit_bytes=56 << 20
        ),
        cost_estimate=pl.CostEstimate(
            flops=0, bytes_accessed=6 * width * width * 8, transcendentals=0
        ),
    )(
        source.reshape(-1),
        spare_at,
        jnp.broadcast_to(jnp.any(slot_hot, axis=1).astype(jnp.int32)[:, None, None], (slots - CAPACITY, 1, narrow)),
        early.reshape(groups, GROUP, 3 * narrow),
        late.reshape(3, groups, GROUP, narrow),
        padded,
    )
    return (slot_grad.reshape(slots, piece, width), gain_sum[:2])


def reduce_all(early, late, gains, owners, slots, piece, few):
    if few:
        return reduce_slots(early, late, gains, owners, slots, piece)
    width = late.shape[1]
    narrow = width // 2
    dp_pos = lax.axis_index("chip") * 2 + lax.axis_index("core")
    pieces = owners.shape[0] - 2
    chips = lax.axis_size("chip")
    local = jnp.concatenate([jnp.transpose(early.reshape(width, 3, narrow), (1, 0, 2)), late], axis=0)
    share = lax.psum_scatter(
        local.reshape(6 * width, narrow), ("chip", "seq"), scatter_dimension=0, tiled=True
    )
    sums = lax.all_gather(share, ALL, axis=0, tiled=False).reshape(chips, 2, 2, -1, narrow)
    sums = jnp.transpose(sums, (0, 2, 3, 1, 4)).reshape(pieces, piece, width)
    piece_owner, rank = owner_slots(owners, slots)
    labels = jnp.arange(slots, dtype=jnp.int32)
    match = (piece_owner == dp_pos) & (rank == labels[:, None])
    slot_grad = jnp.where(jnp.any(match, axis=1)[:, None, None], sums[jnp.argmax(match, axis=1)], 0)
    return (slot_grad, lax.psum(gains, ALL))


def adam_kernel(rate_ref, master_ref, first_ref, second_ref, grad_ref, *outs):
    count = master_ref.shape[0]
    for i in range(count):
        new, first_new, second_new = adam_update(
            master_ref[i],
            first_ref[i],
            second_ref[i],
            grad_ref[i].astype(jnp.float32),
            rate_ref[pl.program_id(0) * count + i],
            MATRIX_DECAY,
        )
        outs[0][i] = new
        outs[1][i] = first_new
        outs[2][i] = second_new
        outs[3][i] = new.astype(jnp.bfloat16)


def adam_slots(master, first, second, grad, rate):
    slots, piece, width = master.shape
    count = min(slots, 2)
    block = pl.BlockSpec((count, piece, width), lambda i: (i, 0, 0))
    shape = jax.ShapeDtypeStruct(master.shape, jnp.float32)
    return pl.pallas_call(
        adam_kernel,
        grid=(slots // count,),
        in_specs=[pl.BlockSpec(memory_space=pltpu.SMEM)] + [block] * 4,
        out_specs=[block] * 4,
        out_shape=[shape] * 3 + [jax.ShapeDtypeStruct(master.shape, jnp.bfloat16)],
        compiler_params=pltpu.CompilerParams(vmem_limit_bytes=60 << 20),
        cost_estimate=pl.CostEstimate(
            flops=20 * slots * piece * width,
            bytes_accessed=28 * slots * piece * width,
            transcendentals=slots * piece * width,
        ),
    )(rate, master, first, second, grad)


def local(*arrays):
    owners, weight_store = arrays[3:5]
    if not kernels_fit(*weight_store.shape):
        return step(False, *arrays)
    order = spare_pieces(owners, weight_store.shape[0])[3]
    few = order[-1] < SPARE
    return lax.cond(few, functools.partial(step, True), functools.partial(step, False), *arrays)


def step(
    few,
    tokens,
    cotangent,
    parents,
    owners,
    weight_store,
    gain_store,
    weight_first,
    gain_first,
    weight_second,
    gain_second,
):
    core = lax.axis_index("core")
    dp_pos = lax.axis_index("chip") * 2 + core
    slot_dev, piece, width = weight_store.shape
    pieces = owners.shape[0] - 2
    piece_owner, rank = owner_slots(owners, slot_dev)
    gain_owner = owners[pieces:]
    micro, _, rows, _ = tokens.shape
    half = width // 2
    own_rows = core * rows
    own_columns = core * half

    def mine(value, axis, size, index):
        return lax.dynamic_slice_in_dim(value, index * size, size, axis=axis)

    limit, branch = tail_limits(transposed(parents[:, 0]))
    arrived = moved(tokens[:, 0])
    qkv_weight, out_weight, up_weight, down_weight, gain_low = gather_store(
        weight_store, gain_store.astype(jnp.bfloat16), owners, True, few
    )
    gain_low, arrived, cot = lax.optimization_barrier((gain_low, arrived, cotangent[:, 0]))
    own_tokens = settled(tokens[:, 0], arrived)
    own_cot = transposed(cot)
    other_tokens = partner(own_tokens)

    def by_core(own, other, axis):
        return jnp.where(
            core == 0,
            jnp.concatenate([own, other], axis=axis),
            jnp.concatenate([other, own], axis=axis),
        )

    gain_one = gain_low[0].astype(jnp.float32)
    gain_two = gain_low[1].astype(jnp.float32)

    def unit(values):
        scale = lax.rsqrt(jnp.mean(values * values, axis=-1, keepdims=True) + NORM_EPS)
        return (values * scale, scale)

    normed_one = norm_all(own_tokens, other_tokens, gain_one, core)
    qkv = product(normed_one, qkv_weight, "mtd,de->mte").astype(jnp.bfloat16)
    attended_half, lse = attend(qkv, limit, branch)
    attended = by_core(
        mine(attended_half, 1, rows, core), partner(mine(attended_half, 1, rows, 1 - core)), 2
    )
    residual = own_tokens.astype(jnp.float32)
    hidden_one = residual + product(attended, out_weight, "mti,io->mto")
    unit_two, scale_two = unit(hidden_one)
    normed_two = (unit_two * gain_two).astype(jnp.bfloat16)
    up_rows = product(normed_two, up_weight, "mti,io->mto")
    sigmoid_up = jax.nn.sigmoid(up_rows)
    activated = (up_rows * sigmoid_up).astype(jnp.bfloat16)
    mixed_rows = (hidden_one + product(activated, down_weight, "mti,io->mto")).astype(jnp.bfloat16)
    mixed = transposed(mixed_rows)

    grad_down = product(activated, own_cot, "mti,mto->io")
    grad_hidden = product(own_cot, down_weight, "mto,io->mti")
    grad_up_rows = (grad_hidden * (sigmoid_up * (1.0 + up_rows * (1.0 - sigmoid_up)))).astype(
        jnp.bfloat16
    )
    grad_up = product(normed_two, grad_up_rows, "mti,mto->io")
    grad_normed_two = product(grad_up_rows, up_weight, "mto,io->mti")
    gain_two_grad = jnp.sum(grad_normed_two * unit_two, axis=(0, 1))
    grad_hidden_one = own_cot.astype(jnp.float32) + norm_back(
        grad_normed_two, unit_two, scale_two, gain_two
    )
    branch_grad = grad_hidden_one.astype(jnp.bfloat16)
    grad_out = product(attended, branch_grad, "mti,mto->io")
    late = jnp.stack([grad_out, grad_up, grad_down]).astype(jnp.bfloat16)
    late_back = partner(mine(late, 2, half, 1 - core))

    branch_grad, late = lax.optimization_barrier((branch_grad, late))
    grad_attended = product(branch_grad, out_weight, "mto,io->mti").astype(jnp.bfloat16)
    grad_half = by_core(
        mine(grad_attended, 2, half, core), partner(mine(grad_attended, 2, half, 1 - core)), 1
    )
    grad_qkv_rows = attend_back(qkv, grad_half, attended_half, lse, limit, branch)
    grad_qkv = product(normed_one, grad_qkv_rows, "mti,mto->io")
    early = grad_qkv.astype(jnp.bfloat16)

    grad_normed_part = product(grad_qkv_rows, qkv_weight, "mte,de->mtd").astype(jnp.bfloat16)
    grad_back = partner(mine(grad_normed_part, 1, rows, 1 - core))
    token_rows, gain_one_grad = token_grads(
        grad_normed_part, grad_back, own_tokens, grad_hidden_one, gain_one, core
    )
    token_grad = transposed(token_rows)
    gain_grads = jnp.stack([gain_one_grad, gain_two_grad])
    late = (mine(late, 2, half, core).astype(jnp.float32) + late_back.astype(jnp.float32)).astype(
        jnp.bfloat16
    )

    labels = jnp.arange(slot_dev, dtype=jnp.int32)
    match = (piece_owner[None, :] == dp_pos) & (rank[None, :] == labels[:, None])
    held = jnp.any(match, axis=1)
    piece_of = jnp.sum(jnp.where(match, jnp.arange(pieces, dtype=jnp.int32)[None, :], 0), axis=1)
    slot_grad, gain_sum = reduce_all(early, late, gain_grads, owners, slot_dev, piece, few)
    is_out = held & (piece_of // (width // piece) == 3)
    slot_rate = jnp.where(is_out, RATE_OUT, RATE_QKV).astype(jnp.float32)
    weight_new, weight_first_new, weight_second_new, weight_low = adam_slots(
        weight_store, weight_first, weight_second, slot_grad, slot_rate
    )
    gain_slot_grad = jnp.where((gain_owner == dp_pos)[:, None], gain_sum, 0.0)
    gain_new, gain_first_new, gain_second_new = adam_update(
        gain_store, gain_first, gain_second, gain_slot_grad, RATE_GAIN, 0.0
    )
    weight_copies, gain_copies = gather_store(
        weight_low, gain_new.astype(jnp.bfloat16), owners, False, few
    )
    return (
        mixed[:, None],
        token_grad[:, None],
        weight_new,
        gain_new,
        weight_first_new,
        gain_first_new,
        weight_second_new,
        gain_second_new,
        weight_copies,
        gain_copies,
    )


def solution(mesh):
    dp_count, seq_count = mesh.devices.shape
    fine = Mesh(mesh.devices.reshape(dp_count // 2, 2, seq_count), ALL)
    dp = ("chip", "core")
    rows = P(None, dp, "seq", None)
    store = P(dp, None, None)
    gains = P(dp, None)
    in_specs = (rows, rows, P(None, dp, None), P(), store, gains, store, gains, store, gains)
    out_specs = (rows, rows, store, gains, store, gains, store, gains, P(), P())
    return jax.shard_map(local, mesh=fine, in_specs=in_specs, out_specs=out_specs, check_vma=False)
```

```python
import functools

import jax
import jax.numpy as jnp
from jax import lax
from jax.experimental import pallas as pl
from jax.experimental.pallas import tpu as pltpu
from jax.sharding import Mesh
from jax.sharding import PartitionSpec as P

HEAD = 80
SEG = 32
TRUNK_SEGS = 32
ALWAYS_SEGS = TRUNK_SEGS // 2
STEP = 7
LANES = 128
WINDOW = 256
QUERY_BLOCK = 256
KEY_BLOCK = 512

NORM_EPS = 1e-06
BETA_ONE = 0.5
BETA_TWO = 0.5
ADAM_EPS = 1e-08
MATRIX_DECAY = 0.1
RATE_QKV = 0.03
RATE_OUT = 0.4
RATE_GAIN = 0.4
MASKED = -1e30
SCALE = HEAD**-0.5
LOG2E = 1.4426950408889634
ALL = ("chip", "core", "seq")
NT = (((1,), (1,)), ((), ()))
TN = (((0,), (0,)), ((), ()))


def moved(value):
    chips = lax.axis_size("chip")
    pairs = [(k * 4 + c * 2 + 1 - c, k * 4 + 2 - 2 * c + c) for k in range(chips) for c in range(2)]
    return lax.ppermute(value, ALL, pairs)


def settled(value, arrived):
    return jnp.where(lax.axis_index("core") == lax.axis_index("seq"), value, arrived)


def transposed(value):
    return settled(value, moved(value))


def partner(value):
    return lax.ppermute(value, "core", [(0, 1), (1, 0)])


def owner_slots(owners, slot_dev):
    count = owners.shape[0] - 2
    piece_owner = owners[:count]
    labels = jnp.arange(count, dtype=jnp.int32)
    same = (piece_owner[:, None] == piece_owner[None, :]) & (labels[None, :] < labels[:, None])
    rank = jnp.sum(same.astype(jnp.int32), axis=1)
    return (piece_owner, rank)


def tail_limits(parents):
    up = parents[:, TRUNK_SEGS:]
    leaf = up >= TRUNK_SEGS
    above = jnp.where(leaf, up - TRUNK_SEGS, 0)
    labels = jnp.arange(up.shape[1], dtype=jnp.int32)
    hot = above[:, :, None] == labels[None, None, :]
    upper = jnp.sum(jnp.where(hot, up[:, None, :], 0), axis=2)
    attach = jnp.where(leaf, upper, up)
    limit = (attach + 1) * SEG
    branch = jnp.where(leaf, above, -1)
    return (jnp.repeat(limit, SEG, axis=1), jnp.repeat(branch, SEG, axis=1))


def query_blocks(length):
    trunk = TRUNK_SEGS * SEG
    blocks = []
    for first in range(0, trunk, QUERY_BLOCK):
        parts = [(0, first, "all")] if first else []
        blocks.append((first, QUERY_BLOCK, parts + [(first, QUERY_BLOCK, "causal")]))
    always = ALWAYS_SEGS * SEG
    tail = length - trunk
    blocks.append(
        (trunk, tail, [(0, always, "all"), (always, trunk - always, "trunk"), (trunk, tail, "tail")])
    )
    return blocks


def allowed_pairs(kind, key_first, key, query, limit, branch):
    if kind == "causal":
        return key <= query
    if kind == "trunk":
        return key + key_first < limit
    key_seg = key // SEG
    return ((key_seg == query // SEG) & (key <= query)) | (key_seg == branch)


def head_window(head, width):
    start = pl.multiple_of(
        jnp.minimum((head * HEAD) // LANES, width // LANES - WINDOW // LANES) * LANES, LANES
    )
    lane = lax.broadcasted_iota(jnp.int32, (1, WINDOW), 1) + start
    mine = (lane >= head * HEAD) & (lane < (head + 1) * HEAD)
    return (pl.ds(start, WINDOW), mine)


def scaled_query(rows, mine):
    return jnp.where(mine, rows.astype(jnp.float32) * (SCALE * LOG2E), 0.0).astype(jnp.bfloat16)


def attend_kernel(limit_ref, branch_ref, q_ref, k_ref, v_ref, out_ref, lse_ref):
    head = pl.program_id(1)
    window, mine = head_window(head, q_ref.shape[2])
    stat_lane = lax.broadcasted_iota(jnp.int32, (1, LANES), 1)
    values = jnp.where(mine, v_ref[0, :, window], 1)
    keys_side = k_ref[0, :, window].T

    def score(first, count, parts):
        query = scaled_query(q_ref[0, pl.ds(first, count), window], mine)
        scores = []
        for key_first, keys, kind in parts:
            raw = jnp.dot(
                query, keys_side[:, key_first : key_first + keys], preferred_element_type=jnp.float32
            )
            if kind != "all":
                ok = allowed_pairs(
                    kind,
                    key_first,
                    lax.broadcasted_iota(jnp.int32, (count, keys), 1),
                    lax.broadcasted_iota(jnp.int32, (count, keys), 0),
                    limit_ref[0],
                    branch_ref[0],
                )
                raw = jnp.where(ok, raw, MASKED)
            scores.append(raw)
        return scores

    def weigh(scores):
        top = functools.reduce(jnp.maximum, [jnp.max(s, axis=1, keepdims=True) for s in scores])
        return (top, [jnp.exp2(raw - top).astype(jnp.bfloat16) for raw in scores])

    def collect(weighed, first, count, parts):
        top, weights = weighed
        rows = pl.ds(first, count)
        gained = 0.0
        for weight, (key_first, keys, kind) in zip(weights, parts):
            gained = gained + jnp.dot(
                weight, values[key_first : key_first + keys], preferred_element_type=jnp.float32
            )
        weight_sum = jnp.max(jnp.where(mine, 0.0, gained), axis=1, keepdims=True)
        gained = (gained * (1.0 / weight_sum)).astype(jnp.bfloat16)
        out_ref[0, rows, window] = jnp.where(mine, gained, out_ref[0, rows, window])
        lse_ref[0, rows, :] = jnp.where(
            stat_lane == head, top + jnp.log2(weight_sum), lse_ref[0, rows, :]
        )

    blocks = query_blocks(q_ref.shape[1])
    scores = score(*blocks[0])
    weighed = None
    for i in range(len(blocks)):
        later = score(*blocks[i + 1]) if i + 1 < len(blocks) else None
        before = weighed
        weighed = weigh(scores)
        if i:
            collect(before, *blocks[i - 1])
        scores = later
    collect(weighed, *blocks[-1])


def attend(qkv, limit, branch):
    micro, length, columns = qkv.shape
    width = columns // 3
    heads = width // HEAD
    tail = length - TRUNK_SEGS * SEG

    def part(index):
        return pl.BlockSpec((1, length, width), lambda m, h, index=index: (m, 0, index))

    column = pl.BlockSpec((1, tail, 1), lambda m, h: (m, 0, 0))
    return pl.pallas_call(
        attend_kernel,
        grid=(micro, heads),
        in_specs=[column, column, part(0), part(1), part(2)],
        out_specs=[
            pl.BlockSpec((1, length, width), lambda m, h: (m, 0, 0)),
            pl.BlockSpec((1, length, LANES), lambda m, h: (m, 0, 0)),
        ],
        out_shape=[
            jax.ShapeDtypeStruct((micro, length, width), jnp.bfloat16),
            jax.ShapeDtypeStruct((micro, length, LANES), jnp.float32),
        ],
        compiler_params=pltpu.CompilerParams(vmem_limit_bytes=48 << 20),
        cost_estimate=pl.CostEstimate(
            flops=micro * heads * length * length * WINDOW * 3,
            bytes_accessed=micro * length * width * 8,
            transcendentals=micro * heads * length * length // 2,
        ),
    )(limit[:, :, None], branch[:, :, None], qkv, qkv, qkv)


def attend_back_kernel(
    limit_ref, branch_ref, lse_ref, q_ref, k_ref, v_ref, g_ref, a_ref, out_ref, dk_sum, dv_sum
):
    head = pl.program_id(1)
    width = q_ref.shape[2]
    window, mine = head_window(head, width)

    @pl.when(head == 0)
    def clear():
        dk_sum[...] = jnp.zeros_like(dk_sum)
        dv_sum[...] = jnp.zeros_like(dv_sum)

    lane = lax.broadcasted_iota(jnp.int32, (1, WINDOW), 1)
    after = (head + 1) * HEAD - window.start
    spots = [lane == lax.rem(after + i, WINDOW) for i in range(3)]
    stat_lane = lax.broadcasted_iota(jnp.int32, (1, LANES), 1)
    keys_all = jnp.where(spots[0] | spots[1] | spots[2], 1, k_ref[0, :, window])
    values_all = jnp.where(spots[0] | spots[1], 1, v_ref[0, :, window])

    def less(rows, column, count):
        rest = column
        for spot in spots[:count]:
            piece = rest.astype(jnp.bfloat16).astype(jnp.float32)
            rows = jnp.where(spot, -piece, rows)
            rest = rest - piece
        return rows.astype(jnp.bfloat16)

    def factors(first, count):
        rows = pl.ds(first, count)
        raw_query = q_ref[0, rows, window]
        query = jnp.where(mine, raw_query, 0)
        grad = jnp.where(mine, g_ref[0, rows, window], 0)
        wide_grad = grad.astype(jnp.float32)
        lse = jnp.sum(jnp.where(stat_lane == head, lse_ref[0, rows, :], 0.0), axis=1, keepdims=True)
        row_total = jnp.sum(
            wide_grad * a_ref[0, rows, window].astype(jnp.float32), axis=1, keepdims=True
        )
        query_less = less(scaled_query(raw_query, mine).astype(jnp.float32), lse, 3)
        return (query, grad, query_less, less(wide_grad, row_total, 2))

    def scores(part, block):
        query, grad, query_less, grad_less = block
        return (
            lax.dot_general(keys_all[part], query_less, NT, preferred_element_type=jnp.float32),
            lax.dot_general(values_all[part], grad_less, NT, preferred_element_type=jnp.float32),
        )

    def weigh(found, part, kind):
        raw, grad_prob = found
        prob = jnp.exp2(raw)
        if kind != "all":
            ok = allowed_pairs(
                kind,
                part.start,
                lax.broadcasted_iota(jnp.int32, raw.shape, 0),
                lax.broadcasted_iota(jnp.int32, raw.shape, 1),
                limit_ref[0],
                branch_ref[0],
            )
            prob = jnp.where(ok, prob, 0.0)
        return (prob.astype(jnp.bfloat16), (prob * grad_prob).astype(jnp.bfloat16))

    def collect(weighed, part, block):
        prob, grad_raw = weighed
        query, grad = block[:2]
        dv_sum[part, window] += jnp.dot(prob, grad, preferred_element_type=jnp.float32)
        dk_sum[part, window] += jnp.dot(grad_raw, query, preferred_element_type=jnp.float32)
        return lax.dot_general(grad_raw, keys_all[part], TN, preferred_element_type=jnp.float32)

    units = []
    for first, count, parts in query_blocks(q_ref.shape[1]):
        for key_first, keys, kind in parts:
            for cut in range(key_first, key_first + keys, KEY_BLOCK):
                part = slice(cut, min(cut + KEY_BLOCK, key_first + keys))
                units.append((first, count, part, kind))
    def finish(i, weighed, block, grad_query):
        first, count, part, kind = units[i]
        grad_query = grad_query + collect(weighed, part, block)
        if i + 1 < len(units) and units[i + 1][0] == first:
            return grad_query
        rows = pl.ds(first, count)
        out_ref[0, rows, window] = jnp.where(
            mine, (grad_query * SCALE).astype(jnp.bfloat16), out_ref[0, rows, window]
        )
        return 0.0

    held = {units[0][0]: factors(*units[0][:2])}
    found = scores(units[0][2], held[units[0][0]])
    weighed = None
    grad_query = 0.0
    for i, (first, count, part, kind) in enumerate(units):
        later = None
        if i + 1 < len(units):
            following = units[i + 1]
            if following[0] not in held:
                held[following[0]] = factors(*following[:2])
            later = scores(following[2], held[following[0]])
        before = weighed
        weighed = weigh(found, part, kind)
        if i:
            grad_query = finish(i - 1, before, held[units[i - 1][0]], grad_query)
        found = later
    finish(len(units) - 1, weighed, held[units[-1][0]], grad_query)

    @pl.when(head == pl.num_programs(1) - 1)
    def write():
        out_ref[0, :, pl.ds(width, width)] = (dk_sum[...] * SCALE).astype(jnp.bfloat16)
        out_ref[0, :, pl.ds(2 * width, width)] = dv_sum[...].astype(jnp.bfloat16)


def attend_back(qkv, grad, attended, lse, limit, branch):
    micro, length, columns = qkv.shape
    width = columns // 3
    heads = width // HEAD
    tail = length - TRUNK_SEGS * SEG

    def part(index):
        return pl.BlockSpec((1, length, width), lambda m, h, index=index: (m, 0, index))

    row = pl.BlockSpec((1, 1, tail), lambda m, h: (m, 0, 0))
    return pl.pallas_call(
        attend_back_kernel,
        grid=(micro, heads),
        in_specs=[
            row,
            row,
            pl.BlockSpec((1, length, LANES), lambda m, h: (m, 0, 0)),
            part(0),
            part(1),
            part(2),
            part(0),
            part(0),
        ],
        out_specs=pl.BlockSpec((1, length, columns), lambda m, h: (m, 0, 0)),
        out_shape=jax.ShapeDtypeStruct((micro, length, columns), jnp.bfloat16),
        scratch_shapes=[pltpu.VMEM((length, width), jnp.float32)] * 2,
        compiler_params=pltpu.CompilerParams(vmem_limit_bytes=56 << 20),
        cost_estimate=pl.CostEstimate(
            flops=micro * heads * length * length * WINDOW * 7,
            bytes_accessed=micro * length * width * 14,
            transcendentals=micro * heads * length * length // 2,
        ),
    )(limit[:, None, :], branch[:, None, :], lse, qkv, qkv, qkv, grad, attended)


def norm_back(grad_normed, normed_unit, scale_rows, gain_row):
    scaled_grad = grad_normed * gain_row
    return scale_rows * (
        scaled_grad - normed_unit * jnp.mean(scaled_grad * normed_unit, axis=-1, keepdims=True)
    )


def norm_kernel(core_ref, own_ref, other_ref, gain_ref, out_ref):
    def write(source):
        rows = source[0].astype(jnp.float32)
        scale = lax.rsqrt(jnp.mean(rows * rows, axis=-1, keepdims=True) + NORM_EPS)
        out_ref[0] = (rows * scale * gain_ref[...]).astype(jnp.bfloat16)

    @pl.when(pl.program_id(1) == 0)
    def own():
        write(own_ref)

    @pl.when(pl.program_id(1) == 1)
    def other():
        write(other_ref)


def norm_all(own, other, gain, core):
    micro, rows, width = own.shape
    cuts = 2
    block = (1, rows // cuts, width)

    def source(which):
        return lambda m, s, i, core_ref: (m, jnp.where(s == which, i, (cuts - 1) * (1 - which)), 0)

    def target(m, s, i, core_ref):
        return (m, jnp.where(s == 0, core_ref[0], 1 - core_ref[0]) * cuts + i, 0)

    return pl.pallas_call(
        norm_kernel,
        grid_spec=pltpu.PrefetchScalarGridSpec(
            num_scalar_prefetch=1,
            grid=(micro, 2, cuts),
            in_specs=[
                pl.BlockSpec(block, source(0)),
                pl.BlockSpec(block, source(1)),
                pl.BlockSpec((1, width), lambda m, s, i, core_ref: (0, 0)),
            ],
            out_specs=pl.BlockSpec(block, target),
        ),
        out_shape=jax.ShapeDtypeStruct((micro, 2 * rows, width), jnp.bfloat16),
        compiler_params=pltpu.CompilerParams(vmem_limit_bytes=48 << 20),
        cost_estimate=pl.CostEstimate(
            flops=8 * micro * rows * width, bytes_accessed=8 * micro * rows * width, transcendentals=0
        ),
    )(core.reshape(1), own, other, gain[None])


def token_grad_kernel(core_ref, part_ref, back_ref, token_ref, hidden_ref, gain_ref, out_ref, sum_ref):
    rows = token_ref[0].astype(jnp.float32)
    scale = lax.rsqrt(jnp.mean(rows * rows, axis=-1, keepdims=True) + NORM_EPS)
    unit = rows * scale
    grad = part_ref[0].astype(jnp.float32) + back_ref[0].astype(jnp.float32)
    back = norm_back(grad, unit, scale, gain_ref[...])
    out_ref[0] = (hidden_ref[0] + back).astype(jnp.bfloat16)

    @pl.when((pl.program_id(0) == 0) & (pl.program_id(1) == 0))
    def clear():
        sum_ref[...] = jnp.zeros_like(sum_ref)

    sum_ref[0:1] += jnp.sum(grad * unit, axis=0, keepdims=True)


def token_grads(part, back, tokens, hidden, gain, core):
    micro, rows, width = tokens.shape
    cuts = 2
    block = (1, rows // cuts, width)
    here = pl.BlockSpec(block, lambda m, i, core_ref: (m, i, 0))
    token_rows, sums = pl.pallas_call(
        token_grad_kernel,
        grid_spec=pltpu.PrefetchScalarGridSpec(
            num_scalar_prefetch=1,
            grid=(micro, cuts),
            in_specs=[
                pl.BlockSpec(block, lambda m, i, core_ref: (m, core_ref[0] * cuts + i, 0)),
                here,
                here,
                here,
                pl.BlockSpec((1, width), lambda m, i, core_ref: (0, 0)),
            ],
            out_specs=[here, pl.BlockSpec((8, width), lambda m, i, core_ref: (0, 0))],
        ),
        out_shape=[
            jax.ShapeDtypeStruct(tokens.shape, jnp.bfloat16),
            jax.ShapeDtypeStruct((8, width), jnp.float32),
        ],
        compiler_params=pltpu.CompilerParams(vmem_limit_bytes=48 << 20),
        cost_estimate=pl.CostEstimate(
            flops=20 * micro * rows * width, bytes_accessed=12 * micro * rows * width, transcendentals=0
        ),
    )(core.reshape(1), part, back, tokens, hidden, gain[None])
    return (token_rows, sums[0])


def adam_update(master, first, second, grad, rate, decay):
    first_new = BETA_ONE * first + (1.0 - BETA_ONE) * grad
    second_new = BETA_TWO * second + (1.0 - BETA_TWO) * grad * grad
    fix_one = 1.0 - BETA_ONE**STEP
    fix_two = 1.0 - BETA_TWO**STEP
    step_size = first_new / fix_one / (jnp.sqrt(second_new / fix_two) + ADAM_EPS)
    return (master - rate * (step_size + decay * master), first_new, second_new)


def product(left, right, spec):
    return jnp.einsum(spec, left, right, preferred_element_type=jnp.float32)


Y_CHIPS = 2
CAPACITY = 8
SPARE = 8
GROUP = 16
CHUNK = 256
MESH_IDS = pl.DeviceIdType.MESH


def place():
    chip = lax.axis_index("chip")
    return (
        chip // Y_CHIPS,
        lax.rem(chip, Y_CHIPS),
        lax.axis_index("core"),
        lax.axis_index("seq"),
        lax.axis_size("chip") // Y_CHIPS,
    )


def at_z(z, y):
    return {"chip": z * Y_CHIPS + y}


def ahead(d):
    z, y, core, x, depth = place()
    return at_z(lax.rem(z + d, depth), y)


def across(axis):
    z, y, core, x, _ = place()
    return {"y": at_z(z, 1 - y), "x": {"seq": 1 - x}, "core": {"core": 1 - core}}[axis]


def greet():
    depth = place()[4]
    barrier = pltpu.get_barrier_semaphore()
    peers = [ahead(d) for d in range(1, depth)] + [across("y"), across("x"), across("core")]
    for peer in peers:
        pl.semaphore_signal(barrier, inc=1, device_id=peer, device_id_type=MESH_IDS)
    pl.semaphore_wait(barrier, len(peers))


def sem_pair(*shape):
    return [pltpu.SemaphoreType.DMA(shape), pltpu.SemaphoreType.DMA(shape)]


def remote(source, target, sems, index, device):
    return pltpu.make_async_remote_copy(
        src_ref=source,
        dst_ref=target,
        send_sem=sems[0].at[index],
        recv_sem=sems[1].at[index],
        device_id=device,
        device_id_type=MESH_IDS,
    )


def total(*parts):
    return functools.reduce(jnp.add, [p.astype(jnp.float32) for p in parts]).astype(jnp.bfloat16)


class Flow:
    def __init__(self):
        self.sent = []

    def push(self, source, target, sems, index, device):
        copy = remote(source, target, sems, index, device)
        copy.start()
        self.sent.append(copy)

    def arrive(self, here, sems, index):
        remote(here, here, sems, index, across("core")).wait_recv()

    def drain(self):
        for copy in self.sent:
            copy.wait_send()


class Total(Flow):
    def __init__(self, axes, sums, inbox, sems):
        super().__init__()
        self.axes, self.sums, self.inbox, self.sems = (axes, sums, inbox, sems)
        self.done = 0

    def begin(self, value):
        self.sums[0] = value
        self.push(self.sums.at[0], self.inbox.at[0], self.sems, (0,), across(self.axes[0]))

    def step(self):
        i = self.done
        self.done += 1
        self.arrive(self.inbox.at[i], self.sems, (i,))
        self.sums[i + 1] = self.sums[i] + self.inbox[i]
        here = self.sums.at[i + 1]
        if i + 1 < len(self.axes):
            self.push(here, self.inbox.at[i + 1], self.sems, (i + 1,), across(self.axes[i + 1]))
            return
        for d in range(1, place()[4]):
            self.push(here, self.inbox.at[i + d], self.sems, (i + d,), ahead(d))

    def result(self):
        last = len(self.axes)
        value = self.sums[last]
        for d in range(1, place()[4]):
            self.arrive(self.inbox.at[last - 1 + d], self.sems, (last - 1 + d,))
            value = value + self.inbox[last - 1 + d]
        self.drain()
        return value


def distances(depth):
    return sorted(range(1, depth), key=lambda d: min(d, depth - d))


def total_scratch(axes, depth, width):
    return [
        pltpu.VMEM((axes + 1, 8, width), jnp.float32),
        pltpu.VMEM((axes + depth - 1, 8, width), jnp.float32),
    ] + sem_pair(axes + depth - 1)


def spread_sems(depth):
    return sem_pair(depth) + sem_pair(depth) + sem_pair(depth, 2) + sem_pair(depth, 4)


class Spread(Flow):
    def __init__(self, window, second, sems, keep=None):
        super().__init__()
        self.window = window
        self.keep = keep
        self.second = second
        self.third = "x" if second == "y" else "y"
        self.sems = [(sems[2 * i], sems[2 * i + 1]) for i in range(4)]

    def where(self, d, second=False, third=False, other_core=False):
        z, y, core, x, depth = place()
        if second if self.second == "y" else third:
            y = 1 - y
        if third if self.second == "y" else second:
            x = 1 - x
        return self.window(lax.rem(z - d + depth, depth), y, 1 - core if other_core else core, x)

    def forward(self, stage, index, block, device):
        self.push(block, block, self.sems[stage], index, device)

    def came(self, d, second, third, other_core, sems, index):
        block = self.where(d, second, third, other_core)
        self.arrive(block, sems, index)
        self.store(block, d, second, third, other_core)
        return block

    def store(self, block, *who):
        if self.keep:
            window, self.window = (self.window, self.keep[0])
            target = self.where(*who)
            self.window = window
            pltpu.make_async_copy(block, target, self.keep[1]).start()

    def begin(self):
        self.waiting = distances(place()[4])
        self.along_z()
        self.store(self.where(0), 0)
        self.onward(0)

    def along_z(self):
        if self.waiting:
            d = self.waiting.pop(0)
            self.forward(0, (d,), self.where(0), ahead(d))

    def onward(self, d):
        block = self.where(d)
        self.forward(1, (d,), block, across(self.second))
        self.forward(2, (d, 0), block, across(self.third))
        self.forward(3, (d, 0), block, across("core"))

    def from_z(self, d):
        self.came(d, False, False, False, self.sems[0], (d,))
        self.along_z()
        self.onward(d)

    def from_second(self, d):
        block = self.came(d, True, False, False, self.sems[1], (d,))
        self.forward(2, (d, 1), block, across(self.third))
        self.forward(3, (d, 2), block, across("core"))

    def from_third(self, d):
        for second in range(2):
            block = self.came(d, bool(second), True, False, self.sems[2], (d, second))
            self.forward(3, (d, 2 * second + 1), block, across("core"))

    def finish(self):
        for d in range(place()[4]):
            for second in range(2):
                for third in range(2):
                    index = (d, 2 * second + third)
                    self.came(d, bool(second), bool(third), True, self.sems[3], index)
        self.drain()


def device_block(z, y, core, x):
    return ((z * Y_CHIPS + y) * 2 + core) * 2 + x


def chip_block(z, y, x):
    return (z * Y_CHIPS + y) * 2 + x


def gather_kernel(
    split,
    cut,
    block_ref,
    row_ref,
    spare_rank_ref,
    spare_mine_ref,
    low_ref,
    gain_ref,
    *refs,
):
    outs = refs[: 4 if split else 1]
    gain_out, whole, stage, stage_sem, spare, core_in, y_in, z_in, held = refs[len(outs) : len(outs) + 9]
    gain_sum, gain_in = refs[len(outs) + 9 : len(outs) + 11]
    sems = refs[len(outs) + 11 :]
    z, y, core, x, depth = place()
    piece, width = low_ref.shape[1:]
    half = CAPACITY // 2
    base = half * piece // GROUP
    me = device_block(z, y, core, x)
    per_piece = piece // GROUP
    for i in range(base):
        source = pl.ds(i % per_piece * GROUP, GROUP)
        whole[me, i] = low_ref[x * half + i // per_piece, source].astype(jnp.bfloat16)
    greet()

    def window(held, first, count):
        return lambda *who: held.at[device_block(*who), pl.ds(first, count)]

    def flow(first, count, second, at):
        keep = None if split else (window(outs[0], first, count), stage_sem.at[0])
        return Spread(window(whole, first, count), second, sems[at : at + 8], keep)

    early = flow(0, cut, "y", 2)
    late = flow(cut, base - cut, "x", 10)
    loose = flow(base, 1, "x", 18)
    gains = Total(["core", "y"], gain_sum, gain_in, sems[0:2])
    spare_sems = sems[26:32]
    spare_flow = Flow()
    early.begin()
    late.begin()
    gains.begin(gain_ref[...])
    count = SPARE // 2
    for i in range(count):
        found = low_ref[spare_rank_ref[x * count + i]].astype(jnp.bfloat16)
        spare[pl.ds(i * piece, piece)] = jnp.where(spare_mine_ref[x * count + i] > 0, found, 0)
    rows = core_in.shape[0]

    def part(index, size):
        return pl.ds(pl.multiple_of(index * size, GROUP), size)

    spare_flow.push(spare.at[part(1 - core, rows)], core_in, spare_sems[0:2], (0,), across("core"))
    flows = [early, late]

    def from_z(d):
        for flow in flows:
            flow.from_z(d)

    def from_second(d):
        for flow in flows:
            flow.from_second(d)

    order = distances(depth)
    from_z(order[0])
    spare_flow.arrive(core_in, spare_sems[0:2], (0,))
    held[...] = total(spare[part(core, rows)], core_in[...])
    spare_flow.push(held.at[part(1 - y, rows // 2)], y_in, spare_sems[2:4], (0,), across("y"))
    gains.step()
    from_second(0)
    for i in range(1, depth - 1):
        from_z(order[i])
        if i == 1:
            spare_flow.arrive(y_in, spare_sems[2:4], (0,))
            y_in[...] = total(held[part(y, rows // 2)], y_in[...])
            for e in range(1, depth):
                to = part(lax.rem(z + e, depth), GROUP)
                spare_flow.push(y_in.at[to], z_in.at[e], spare_sems[4:6], (e,), ahead(e))
            gains.step()
        from_second(order[i - 1])
        for flow in flows:
            flow.from_third(([0] + order)[i - 1])
    for d in range(1, depth):
        spare_flow.arrive(z_in.at[d], spare_sems[4:6], (d,))
    whole[me, base] = total(y_in[part(z, GROUP)], *[z_in[d] for d in range(1, depth)])
    loose.begin()
    from_second(order[-1])
    gain_out[...] = gains.result()
    for d in order:
        loose.from_z(d)
    for flow in flows:
        flow.from_third(order[-2])
    for d in range(depth):
        loose.from_second(d)
    for flow in flows:
        flow.from_third(order[-1])
    for d in range(depth):
        loose.from_third(d)
    for flow in flows + [loose]:
        flow.finish()
    spare_flow.drain()
    if not split:
        pltpu.make_async_copy(whole, outs[0], stage_sem.at[0]).wait()
        return

    buffers = stage.shape[0]
    per_chunk = CHUNK // GROUP
    narrow = width // 2
    copies = []
    for index in range(6 * width // CHUNK):
        matrix, first = divmod(index * CHUNK, width)
        slot = index % buffers
        if index >= buffers:
            copies[index - buffers].wait()
        thin = matrix < 3
        columns = pl.ds(pl.multiple_of(core * narrow, LANES), narrow) if thin else slice(None)
        count = narrow if thin else width

        def step(i, carry, index=index, slot=slot, columns=columns, count=count):
            for g in range(per_piece):
                at = index * per_chunk + i * per_piece + g
                target = pl.ds(pl.multiple_of(i * piece + g * GROUP, GROUP), GROUP)
                stage[slot, target, pl.ds(0, count)] = whole[block_ref[at], row_ref[at], :, columns]
            return carry

        lax.fori_loop(0, per_chunk // per_piece, step, 0)
        if thin:
            target = outs[0].at[pl.ds(first, CHUNK), pl.ds(matrix * narrow, narrow)]
        else:
            target = outs[matrix - 2].at[pl.ds(first, CHUNK)]
        copies.append(
            pltpu.make_async_copy(stage.at[slot, :, pl.ds(0, count)], target, stage_sem.at[slot])
        )
        copies[-1].start()
    for copy in copies[-buffers:]:
        copy.wait()


def gather_pieces(low, gains, plan, split):
    slots, piece, width = low.shape
    block, row, spare_rank, spare_mine, gain_mine, loose = plan
    chips = lax.axis_size("chip")
    depth = chips // Y_CHIPS
    base = CAPACITY // 2 * piece // GROUP
    whole = (4 * chips, base + 1, GROUP, width)
    shapes = [(width, 3 * (width // 2))] + [(width, width)] * 3 if split else [whole]
    lane = SPARE * piece // 4
    buffers = 4
    picked = jnp.where(gain_mine[:, None], gains[: gain_mine.shape[0]].astype(jnp.float32), 0.0)
    padded = jnp.concatenate([picked, jnp.zeros((6, width), jnp.float32)], axis=0)
    vmem = pl.BlockSpec(memory_space=pltpu.VMEM)
    smem = pl.BlockSpec(memory_space=pltpu.SMEM)
    outs = pl.pallas_call(
        functools.partial(gather_kernel, split, 3 * base // 16 if split else base // 2),
        in_specs=[smem] * 3 + [vmem] * 3,
        out_specs=[pl.BlockSpec(memory_space=pl.ANY)] * len(shapes) + [vmem],
        out_shape=[jax.ShapeDtypeStruct(s, jnp.bfloat16) for s in shapes]
        + [jax.ShapeDtypeStruct((8, width), jnp.float32)],
        scratch_shapes=[
            pltpu.VMEM(whole, jnp.bfloat16),
            pltpu.VMEM((buffers, CHUNK, width), jnp.bfloat16),
            pltpu.SemaphoreType.DMA((buffers,)),
            pltpu.VMEM((2 * lane, width), jnp.bfloat16),
            pltpu.VMEM((lane, width), jnp.bfloat16),
            pltpu.VMEM((lane // 2, width), jnp.bfloat16),
            pltpu.VMEM((depth, GROUP, width), jnp.bfloat16),
            pltpu.VMEM((lane, width), jnp.bfloat16),
        ]
        + total_scratch(2, depth, width)
        + spread_sems(depth) * 3
        + sem_pair(1)
        + sem_pair(1)
        + sem_pair(depth),
        compiler_params=pltpu.CompilerParams(
            collective_id=0 if split else 1, has_side_effects=True, vmem_limit_bytes=48 << 20
        ),
        cost_estimate=pl.CostEstimate(
            flops=0, bytes_accessed=6 * width * width * 16, transcendentals=0
        ),
    )(
        block.reshape(-1),
        row.reshape(-1),
        spare_rank,
        jnp.broadcast_to(spare_mine[:, None, None], (SPARE, 1, width)),
        low,
        padded,
    )
    gain_rows = outs[-1][:2].astype(jnp.bfloat16)
    if split:
        return (*outs[:-1], gain_rows)
    return (place_pieces(outs[0], block, row, loose, piece), gain_rows)


def place_kernel(piece_groups, block_ref, row_ref, loose_ref, whole_ref, out_ref, held, load_sem, store_sem):
    buffers, groups = held.shape[:2]
    per_chunk = groups // piece_groups
    chunks = out_ref.shape[0]

    def load(chunk):
        slot = lax.rem(chunk, buffers)
        for i in range(per_chunk):
            piece = chunk * per_chunk + i
            at = piece * piece_groups

            @pl.when(loose_ref[piece] == 0)
            def one():
                source = whole_ref.at[block_ref[at], pl.ds(row_ref[at], piece_groups)]
                target = held.at[slot, pl.ds(i * piece_groups, piece_groups)]
                pltpu.make_async_copy(source, target, load_sem.at[slot]).start()

            @pl.when(loose_ref[piece] != 0)
            def several():
                for g in range(piece_groups):
                    source = whole_ref.at[block_ref[at + g], row_ref[at + g]]
                    target = held.at[slot, i * piece_groups + g]
                    pltpu.make_async_copy(source, target, load_sem.at[slot]).start()

    def store(chunk):
        slot = lax.rem(chunk, buffers)
        return pltpu.make_async_copy(held.at[slot], out_ref.at[chunk], store_sem.at[slot])

    for chunk in range(buffers - 1):
        load(chunk)

    def step(chunk, carry):
        slot = lax.rem(chunk, buffers)
        pltpu.make_async_copy(out_ref.at[chunk], held.at[slot], load_sem.at[slot]).wait()
        store(chunk).start()

        @pl.when(chunk + buffers - 1 < chunks)
        def more():
            @pl.when(chunk > 0)
            def free():
                store(chunk - 1).wait()

            load(chunk + buffers - 1)

        return carry

    lax.fori_loop(0, chunks, step, 0)
    for chunk in range(chunks - buffers, chunks):
        store(chunk).wait()


def place_pieces(whole, block, row, loose, piece):
    width = whole.shape[3]
    groups = CHUNK // GROUP
    chunks = 6 * width // CHUNK
    buffers = 6
    placed = pl.pallas_call(
        functools.partial(place_kernel, piece // GROUP),
        grid_spec=pltpu.PrefetchScalarGridSpec(
            num_scalar_prefetch=3,
            grid=(1,),
            in_specs=[pl.BlockSpec(memory_space=pl.ANY)],
            out_specs=pl.BlockSpec(memory_space=pl.ANY),
            scratch_shapes=[
                pltpu.VMEM((buffers, groups, GROUP, width), jnp.bfloat16),
                pltpu.SemaphoreType.DMA((buffers,)),
                pltpu.SemaphoreType.DMA((buffers,)),
            ],
        ),
        out_shape=jax.ShapeDtypeStruct((chunks, groups, GROUP, width), jnp.bfloat16),
        compiler_params=pltpu.CompilerParams(vmem_limit_bytes=60 << 20),
        cost_estimate=pl.CostEstimate(
            flops=0, bytes_accessed=24 * width * width, transcendentals=0
        ),
    )(block.reshape(-1), row.reshape(-1), loose, whole)
    return placed.reshape(6, width, width)


def halves(matrices, split):
    if not split:
        return (matrices,)
    width = matrices.shape[1]
    narrow = width // 2
    thin = lax.dynamic_slice_in_dim(matrices[:3], lax.axis_index("core") * narrow, narrow, axis=2)
    side = jnp.concatenate([thin[0], thin[1], thin[2]], axis=1)
    return (side, matrices[3], matrices[4], matrices[5])


def gather_slots(low, gains, owners, split):
    slots, piece, width = low.shape
    low = low.astype(jnp.bfloat16)
    piece_owner, rank = owner_slots(owners, slots)
    rows = slots * piece
    half = -(-(rows // 2 + 1) // GROUP) * GROUP
    filler = jnp.zeros((2 * half - rows - 2, width), jnp.bfloat16)
    packed = jnp.concatenate([low.reshape(rows, width), gains, filler], axis=0)
    share = lax.dynamic_slice_in_dim(packed, lax.axis_index("seq") * half, half, axis=0)
    groups = lax.all_gather(share, ALL, axis=0, tiled=True).reshape(-1, GROUP, width)
    per_owner = 2 * half // GROUP
    base = piece_owner * per_owner + rank * (piece // GROUP)
    index = base[:, None] + jnp.arange(piece // GROUP, dtype=jnp.int32)[None, :]
    matrices = groups[index.reshape(-1)].reshape(6, width, width)
    gain_rows = groups[owners[-2:] * per_owner + rows // GROUP][jnp.arange(2), jnp.arange(2)]
    return (*halves(matrices, split), gain_rows)


def kernels_fit(slots, piece, width):
    chips = lax.axis_size("chip")
    return slots == 2 * CAPACITY and piece == GROUP * (chips // Y_CHIPS) and width % CHUNK == 0


def spare_pieces(owners, slots):
    piece_owner, rank = owner_slots(owners, slots)
    spare = rank >= CAPACITY
    return (piece_owner, rank, spare, jnp.cumsum(spare.astype(jnp.int32)) - 1)


def gather_store(low, gains, owners, split, few):
    if not few:
        return gather_slots(low, gains, owners, split)
    slots, piece, width = low.shape
    dp_pos = lax.axis_index("chip") * 2 + lax.axis_index("core")
    piece_owner, rank, spare, order = spare_pieces(owners, slots)
    half = CAPACITY // 2
    groups = piece // GROUP
    group = jnp.arange(groups, dtype=jnp.int32)[None, :]
    block = jnp.where(
        spare[:, None],
        device_block(group, (order % 2)[:, None], ((order // 2) % 2)[:, None], (order // 4)[:, None]),
        (piece_owner * 2 + rank // half)[:, None],
    )
    row = jnp.where(spare[:, None], half * groups, (rank % half)[:, None] * groups + group)
    labels = jnp.arange(SPARE, dtype=jnp.int32)
    own = (spare & (piece_owner == dp_pos))[None, :] & (order[None, :] == labels[:, None])
    spare_rank = jnp.sum(jnp.where(own, rank[None, :], 0), axis=1)
    spare_mine = jnp.any(own, axis=1).astype(jnp.int32)
    loose = spare.astype(jnp.int32)
    plan = (block, row, spare_rank, spare_mine, owners[-2:] == dp_pos, loose)
    return gather_pieces(low, gains, plan, split)


class Reduce(Flow):
    def __init__(self, first, shard, one, two, three, sems):
        super().__init__()
        self.first = first
        self.other = "y" if first == "x" else "x"
        self.shard = shard
        self.one, self.two, self.three = (one, two, three)
        self.sems = [sems[0:2], sems[2:4], sems[4:6]]

    def start(self, d, b):
        self.push(self.shard(d, b, 1), self.one.at[d, b], self.sems[0], (d, b), across(self.first))

    def from_first(self, d, b):
        here = self.one.at[d, b]
        self.arrive(here, self.sems[0], (d, b))
        here[...] = total(here[...], self.shard(d, b, 0)[...])
        if b:
            self.push(here, self.two.at[d], self.sems[1], (d,), across(self.other))

    def from_second(self, d):
        here = self.two.at[d]
        self.arrive(here, self.sems[1], (d,))
        here[...] = total(here[...], self.one[d, 0])
        if d:
            self.push(here, self.three.at[d], self.sems[2], (d,), ahead(d))

    def result(self):
        depth = place()[4]
        for d in range(1, depth):
            self.arrive(self.three.at[d], self.sems[2], (d,))
        value = total(self.two[0], *[self.three[d] for d in range(1, depth)])
        self.drain()
        return value


def reduce_kernel(
    source_ref,
    spare_ref,
    spare_mine_ref,
    early_ref,
    late_ref,
    gain_ref,
    slot_ref,
    gain_out,
    pieces,
    blocks,
    early_one,
    early_two,
    early_three,
    late_one,
    late_two,
    late_three,
    final,
    pair_in,
    own_in,
    other_in,
    spares,
    gain_sum,
    gain_in,
    load_sem,
    *sems,
):
    z, y, core, x, depth = place()
    narrow = pieces.shape[2]
    groups = late_ref.shape[1]
    per_block = blocks.shape[1]
    cut = early_one.shape[2]
    owned = CAPACITY // 2 * slot_ref.shape[1]
    order = distances(depth)[::-1] + [0]
    loads = []
    for matrix in range(3):
        columns = pl.ds(matrix * narrow, narrow)
        loads.append((early_ref.at[:, :, columns], matrix))
        loads.append((late_ref.at[matrix], matrix + 3))
    loads = [
        pltpu.make_async_copy(source, pieces.at[pl.ds(m * groups, groups)], load_sem.at[m])
        for source, m in loads
    ]
    for load in loads:
        load.start()
    pieces[6 * groups] = jnp.zeros((GROUP, narrow), jnp.bfloat16)
    greet()
    gains = Total(["core", "x", "y"], gain_sum, gain_in, sems[0:2])
    gains.begin(gain_ref[...])
    for load in loads:
        load.wait()

    def block_at(d, swap_y, swap_x):
        return chip_block(
            lax.rem(z + d, depth), 1 - y if swap_y else y, 1 - x if swap_x else x
        )

    early = Reduce(
        "x",
        lambda d, b, a: blocks.at[block_at(d, b, a), pl.ds(0, cut)],
        early_one,
        early_two,
        early_three,
        sems[2:8],
    )
    late = Reduce(
        "y",
        lambda d, b, a: blocks.at[block_at(d, a, b), pl.ds(cut, per_block - cut)],
        late_one,
        late_two,
        late_three,
        sems[8:14],
    )

    def fill(d, swap_y, swap_x):
        block = block_at(d, swap_y, swap_x)

        def step(i, carry):
            for g in range(2):
                blocks[block, 2 * i + g] = pieces[source_ref[block * per_block + 2 * i + g]]
            return carry

        lax.fori_loop(0, per_block // 2, step, 0)

    def start(d, b):
        for flow in (early, late):
            flow.start(d, b)

    fill(order[0], 1, 1)
    start(order[0], 1)
    fill(order[0], 0, 1)
    fill(order[0], 1, 0)
    start(order[0], 0)
    fill(order[0], 0, 0)
    for i, d in enumerate(order):
        later = order[i + 1] if i + 1 < len(order) else None
        if later is not None:
            fill(later, 1, 1)
        for flow in (early, late):
            flow.from_first(d, 1)
        if later is not None:
            start(later, 1)
            fill(later, 0, 1)
            fill(later, 1, 0)
        for flow in (early, late):
            flow.from_first(d, 0)
        if later is not None:
            start(later, 0)
            fill(later, 0, 0)
        if i:
            for flow in (early, late):
                flow.from_second(order[i - 1])
        if i < 3:
            gains.step()
    for flow in (early, late):
        flow.from_second(order[-1])
    final[pl.ds(0, cut)] = early.result()
    final[pl.ds(cut, per_block - cut)] = late.result()

    ends = Flow()
    own_spare = spares.at[z, y, x, core]
    ends.push(final.at[pl.ds((1 - core) * owned, owned)], pair_in, sems[14:16], (0,), across("core"))
    ends.push(final.at[pl.ds(core * owned, owned)], own_in, sems[14:16], (1,), across("x"))
    spares[z, y, x, core] = final[pl.ds(2 * owned, 2)]
    for d in range(1, depth):
        ends.push(own_spare, own_spare, sems[16:18], (d,), ahead(d))
    gain_out[...] = gains.result()
    ends.arrive(pair_in, sems[14:16], (0,))
    ends.push(pair_in, other_in, sems[14:16], (5,), across("x"))
    for d in range(1, depth):
        from_z = spares.at[lax.rem(z - d + depth, depth), y, x, core]
        ends.arrive(from_z, sems[16:18], (d,))
    here = spares.at[:, y, x, core]
    ends.push(here, here, sems[14:16], (2,), across("y"))
    ends.arrive(spares.at[:, 1 - y, x, core], sems[14:16], (2,))
    here = spares.at[:, :, x, core]
    ends.push(here, here, sems[14:16], (3,), across("x"))
    ends.arrive(spares.at[:, :, 1 - x, core], sems[14:16], (3,))
    here = spares.at[:, :, :, core]
    ends.push(here, here, sems[14:16], (4,), across("core"))
    ends.arrive(spares.at[:, :, :, 1 - core], sems[14:16], (4,))
    ends.arrive(own_in, sems[14:16], (1,))
    ends.arrive(other_in, sems[14:16], (5,))
    per_piece = slot_ref.shape[1]
    half = CAPACITY // 2
    own_columns = pl.ds(pl.multiple_of(core * narrow, LANES), narrow)
    other_columns = pl.ds(pl.multiple_of((1 - core) * narrow, LANES), narrow)
    for i in range(half):
        for g in range(per_piece):
            at = i * per_piece + g
            slot_ref[x * half + i, g, :, own_columns] = final[core * owned + at]
            slot_ref[x * half + i, g, :, other_columns] = pair_in[at]
            slot_ref[(1 - x) * half + i, g, :, own_columns] = own_in[at]
            slot_ref[(1 - x) * half + i, g, :, other_columns] = other_in[at]

    def pick(slot, carry):
        for g in range(per_piece):
            at = spare_ref[slot] * per_piece + g
            sub = spares.shape[4]
            chip = lax.div(at, 2 * sub)
            where = (lax.div(chip, Y_CHIPS), lax.rem(chip, Y_CHIPS), lax.rem(lax.div(at, sub), 2))
            for side in range(2):
                found = spares[(*where, side, lax.rem(at, sub))]
                slot_ref[CAPACITY + slot, g, :, pl.ds(side * narrow, narrow)] = jnp.where(
                    spare_mine_ref[slot] > 0, found, 0
                )
        return carry

    lax.fori_loop(0, slot_ref.shape[0] - CAPACITY, pick, 0)
    ends.drain()


def reduce_slots(early, late, gains, owners, slots, piece):
    width = late.shape[1]
    narrow = width // 2
    chips = lax.axis_size("chip")
    depth = chips // Y_CHIPS
    groups = width // GROUP
    per_piece = piece // GROUP
    dp_pos = lax.axis_index("chip") * 2 + lax.axis_index("core")
    piece_owner, rank, spare, order = spare_pieces(owners, slots)
    half = CAPACITY // 2
    labels = jnp.arange(piece_owner.shape[0], dtype=jnp.int32)
    empty = 6 * groups

    def groups_of(match):
        first = jnp.sum(jnp.where(match, labels, 0), axis=-1)[..., None] * per_piece
        groups_at = first + jnp.arange(per_piece, dtype=jnp.int32)
        return jnp.where(jnp.any(match, axis=-1)[..., None], groups_at, empty)

    block = jnp.arange(2 * chips, dtype=jnp.int32)[:, None]
    entry = jnp.arange(CAPACITY, dtype=jnp.int32)[None, :]
    owner_at = block // 2 * 2 + entry // half
    rank_at = block % 2 * half + entry % half
    base_groups = groups_of(
        (piece_owner == owner_at[..., None]) & (rank == rank_at[..., None])
    ).reshape(2 * chips, -1)
    spare_hot = spare & (order == jnp.arange(SPARE, dtype=jnp.int32)[:, None])
    spare_groups = groups_of(spare_hot).reshape(2 * chips, -1)
    source = jnp.concatenate([base_groups, spare_groups], axis=1)
    per_block = source.shape[1]
    mine = (piece_owner == dp_pos) & spare & (order < SPARE)
    slot_hot = mine & (rank == CAPACITY + jnp.arange(slots - CAPACITY, dtype=jnp.int32)[:, None])
    spare_at = jnp.sum(jnp.where(slot_hot, order, 0), axis=1)
    subs = SPARE * per_piece // (2 * chips)

    vmem = pl.BlockSpec(memory_space=pltpu.VMEM)
    smem = pl.BlockSpec(memory_space=pltpu.SMEM)
    hbm = pl.BlockSpec(memory_space=pl.ANY)
    cut = per_block // 6 + 1
    owned = half * per_piece
    padded = jnp.concatenate([gains, jnp.zeros((8 - gains.shape[0], width), jnp.float32)], axis=0)

    def group_block(*shape):
        return pltpu.VMEM(shape + (GROUP, narrow), jnp.bfloat16)

    def flow_blocks(count):
        return [group_block(depth, 2, count), group_block(depth, count), group_block(depth, count)]

    flow_sems = sem_pair(depth, 2) + sem_pair(depth) + sem_pair(depth)
    slot_grad, gain_sum = pl.pallas_call(
        reduce_kernel,
        in_specs=[smem] * 2 + [vmem, hbm, hbm, vmem],
        out_specs=[vmem, vmem],
        out_shape=[
            jax.ShapeDtypeStruct((slots, per_piece, GROUP, width), jnp.bfloat16),
            jax.ShapeDtypeStruct((8, width), jnp.float32),
        ],
        scratch_shapes=[group_block(6 * groups + 1), group_block(2 * chips, per_block)]
        + flow_blocks(cut)
        + flow_blocks(per_block - cut)
        + [
            group_block(per_block),
            group_block(owned),
            group_block(owned),
            group_block(owned),
            group_block(depth, Y_CHIPS, 2, 2, subs),
        ]
        + total_scratch(3, depth, width)[:2]
        + [pltpu.SemaphoreType.DMA((6,))]
        + total_scratch(3, depth, width)[2:]
        + flow_sems
        + flow_sems
        + sem_pair(6)
        + sem_pair(depth),
        compiler_params=pltpu.CompilerParams(
            collective_id=2, has_side_effects=True, vmem_limit_bytes=56 << 20
        ),
        cost_estimate=pl.CostEstimate(
            flops=0, bytes_accessed=6 * width * width * 8, transcendentals=0
        ),
    )(
        source.reshape(-1),
        spare_at,
        jnp.broadcast_to(jnp.any(slot_hot, axis=1).astype(jnp.int32)[:, None, None], (slots - CAPACITY, 1, narrow)),
        early.reshape(groups, GROUP, 3 * narrow),
        late.reshape(3, groups, GROUP, narrow),
        padded,
    )
    return (slot_grad.reshape(slots, piece, width), gain_sum[:2])


def reduce_all(early, late, gains, owners, slots, piece, few):
    if few:
        return reduce_slots(early, late, gains, owners, slots, piece)
    width = late.shape[1]
    narrow = width // 2
    dp_pos = lax.axis_index("chip") * 2 + lax.axis_index("core")
    pieces = owners.shape[0] - 2
    chips = lax.axis_size("chip")
    local = jnp.concatenate([jnp.transpose(early.reshape(width, 3, narrow), (1, 0, 2)), late], axis=0)
    share = lax.psum_scatter(
        local.reshape(6 * width, narrow), ("chip", "seq"), scatter_dimension=0, tiled=True
    )
    sums = lax.all_gather(share, ALL, axis=0, tiled=False).reshape(chips, 2, 2, -1, narrow)
    sums = jnp.transpose(sums, (0, 2, 3, 1, 4)).reshape(pieces, piece, width)
    piece_owner, rank = owner_slots(owners, slots)
    labels = jnp.arange(slots, dtype=jnp.int32)
    match = (piece_owner == dp_pos) & (rank == labels[:, None])
    slot_grad = jnp.where(jnp.any(match, axis=1)[:, None, None], sums[jnp.argmax(match, axis=1)], 0)
    return (slot_grad, lax.psum(gains, ALL))


def adam_kernel(rate_ref, master_ref, first_ref, second_ref, grad_ref, *outs):
    count = master_ref.shape[0]
    for i in range(count):
        new, first_new, second_new = adam_update(
            master_ref[i],
            first_ref[i],
            second_ref[i],
            grad_ref[i].astype(jnp.float32),
            rate_ref[pl.program_id(0) * count + i],
            MATRIX_DECAY,
        )
        outs[0][i] = new
        outs[1][i] = first_new
        outs[2][i] = second_new
        outs[3][i] = new.astype(jnp.bfloat16)


def adam_slots(master, first, second, grad, rate):
    slots, piece, width = master.shape
    count = min(slots, 2)
    block = pl.BlockSpec((count, piece, width), lambda i: (i, 0, 0))
    shape = jax.ShapeDtypeStruct(master.shape, jnp.float32)
    return pl.pallas_call(
        adam_kernel,
        grid=(slots // count,),
        in_specs=[pl.BlockSpec(memory_space=pltpu.SMEM)] + [block] * 4,
        out_specs=[block] * 4,
        out_shape=[shape] * 3 + [jax.ShapeDtypeStruct(master.shape, jnp.bfloat16)],
        compiler_params=pltpu.CompilerParams(vmem_limit_bytes=60 << 20),
        cost_estimate=pl.CostEstimate(
            flops=20 * slots * piece * width,
            bytes_accessed=28 * slots * piece * width,
            transcendentals=slots * piece * width,
        ),
    )(rate, master, first, second, grad)


def local(*arrays):
    owners, weight_store = arrays[3:5]
    if not kernels_fit(*weight_store.shape):
        return step(False, *arrays)
    order = spare_pieces(owners, weight_store.shape[0])[3]
    few = order[-1] < SPARE
    return lax.cond(few, functools.partial(step, True), functools.partial(step, False), *arrays)


def step(
    few,
    tokens,
    cotangent,
    parents,
    owners,
    weight_store,
    gain_store,
    weight_first,
    gain_first,
    weight_second,
    gain_second,
):
    core = lax.axis_index("core")
    dp_pos = lax.axis_index("chip") * 2 + core
    slot_dev, piece, width = weight_store.shape
    pieces = owners.shape[0] - 2
    piece_owner, rank = owner_slots(owners, slot_dev)
    gain_owner = owners[pieces:]
    micro, _, rows, _ = tokens.shape
    half = width // 2
    own_rows = core * rows
    own_columns = core * half

    def mine(value, axis, size, index):
        return lax.dynamic_slice_in_dim(value, index * size, size, axis=axis)

    limit, branch = tail_limits(transposed(parents[:, 0]))
    arrived = moved(tokens[:, 0])
    qkv_weight, out_weight, up_weight, down_weight, gain_low = gather_store(
        weight_store, gain_store.astype(jnp.bfloat16), owners, True, few
    )
    gain_low, arrived, cot = lax.optimization_barrier((gain_low, arrived, cotangent[:, 0]))
    own_tokens = settled(tokens[:, 0], arrived)
    own_cot = transposed(cot)
    other_tokens = partner(own_tokens)

    def by_core(own, other, axis):
        return jnp.where(
            core == 0,
            jnp.concatenate([own, other], axis=axis),
            jnp.concatenate([other, own], axis=axis),
        )

    gain_one = gain_low[0].astype(jnp.float32)
    gain_two = gain_low[1].astype(jnp.float32)

    def unit(values):
        scale = lax.rsqrt(jnp.mean(values * values, axis=-1, keepdims=True) + NORM_EPS)
        return (values * scale, scale)

    normed_one = norm_all(own_tokens, other_tokens, gain_one, core)
    qkv = product(normed_one, qkv_weight, "mtd,de->mte").astype(jnp.bfloat16)
    attended_half, lse = attend(qkv, limit, branch)
    attended = by_core(
        mine(attended_half, 1, rows, core), partner(mine(attended_half, 1, rows, 1 - core)), 2
    )
    residual = own_tokens.astype(jnp.float32)
    hidden_one = residual + product(attended, out_weight, "mti,io->mto")
    unit_two, scale_two = unit(hidden_one)
    normed_two = (unit_two * gain_two).astype(jnp.bfloat16)
    up_rows = product(normed_two, up_weight, "mti,io->mto")
    sigmoid_up = jax.nn.sigmoid(up_rows)
    activated = (up_rows * sigmoid_up).astype(jnp.bfloat16)
    mixed_rows = (hidden_one + product(activated, down_weight, "mti,io->mto")).astype(jnp.bfloat16)
    mixed = transposed(mixed_rows)

    grad_down = product(activated, own_cot, "mti,mto->io")
    grad_hidden = product(own_cot, down_weight, "mto,io->mti")
    grad_up_rows = (grad_hidden * (sigmoid_up * (1.0 + up_rows * (1.0 - sigmoid_up)))).astype(
        jnp.bfloat16
    )
    grad_up = product(normed_two, grad_up_rows, "mti,mto->io")
    grad_normed_two = product(grad_up_rows, up_weight, "mto,io->mti")
    gain_two_grad = jnp.sum(grad_normed_two * unit_two, axis=(0, 1))
    grad_hidden_one = own_cot.astype(jnp.float32) + norm_back(
        grad_normed_two, unit_two, scale_two, gain_two
    )
    branch_grad = grad_hidden_one.astype(jnp.bfloat16)
    grad_out = product(attended, branch_grad, "mti,mto->io")
    late = jnp.stack([grad_out, grad_up, grad_down]).astype(jnp.bfloat16)
    late_back = partner(mine(late, 2, half, 1 - core))

    branch_grad, late = lax.optimization_barrier((branch_grad, late))
    grad_attended = product(branch_grad, out_weight, "mto,io->mti").astype(jnp.bfloat16)
    grad_half = by_core(
        mine(grad_attended, 2, half, core), partner(mine(grad_attended, 2, half, 1 - core)), 1
    )
    grad_qkv_rows = attend_back(qkv, grad_half, attended_half, lse, limit, branch)
    grad_qkv = product(normed_one, grad_qkv_rows, "mti,mto->io")
    early = grad_qkv.astype(jnp.bfloat16)

    grad_normed_part = product(grad_qkv_rows, qkv_weight, "mte,de->mtd").astype(jnp.bfloat16)
    grad_back = partner(mine(grad_normed_part, 1, rows, 1 - core))
    token_rows, gain_one_grad = token_grads(
        grad_normed_part, grad_back, own_tokens, grad_hidden_one, gain_one, core
    )
    token_grad = transposed(token_rows)
    gain_grads = jnp.stack([gain_one_grad, gain_two_grad])
    late = (mine(late, 2, half, core).astype(jnp.float32) + late_back.astype(jnp.float32)).astype(
        jnp.bfloat16
    )

    labels = jnp.arange(slot_dev, dtype=jnp.int32)
    match = (piece_owner[None, :] == dp_pos) & (rank[None, :] == labels[:, None])
    held = jnp.any(match, axis=1)
    piece_of = jnp.sum(jnp.where(match, jnp.arange(pieces, dtype=jnp.int32)[None, :], 0), axis=1)
    slot_grad, gain_sum = reduce_all(early, late, gain_grads, owners, slot_dev, piece, few)
    is_out = held & (piece_of // (width // piece) == 3)
    slot_rate = jnp.where(is_out, RATE_OUT, RATE_QKV).astype(jnp.float32)
    weight_new, weight_first_new, weight_second_new, weight_low = adam_slots(
        weight_store, weight_first, weight_second, slot_grad, slot_rate
    )
    gain_slot_grad = jnp.where((gain_owner == dp_pos)[:, None], gain_sum, 0.0)
    gain_new, gain_first_new, gain_second_new = adam_update(
        gain_store, gain_first, gain_second, gain_slot_grad, RATE_GAIN, 0.0
    )
    weight_copies, gain_copies = gather_store(
        weight_low, gain_new.astype(jnp.bfloat16), owners, False, few
    )
    return (
        mixed[:, None],
        token_grad[:, None],
        weight_new,
        gain_new,
        weight_first_new,
        gain_first_new,
        weight_second_new,
        gain_second_new,
        weight_copies,
        gain_copies,
    )


def solution(mesh):
    dp_count, seq_count = mesh.devices.shape
    fine = Mesh(mesh.devices.reshape(dp_count // 2, 2, seq_count), ALL)
    dp = ("chip", "core")
    rows = P(None, dp, "seq", None)
    store = P(dp, None, None)
    gains = P(dp, None)
    in_specs = (rows, rows, P(None, dp, None), P(), store, gains, store, gains, store, gains)
    out_specs = (rows, rows, store, gains, store, gains, store, gains, P(), P())
    return jax.shard_map(local, mesh=fine, in_specs=in_specs, out_specs=out_specs, check_vma=False)
```
